32 devices in a mesh: grp: 2 (over y), blk: 4 (over z), head: 2 (over x), sub: 2 (over core).
Axes of the slice: x: 2, y: 2, z: 4, core: 2. Of those that a mesh axis runs over, the one named last changes fastest.
Arguments:
- queries: bfloat16 [4096, 4096], P(('grp', 'blk', 'head', 'sub')), parts along dimension 0, may hold values from -46 to 46
- keys: bfloat16 [4096, 4096], P(('grp', 'blk', 'head', 'sub')), parts along dimension 0, may hold values from -4 to 4
- values: bfloat16 [4096, 4096], P(('grp', 'blk', 'head', 'sub')), parts along dimension 0, may hold values from -6 to 6
- block_lists: int32 [32, 16, 8], replicated, may hold values from 0 to 15, as said below
Outputs:
- attended: bfloat16 [4096, 4096], P(('grp', 'blk', 'head', 'sub')), parts along dimension 0
The draws below stay inside these ranges and needn't reach their ends.
There are 2 independent parts, one for each index of `grp`. The reference program is written for one: setup_inputs(seed, part) draws one part's arguments, and reference() takes and returns one part's arrays. A program takes and returns all parts, laid end to end along the dimension named above; an argument that names none is the same for every part. Nothing has to cross between parts.
Inputs may be any that keep to these rules, and one draw needn't show every extreme that they name: `block_lists`: the first entry of every list is the query tile itself; entries may repeat. Tiles are numbered frame by frame, 4 to a frame. In each head either all entries lie in the query tile's frame or the frames next to it, or all entries have the query tile's position within its frame.
All inputs are finite; a program needn't handle non-finite values.
Results may differ from the reference program's by a relative error of at most 0.0065.
Values may be sent and summed in bfloat16 or wider, within the bound.
No kernel may reach another device: no remote copies, remote signals or barrier semaphores. Data moves between devices by JAX's collectives and lax.ppermute only.
A program may use at most 64 MiB of HBM per device.

```python
import math
import jax
import jax.numpy as jnp
from jax import lax

HEADS = 32
HEAD_DIM = 128
TILE = 128
LIST = 8
FRAME_TILES = 4
SEQ = 2048
QTILES = 16


def draw_pair(key):
    col_count = HEADS * HEAD_DIM
    seed_query, seed_keys = jax.random.split(jax.random.fold_in(key, 11), 2)
    query_draw = jnp.clip(jax.random.normal(seed_query, (SEQ, col_count), jnp.float32), -4.0, 4.0)
    keys_draw = jnp.clip(jax.random.normal(seed_keys, (SEQ, col_count), jnp.float32), -4.0, 4.0)
    return (query_draw, keys_draw)


def draw_queries(key, part):
    query_draw, keys_draw = draw_pair(key)
    return query_draw.astype(jnp.bfloat16)


def draw_keys(key, part):
    query_draw, keys_draw = draw_pair(key)
    return keys_draw.astype(jnp.bfloat16)


def draw_block_lists(key, part):
    seed_one, seed_two, seed_three, seed_four = jax.random.split(jax.random.fold_in(key, 23), 4)
    frame_count = QTILES // FRAME_TILES
    shape_all = (HEADS, QTILES, LIST)
    pattern = jax.random.randint(seed_one, (HEADS, 1, 1), 0, 2)
    tile_index = jnp.arange(QTILES, dtype=jnp.int32)[None, :, None]
    frame_no = tile_index // FRAME_TILES
    slot_no = tile_index % FRAME_TILES
    frame_step = jax.random.randint(seed_two, shape_all, -1, 2)
    near_frame = jnp.clip(frame_no + frame_step, 0, frame_count - 1)
    near_slot = jax.random.randint(seed_three, shape_all, 0, FRAME_TILES)
    spatial_tile = near_frame * FRAME_TILES + near_slot
    far_frame = jax.random.randint(seed_four, shape_all, 0, frame_count)
    temporal_tile = far_frame * FRAME_TILES + slot_no
    chosen = jnp.where(pattern == 1, temporal_tile, spatial_tile)
    first_col = jnp.arange(LIST, dtype=jnp.int32)[None, None, :] == 0
    return jnp.where(first_col, tile_index, chosen).astype(jnp.int32)


def block_levels(stream_key, dims, shards, low, largest):
    factor_of = 1.0
    for position, shards_of in shards:
        heights = jax.random.uniform(jax.random.fold_in(jax.random.fold_in(stream_key, 6), position), (shards_of,), jnp.float32, low / len(shards), largest / len(shards))
        factor_of = factor_of * jnp.repeat(jnp.exp(heights), dims[position] // shards_of).reshape((-1,) + (1,) * (len(dims) - 1 - position))
    return factor_of


def gaussian(stream_key, extent, width, reach, cuts=(), kind=jnp.bfloat16):
    gain = block_levels(stream_key, extent, cuts, -0.22, 0.18) if cuts else 1.0
    result = jax.random.normal(stream_key, extent, jnp.float32) * width * gain
    return jnp.minimum(jnp.maximum(result, -reach), reach).astype(kind)


def setup_inputs(seed: int = 0, part: int = 0) -> dict:
    splits = jax.random.split(jax.random.key(seed), 5)
    part_splits = jax.random.split(jax.random.fold_in(splits[4], part), 5)
    return {
        "queries": draw_queries(jax.random.fold_in(jax.random.fold_in(splits[4], part), 71), part),
        "keys": draw_keys(jax.random.fold_in(jax.random.fold_in(splits[4], part), 71), part),
        "values": gaussian(part_splits[2], (SEQ, HEADS * HEAD_DIM), 1.0, 6.0, ((0, 16),)),
        "block_lists": draw_block_lists(jax.random.fold_in(splits[4], 71), part),
    }


def reference(queries, keys, values, block_lists):
    tile_ids = jnp.arange(QTILES, dtype=jnp.int32)
    tile_mask = jnp.any(block_lists[:, :, :, None] == tile_ids, axis=2)
    score_scale = 1.0 / math.sqrt(HEAD_DIM)

    def one_head(head_no):
        col_start = (head_no * HEAD_DIM).astype(jnp.int32)
        q_head = lax.dynamic_slice_in_dim(queries, col_start, HEAD_DIM, 1)
        k_head = lax.dynamic_slice_in_dim(keys, col_start, HEAD_DIM, 1)
        v_head = lax.dynamic_slice_in_dim(values, col_start, HEAD_DIM, 1)
        allowed = jnp.repeat(jnp.repeat(tile_mask[head_no], TILE, axis=0), TILE, axis=1)
        scores = jnp.dot(q_head, k_head.T, preferred_element_type=jnp.float32) * score_scale
        row_top = lax.optimization_barrier(jnp.max(jnp.where(allowed, scores, -jnp.inf), axis=1, keepdims=True))
        weights = jnp.where(allowed, jnp.exp(scores - row_top), 0.0)
        row_total = lax.optimization_barrier(jnp.sum(weights, axis=1, keepdims=True))
        numerator = jnp.dot(weights.astype(jnp.bfloat16), v_head, preferred_element_type=jnp.float32)
        return (numerator / row_total).astype(jnp.bfloat16)
    heads_out = lax.map(one_head, jnp.arange(HEADS, dtype=jnp.int32))
    return jnp.transpose(heads_out, (1, 0, 2)).reshape(SEQ, HEADS * HEAD_DIM)
```

```python
import functools
import math

import jax
import jax.numpy as jnp
from jax import lax
from jax.experimental import pallas as pl
from jax.experimental.pallas import tpu as pltpu
from jax.sharding import PartitionSpec as P

HEADS = 32
HEAD_DIM = 128
TILE = 128
FRAME_TILES = 4


NEG_FLOOR = -1e30


def query_rows(block_lists, first_head, heads_here, query_tokens):
    tile_ids = jnp.arange(block_lists.shape[1], dtype=jnp.int32)
    lists_local = lax.dynamic_slice_in_dim(block_lists, first_head, heads_here, 0)
    tile_mask = jnp.any(lists_local[:, :, :, None] == tile_ids, axis=2).astype(jnp.bfloat16)
    query_onehot = ((query_tokens // TILE)[:, None] == tile_ids[None, :]).astype(jnp.bfloat16)
    listed = jnp.einsum("qi,hij->hqj", query_onehot, tile_mask, preferred_element_type=jnp.float32)
    return listed.astype(jnp.bfloat16)


def attend_block(state_now, key_block, value_block, allowed, query_local, score_scale):
    top_old, total_old, accum_old = state_now
    scores = (
        jnp.einsum("qhd,khd->hqk", query_local, key_block, preferred_element_type=jnp.float32)
        * score_scale
    )
    top_new = jnp.maximum(top_old, jnp.max(jnp.where(allowed, scores, NEG_FLOOR), axis=2))
    factor = jnp.exp(top_old - top_new)
    weights = jnp.where(allowed, jnp.exp(scores - top_new[:, :, None]), 0.0)
    total_new = total_old * factor + jnp.sum(weights, axis=2)
    product = jnp.einsum(
        "hqk,khd->qhd",
        weights.astype(jnp.bfloat16),
        value_block,
        preferred_element_type=jnp.float32,
    )
    accum_new = accum_old * jnp.transpose(factor)[:, :, None] + product
    return (top_new, total_new, accum_new)


def make_step(query_local, listed_rows, key_token, block_len, tile_total):
    score_scale = 1.0 / math.sqrt(HEAD_DIM)
    tile_ids = jnp.arange(tile_total, dtype=jnp.int32)

    def fold_step(state_now, piece, first_row):
        key_piece, value_piece = piece
        block_count = key_piece.shape[0] // block_len

        def one_block(block_index, state_in):
            key_block = lax.dynamic_slice_in_dim(key_piece, block_index * block_len, block_len, 0)
            value_block = lax.dynamic_slice_in_dim(
                value_piece, block_index * block_len, block_len, 0
            )
            positions = block_index * block_len + jnp.arange(block_len, dtype=jnp.int32)
            key_tiles = key_token(positions) // TILE
            key_onehot = (tile_ids[:, None] == key_tiles[None, :]).astype(jnp.bfloat16)
            allowed = (
                jnp.einsum(
                    "hqj,jk->hqk", listed_rows, key_onehot, preferred_element_type=jnp.float32
                )
                > 0.5
            )
            result = attend_block(
                state_in, key_block, value_block, allowed, query_local, score_scale
            )
            return result

        return lax.fori_loop(0, block_count, one_block, state_now)

    return fold_step


def start_state(heads_here, block_len):
    top_all = jnp.full((heads_here, block_len), NEG_FLOOR, jnp.float32)
    total_all = jnp.zeros((heads_here, block_len), jnp.float32)
    accum_all = jnp.zeros((block_len, heads_here, HEAD_DIM), jnp.float32)
    return (top_all, total_all, accum_all)


def normalize(state_end):
    top_all, total_all, accum_all = state_end
    return (accum_all / jnp.transpose(total_all)[:, :, None]).astype(jnp.bfloat16)


def gathered_plan(queries, keys, values, block_lists):
    row_count, col_count = queries.shape
    n_head = lax.axis_size("head")
    n_sub = lax.axis_size("sub")
    blk_index = lax.axis_index("blk")
    head_index = lax.axis_index("head")
    sub_index = lax.axis_index("sub")
    tile_total = block_lists.shape[1]
    heads_here = HEADS // (n_head * n_sub)
    block_len = row_count * n_head * n_sub

    def inward(tensor):
        return tensor.reshape(1, 1, row_count, n_head, n_sub, heads_here * HEAD_DIM)

    query_six, keys_six, values_six = (
        lax.all_to_all(
            lax.all_to_all(inward(queries), "head", split_axis=3, concat_axis=1, tiled=True),
            "sub",
            split_axis=4,
            concat_axis=0,
            tiled=True,
        ),
        lax.all_to_all(
            lax.all_to_all(inward(keys), "head", split_axis=3, concat_axis=1, tiled=True),
            "sub",
            split_axis=4,
            concat_axis=0,
            tiled=True,
        ),
        lax.all_to_all(
            lax.all_to_all(inward(values), "head", split_axis=3, concat_axis=1, tiled=True),
            "sub",
            split_axis=4,
            concat_axis=0,
            tiled=True,
        ),
    )
    query_local = query_six.reshape(block_len, heads_here, HEAD_DIM)
    keys_local = keys_six.reshape(block_len, heads_here, HEAD_DIM)
    values_local = values_six.reshape(block_len, heads_here, HEAD_DIM)

    def key_token(positions):
        source_dev = positions // block_len
        within = positions % block_len
        sub_source = within // (n_head * row_count)
        head_source = within // row_count % n_head
        offset = within % row_count
        return ((source_dev * n_head + head_source) * n_sub + sub_source) * row_count + offset

    query_tokens = key_token(blk_index * block_len + jnp.arange(block_len, dtype=jnp.int32))
    first_head = (head_index * n_sub + sub_index) * heads_here
    listed_rows = query_rows(block_lists, first_head, heads_here, query_tokens)
    fold_step = make_step(query_local, listed_rows, key_token, block_len, tile_total)
    state_end = fold_step(
        start_state(heads_here, block_len),
        (
            lax.all_gather(keys_local, "blk", axis=0, tiled=True),
            lax.all_gather(values_local, "blk", axis=0, tiled=True),
        ),
        jnp.int32(0),
    )
    result_rows = normalize(state_end)
    attended = result_rows.reshape(n_sub, n_head, row_count, 1, 1, heads_here * HEAD_DIM)
    returned = lax.all_to_all(
        lax.all_to_all(attended, "head", split_axis=1, concat_axis=3, tiled=True),
        "sub",
        split_axis=0,
        concat_axis=4,
        tiled=True,
    )
    return returned.reshape(row_count, col_count)


MESH_TAIL = ("head", "sub")
EXP2_SCALE = math.log2(math.e) / math.sqrt(HEAD_DIM)
VMEM_LIMIT = 32 * 1024 * 1024


class Plan:
    def __init__(self, heads, frames, slots, tiles, entries):
        self.heads, self.frames, self.slots = heads, frames, slots
        self.tiles, self.entries = tiles, entries
        self.count_at = 2 * heads
        self.frame_at = 2 * heads + 2
        self.slot_at = 2 * heads + 3


def fill_order(plan, kind, table_ref, order_ref):
    def clear(p, _):
        order_ref[p] = 0
        return 0

    def place(h, _):
        order_ref[table_ref[kind * plan.heads + h]] = h
        return 0

    lax.fori_loop(0, plan.heads + 1, clear, 0)
    lax.fori_loop(0, plan.heads, place, 0)


def head_columns(head):
    return pl.ds(pl.multiple_of(head * HEAD_DIM, HEAD_DIM), HEAD_DIM)


def temporal_group(plan, table_ref, step):
    return lax.rem(table_ref[plan.frame_at] + step, plan.frames)


def spatial_group(plan, table_ref, step):
    return table_ref[plan.slot_at] ^ step


def pack_temporal_kernel(plan, count, table_ref, q_ref, k_ref, v_ref, *rest):
    outs, order_ref = rest[:-1], rest[-1]
    fill_order(plan, 0, table_ref, order_ref)
    for step, out_ref in enumerate(outs):
        group = temporal_group(plan, table_ref, step)

        def one(index, _, group=group, out_ref=out_ref):
            columns = head_columns(order_ref[index * plan.frames + group])
            out_ref[index, 0] = q_ref[:, columns]
            out_ref[index, 1] = k_ref[:, columns]
            out_ref[index, 2] = v_ref[:, columns]
            return 0

        lax.fori_loop(0, count, one, 0)


def pack_spatial_kernel(plan, count, table_ref, q_ref, k_ref, v_ref, *rest):
    outs, order_ref = rest[:-1], rest[-1]
    fill_order(plan, 1, table_ref, order_ref)
    for step in range(plan.slots):
        kv_ref, out_ref = outs[step], outs[plan.slots + step]
        group = spatial_group(plan, table_ref, step)

        def one(index, _, group=group, kv_ref=kv_ref, out_ref=out_ref):
            columns = head_columns(order_ref[index * plan.slots + group])
            kv_ref[index, 0] = k_ref[:, columns]
            kv_ref[index, 1] = v_ref[:, columns]
            out_ref[index] = q_ref[:, columns]
            return 0

        lax.fori_loop(0, count, one, 0)


def softmax_tiles(query, key_tiles, value_tiles, biases):
    scores = [
        lax.dot_general(query, key, (((1,), (1,)), ((), ())), preferred_element_type=jnp.float32)
        + bias
        for key, bias in zip(key_tiles, biases)
    ]
    top = jnp.max(functools.reduce(jnp.maximum, scores), axis=1, keepdims=True)
    weights = [jnp.exp2((score - top) * EXP2_SCALE) for score in scores]
    total = jnp.sum(functools.reduce(jnp.add, weights), axis=1, keepdims=True)
    accum = functools.reduce(
        jnp.add,
        [
            jnp.dot(weight.astype(jnp.bfloat16), value, preferred_element_type=jnp.float32)
            for weight, value in zip(weights, value_tiles)
        ],
    )
    return (accum / total).astype(jnp.bfloat16)


def temporal_kernel(plan, count, table_ref, lists_ref, *rest):
    frames = plan.frames
    tiles, outs, order_ref = rest[:frames], rest[frames : 2 * frames], rest[-1]
    fill_order(plan, 0, table_ref, order_ref)
    frame, slot = table_ref[plan.frame_at], table_ref[plan.slot_at]
    held = [lax.rem(frame + frames - step, frames) for step in range(frames)]

    def one(index, _):
        head = order_ref[index * frames + frame]
        keys = [tiles[step][index, 1] for step in range(frames)]
        values = [tiles[step][index, 2] for step in range(frames)]
        for step in range(frames):
            first = (held[step] * plan.slots + slot) * plan.entries
            listed = jnp.int32(0)
            for entry in range(plan.entries):
                listed |= jnp.int32(1) << (lists_ref[head, first + entry] // plan.slots)
            biases = [
                jnp.where((listed >> held[other]) & 1 == 1, jnp.float32(0), jnp.float32(NEG_FLOOR))
                for other in range(frames)
            ]
            outs[step][index] = softmax_tiles(tiles[step][index, 0], keys, values, biases)
        return 0

    lax.fori_loop(0, count, one, 0)


def spatial_kernel(plan, count, table_ref, lists_ref, *rest):
    slots = plan.slots
    queries, pieces = rest[:slots], rest[slots : 4 * slots]
    outs = rest[4 * slots : 5 * slots]
    kv_ref, order_ref, sems = rest[5 * slots :]
    copies = [
        pltpu.make_async_copy(piece, kv_ref.at[place], sems.at[place])
        for place, piece in enumerate(pieces)
    ]
    for copy in copies:
        copy.start()
    fill_order(plan, 1, table_ref, order_ref)
    frame, slot = table_ref[plan.frame_at], table_ref[plan.slot_at]
    for copy in copies:
        copy.wait()

    def one(index, _):
        head = order_ref[index * slots + slot]
        for step in range(slots):
            first = (frame * slots + (slot ^ step)) * plan.entries
            seen = jnp.int32(0)
            keys, values, biases = [], [], []
            for entry in range(plan.entries):
                tile = lists_ref[head, first + entry]
                place = (tile // slots - frame + 1) * slots + (lax.rem(tile, slots) ^ slot)
                place = jnp.clip(place, 0, 3 * slots - 1)
                fresh = (seen >> place) & 1 == 0
                seen |= jnp.int32(1) << place
                keys.append(kv_ref[place, index, 0])
                values.append(kv_ref[place, index, 1])
                biases.append(jnp.where(fresh, jnp.float32(0), jnp.float32(NEG_FLOOR)))
            outs[step][index] = softmax_tiles(queries[step][index], keys, values, biases)
        return 0

    lax.fori_loop(0, count, one, 0)


def unpack_kernel(plan, counts, table_ref, *rest):
    out_ref, order_ref = rest[-2], rest[-1]
    pieces = list(rest[:-2])
    for kind, (size, group_of) in enumerate(
        ((plan.frames, temporal_group), (plan.slots, spatial_group))
    ):
        if counts[kind] == 0:
            continue
        fill_order(plan, kind, table_ref, order_ref)
        total = table_ref[plan.count_at + kind]
        for step in range(size):
            piece = pieces.pop(0)
            group = group_of(plan, table_ref, step)

            def one(index, _, piece=piece, group=group, size=size):
                out_ref[:, head_columns(order_ref[index * size + group])] = piece[index]
                return 0

            here = lax.min((total - group + size - 1) // size, counts[kind])
            lax.fori_loop(0, here, one, 0)


def call(kernel, outs, operands, in_place, scratch, flops=0):
    spaces = {"s": pltpu.SMEM, "v": pltpu.VMEM, "a": pl.ANY}
    nbytes = sum(math.prod(o.shape) * 2 for o in outs) * 2
    return pl.pallas_call(
        kernel,
        out_shape=outs,
        in_specs=[pl.BlockSpec(memory_space=spaces[c]) for c in in_place],
        out_specs=[pl.BlockSpec(memory_space=pltpu.VMEM) for _ in outs],
        scratch_shapes=scratch,
        compiler_params=pltpu.CompilerParams(vmem_limit_bytes=VMEM_LIMIT),
        cost_estimate=pl.CostEstimate(flops=flops, bytes_accessed=nbytes, transcendentals=0),
    )(*operands)


def tiles_of(*lead):
    return jax.ShapeDtypeStruct((*lead, TILE, HEAD_DIM), jnp.bfloat16)


def by_kind(plan, t_count, s_count, queries, keys, values, lists, table):
    frames, slots = plan.frames, plan.slots
    order = pltpu.SMEM((plan.heads + 1,), jnp.int32)
    pair_flops = 4 * TILE * TILE * HEAD_DIM

    def to_frame(array, step):
        pairs = [(z, (z + step) % frames) for z in range(frames)]
        return array if step % frames == 0 else lax.ppermute(array, "blk", pairs)

    def to_slot(array, step):
        pairs = [(s, s ^ step) for s in range(slots)]
        return array if step == 0 else lax.ppermute(array, MESH_TAIL, pairs)

    def halo(array, step):
        pairs = [(z, z + step) for z in range(frames) if 0 <= z + step < frames]
        return lax.ppermute(array, "blk", pairs)

    pieces = []
    if t_count:
        packed = call(
            functools.partial(pack_temporal_kernel, plan, t_count),
            [tiles_of(t_count, 3)] * frames,
            (table, queries, keys, values),
            "svvv",
            [order],
        )
        arrived = [to_frame(block, step) for step, block in enumerate(packed)]
    if s_count:
        packed_s = call(
            functools.partial(pack_spatial_kernel, plan, s_count),
            [tiles_of(s_count, 2)] * slots + [tiles_of(s_count)] * slots,
            (table, queries, keys, values),
            "svvv",
            [order],
        )
        kv_here = [to_slot(block, step) for step, block in enumerate(packed_s[:slots])]
        q_here = [to_slot(block, step) for step, block in enumerate(packed_s[slots:])]
        below = [halo(block, 1) for block in kv_here]
        above = [halo(block, -1) for block in kv_here]
    if t_count:
        attended = call(
            functools.partial(temporal_kernel, plan, t_count),
            [tiles_of(t_count)] * frames,
            (table, lists, *arrived),
            "ss" + "v" * frames,
            [order],
            flops=t_count * frames * frames * pair_flops,
        )
        pieces += [to_frame(block, -step) for step, block in enumerate(attended)]
    if s_count:
        attended_s = call(
            functools.partial(spatial_kernel, plan, s_count),
            [tiles_of(s_count)] * slots,
            (table, lists, *q_here, *below, *kv_here, *above),
            "ss" + "v" * slots + "a" * (3 * slots),
            [
                pltpu.VMEM((3 * slots, s_count, 2, TILE, HEAD_DIM), jnp.bfloat16),
                order,
                pltpu.SemaphoreType.DMA((3 * slots,)),
            ],
            flops=s_count * slots * plan.entries * pair_flops,
        )
        pieces += [to_slot(block, step) for step, block in enumerate(attended_s)]
    (out,) = call(
        functools.partial(unpack_kernel, plan, (t_count, s_count)),
        [jax.ShapeDtypeStruct((TILE, plan.heads * HEAD_DIM), jnp.bfloat16)],
        (table, *pieces),
        "s" + "v" * len(pieces),
        [order],
    )
    return out


def kind_plan(queries, keys, values, block_lists):
    heads, tiles, entries = block_lists.shape
    frames = lax.axis_size("blk")
    slots = lax.axis_size(MESH_TAIL)
    plan = Plan(heads, frames, slots, tiles, entries)
    head_ids = jnp.arange(heads, dtype=jnp.int32)
    tile_slot = jnp.arange(tiles, dtype=jnp.int32) % slots
    temporal = jnp.all(block_lists % slots == tile_slot[None, :, None], axis=(1, 2))
    before = head_ids[None, :] < head_ids[:, None]
    rank_t = jnp.sum((before & temporal[None, :]).astype(jnp.int32), axis=1)
    total_t = jnp.sum(temporal.astype(jnp.int32))
    table = jnp.concatenate(
        [
            jnp.where(temporal, rank_t, heads),
            jnp.where(temporal, heads, head_ids - rank_t),
            jnp.stack(
                [
                    total_t,
                    heads - total_t,
                    lax.axis_index("blk").astype(jnp.int32),
                    lax.axis_index(MESH_TAIL).astype(jnp.int32),
                ]
            ),
        ]
    )
    lists = block_lists.reshape(heads, tiles * entries)
    pairs = []
    for chunks in range(-(-heads // frames) + 1):
        fewest = 0 if chunks == 0 else (chunks - 1) * frames + 1
        pairs.append((chunks, -(-(heads - fewest) // slots)))
    branches = [functools.partial(by_kind, plan, t, s) for t, s in pairs]
    return lax.switch(
        (total_t + frames - 1) // frames, branches, queries, keys, values, lists, table
    )


def per_device(queries, keys, values, block_lists):
    slots = lax.axis_size(MESH_TAIL)
    whole_tiles = queries.shape[0] == TILE and slots == FRAME_TILES
    if whole_tiles and lax.axis_size("blk") * slots == block_lists.shape[1]:
        return kind_plan(queries, keys, values, block_lists)
    return gathered_plan(queries, keys, values, block_lists)


def solution(mesh):
    in_specs = (
        P(("grp", "blk", "head", "sub"), None),
        P(("grp", "blk", "head", "sub"), None),
        P(("grp", "blk", "head", "sub"), None),
        P(),
    )
    out_specs = P(("grp", "blk", "head", "sub"), None)
    return jax.shard_map(
        per_device, mesh=mesh, in_specs=in_specs, out_specs=out_specs, check_vma=False
    )
```

```python
import functools
import math

import jax
import jax.numpy as jnp
from jax import lax
from jax.experimental import pallas as pl
from jax.experimental.pallas import tpu as pltpu
from jax.sharding import PartitionSpec as P

HEADS = 32
HEAD_DIM = 128
TILE = 128
FRAME_TILES = 4


NEG_FLOOR = -1e30


def query_rows(block_lists, first_head, heads_here, query_tokens):
    tile_ids = jnp.arange(block_lists.shape[1], dtype=jnp.int32)
    lists_local = lax.dynamic_slice_in_dim(block_lists, first_head, heads_here, 0)
    tile_mask = jnp.any(lists_local[:, :, :, None] == tile_ids, axis=2).astype(jnp.bfloat16)
    query_onehot = ((query_tokens // TILE)[:, None] == tile_ids[None, :]).astype(jnp.bfloat16)
    listed = jnp.einsum("qi,hij->hqj", query_onehot, tile_mask, preferred_element_type=jnp.float32)
    return listed.astype(jnp.bfloat16)


def attend_block(state_now, key_block, value_block, allowed, query_local, score_scale):
    top_old, total_old, accum_old = state_now
    scores = (
        jnp.einsum("qhd,khd->hqk", query_local, key_block, preferred_element_type=jnp.float32)
        * score_scale
    )
    top_new = jnp.maximum(top_old, jnp.max(jnp.where(allowed, scores, NEG_FLOOR), axis=2))
    factor = jnp.exp(top_old - top_new)
    weights = jnp.where(allowed, jnp.exp(scores - top_new[:, :, None]), 0.0)
    total_new = total_old * factor + jnp.sum(weights, axis=2)
    product = jnp.einsum(
        "hqk,khd->qhd",
        weights.astype(jnp.bfloat16),
        value_block,
        preferred_element_type=jnp.float32,
    )
    accum_new = accum_old * jnp.transpose(factor)[:, :, None] + product
    return (top_new, total_new, accum_new)


def make_step(query_local, listed_rows, key_token, block_len, tile_total):
    score_scale = 1.0 / math.sqrt(HEAD_DIM)
    tile_ids = jnp.arange(tile_total, dtype=jnp.int32)

    def fold_step(state_now, piece, first_row):
        key_piece, value_piece = piece
        block_count = key_piece.shape[0] // block_len

        def one_block(block_index, state_in):
            key_block = lax.dynamic_slice_in_dim(key_piece, block_index * block_len, block_len, 0)
            value_block = lax.dynamic_slice_in_dim(
                value_piece, block_index * block_len, block_len, 0
            )
            positions = block_index * block_len + jnp.arange(block_len, dtype=jnp.int32)
            key_tiles = key_token(positions) // TILE
            key_onehot = (tile_ids[:, None] == key_tiles[None, :]).astype(jnp.bfloat16)
            allowed = (
                jnp.einsum(
                    "hqj,jk->hqk", listed_rows, key_onehot, preferred_element_type=jnp.float32
                )
                > 0.5
            )
            result = attend_block(
                state_in, key_block, value_block, allowed, query_local, score_scale
            )
            return result

        return lax.fori_loop(0, block_count, one_block, state_now)

    return fold_step


def start_state(heads_here, block_len):
    top_all = jnp.full((heads_here, block_len), NEG_FLOOR, jnp.float32)
    total_all = jnp.zeros((heads_here, block_len), jnp.float32)
    accum_all = jnp.zeros((block_len, heads_here, HEAD_DIM), jnp.float32)
    return (top_all, total_all, accum_all)


def normalize(state_end):
    top_all, total_all, accum_all = state_end
    return (accum_all / jnp.transpose(total_all)[:, :, None]).astype(jnp.bfloat16)


def gathered_plan(queries, keys, values, block_lists):
    row_count, col_count = queries.shape
    n_head = lax.axis_size("head")
    n_sub = lax.axis_size("sub")
    blk_index = lax.axis_index("blk")
    head_index = lax.axis_index("head")
    sub_index = lax.axis_index("sub")
    tile_total = block_lists.shape[1]
    heads_here = HEADS // (n_head * n_sub)
    block_len = row_count * n_head * n_sub

    def inward(tensor):
        return tensor.reshape(1, 1, row_count, n_head, n_sub, heads_here * HEAD_DIM)

    query_six, keys_six, values_six = (
        lax.all_to_all(
            lax.all_to_all(inward(queries), "head", split_axis=3, concat_axis=1, tiled=True),
            "sub",
            split_axis=4,
            concat_axis=0,
            tiled=True,
        ),
        lax.all_to_all(
            lax.all_to_all(inward(keys), "head", split_axis=3, concat_axis=1, tiled=True),
            "sub",
            split_axis=4,
            concat_axis=0,
            tiled=True,
        ),
        lax.all_to_all(
            lax.all_to_all(inward(values), "head", split_axis=3, concat_axis=1, tiled=True),
            "sub",
            split_axis=4,
            concat_axis=0,
            tiled=True,
        ),
    )
    query_local = query_six.reshape(block_len, heads_here, HEAD_DIM)
    keys_local = keys_six.reshape(block_len, heads_here, HEAD_DIM)
    values_local = values_six.reshape(block_len, heads_here, HEAD_DIM)

    def key_token(positions):
        source_dev = positions // block_len
        within = positions % block_len
        sub_source = within // (n_head * row_count)
        head_source = within // row_count % n_head
        offset = within % row_count
        return ((source_dev * n_head + head_source) * n_sub + sub_source) * row_count + offset

    query_tokens = key_token(blk_index * block_len + jnp.arange(block_len, dtype=jnp.int32))
    first_head = (head_index * n_sub + sub_index) * heads_here
    listed_rows = query_rows(block_lists, first_head, heads_here, query_tokens)
    fold_step = make_step(query_local, listed_rows, key_token, block_len, tile_total)
    state_end = fold_step(
        start_state(heads_here, block_len),
        (
            lax.all_gather(keys_local, "blk", axis=0, tiled=True),
            lax.all_gather(values_local, "blk", axis=0, tiled=True),
        ),
        jnp.int32(0),
    )
    result_rows = normalize(state_end)
    attended = result_rows.reshape(n_sub, n_head, row_count, 1, 1, heads_here * HEAD_DIM)
    returned = lax.all_to_all(
        lax.all_to_all(attended, "head", split_axis=1, concat_axis=3, tiled=True),
        "sub",
        split_axis=0,
        concat_axis=4,
        tiled=True,
    )
    return returned.reshape(row_count, col_count)


MESH_TAIL = ("head", "sub")
EXP2_SCALE = math.log2(math.e) / math.sqrt(HEAD_DIM)
VMEM_LIMIT = 16 * 1024 * 1024


class Plan:
    def __init__(self, heads, frames, slots, entries):
        self.heads, self.frames, self.slots, self.entries = heads, frames, slots, entries
        self.count_at = 2 * heads
        self.frame_at = 2 * heads + 2
        self.slot_at = 2 * heads + 3
        self.kind_stride = heads + 1

    def sizes(self, kind):
        return (self.frames, self.slots)[kind]

    def temporal_group(self, table_ref, step):
        return lax.rem(table_ref[self.frame_at] + step, self.frames)

    def heads_in_group(self, kind, table_ref, group):
        size = self.sizes(kind)
        return (table_ref[self.count_at + kind] - group + size - 1) // size


def head_columns(head):
    return pl.ds(pl.multiple_of(head * HEAD_DIM, HEAD_DIM), HEAD_DIM)


def order_kernel(plan, table_ref, order_ref):
    def clear(p, _):
        order_ref[p] = 0
        return 0

    def place(h, _):
        order_ref[table_ref[h]] = h
        order_ref[plan.kind_stride + table_ref[plan.heads + h]] = h
        return 0

    lax.fori_loop(0, 2 * plan.kind_stride, clear, 0)
    lax.fori_loop(0, plan.heads, place, 0)


def wait_all(ref, sem):
    pltpu.make_async_copy(ref, ref, sem).wait()


def copy_heads(plan, kind, group, count, table_ref, order_ref, moves, sem):
    size = plan.sizes(kind)

    def one(index, _):
        head = order_ref[kind * plan.kind_stride + index * size + group]
        for ref, tile_of in moves:
            pltpu.make_async_copy(ref.at[:, head_columns(head)], tile_of(index), sem).start()
        return 0

    lax.fori_loop(0, count, one, 0)


def pack_temporal_kernel(plan, count, table_ref, order_ref, q_ref, k_ref, v_ref, *rest):
    outs, sems = rest[:-1], rest[-1]
    for step, out_ref in enumerate(outs):
        group = plan.temporal_group(table_ref, step)
        moves = [
            (ref, lambda index, out_ref=out_ref, place=place: out_ref.at[index, place])
            for place, ref in enumerate((q_ref, k_ref, v_ref))
        ]
        copy_heads(plan, 0, group, count, table_ref, order_ref, moves, sems.at[step])
    for step, out_ref in enumerate(outs):
        wait_all(out_ref, sems.at[step])


def pack_spatial_kernel(plan, count, table_ref, order_ref, q_ref, k_ref, v_ref, *rest):
    kv_out, q_out, sems = rest
    for group in range(plan.slots):
        moves = [
            (k_ref, lambda index, group=group: kv_out.at[group, index, 0]),
            (v_ref, lambda index, group=group: kv_out.at[group, index, 1]),
        ]
        copy_heads(plan, 1, group, count, table_ref, order_ref, moves, sems.at[0])
    for group in range(plan.slots):
        moves = [(q_ref, lambda index, group=group: q_out.at[group, index])]
        copy_heads(plan, 1, group, count, table_ref, order_ref, moves, sems.at[1])
    wait_all(kv_out, sems.at[0])
    wait_all(q_out, sems.at[1])


def attend_tiles(queries, keys, values, biases):
    scores = lax.dot_general(
        jnp.concatenate(queries, 0),
        jnp.concatenate(keys, 0),
        (((1,), (1,)), ((), ())),
        preferred_element_type=jnp.float32,
    )
    rows, totals = [], []
    for a, bias in enumerate(biases):
        tiles = [
            scores[a * TILE : (a + 1) * TILE, b * TILE : (b + 1) * TILE] + bias[b]
            for b in range(len(keys))
        ]
        top = jnp.max(functools.reduce(jnp.maximum, tiles), axis=1, keepdims=True)
        weights = [jnp.exp2((tile - top) * EXP2_SCALE) for tile in tiles]
        totals.append(jnp.sum(functools.reduce(jnp.add, weights), axis=1, keepdims=True))
        rows.append(jnp.concatenate([w.astype(jnp.bfloat16) for w in weights], 1))
    accum = jnp.dot(
        jnp.concatenate(rows, 0), jnp.concatenate(values, 0), preferred_element_type=jnp.float32
    )
    return [
        (accum[a * TILE : (a + 1) * TILE] / total).astype(jnp.bfloat16)
        for a, total in enumerate(totals)
    ]


def bias_of(listed, place):
    return jnp.where((listed >> place) & 1 == 1, jnp.float32(0), jnp.float32(NEG_FLOOR))


def temporal_kernel(plan, table_ref, order_ref, lists_ref, *rest):
    frames = plan.frames
    tiles, outs = rest[:frames], rest[frames : 2 * frames]
    frame, slot = table_ref[plan.frame_at], table_ref[plan.slot_at]
    held = [lax.rem(frame + frames - step, frames) for step in range(frames)]

    def one(index, _):
        head = order_ref[index * frames + frame]
        biases = []
        for step in range(frames):
            first = (held[step] * plan.slots + slot) * plan.entries
            listed = jnp.int32(0)
            for entry in range(plan.entries):
                listed |= jnp.int32(1) << (lists_ref[head, first + entry] // plan.slots)
            biases.append([bias_of(listed, held[other]) for other in range(frames)])
        results = attend_tiles(
            *([tile[index, place] for tile in tiles] for place in range(3)), biases
        )
        for out_ref, result in zip(outs, results):
            out_ref[index] = result
        return 0

    lax.fori_loop(0, plan.heads_in_group(0, table_ref, frame), one, 0)


def spatial_kernel(plan, table_ref, order_ref, lists_ref, q_ref, below, here, above, out_ref):
    slots = plan.slots
    frame, slot = table_ref[plan.frame_at], table_ref[plan.slot_at]

    def one(index, _):
        head = order_ref[plan.kind_stride + index * slots + slot]
        biases = []
        for row in range(slots):
            first = (frame * slots + row) * plan.entries
            listed = jnp.int32(0)
            for entry in range(plan.entries):
                tile = lists_ref[head, first + entry] - (frame - 1) * slots
                listed |= jnp.int32(1) << tile
            biases.append([bias_of(listed, place) for place in range(3 * slots)])
        keys, values = (
            [ref[row, index, place] for ref in (below, here, above) for row in range(slots)]
            for place in range(2)
        )
        results = attend_tiles([q_ref[row, index] for row in range(slots)], keys, values, biases)
        for row, result in enumerate(results):
            out_ref[row, index] = result
        return 0

    lax.fori_loop(0, plan.heads_in_group(1, table_ref, slot), one, 0)


def unpack_kernel(plan, kinds, table_ref, order_ref, *rest):
    pieces, out_ref, sem = list(rest[:-2]), rest[-2], rest[-1]

    def place(kind, group, tile_of):
        size = plan.sizes(kind)

        def one(index, _):
            head = order_ref[kind * plan.kind_stride + index * size + group]
            pltpu.make_async_copy(tile_of(index), out_ref.at[:, head_columns(head)], sem).start()
            return 0

        lax.fori_loop(0, plan.heads_in_group(kind, table_ref, group), one, 0)

    if 0 in kinds:
        for step in range(plan.frames):
            piece = pieces.pop(0)
            group = plan.temporal_group(table_ref, step)
            place(0, group, lambda index, piece=piece: piece.at[index])
    if 1 in kinds:
        piece = pieces.pop(0)
        for group in range(plan.slots):
            place(1, group, lambda index, group=group: piece.at[group, index])
    wait_all(out_ref, sem)


SPACES = {"s": pltpu.SMEM, "v": pltpu.VMEM, "a": pl.ANY}


def call(kernel, outs, operands, places, out_place, scratch=(), flops=0):
    nbytes = sum(math.prod(o.shape) * 2 for o in outs) * 2
    return pl.pallas_call(
        kernel,
        out_shape=outs,
        in_specs=[pl.BlockSpec(memory_space=SPACES[c]) for c in places],
        out_specs=[pl.BlockSpec(memory_space=SPACES[out_place]) for _ in outs],
        scratch_shapes=list(scratch),
        compiler_params=pltpu.CompilerParams(vmem_limit_bytes=VMEM_LIMIT),
        cost_estimate=pl.CostEstimate(flops=flops, bytes_accessed=nbytes, transcendentals=0),
    )(*operands)


def tiles_of(*lead):
    return jax.ShapeDtypeStruct((*lead, TILE, HEAD_DIM), jnp.bfloat16)


def by_kind(plan, t_count, s_count, queries, keys, values, lists, table, order):
    frames, slots = plan.frames, plan.slots
    pair_flops = 4 * TILE * TILE * HEAD_DIM

    def to_frame(array, step):
        pairs = [(z, (z + step) % frames) for z in range(frames)]
        return array if step % frames == 0 else lax.ppermute(array, "blk", pairs)

    def between_slots(array):
        return lax.all_to_all(array, MESH_TAIL, split_axis=0, concat_axis=0, tiled=True)

    def halo(array, step):
        pairs = [(z, z + step) for z in range(frames) if 0 <= z + step < frames]
        return lax.ppermute(array, "blk", pairs)

    pieces = []
    if t_count:
        packed = call(
            functools.partial(pack_temporal_kernel, plan, t_count),
            [tiles_of(t_count, 3)] * frames,
            (table, order, queries, keys, values),
            "ssaaa",
            "v",
            [pltpu.SemaphoreType.DMA((frames,))],
        )
        arrived = [to_frame(block, step) for step, block in enumerate(packed)]
    if s_count:
        kv_packed, q_packed = call(
            functools.partial(pack_spatial_kernel, plan, s_count),
            [tiles_of(slots, s_count, 2), tiles_of(slots, s_count)],
            (table, order, queries, keys, values),
            "ssaaa",
            "v",
            [pltpu.SemaphoreType.DMA((2,))],
        )
        kv_here, q_here = between_slots(kv_packed), between_slots(q_packed)
        below, above = halo(kv_here, 1), halo(kv_here, -1)
    if t_count:
        attended = call(
            functools.partial(temporal_kernel, plan),
            [tiles_of(t_count)] * frames,
            (table, order, lists, *arrived),
            "sss" + "v" * frames,
            "v",
            flops=t_count * frames * frames * pair_flops,
        )
        pieces += [to_frame(block, -step) for step, block in enumerate(attended)]
    if s_count:
        (attended,) = call(
            functools.partial(spatial_kernel, plan),
            [tiles_of(slots, s_count)],
            (table, order, lists, q_here, below, kv_here, above),
            "sssvvvv",
            "v",
            flops=s_count * slots * 3 * slots * pair_flops,
        )
        pieces.append(between_slots(attended))
    kinds = [kind for kind, count in enumerate((t_count, s_count)) if count]
    (out,) = call(
        functools.partial(unpack_kernel, plan, kinds),
        [jax.ShapeDtypeStruct((TILE, plan.heads * HEAD_DIM), jnp.bfloat16)],
        (table, order, *pieces),
        "ss" + "v" * len(pieces),
        "a",
        [pltpu.SemaphoreType.DMA],
    )
    return out


def kind_plan(queries, keys, values, block_lists):
    heads, tiles, entries = block_lists.shape
    frames = lax.axis_size("blk")
    slots = lax.axis_size(MESH_TAIL)
    plan = Plan(heads, frames, slots, entries)
    head_ids = jnp.arange(heads, dtype=jnp.int32)
    tile_slot = jnp.arange(tiles, dtype=jnp.int32) % slots
    temporal = jnp.all(block_lists % slots == tile_slot[None, :, None], axis=(1, 2))
    before = head_ids[None, :] < head_ids[:, None]
    rank_t = jnp.sum((before & temporal[None, :]).astype(jnp.int32), axis=1)
    total_t = jnp.sum(temporal.astype(jnp.int32))
    table = jnp.concatenate(
        [
            jnp.where(temporal, rank_t, heads),
            jnp.where(temporal, heads, head_ids - rank_t),
            jnp.stack(
                [
                    total_t,
                    heads - total_t,
                    lax.axis_index("blk").astype(jnp.int32),
                    lax.axis_index(MESH_TAIL).astype(jnp.int32),
                ]
            ),
        ]
    )
    lists = block_lists.reshape(heads, tiles * entries)
    (order,) = call(
        functools.partial(order_kernel, plan),
        [jax.ShapeDtypeStruct((2 * plan.kind_stride,), jnp.int32)],
        (table,),
        "s",
        "s",
    )
    pairs = []
    for chunks in range(-(-heads // frames) + 1):
        fewest = 0 if chunks == 0 else (chunks - 1) * frames + 1
        pairs.append((chunks, -(-(heads - fewest) // slots)))
    branches = [functools.partial(by_kind, plan, t, s) for t, s in pairs]
    return lax.switch(
        (total_t + frames - 1) // frames, branches, queries, keys, values, lists, table, order
    )


def per_device(queries, keys, values, block_lists):
    slots = lax.axis_size(MESH_TAIL)
    whole_tiles = queries.shape[0] == TILE and slots == FRAME_TILES
    if whole_tiles and lax.axis_size("blk") * slots == block_lists.shape[1]:
        return kind_plan(queries, keys, values, block_lists)
    return gathered_plan(queries, keys, values, block_lists)


def solution(mesh):
    in_specs = (
        P(("grp", "blk", "head", "sub"), None),
        P(("grp", "blk", "head", "sub"), None),
        P(("grp", "blk", "head", "sub"), None),
        P(),
    )
    out_specs = P(("grp", "blk", "head", "sub"), None)
    return jax.shard_map(
        per_device, mesh=mesh, in_specs=in_specs, out_specs=out_specs, check_vma=False
    )
```

```python
import functools
import math

import jax
import jax.numpy as jnp
from jax import lax
from jax.experimental import pallas as pl
from jax.experimental.pallas import tpu as pltpu
from jax.sharding import PartitionSpec as P

HEADS = 32
HEAD_DIM = 128
TILE = 128
FRAME_TILES = 4


NEG_FLOOR = -1e30


def query_rows(block_lists, first_head, heads_here, query_tokens):
    tile_ids = jnp.arange(block_lists.shape[1], dtype=jnp.int32)
    lists_local = lax.dynamic_slice_in_dim(block_lists, first_head, heads_here, 0)
    tile_mask = jnp.any(lists_local[:, :, :, None] == tile_ids, axis=2).astype(jnp.bfloat16)
    query_onehot = ((query_tokens // TILE)[:, None] == tile_ids[None, :]).astype(jnp.bfloat16)
    listed = jnp.einsum("qi,hij->hqj", query_onehot, tile_mask, preferred_element_type=jnp.float32)
    return listed.astype(jnp.bfloat16)


def attend_block(state_now, key_block, value_block, allowed, query_local, score_scale):
    top_old, total_old, accum_old = state_now
    scores = (
        jnp.einsum("qhd,khd->hqk", query_local, key_block, preferred_element_type=jnp.float32)
        * score_scale
    )
    top_new = jnp.maximum(top_old, jnp.max(jnp.where(allowed, scores, NEG_FLOOR), axis=2))
    factor = jnp.exp(top_old - top_new)
    weights = jnp.where(allowed, jnp.exp(scores - top_new[:, :, None]), 0.0)
    total_new = total_old * factor + jnp.sum(weights, axis=2)
    product = jnp.einsum(
        "hqk,khd->qhd",
        weights.astype(jnp.bfloat16),
        value_block,
        preferred_element_type=jnp.float32,
    )
    accum_new = accum_old * jnp.transpose(factor)[:, :, None] + product
    return (top_new, total_new, accum_new)


def make_step(query_local, listed_rows, key_token, block_len, tile_total):
    score_scale = 1.0 / math.sqrt(HEAD_DIM)
    tile_ids = jnp.arange(tile_total, dtype=jnp.int32)

    def fold_step(state_now, piece, first_row):
        key_piece, value_piece = piece
        block_count = key_piece.shape[0] // block_len

        def one_block(block_index, state_in):
            key_block = lax.dynamic_slice_in_dim(key_piece, block_index * block_len, block_len, 0)
            value_block = lax.dynamic_slice_in_dim(
                value_piece, block_index * block_len, block_len, 0
            )
            positions = block_index * block_len + jnp.arange(block_len, dtype=jnp.int32)
            key_tiles = key_token(positions) // TILE
            key_onehot = (tile_ids[:, None] == key_tiles[None, :]).astype(jnp.bfloat16)
            allowed = (
                jnp.einsum(
                    "hqj,jk->hqk", listed_rows, key_onehot, preferred_element_type=jnp.float32
                )
                > 0.5
            )
            result = attend_block(
                state_in, key_block, value_block, allowed, query_local, score_scale
            )
            return result

        return lax.fori_loop(0, block_count, one_block, state_now)

    return fold_step


def start_state(heads_here, block_len):
    top_all = jnp.full((heads_here, block_len), NEG_FLOOR, jnp.float32)
    total_all = jnp.zeros((heads_here, block_len), jnp.float32)
    accum_all = jnp.zeros((block_len, heads_here, HEAD_DIM), jnp.float32)
    return (top_all, total_all, accum_all)


def normalize(state_end):
    top_all, total_all, accum_all = state_end
    return (accum_all / jnp.transpose(total_all)[:, :, None]).astype(jnp.bfloat16)


def gathered_plan(queries, keys, values, block_lists):
    row_count, col_count = queries.shape
    n_head = lax.axis_size("head")
    n_sub = lax.axis_size("sub")
    blk_index = lax.axis_index("blk")
    head_index = lax.axis_index("head")
    sub_index = lax.axis_index("sub")
    tile_total = block_lists.shape[1]
    heads_here = HEADS // (n_head * n_sub)
    block_len = row_count * n_head * n_sub

    def inward(tensor):
        return tensor.reshape(1, 1, row_count, n_head, n_sub, heads_here * HEAD_DIM)

    query_six, keys_six, values_six = (
        lax.all_to_all(
            lax.all_to_all(inward(queries), "head", split_axis=3, concat_axis=1, tiled=True),
            "sub",
            split_axis=4,
            concat_axis=0,
            tiled=True,
        ),
        lax.all_to_all(
            lax.all_to_all(inward(keys), "head", split_axis=3, concat_axis=1, tiled=True),
            "sub",
            split_axis=4,
            concat_axis=0,
            tiled=True,
        ),
        lax.all_to_all(
            lax.all_to_all(inward(values), "head", split_axis=3, concat_axis=1, tiled=True),
            "sub",
            split_axis=4,
            concat_axis=0,
            tiled=True,
        ),
    )
    query_local = query_six.reshape(block_len, heads_here, HEAD_DIM)
    keys_local = keys_six.reshape(block_len, heads_here, HEAD_DIM)
    values_local = values_six.reshape(block_len, heads_here, HEAD_DIM)

    def key_token(positions):
        source_dev = positions // block_len
        within = positions % block_len
        sub_source = within // (n_head * row_count)
        head_source = within // row_count % n_head
        offset = within % row_count
        return ((source_dev * n_head + head_source) * n_sub + sub_source) * row_count + offset

    query_tokens = key_token(blk_index * block_len + jnp.arange(block_len, dtype=jnp.int32))
    first_head = (head_index * n_sub + sub_index) * heads_here
    listed_rows = query_rows(block_lists, first_head, heads_here, query_tokens)
    fold_step = make_step(query_local, listed_rows, key_token, block_len, tile_total)
    state_end = fold_step(
        start_state(heads_here, block_len),
        (
            lax.all_gather(keys_local, "blk", axis=0, tiled=True),
            lax.all_gather(values_local, "blk", axis=0, tiled=True),
        ),
        jnp.int32(0),
    )
    result_rows = normalize(state_end)
    attended = result_rows.reshape(n_sub, n_head, row_count, 1, 1, heads_here * HEAD_DIM)
    returned = lax.all_to_all(
        lax.all_to_all(attended, "head", split_axis=1, concat_axis=3, tiled=True),
        "sub",
        split_axis=0,
        concat_axis=4,
        tiled=True,
    )
    return returned.reshape(row_count, col_count)


MESH_TAIL = ("head", "sub")
EXP2_SCALE = math.log2(math.e) / math.sqrt(HEAD_DIM)
VMEM_LIMIT = 16 * 1024 * 1024


class Plan:
    def __init__(self, heads, frames, slots, entries):
        self.heads, self.frames, self.slots, self.entries = heads, frames, slots, entries
        self.count_at = 2 * heads
        self.frame_at = 2 * heads + 2
        self.slot_at = 2 * heads + 3
        self.kind_stride = heads + 1

    def sizes(self, kind):
        return (self.frames, self.slots)[kind]

    def own(self, kind, table_ref):
        return table_ref[(self.frame_at, self.slot_at)[kind]]

    def group(self, kind, table_ref, step):
        own = self.own(kind, table_ref)
        return own ^ step if kind else lax.rem(own + step, self.frames)

    def heads_in_group(self, kind, table_ref, group):
        size = self.sizes(kind)
        return (table_ref[self.count_at + kind] - group + size - 1) // size


def head_columns(head):
    return pl.ds(pl.multiple_of(head * HEAD_DIM, HEAD_DIM), HEAD_DIM)


def order_kernel(plan, table_ref, order_ref):
    def clear(p, _):
        order_ref[p] = 0
        return 0

    def place(h, _):
        order_ref[table_ref[h]] = h
        order_ref[plan.kind_stride + table_ref[plan.heads + h]] = h
        return 0

    lax.fori_loop(0, 2 * plan.kind_stride, clear, 0)
    lax.fori_loop(0, plan.heads, place, 0)


def wait_all(ref, sem):
    pltpu.make_async_copy(ref, ref, sem).wait()


def pack_kernel(plan, kind, count, table_ref, order_ref, q_ref, k_ref, v_ref, *rest):
    size = plan.sizes(kind)
    outs, sems = rest[-1 - size : -1], rest[-1]
    for step, out_ref in enumerate(outs):
        group = plan.group(kind, table_ref, step)

        def one(index, _, group=group, out_ref=out_ref, step=step):
            head = order_ref[kind * plan.kind_stride + index * size + group]
            for place, ref in enumerate((q_ref, k_ref, v_ref)):
                pltpu.make_async_copy(
                    ref.at[:, head_columns(head)], out_ref.at[index, place], sems.at[step]
                ).start()
            return 0

        lax.fori_loop(0, count, one, 0)
    for step, out_ref in enumerate(outs):
        wait_all(out_ref, sems.at[step])


def join_kernel(plan, *refs):
    pieces, out_ref, sems = refs[: plan.slots], refs[-2], refs[-1]
    copies = [
        pltpu.make_async_copy(piece.at[:, pl.ds(1, 2)], out_ref.at[step], sems.at[step])
        for step, piece in enumerate(pieces)
    ]
    for copy in copies:
        copy.start()
    for copy in copies:
        copy.wait()


def attend_tiles(queries, keys, values, biases):
    scores = lax.dot_general(
        jnp.concatenate(queries, 0),
        jnp.concatenate(keys, 0),
        (((1,), (1,)), ((), ())),
        preferred_element_type=jnp.float32,
    )
    rows, totals = [], []
    for a, bias in enumerate(biases):
        tiles = [
            scores[a * TILE : (a + 1) * TILE, b * TILE : (b + 1) * TILE] + bias[b]
            for b in range(len(keys))
        ]
        top = jnp.max(functools.reduce(jnp.maximum, tiles), axis=1, keepdims=True)
        weights = [jnp.exp2((tile - top) * EXP2_SCALE) for tile in tiles]
        totals.append(jnp.sum(functools.reduce(jnp.add, weights), axis=1, keepdims=True))
        rows.append(jnp.concatenate([w.astype(jnp.bfloat16) for w in weights], 1))
    accum = jnp.dot(
        jnp.concatenate(rows, 0), jnp.concatenate(values, 0), preferred_element_type=jnp.float32
    )
    return [
        (accum[a * TILE : (a + 1) * TILE] / total).astype(jnp.bfloat16)
        for a, total in enumerate(totals)
    ]


def bias_of(listed, place):
    return jnp.where((listed >> place) & 1 == 1, jnp.float32(0), jnp.float32(NEG_FLOOR))


def temporal_kernel(plan, table_ref, order_ref, lists_ref, *rest):
    frames = plan.frames
    tiles, outs = rest[:frames], rest[frames : 2 * frames]
    frame, slot = table_ref[plan.frame_at], table_ref[plan.slot_at]
    held = [lax.rem(frame + frames - step, frames) for step in range(frames)]

    def one(index, _):
        head = order_ref[index * frames + frame]
        biases = []
        for step in range(frames):
            first = (held[step] * plan.slots + slot) * plan.entries
            listed = jnp.int32(0)
            for entry in range(plan.entries):
                listed |= jnp.int32(1) << (lists_ref[head, first + entry] // plan.slots)
            biases.append([bias_of(listed, held[other]) for other in range(frames)])
        results = attend_tiles(
            *([tile[index, place] for tile in tiles] for place in range(3)), biases
        )
        for out_ref, result in zip(outs, results):
            out_ref[index] = result
        return 0

    lax.fori_loop(0, plan.heads_in_group(0, table_ref, frame), one, 0)


def spatial_kernel(plan, table_ref, order_ref, lists_ref, *rest):
    slots = plan.slots
    here, below, above, outs = rest[:slots], rest[slots], rest[slots + 1], rest[slots + 2 :]
    frame, slot = table_ref[plan.frame_at], table_ref[plan.slot_at]

    def one(index, _):
        head = order_ref[plan.kind_stride + index * slots + slot]
        biases = []
        for step in range(slots):
            first = (frame * slots + (slot ^ step)) * plan.entries
            listed = jnp.int32(0)
            for entry in range(plan.entries):
                tile = lists_ref[head, first + entry]
                place = (tile // slots - frame + 1) * slots + (lax.rem(tile, slots) ^ slot)
                listed |= jnp.int32(1) << place
            biases.append([bias_of(listed, place) for place in range(3 * slots)])
        keys, values = (
            [below[step, index, place] for step in range(slots)]
            + [tile[index, 1 + place] for tile in here]
            + [above[step, index, place] for step in range(slots)]
            for place in range(2)
        )
        results = attend_tiles([tile[index, 0] for tile in here], keys, values, biases)
        for out_ref, result in zip(outs, results):
            out_ref[index] = result
        return 0

    lax.fori_loop(0, plan.heads_in_group(1, table_ref, slot), one, 0)


def unpack_kernel(plan, kinds, table_ref, order_ref, *rest):
    pieces, out_ref, sem = list(rest[:-2]), rest[-2], rest[-1]
    for kind in kinds:
        size = plan.sizes(kind)
        for step in range(size):
            piece = pieces.pop(0)
            group = plan.group(kind, table_ref, step)

            def one(index, _, kind=kind, piece=piece, group=group, size=size):
                head = order_ref[kind * plan.kind_stride + index * size + group]
                pltpu.make_async_copy(
                    piece.at[index], out_ref.at[:, head_columns(head)], sem
                ).start()
                return 0

            lax.fori_loop(0, plan.heads_in_group(kind, table_ref, group), one, 0)
    wait_all(out_ref, sem)


SPACES = {"s": pltpu.SMEM, "v": pltpu.VMEM, "a": pl.ANY}


def call(kernel, outs, operands, places, out_place, scratch=(), flops=0):
    nbytes = sum(math.prod(o.shape) * 2 for o in outs) * 2
    return pl.pallas_call(
        kernel,
        out_shape=outs,
        in_specs=[pl.BlockSpec(memory_space=SPACES[c]) for c in places],
        out_specs=[pl.BlockSpec(memory_space=SPACES[out_place]) for _ in outs],
        scratch_shapes=list(scratch),
        compiler_params=pltpu.CompilerParams(vmem_limit_bytes=VMEM_LIMIT),
        cost_estimate=pl.CostEstimate(flops=flops, bytes_accessed=nbytes, transcendentals=0),
    )(*operands)


def after(arrays, others):
    if not arrays or not others:
        return arrays
    return pl.pallas_call(
        lambda *refs: None,
        out_shape=[jax.ShapeDtypeStruct(a.shape, a.dtype) for a in arrays],
        in_specs=[pl.BlockSpec(memory_space=pltpu.VMEM)] * (len(arrays) + len(others)),
        out_specs=[pl.BlockSpec(memory_space=pltpu.VMEM)] * len(arrays),
        input_output_aliases={i: i for i in range(len(arrays))},
        compiler_params=pltpu.CompilerParams(vmem_limit_bytes=VMEM_LIMIT),
    )(*arrays, *others)


def tiles_of(*lead):
    return jax.ShapeDtypeStruct((*lead, TILE, HEAD_DIM), jnp.bfloat16)


def by_kind(plan, t_count, s_count, queries, keys, values, lists, table, order):
    frames, slots = plan.frames, plan.slots
    pair_flops = 4 * TILE * TILE * HEAD_DIM

    def to_frame(array, step):
        pairs = [(z, (z + step) % frames) for z in range(frames)]
        return array if step % frames == 0 else lax.ppermute(array, "blk", pairs)

    def to_slot(array, step):
        pairs = [(s, s ^ step) for s in range(slots)]
        return array if step == 0 else lax.ppermute(array, MESH_TAIL, pairs)

    def halo(array, step):
        pairs = [(z, z + step) for z in range(frames) if 0 <= z + step < frames]
        return lax.ppermute(array, "blk", pairs)

    def pack(kind, count, *earlier):
        size = plan.sizes(kind)
        return call(
            functools.partial(pack_kernel, plan, kind, count),
            [tiles_of(count, 3)] * size,
            (table, order, queries, keys, values, *earlier),
            "ssaaa" + "v" * len(earlier),
            "v",
            [pltpu.SemaphoreType.DMA((size,))],
        )

    pieces, arrived = [], []
    if t_count:
        arrived = [to_frame(block, step) for step, block in enumerate(pack(0, t_count))]
    if s_count:
        here = [to_slot(block, step) for step, block in enumerate(pack(1, s_count, *arrived[:1]))]
        (joined,) = call(
            functools.partial(join_kernel, plan),
            [tiles_of(slots, s_count, 2)],
            here,
            "v" * slots,
            "v",
            [pltpu.SemaphoreType.DMA((slots,))],
        )
        (joined,) = after([joined], arrived[1:])
        below, above = halo(joined, 1), halo(joined, -1)
    if t_count:
        attended = call(
            functools.partial(temporal_kernel, plan),
            [tiles_of(t_count)] * frames,
            (table, order, lists, *arrived),
            "sss" + "v" * frames,
            "v",
            flops=t_count * frames * frames * pair_flops,
        )
        if s_count:
            attended = [attended[0], *after(attended[1:], (below, above))]
        pieces += [to_frame(block, -step) for step, block in enumerate(attended)]
    if s_count:
        attended = call(
            functools.partial(spatial_kernel, plan),
            [tiles_of(s_count)] * slots,
            (table, order, lists, *here, below, above),
            "sss" + "v" * (slots + 2),
            "v",
            flops=s_count * slots * 3 * slots * pair_flops,
        )
        attended = [attended[0], *after(attended[1:2], pieces[1:]), *attended[2:]]
        pieces += [to_slot(block, step) for step, block in enumerate(attended)]
    kinds = [kind for kind, count in enumerate((t_count, s_count)) if count]
    (out,) = call(
        functools.partial(unpack_kernel, plan, kinds),
        [jax.ShapeDtypeStruct((TILE, plan.heads * HEAD_DIM), jnp.bfloat16)],
        (table, order, *pieces),
        "ss" + "v" * len(pieces),
        "a",
        [pltpu.SemaphoreType.DMA],
    )
    return out


def kind_plan(queries, keys, values, block_lists):
    heads, tiles, entries = block_lists.shape
    frames = lax.axis_size("blk")
    slots = lax.axis_size(MESH_TAIL)
    plan = Plan(heads, frames, slots, entries)
    head_ids = jnp.arange(heads, dtype=jnp.int32)
    tile_slot = jnp.arange(tiles, dtype=jnp.int32) % slots
    temporal = jnp.all(block_lists % slots == tile_slot[None, :, None], axis=(1, 2))
    before = head_ids[None, :] < head_ids[:, None]
    rank_t = jnp.sum((before & temporal[None, :]).astype(jnp.int32), axis=1)
    total_t = jnp.sum(temporal.astype(jnp.int32))
    table = jnp.concatenate(
        [
            jnp.where(temporal, rank_t, heads),
            jnp.where(temporal, heads, head_ids - rank_t),
            jnp.stack(
                [
                    total_t,
                    heads - total_t,
                    lax.axis_index("blk").astype(jnp.int32),
                    lax.axis_index(MESH_TAIL).astype(jnp.int32),
                ]
            ),
        ]
    )
    lists = block_lists.reshape(heads, tiles * entries)
    (order,) = call(
        functools.partial(order_kernel, plan),
        [jax.ShapeDtypeStruct((2 * plan.kind_stride,), jnp.int32)],
        (table,),
        "s",
        "s",
    )
    pairs = []
    for chunks in range(-(-heads // frames) + 1):
        fewest = 0 if chunks == 0 else (chunks - 1) * frames + 1
        pairs.append((chunks, -(-(heads - fewest) // slots)))
    branches = [functools.partial(by_kind, plan, t, s) for t, s in pairs]
    return lax.switch(
        (total_t + frames - 1) // frames, branches, queries, keys, values, lists, table, order
    )


def per_device(queries, keys, values, block_lists):
    slots = lax.axis_size(MESH_TAIL)
    whole_tiles = queries.shape[0] == TILE and slots == FRAME_TILES
    if whole_tiles and lax.axis_size("blk") * slots == block_lists.shape[1]:
        return kind_plan(queries, keys, values, block_lists)
    return gathered_plan(queries, keys, values, block_lists)


def solution(mesh):
    in_specs = (
        P(("grp", "blk", "head", "sub"), None),
        P(("grp", "blk", "head", "sub"), None),
        P(("grp", "blk", "head", "sub"), None),
        P(),
    )
    out_specs = P(("grp", "blk", "head", "sub"), None)
    return jax.shard_map(
        per_device, mesh=mesh, in_specs=in_specs, out_specs=out_specs, check_vma=False
    )
```

```python
import functools
import math

import jax
import jax.numpy as jnp
from jax import lax
from jax.experimental import pallas as pl
from jax.experimental.pallas import tpu as pltpu
from jax.sharding import PartitionSpec as P

HEADS = 32
HEAD_DIM = 128
TILE = 128
FRAME_TILES = 4


NEG_FLOOR = -1e30


def query_rows(block_lists, first_head, heads_here, query_tokens):
    tile_ids = jnp.arange(block_lists.shape[1], dtype=jnp.int32)
    lists_local = lax.dynamic_slice_in_dim(block_lists, first_head, heads_here, 0)
    tile_mask = jnp.any(lists_local[:, :, :, None] == tile_ids, axis=2).astype(jnp.bfloat16)
    query_onehot = ((query_tokens // TILE)[:, None] == tile_ids[None, :]).astype(jnp.bfloat16)
    listed = jnp.einsum("qi,hij->hqj", query_onehot, tile_mask, preferred_element_type=jnp.float32)
    return listed.astype(jnp.bfloat16)


def attend_block(state_now, key_block, value_block, allowed, query_local, score_scale):
    top_old, total_old, accum_old = state_now
    scores = (
        jnp.einsum("qhd,khd->hqk", query_local, key_block, preferred_element_type=jnp.float32)
        * score_scale
    )
    top_new = jnp.maximum(top_old, jnp.max(jnp.where(allowed, scores, NEG_FLOOR), axis=2))
    factor = jnp.exp(top_old - top_new)
    weights = jnp.where(allowed, jnp.exp(scores - top_new[:, :, None]), 0.0)
    total_new = total_old * factor + jnp.sum(weights, axis=2)
    product = jnp.einsum(
        "hqk,khd->qhd",
        weights.astype(jnp.bfloat16),
        value_block,
        preferred_element_type=jnp.float32,
    )
    accum_new = accum_old * jnp.transpose(factor)[:, :, None] + product
    return (top_new, total_new, accum_new)


def make_step(query_local, listed_rows, key_token, block_len, tile_total):
    score_scale = 1.0 / math.sqrt(HEAD_DIM)
    tile_ids = jnp.arange(tile_total, dtype=jnp.int32)

    def fold_step(state_now, piece, first_row):
        key_piece, value_piece = piece
        block_count = key_piece.shape[0] // block_len

        def one_block(block_index, state_in):
            key_block = lax.dynamic_slice_in_dim(key_piece, block_index * block_len, block_len, 0)
            value_block = lax.dynamic_slice_in_dim(
                value_piece, block_index * block_len, block_len, 0
            )
            positions = block_index * block_len + jnp.arange(block_len, dtype=jnp.int32)
            key_tiles = key_token(positions) // TILE
            key_onehot = (tile_ids[:, None] == key_tiles[None, :]).astype(jnp.bfloat16)
            allowed = (
                jnp.einsum(
                    "hqj,jk->hqk", listed_rows, key_onehot, preferred_element_type=jnp.float32
                )
                > 0.5
            )
            result = attend_block(
                state_in, key_block, value_block, allowed, query_local, score_scale
            )
            return result

        return lax.fori_loop(0, block_count, one_block, state_now)

    return fold_step


def start_state(heads_here, block_len):
    top_all = jnp.full((heads_here, block_len), NEG_FLOOR, jnp.float32)
    total_all = jnp.zeros((heads_here, block_len), jnp.float32)
    accum_all = jnp.zeros((block_len, heads_here, HEAD_DIM), jnp.float32)
    return (top_all, total_all, accum_all)


def normalize(state_end):
    top_all, total_all, accum_all = state_end
    return (accum_all / jnp.transpose(total_all)[:, :, None]).astype(jnp.bfloat16)


def gathered_plan(queries, keys, values, block_lists):
    row_count, col_count = queries.shape
    n_head = lax.axis_size("head")
    n_sub = lax.axis_size("sub")
    blk_index = lax.axis_index("blk")
    head_index = lax.axis_index("head")
    sub_index = lax.axis_index("sub")
    tile_total = block_lists.shape[1]
    heads_here = HEADS // (n_head * n_sub)
    block_len = row_count * n_head * n_sub

    def inward(tensor):
        return tensor.reshape(1, 1, row_count, n_head, n_sub, heads_here * HEAD_DIM)

    query_six, keys_six, values_six = (
        lax.all_to_all(
            lax.all_to_all(inward(queries), "head", split_axis=3, concat_axis=1, tiled=True),
            "sub",
            split_axis=4,
            concat_axis=0,
            tiled=True,
        ),
        lax.all_to_all(
            lax.all_to_all(inward(keys), "head", split_axis=3, concat_axis=1, tiled=True),
            "sub",
            split_axis=4,
            concat_axis=0,
            tiled=True,
        ),
        lax.all_to_all(
            lax.all_to_all(inward(values), "head", split_axis=3, concat_axis=1, tiled=True),
            "sub",
            split_axis=4,
            concat_axis=0,
            tiled=True,
        ),
    )
    query_local = query_six.reshape(block_len, heads_here, HEAD_DIM)
    keys_local = keys_six.reshape(block_len, heads_here, HEAD_DIM)
    values_local = values_six.reshape(block_len, heads_here, HEAD_DIM)

    def key_token(positions):
        source_dev = positions // block_len
        within = positions % block_len
        sub_source = within // (n_head * row_count)
        head_source = within // row_count % n_head
        offset = within % row_count
        return ((source_dev * n_head + head_source) * n_sub + sub_source) * row_count + offset

    query_tokens = key_token(blk_index * block_len + jnp.arange(block_len, dtype=jnp.int32))
    first_head = (head_index * n_sub + sub_index) * heads_here
    listed_rows = query_rows(block_lists, first_head, heads_here, query_tokens)
    fold_step = make_step(query_local, listed_rows, key_token, block_len, tile_total)
    state_end = fold_step(
        start_state(heads_here, block_len),
        (
            lax.all_gather(keys_local, "blk", axis=0, tiled=True),
            lax.all_gather(values_local, "blk", axis=0, tiled=True),
        ),
        jnp.int32(0),
    )
    result_rows = normalize(state_end)
    attended = result_rows.reshape(n_sub, n_head, row_count, 1, 1, heads_here * HEAD_DIM)
    returned = lax.all_to_all(
        lax.all_to_all(attended, "head", split_axis=1, concat_axis=3, tiled=True),
        "sub",
        split_axis=0,
        concat_axis=4,
        tiled=True,
    )
    return returned.reshape(row_count, col_count)


MESH_TAIL = ("head", "sub")
EXP2_SCALE = math.log2(math.e) / math.sqrt(HEAD_DIM)
TEMPORAL_WEIGHT = 100
VMEM_LIMIT = 16 * 1024 * 1024


class Plan:
    def __init__(self, heads, frames, slots, entries):
        self.heads, self.frames, self.slots, self.entries = heads, frames, slots, entries
        self.count_at = 2 * heads
        self.frame_at = 2 * heads + 2
        self.slot_at = 2 * heads + 3
        self.kind_stride = heads + 1

    def sizes(self, kind):
        return (self.frames, self.slots)[kind]

    def own(self, kind, table_ref):
        return table_ref[(self.frame_at, self.slot_at)[kind]]

    def group(self, kind, table_ref, step):
        own = self.own(kind, table_ref)
        return own ^ step if kind else lax.rem(own + step, self.frames)

    def heads_in_group(self, kind, table_ref, group):
        size = self.sizes(kind)
        return (table_ref[self.count_at + kind] - group + size - 1) // size


def head_columns(head):
    return pl.ds(pl.multiple_of(head * HEAD_DIM, HEAD_DIM), HEAD_DIM)


def fill_order(plan, table_ref, order_ref):
    def clear(p, _):
        order_ref[p] = 0
        return 0

    def place(h, _):
        order_ref[table_ref[h]] = h
        order_ref[plan.kind_stride + table_ref[plan.heads + h]] = h
        return 0

    lax.fori_loop(0, 2 * plan.kind_stride, clear, 0)
    lax.fori_loop(0, plan.heads, place, 0)


def wait_all(ref, sem):
    pltpu.make_async_copy(ref, ref, sem).wait()


def pack_kernel(plan, kind, count, first, table_ref, q_ref, k_ref, v_ref, *rest):
    size = plan.sizes(kind)
    if first:
        outs, order_ref = rest[:size], rest[size]
    else:
        order_ref, outs = rest[0], rest[1 : 1 + size]
    sems = rest[-1]
    if first:
        fill_order(plan, table_ref, order_ref)
    for step in range(size):
        out_ref = outs[step]
        group = plan.group(kind, table_ref, step)

        def one(index, _, group=group, out_ref=out_ref, step=step):
            head = order_ref[kind * plan.kind_stride + index * size + group]
            for place, ref in enumerate((q_ref, k_ref, v_ref)):
                pltpu.make_async_copy(
                    ref.at[:, head_columns(head)], out_ref.at[index, place], sems.at[step]
                ).start()
            return 0

        lax.fori_loop(0, count, one, 0)
    for step, out_ref in enumerate(outs):
        wait_all(out_ref, sems.at[step])


def join_kernel(plan, *refs):
    pieces, out_ref, sems = refs[: plan.slots], refs[-2], refs[-1]
    copies = [
        pltpu.make_async_copy(piece.at[:, pl.ds(1, 2)], out_ref.at[step], sems.at[step])
        for step, piece in enumerate(pieces)
    ]
    for copy in copies:
        copy.start()
    for copy in copies:
        copy.wait()


def attend_tiles(queries, keys, values, biases):
    scores = lax.dot_general(
        jnp.concatenate(queries, 0),
        jnp.concatenate(keys, 0),
        (((1,), (1,)), ((), ())),
        preferred_element_type=jnp.float32,
    )
    rows, totals = [], []
    for a, bias in enumerate(biases):
        tiles = [
            scores[a * TILE : (a + 1) * TILE, b * TILE : (b + 1) * TILE] + bias[b]
            for b in range(len(keys))
        ]
        top = jnp.max(functools.reduce(jnp.maximum, tiles), axis=1, keepdims=True)
        weights = [jnp.exp2((tile - top) * EXP2_SCALE) for tile in tiles]
        totals.append(jnp.sum(functools.reduce(jnp.add, weights), axis=1, keepdims=True))
        rows.append(jnp.concatenate([w.astype(jnp.bfloat16) for w in weights], 1))
    accum = jnp.dot(
        jnp.concatenate(rows, 0), jnp.concatenate(values, 0), preferred_element_type=jnp.float32
    )
    return [
        (accum[a * TILE : (a + 1) * TILE] / total).astype(jnp.bfloat16)
        for a, total in enumerate(totals)
    ]


def bias_of(listed, place):
    return jnp.where((listed >> place) & 1 == 1, jnp.float32(0), jnp.float32(NEG_FLOOR))


def temporal_kernel(plan, table_ref, order_ref, lists_ref, *rest):
    frames = plan.frames
    tiles, outs = rest[:frames], rest[frames : 2 * frames]
    frame, slot = table_ref[plan.frame_at], table_ref[plan.slot_at]
    held = [lax.rem(frame + frames - step, frames) for step in range(frames)]

    def one(index, _):
        head = order_ref[index * frames + frame]
        biases = []
        for step in range(frames):
            first = (held[step] * plan.slots + slot) * plan.entries
            listed = jnp.int32(0)
            for entry in range(plan.entries):
                listed |= jnp.int32(1) << (lists_ref[first + entry, head] // plan.slots)
            biases.append([bias_of(listed, held[other]) for other in range(frames)])
        results = attend_tiles(
            *([tile[index, place] for tile in tiles] for place in range(3)), biases
        )
        for out_ref, result in zip(outs, results):
            out_ref[index] = result
        return 0

    lax.fori_loop(0, plan.heads_in_group(0, table_ref, frame), one, 0)


def spatial_kernel(plan, table_ref, order_ref, lists_ref, *rest):
    slots = plan.slots
    here, below, above, outs = rest[:slots], rest[slots], rest[slots + 1], rest[slots + 2 :]
    frame, slot = table_ref[plan.frame_at], table_ref[plan.slot_at]

    def one(index, _):
        head = order_ref[plan.kind_stride + index * slots + slot]
        biases = []
        for step in range(slots):
            first = (frame * slots + (slot ^ step)) * plan.entries
            listed = jnp.int32(0)
            for entry in range(plan.entries):
                tile = lists_ref[first + entry, head]
                place = (tile // slots - frame + 1) * slots + (lax.rem(tile, slots) ^ slot)
                listed |= jnp.int32(1) << place
            biases.append([bias_of(listed, place) for place in range(3 * slots)])
        keys, values = (
            [below[step, index, place] for step in range(slots)]
            + [tile[index, 1 + place] for tile in here]
            + [above[step, index, place] for step in range(slots)]
            for place in range(2)
        )
        results = attend_tiles([tile[index, 0] for tile in here], keys, values, biases)
        for out_ref, result in zip(outs, results):
            out_ref[index] = result
        return 0

    lax.fori_loop(0, plan.heads_in_group(1, table_ref, slot), one, 0)


def unpack_kernel(plan, kinds, table_ref, order_ref, *rest):
    pieces, out_ref, sem = list(rest[:-2]), rest[-2], rest[-1]
    for kind in kinds:
        size = plan.sizes(kind)
        for step in range(size):
            piece = pieces.pop(0)
            group = plan.group(kind, table_ref, step)

            def one(index, _, kind=kind, piece=piece, group=group, size=size):
                head = order_ref[kind * plan.kind_stride + index * size + group]
                pltpu.make_async_copy(
                    piece.at[index], out_ref.at[:, head_columns(head)], sem
                ).start()
                return 0

            lax.fori_loop(0, plan.heads_in_group(kind, table_ref, group), one, 0)
    wait_all(out_ref, sem)


SPACES = {"s": pltpu.SMEM, "v": pltpu.VMEM, "a": pl.ANY}


def call(kernel, outs, operands, places, out_place, scratch=(), flops=0):
    nbytes = sum(math.prod(o.shape) * 2 for o in outs) * 2
    return pl.pallas_call(
        kernel,
        out_shape=outs,
        in_specs=[pl.BlockSpec(memory_space=SPACES[c]) for c in places],
        out_specs=[pl.BlockSpec(memory_space=SPACES[c]) for c in out_place],
        scratch_shapes=list(scratch),
        compiler_params=pltpu.CompilerParams(vmem_limit_bytes=VMEM_LIMIT),
        cost_estimate=pl.CostEstimate(flops=flops, bytes_accessed=nbytes, transcendentals=0),
    )(*operands)


def after(arrays, others):
    if not arrays or not others:
        return arrays
    return pl.pallas_call(
        lambda *refs: None,
        out_shape=[jax.ShapeDtypeStruct(a.shape, a.dtype) for a in arrays],
        in_specs=[pl.BlockSpec(memory_space=pltpu.VMEM)] * (len(arrays) + len(others)),
        out_specs=[pl.BlockSpec(memory_space=pltpu.VMEM)] * len(arrays),
        input_output_aliases={i: i for i in range(len(arrays))},
        compiler_params=pltpu.CompilerParams(vmem_limit_bytes=VMEM_LIMIT),
    )(*arrays, *others)


def tiles_of(*lead):
    return jax.ShapeDtypeStruct((*lead, TILE, HEAD_DIM), jnp.bfloat16)


def by_kind(plan, t_count, s_count, queries, keys, values, lists, table):
    frames, slots = plan.frames, plan.slots
    pair_flops = 4 * TILE * TILE * HEAD_DIM

    def to_frame(array, step):
        pairs = [(z, (z + step) % frames) for z in range(frames)]
        return array if step % frames == 0 else lax.ppermute(array, "blk", pairs)

    def to_slot(array, step):
        pairs = [(s, s ^ step) for s in range(slots)]
        return array if step == 0 else lax.ppermute(array, MESH_TAIL, pairs)

    def halo(array, step):
        pairs = [(z, z + step) for z in range(frames) if 0 <= z + step < frames]
        return lax.ppermute(array, "blk", pairs)

    def pack(kind, count, order):
        size = plan.sizes(kind)
        outs, out_places = [tiles_of(count, 3)] * size, "v" * size
        if order is None:
            outs.append(jax.ShapeDtypeStruct((2 * plan.kind_stride,), jnp.int32))
            out_places += "s"
        results = call(
            functools.partial(pack_kernel, plan, kind, count, order is None),
            outs,
            (table, queries, keys, values) + (() if order is None else (order,)),
            "saaa" + ("" if order is None else "s"),
            out_places,
            [pltpu.SemaphoreType.DMA((size,))],
        )
        return (*results, order) if order is not None else results

    pieces, order = [], None
    if t_count:
        *packed, order = pack(0, t_count, order)
        arrived = [to_frame(block, step) for step, block in enumerate(packed)]
    if s_count:
        *packed, order = pack(1, s_count, order)
        here = [to_slot(block, step) for step, block in enumerate(packed)]
        (joined,) = call(
            functools.partial(join_kernel, plan),
            [tiles_of(slots, s_count, 2)],
            here,
            "v" * slots,
            "v",
            [pltpu.SemaphoreType.DMA((slots,))],
        )
        below, above = halo(joined, 1), halo(joined, -1)
    if t_count:
        attended = call(
            functools.partial(temporal_kernel, plan),
            [tiles_of(t_count)] * frames,
            (table, order, lists, *arrived),
            "sss" + "v" * frames,
            "v" * frames,
            flops=TEMPORAL_WEIGHT * t_count * frames * frames * pair_flops,
        )
        if s_count:
            attended = [attended[0], *after(attended[1:], (below, above))]
        pieces += [to_frame(block, -step) for step, block in enumerate(attended)]
    if s_count:
        attended = call(
            functools.partial(spatial_kernel, plan),
            [tiles_of(s_count)] * slots,
            (table, order, lists, *here, below, above),
            "sss" + "v" * (slots + 2),
            "v" * slots,
            flops=s_count * slots * 3 * slots * pair_flops,
        )
        attended = [attended[0], *after(attended[1:2], pieces[1:]), *attended[2:]]
        pieces += [to_slot(block, step) for step, block in enumerate(attended)]
    kinds = [kind for kind, count in enumerate((t_count, s_count)) if count]
    (out,) = call(
        functools.partial(unpack_kernel, plan, kinds),
        [jax.ShapeDtypeStruct((TILE, plan.heads * HEAD_DIM), jnp.bfloat16)],
        (table, order, *pieces),
        "ss" + "v" * len(pieces),
        "a",
        [pltpu.SemaphoreType.DMA],
    )
    return out


def kind_plan(queries, keys, values, block_lists):
    heads, tiles, entries = block_lists.shape
    frames = lax.axis_size("blk")
    slots = lax.axis_size(MESH_TAIL)
    plan = Plan(heads, frames, slots, entries)
    head_ids = jnp.arange(heads, dtype=jnp.int32)
    tile_slot = jnp.arange(tiles, dtype=jnp.int32) % slots
    temporal = jnp.all(block_lists % slots == tile_slot[None, :, None], axis=(1, 2))
    before = head_ids[None, :] < head_ids[:, None]
    rank_t = jnp.sum((before & temporal[None, :]).astype(jnp.int32), axis=1)
    total_t = jnp.sum(temporal.astype(jnp.int32))
    table = jnp.concatenate(
        [
            jnp.where(temporal, rank_t, heads),
            jnp.where(temporal, heads, head_ids - rank_t),
            jnp.stack(
                [
                    total_t,
                    heads - total_t,
                    lax.axis_index("blk").astype(jnp.int32),
                    lax.axis_index(MESH_TAIL).astype(jnp.int32),
                ]
            ),
        ]
    )
    lists = jnp.transpose(block_lists, (1, 2, 0)).reshape(tiles * entries, heads)
    pairs = []
    for chunks in range(-(-heads // frames) + 1):
        fewest = 0 if chunks == 0 else (chunks - 1) * frames + 1
        pairs.append((chunks, -(-(heads - fewest) // slots)))
    branches = [functools.partial(by_kind, plan, t, s) for t, s in pairs]
    return lax.switch(
        (total_t + frames - 1) // frames, branches, queries, keys, values, lists, table
    )


def per_device(queries, keys, values, block_lists):
    slots = lax.axis_size(MESH_TAIL)
    whole_tiles = queries.shape[0] == TILE and slots == FRAME_TILES
    if whole_tiles and lax.axis_size("blk") * slots == block_lists.shape[1]:
        return kind_plan(queries, keys, values, block_lists)
    return gathered_plan(queries, keys, values, block_lists)


def solution(mesh):
    in_specs = (
        P(("grp", "blk", "head", "sub"), None),
        P(("grp", "blk", "head", "sub"), None),
        P(("grp", "blk", "head", "sub"), None),
        P(),
    )
    out_specs = P(("grp", "blk", "head", "sub"), None)
    return jax.shard_map(
        per_device, mesh=mesh, in_specs=in_specs, out_specs=out_specs, check_vma=False
    )
```

```python
import functools
import math

import jax
import jax.numpy as jnp
from jax import lax
from jax.experimental import pallas as pl
from jax.experimental.pallas import tpu as pltpu
from jax.sharding import PartitionSpec as P

HEADS = 32
HEAD_DIM = 128
TILE = 128
FRAME_TILES = 4


NEG_FLOOR = -1e30


def query_rows(block_lists, first_head, heads_here, query_tokens):
    tile_ids = jnp.arange(block_lists.shape[1], dtype=jnp.int32)
    lists_local = lax.dynamic_slice_in_dim(block_lists, first_head, heads_here, 0)
    tile_mask = jnp.any(lists_local[:, :, :, None] == tile_ids, axis=2).astype(jnp.bfloat16)
    query_onehot = ((query_tokens // TILE)[:, None] == tile_ids[None, :]).astype(jnp.bfloat16)
    listed = jnp.einsum("qi,hij->hqj", query_onehot, tile_mask, preferred_element_type=jnp.float32)
    return listed.astype(jnp.bfloat16)


def attend_block(state_now, key_block, value_block, allowed, query_local, score_scale):
    top_old, total_old, accum_old = state_now
    scores = (
        jnp.einsum("qhd,khd->hqk", query_local, key_block, preferred_element_type=jnp.float32)
        * score_scale
    )
    top_new = jnp.maximum(top_old, jnp.max(jnp.where(allowed, scores, NEG_FLOOR), axis=2))
    factor = jnp.exp(top_old - top_new)
    weights = jnp.where(allowed, jnp.exp(scores - top_new[:, :, None]), 0.0)
    total_new = total_old * factor + jnp.sum(weights, axis=2)
    product = jnp.einsum(
        "hqk,khd->qhd",
        weights.astype(jnp.bfloat16),
        value_block,
        preferred_element_type=jnp.float32,
    )
    accum_new = accum_old * jnp.transpose(factor)[:, :, None] + product
    return (top_new, total_new, accum_new)


def make_step(query_local, listed_rows, key_token, block_len, tile_total):
    score_scale = 1.0 / math.sqrt(HEAD_DIM)
    tile_ids = jnp.arange(tile_total, dtype=jnp.int32)

    def fold_step(state_now, piece, first_row):
        key_piece, value_piece = piece
        block_count = key_piece.shape[0] // block_len

        def one_block(block_index, state_in):
            key_block = lax.dynamic_slice_in_dim(key_piece, block_index * block_len, block_len, 0)
            value_block = lax.dynamic_slice_in_dim(
                value_piece, block_index * block_len, block_len, 0
            )
            positions = block_index * block_len + jnp.arange(block_len, dtype=jnp.int32)
            key_tiles = key_token(positions) // TILE
            key_onehot = (tile_ids[:, None] == key_tiles[None, :]).astype(jnp.bfloat16)
            allowed = (
                jnp.einsum(
                    "hqj,jk->hqk", listed_rows, key_onehot, preferred_element_type=jnp.float32
                )
                > 0.5
            )
            result = attend_block(
                state_in, key_block, value_block, allowed, query_local, score_scale
            )
            return result

        return lax.fori_loop(0, block_count, one_block, state_now)

    return fold_step


def start_state(heads_here, block_len):
    top_all = jnp.full((heads_here, block_len), NEG_FLOOR, jnp.float32)
    total_all = jnp.zeros((heads_here, block_len), jnp.float32)
    accum_all = jnp.zeros((block_len, heads_here, HEAD_DIM), jnp.float32)
    return (top_all, total_all, accum_all)


def normalize(state_end):
    top_all, total_all, accum_all = state_end
    return (accum_all / jnp.transpose(total_all)[:, :, None]).astype(jnp.bfloat16)


def gathered_plan(queries, keys, values, block_lists):
    row_count, col_count = queries.shape
    n_head = lax.axis_size("head")
    n_sub = lax.axis_size("sub")
    blk_index = lax.axis_index("blk")
    head_index = lax.axis_index("head")
    sub_index = lax.axis_index("sub")
    tile_total = block_lists.shape[1]
    heads_here = HEADS // (n_head * n_sub)
    block_len = row_count * n_head * n_sub

    def inward(tensor):
        return tensor.reshape(1, 1, row_count, n_head, n_sub, heads_here * HEAD_DIM)

    query_six, keys_six, values_six = (
        lax.all_to_all(
            lax.all_to_all(inward(queries), "head", split_axis=3, concat_axis=1, tiled=True),
            "sub",
            split_axis=4,
            concat_axis=0,
            tiled=True,
        ),
        lax.all_to_all(
            lax.all_to_all(inward(keys), "head", split_axis=3, concat_axis=1, tiled=True),
            "sub",
            split_axis=4,
            concat_axis=0,
            tiled=True,
        ),
        lax.all_to_all(
            lax.all_to_all(inward(values), "head", split_axis=3, concat_axis=1, tiled=True),
            "sub",
            split_axis=4,
            concat_axis=0,
            tiled=True,
        ),
    )
    query_local = query_six.reshape(block_len, heads_here, HEAD_DIM)
    keys_local = keys_six.reshape(block_len, heads_here, HEAD_DIM)
    values_local = values_six.reshape(block_len, heads_here, HEAD_DIM)

    def key_token(positions):
        source_dev = positions // block_len
        within = positions % block_len
        sub_source = within // (n_head * row_count)
        head_source = within // row_count % n_head
        offset = within % row_count
        return ((source_dev * n_head + head_source) * n_sub + sub_source) * row_count + offset

    query_tokens = key_token(blk_index * block_len + jnp.arange(block_len, dtype=jnp.int32))
    first_head = (head_index * n_sub + sub_index) * heads_here
    listed_rows = query_rows(block_lists, first_head, heads_here, query_tokens)
    fold_step = make_step(query_local, listed_rows, key_token, block_len, tile_total)
    state_end = fold_step(
        start_state(heads_here, block_len),
        (
            lax.all_gather(keys_local, "blk", axis=0, tiled=True),
            lax.all_gather(values_local, "blk", axis=0, tiled=True),
        ),
        jnp.int32(0),
    )
    result_rows = normalize(state_end)
    attended = result_rows.reshape(n_sub, n_head, row_count, 1, 1, heads_here * HEAD_DIM)
    returned = lax.all_to_all(
        lax.all_to_all(attended, "head", split_axis=1, concat_axis=3, tiled=True),
        "sub",
        split_axis=0,
        concat_axis=4,
        tiled=True,
    )
    return returned.reshape(row_count, col_count)


MESH_TAIL = ("head", "sub")
EXP2_SCALE = math.log2(math.e) / math.sqrt(HEAD_DIM)
TEMPORAL_WEIGHT = 100
VMEM_LIMIT = 16 * 1024 * 1024


class Plan:
    def __init__(self, heads, frames, slots, entries):
        self.heads, self.frames, self.slots, self.entries = heads, frames, slots, entries
        self.count_at = 2 * heads
        self.frame_at = 2 * heads + 2
        self.slot_at = 2 * heads + 3
        self.kind_stride = heads + 1

    def sizes(self, kind):
        return (self.frames, self.slots)[kind]

    def own(self, kind, table_ref):
        return table_ref[(self.frame_at, self.slot_at)[kind]]

    def group(self, kind, table_ref, step):
        own = self.own(kind, table_ref)
        return own ^ step if kind else lax.rem(own + step, self.frames)

    def heads_in_group(self, kind, table_ref, group):
        size = self.sizes(kind)
        return (table_ref[self.count_at + kind] - group + size - 1) // size


def head_columns(head):
    return pl.ds(pl.multiple_of(head * HEAD_DIM, HEAD_DIM), HEAD_DIM)


def fill_order(plan, table_ref, order_ref):
    def clear(p, _):
        order_ref[p] = 0
        return 0

    def place(h, _):
        order_ref[table_ref[h]] = h
        order_ref[plan.kind_stride + table_ref[plan.heads + h]] = h
        return 0

    lax.fori_loop(0, 2 * plan.kind_stride, clear, 0)
    lax.fori_loop(0, plan.heads, place, 0)


def wait_all(ref, sem):
    pltpu.make_async_copy(ref, ref, sem).wait()


def pack_kernel(plan, kind, count, first, table_ref, q_ref, k_ref, v_ref, *rest):
    size = plan.sizes(kind)
    if first:
        outs, order_ref = rest[:size], rest[size]
    else:
        order_ref, outs = rest[0], rest[1 : 1 + size]
    sems = rest[-1]
    if first:
        fill_order(plan, table_ref, order_ref)
    for step in range(size):
        out_ref = outs[step]
        group = plan.group(kind, table_ref, step)

        def one(index, _, group=group, out_ref=out_ref, step=step):
            head = order_ref[kind * plan.kind_stride + index * size + group]
            for place, ref in enumerate((q_ref, k_ref, v_ref)):
                pltpu.make_async_copy(
                    ref.at[:, head_columns(head)], out_ref.at[index, place], sems.at[step]
                ).start()
            return 0

        lax.fori_loop(0, count, one, 0)
    for step, out_ref in enumerate(outs):
        wait_all(out_ref, sems.at[step])


def join_kernel(plan, *refs):
    pieces, out_ref, sems = refs[: plan.slots], refs[-2], refs[-1]
    copies = [
        pltpu.make_async_copy(piece.at[:, pl.ds(1, 2)], out_ref.at[step], sems.at[step])
        for step, piece in enumerate(pieces)
    ]
    for copy in copies:
        copy.start()
    for copy in copies:
        copy.wait()


def attend_tiles(queries, keys, values, biases):
    scores = lax.dot_general(
        jnp.concatenate(queries, 0),
        jnp.concatenate(keys, 0),
        (((1,), (1,)), ((), ())),
        preferred_element_type=jnp.float32,
    )
    rows, totals = [], []
    for a, bias in enumerate(biases):
        tiles = [
            scores[a * TILE : (a + 1) * TILE, b * TILE : (b + 1) * TILE] + bias[b]
            for b in range(len(keys))
        ]
        top = jnp.max(functools.reduce(jnp.maximum, tiles), axis=1, keepdims=True)
        weights = [jnp.exp2((tile - top) * EXP2_SCALE) for tile in tiles]
        totals.append(jnp.sum(functools.reduce(jnp.add, weights), axis=1, keepdims=True))
        rows.append(jnp.concatenate([w.astype(jnp.bfloat16) for w in weights], 1))
    accum = jnp.dot(
        jnp.concatenate(rows, 0), jnp.concatenate(values, 0), preferred_element_type=jnp.float32
    )
    return [
        (accum[a * TILE : (a + 1) * TILE] / total).astype(jnp.bfloat16)
        for a, total in enumerate(totals)
    ]


def bias_of(listed, place):
    return jnp.where((listed >> place) & 1 == 1, jnp.float32(0), jnp.float32(NEG_FLOOR))


def temporal_kernel(plan, table_ref, order_ref, lists_ref, *rest):
    frames = plan.frames
    tiles, outs = rest[:frames], rest[frames : 2 * frames]
    frame, slot = table_ref[plan.frame_at], table_ref[plan.slot_at]
    held = [lax.rem(frame + frames - step, frames) for step in range(frames)]

    def one(index, _):
        head = order_ref[index * frames + frame]
        biases = []
        for step in range(frames):
            first = (held[step] * plan.slots + slot) * plan.entries
            listed = jnp.int32(0)
            for entry in range(plan.entries):
                listed |= jnp.int32(1) << (lists_ref[first + entry, head] // plan.slots)
            biases.append([bias_of(listed, held[other]) for other in range(frames)])
        results = attend_tiles(
            *([tile[index, place] for tile in tiles] for place in range(3)), biases
        )
        for out_ref, result in zip(outs, results):
            out_ref[index] = result
        return 0

    lax.fori_loop(0, plan.heads_in_group(0, table_ref, frame), one, 0)


def spatial_kernel(plan, table_ref, order_ref, lists_ref, *rest):
    slots = plan.slots
    queries, frames_kv = rest[:slots], rest[slots : slots + 3]
    outs, kv_ref, sems = rest[slots + 3 : 2 * slots + 3], rest[-2], rest[-1]
    copies = [
        pltpu.make_async_copy(ref, kv_ref.at[pl.ds(place * slots, slots)], sems.at[place])
        for place, ref in enumerate(frames_kv)
    ]
    for copy in copies:
        copy.start()
    for copy in copies:
        copy.wait()
    frame, slot = table_ref[plan.frame_at], table_ref[plan.slot_at]

    def one(index, _):
        head = order_ref[plan.kind_stride + index * slots + slot]
        for step in range(slots):
            first = (frame * slots + (slot ^ step)) * plan.entries
            listed = jnp.int32(0)
            keys, values, bias = [], [], []
            for entry in range(plan.entries):
                tile = lists_ref[first + entry, head]
                place = (tile // slots - frame + 1) * slots + (lax.rem(tile, slots) ^ slot)
                repeated = (listed >> place) & 1 == 1
                listed |= jnp.int32(1) << place
                bias.append(jnp.where(repeated, jnp.float32(NEG_FLOOR), jnp.float32(0)))
                keys.append(kv_ref[place, index, 0])
                values.append(kv_ref[place, index, 1])
            (outs[step][index],) = attend_tiles([queries[step][index, 0]], keys, values, [bias])
        return 0

    lax.fori_loop(0, plan.heads_in_group(1, table_ref, slot), one, 0)


def unpack_kernel(plan, kinds, table_ref, order_ref, *rest):
    pieces, out_ref, sem = list(rest[:-2]), rest[-2], rest[-1]
    for kind in kinds:
        size = plan.sizes(kind)
        for step in range(size):
            piece = pieces.pop(0)
            group = plan.group(kind, table_ref, step)

            def one(index, _, kind=kind, piece=piece, group=group, size=size):
                head = order_ref[kind * plan.kind_stride + index * size + group]
                pltpu.make_async_copy(
                    piece.at[index], out_ref.at[:, head_columns(head)], sem
                ).start()
                return 0

            lax.fori_loop(0, plan.heads_in_group(kind, table_ref, group), one, 0)
    wait_all(out_ref, sem)


SPACES = {"s": pltpu.SMEM, "v": pltpu.VMEM, "a": pl.ANY}


def call(kernel, outs, operands, places, out_place, scratch=(), flops=0):
    nbytes = sum(math.prod(o.shape) * 2 for o in outs) * 2
    return pl.pallas_call(
        kernel,
        out_shape=outs,
        in_specs=[pl.BlockSpec(memory_space=SPACES[c]) for c in places],
        out_specs=[pl.BlockSpec(memory_space=SPACES[c]) for c in out_place],
        scratch_shapes=list(scratch),
        compiler_params=pltpu.CompilerParams(vmem_limit_bytes=VMEM_LIMIT),
        cost_estimate=pl.CostEstimate(flops=flops, bytes_accessed=nbytes, transcendentals=0),
    )(*operands)


def after(arrays, others):
    if not arrays or not others:
        return arrays
    return pl.pallas_call(
        lambda *refs: None,
        out_shape=[jax.ShapeDtypeStruct(a.shape, a.dtype) for a in arrays],
        in_specs=[pl.BlockSpec(memory_space=pltpu.VMEM)] * (len(arrays) + len(others)),
        out_specs=[pl.BlockSpec(memory_space=pltpu.VMEM)] * len(arrays),
        input_output_aliases={i: i for i in range(len(arrays))},
        compiler_params=pltpu.CompilerParams(vmem_limit_bytes=VMEM_LIMIT),
    )(*arrays, *others)


def tiles_of(*lead):
    return jax.ShapeDtypeStruct((*lead, TILE, HEAD_DIM), jnp.bfloat16)


def by_kind(plan, t_count, s_count, queries, keys, values, lists, table):
    frames, slots = plan.frames, plan.slots
    pair_flops = 4 * TILE * TILE * HEAD_DIM

    def to_frame(array, step):
        pairs = [(z, (z + step) % frames) for z in range(frames)]
        return array if step % frames == 0 else lax.ppermute(array, "blk", pairs)

    def to_slot(array, step):
        pairs = [(s, s ^ step) for s in range(slots)]
        return array if step == 0 else lax.ppermute(array, MESH_TAIL, pairs)

    def halo(array, step):
        pairs = [(z, z + step) for z in range(frames) if 0 <= z + step < frames]
        return lax.ppermute(array, "blk", pairs)

    def pack(kind, count, order):
        size = plan.sizes(kind)
        outs, out_places = [tiles_of(count, 3)] * size, "v" * size
        if order is None:
            outs.append(jax.ShapeDtypeStruct((2 * plan.kind_stride,), jnp.int32))
            out_places += "s"
        results = call(
            functools.partial(pack_kernel, plan, kind, count, order is None),
            outs,
            (table, queries, keys, values) + (() if order is None else (order,)),
            "saaa" + ("" if order is None else "s"),
            out_places,
            [pltpu.SemaphoreType.DMA((size,))],
        )
        return (*results, order) if order is not None else results

    pieces, order = [], None
    if t_count:
        *packed, order = pack(0, t_count, order)
        arrived = [to_frame(block, step) for step, block in enumerate(packed)]
    if s_count:
        *packed, order = pack(1, s_count, order)
        here = [to_slot(block, step) for step, block in enumerate(packed)]
        (joined,) = call(
            functools.partial(join_kernel, plan),
            [tiles_of(slots, s_count, 2)],
            here,
            "v" * slots,
            "v",
            [pltpu.SemaphoreType.DMA((slots,))],
        )
        below, above = halo(joined, 1), halo(joined, -1)
    if t_count:
        attended = call(
            functools.partial(temporal_kernel, plan),
            [tiles_of(t_count)] * frames,
            (table, order, lists, *arrived),
            "sss" + "v" * frames,
            "v" * frames,
            flops=TEMPORAL_WEIGHT * t_count * frames * frames * pair_flops,
        )
        if s_count:
            attended = [attended[0], *after(attended[1:], (below, above))]
        pieces += [to_frame(block, -step) for step, block in enumerate(attended)]
    if s_count:
        attended = call(
            functools.partial(spatial_kernel, plan),
            [tiles_of(s_count)] * slots,
            (table, order, lists, *here, below, joined, above),
            "sss" + "v" * (slots + 3),
            "v" * slots,
            [
                pltpu.VMEM((3 * slots, s_count, 2, TILE, HEAD_DIM), jnp.bfloat16),
                pltpu.SemaphoreType.DMA((3,)),
            ],
            flops=s_count * slots * plan.entries * pair_flops,
        )
        attended = [attended[0], *after(attended[1:2], pieces[1:]), *attended[2:]]
        pieces += [to_slot(block, step) for step, block in enumerate(attended)]
    kinds = [kind for kind, count in enumerate((t_count, s_count)) if count]
    (out,) = call(
        functools.partial(unpack_kernel, plan, kinds),
        [jax.ShapeDtypeStruct((TILE, plan.heads * HEAD_DIM), jnp.bfloat16)],
        (table, order, *pieces),
        "ss" + "v" * len(pieces),
        "a",
        [pltpu.SemaphoreType.DMA],
    )
    return out


def kind_plan(queries, keys, values, block_lists):
    heads, tiles, entries = block_lists.shape
    frames = lax.axis_size("blk")
    slots = lax.axis_size(MESH_TAIL)
    plan = Plan(heads, frames, slots, entries)
    head_ids = jnp.arange(heads, dtype=jnp.int32)
    tile_slot = jnp.arange(tiles, dtype=jnp.int32) % slots
    temporal = jnp.all(block_lists % slots == tile_slot[None, :, None], axis=(1, 2))
    before = head_ids[None, :] < head_ids[:, None]
    rank_t = jnp.sum((before & temporal[None, :]).astype(jnp.int32), axis=1)
    total_t = jnp.sum(temporal.astype(jnp.int32))
    table = jnp.concatenate(
        [
            jnp.where(temporal, rank_t, heads),
            jnp.where(temporal, heads, head_ids - rank_t),
            jnp.stack(
                [
                    total_t,
                    heads - total_t,
                    lax.axis_index("blk").astype(jnp.int32),
                    lax.axis_index(MESH_TAIL).astype(jnp.int32),
                ]
            ),
        ]
    )
    lists = jnp.transpose(block_lists, (1, 2, 0)).reshape(tiles * entries, heads)
    pairs = []
    for chunks in range(-(-heads // frames) + 1):
        fewest = 0 if chunks == 0 else (chunks - 1) * frames + 1
        pairs.append((chunks, -(-(heads - fewest) // slots)))
    branches = [functools.partial(by_kind, plan, t, s) for t, s in pairs]
    return lax.switch(
        (total_t + frames - 1) // frames, branches, queries, keys, values, lists, table
    )


def per_device(queries, keys, values, block_lists):
    slots = lax.axis_size(MESH_TAIL)
    whole_tiles = queries.shape[0] == TILE and slots == FRAME_TILES
    if whole_tiles and lax.axis_size("blk") * slots == block_lists.shape[1]:
        return kind_plan(queries, keys, values, block_lists)
    return gathered_plan(queries, keys, values, block_lists)


def solution(mesh):
    in_specs = (
        P(("grp", "blk", "head", "sub"), None),
        P(("grp", "blk", "head", "sub"), None),
        P(("grp", "blk", "head", "sub"), None),
        P(),
    )
    out_specs = P(("grp", "blk", "head", "sub"), None)
    return jax.shard_map(
        per_device, mesh=mesh, in_specs=in_specs, out_specs=out_specs, check_vma=False
    )
```

```python
import functools
import math

import jax
import jax.numpy as jnp
from jax import lax
from jax.experimental import pallas as pl
from jax.experimental.pallas import tpu as pltpu
from jax.sharding import PartitionSpec as P

HEADS = 32
HEAD_DIM = 128
TILE = 128
FRAME_TILES = 4


NEG_FLOOR = -1e30


def query_rows(block_lists, first_head, heads_here, query_tokens):
    tile_ids = jnp.arange(block_lists.shape[1], dtype=jnp.int32)
    lists_local = lax.dynamic_slice_in_dim(block_lists, first_head, heads_here, 0)
    tile_mask = jnp.any(lists_local[:, :, :, None] == tile_ids, axis=2).astype(jnp.bfloat16)
    query_onehot = ((query_tokens // TILE)[:, None] == tile_ids[None, :]).astype(jnp.bfloat16)
    listed = jnp.einsum("qi,hij->hqj", query_onehot, tile_mask, preferred_element_type=jnp.float32)
    return listed.astype(jnp.bfloat16)


def attend_block(state_now, key_block, value_block, allowed, query_local, score_scale):
    top_old, total_old, accum_old = state_now
    scores = (
        jnp.einsum("qhd,khd->hqk", query_local, key_block, preferred_element_type=jnp.float32)
        * score_scale
    )
    top_new = jnp.maximum(top_old, jnp.max(jnp.where(allowed, scores, NEG_FLOOR), axis=2))
    factor = jnp.exp(top_old - top_new)
    weights = jnp.where(allowed, jnp.exp(scores - top_new[:, :, None]), 0.0)
    total_new = total_old * factor + jnp.sum(weights, axis=2)
    product = jnp.einsum(
        "hqk,khd->qhd",
        weights.astype(jnp.bfloat16),
        value_block,
        preferred_element_type=jnp.float32,
    )
    accum_new = accum_old * jnp.transpose(factor)[:, :, None] + product
    return (top_new, total_new, accum_new)


def make_step(query_local, listed_rows, key_token, block_len, tile_total):
    score_scale = 1.0 / math.sqrt(HEAD_DIM)
    tile_ids = jnp.arange(tile_total, dtype=jnp.int32)

    def fold_step(state_now, piece, first_row):
        key_piece, value_piece = piece
        block_count = key_piece.shape[0] // block_len

        def one_block(block_index, state_in):
            key_block = lax.dynamic_slice_in_dim(key_piece, block_index * block_len, block_len, 0)
            value_block = lax.dynamic_slice_in_dim(
                value_piece, block_index * block_len, block_len, 0
            )
            positions = block_index * block_len + jnp.arange(block_len, dtype=jnp.int32)
            key_tiles = key_token(positions) // TILE
            key_onehot = (tile_ids[:, None] == key_tiles[None, :]).astype(jnp.bfloat16)
            allowed = (
                jnp.einsum(
                    "hqj,jk->hqk", listed_rows, key_onehot, preferred_element_type=jnp.float32
                )
                > 0.5
            )
            result = attend_block(
                state_in, key_block, value_block, allowed, query_local, score_scale
            )
            return result

        return lax.fori_loop(0, block_count, one_block, state_now)

    return fold_step


def start_state(heads_here, block_len):
    top_all = jnp.full((heads_here, block_len), NEG_FLOOR, jnp.float32)
    total_all = jnp.zeros((heads_here, block_len), jnp.float32)
    accum_all = jnp.zeros((block_len, heads_here, HEAD_DIM), jnp.float32)
    return (top_all, total_all, accum_all)


def normalize(state_end):
    top_all, total_all, accum_all = state_end
    return (accum_all / jnp.transpose(total_all)[:, :, None]).astype(jnp.bfloat16)


def gathered_plan(queries, keys, values, block_lists):
    row_count, col_count = queries.shape
    n_head = lax.axis_size("head")
    n_sub = lax.axis_size("sub")
    blk_index = lax.axis_index("blk")
    head_index = lax.axis_index("head")
    sub_index = lax.axis_index("sub")
    tile_total = block_lists.shape[1]
    heads_here = HEADS // (n_head * n_sub)
    block_len = row_count * n_head * n_sub

    def inward(tensor):
        return tensor.reshape(1, 1, row_count, n_head, n_sub, heads_here * HEAD_DIM)

    query_six, keys_six, values_six = (
        lax.all_to_all(
            lax.all_to_all(inward(queries), "head", split_axis=3, concat_axis=1, tiled=True),
            "sub",
            split_axis=4,
            concat_axis=0,
            tiled=True,
        ),
        lax.all_to_all(
            lax.all_to_all(inward(keys), "head", split_axis=3, concat_axis=1, tiled=True),
            "sub",
            split_axis=4,
            concat_axis=0,
            tiled=True,
        ),
        lax.all_to_all(
            lax.all_to_all(inward(values), "head", split_axis=3, concat_axis=1, tiled=True),
            "sub",
            split_axis=4,
            concat_axis=0,
            tiled=True,
        ),
    )
    query_local = query_six.reshape(block_len, heads_here, HEAD_DIM)
    keys_local = keys_six.reshape(block_len, heads_here, HEAD_DIM)
    values_local = values_six.reshape(block_len, heads_here, HEAD_DIM)

    def key_token(positions):
        source_dev = positions // block_len
        within = positions % block_len
        sub_source = within // (n_head * row_count)
        head_source = within // row_count % n_head
        offset = within % row_count
        return ((source_dev * n_head + head_source) * n_sub + sub_source) * row_count + offset

    query_tokens = key_token(blk_index * block_len + jnp.arange(block_len, dtype=jnp.int32))
    first_head = (head_index * n_sub + sub_index) * heads_here
    listed_rows = query_rows(block_lists, first_head, heads_here, query_tokens)
    fold_step = make_step(query_local, listed_rows, key_token, block_len, tile_total)
    state_end = fold_step(
        start_state(heads_here, block_len),
        (
            lax.all_gather(keys_local, "blk", axis=0, tiled=True),
            lax.all_gather(values_local, "blk", axis=0, tiled=True),
        ),
        jnp.int32(0),
    )
    result_rows = normalize(state_end)
    attended = result_rows.reshape(n_sub, n_head, row_count, 1, 1, heads_here * HEAD_DIM)
    returned = lax.all_to_all(
        lax.all_to_all(attended, "head", split_axis=1, concat_axis=3, tiled=True),
        "sub",
        split_axis=0,
        concat_axis=4,
        tiled=True,
    )
    return returned.reshape(row_count, col_count)


MESH_TAIL = ("head", "sub")
EXP2_SCALE = math.log2(math.e) / math.sqrt(HEAD_DIM)
TEMPORAL_WEIGHT = 100
VMEM_LIMIT = 16 * 1024 * 1024


class Plan:
    def __init__(self, heads, frames, slots, entries):
        self.heads, self.frames, self.slots, self.entries = heads, frames, slots, entries
        self.count_at = 2 * heads
        self.frame_at = 2 * heads + 2
        self.slot_at = 2 * heads + 3
        self.kind_stride = heads + 1

    def sizes(self, kind):
        return (self.frames, self.slots)[kind]

    def own(self, kind, table_ref):
        return table_ref[(self.frame_at, self.slot_at)[kind]]

    def group(self, kind, table_ref, step):
        own = self.own(kind, table_ref)
        return own ^ step if kind else lax.rem(own + step, self.frames)

    def heads_in_group(self, kind, table_ref, group):
        size = self.sizes(kind)
        return (table_ref[self.count_at + kind] - group + size - 1) // size


def head_columns(head):
    return pl.ds(pl.multiple_of(head * HEAD_DIM, HEAD_DIM), HEAD_DIM)


def fill_order(plan, table_ref, order_ref):
    def clear(p, _):
        order_ref[p] = 0
        return 0

    def place(h, _):
        order_ref[table_ref[h]] = h
        order_ref[plan.kind_stride + table_ref[plan.heads + h]] = h
        return 0

    lax.fori_loop(0, 2 * plan.kind_stride, clear, 0)
    lax.fori_loop(0, plan.heads, place, 0)


def wait_all(ref, sem):
    pltpu.make_async_copy(ref, ref, sem).wait()


def pack_kernel(plan, kind, count, first, table_ref, q_ref, k_ref, v_ref, *rest):
    size = plan.sizes(kind)
    if first:
        outs, order_ref = rest[:size], rest[size]
    else:
        order_ref, outs = rest[0], rest[1 : 1 + size]
    sems = rest[-1]
    if first:
        fill_order(plan, table_ref, order_ref)
    for step in range(size):
        out_ref = outs[step]
        group = plan.group(kind, table_ref, step)

        def one(index, _, group=group, out_ref=out_ref, step=step):
            head = order_ref[kind * plan.kind_stride + index * size + group]
            for place, ref in enumerate((q_ref, k_ref, v_ref)):
                pltpu.make_async_copy(
                    ref.at[:, head_columns(head)], out_ref.at[index, place], sems.at[step]
                ).start()
            return 0

        lax.fori_loop(0, count, one, 0)
    for step, out_ref in enumerate(outs):
        wait_all(out_ref, sems.at[step])


def join_kernel(plan, *refs):
    pieces, out_ref, sems = refs[: plan.slots], refs[-2], refs[-1]
    copies = [
        pltpu.make_async_copy(piece.at[:, pl.ds(1, 2)], out_ref.at[step], sems.at[step])
        for step, piece in enumerate(pieces)
    ]
    for copy in copies:
        copy.start()
    for copy in copies:
        copy.wait()


def attend_tile(query, keys, values, biases):
    scores = lax.dot_general(
        query,
        jnp.concatenate(keys, 0),
        (((1,), (1,)), ((), ())),
        preferred_element_type=jnp.float32,
    )
    tiles = [scores[:, b * TILE : (b + 1) * TILE] + bias for b, bias in enumerate(biases)]
    top = jnp.max(functools.reduce(jnp.maximum, tiles), axis=1, keepdims=True)
    weights = [jnp.exp2((tile - top) * EXP2_SCALE) for tile in tiles]
    total = jnp.sum(functools.reduce(jnp.add, weights), axis=1, keepdims=True)
    accum = jnp.dot(
        jnp.concatenate([w.astype(jnp.bfloat16) for w in weights], 1),
        jnp.concatenate(values, 0),
        preferred_element_type=jnp.float32,
    )
    return (accum / total).astype(jnp.bfloat16)


def bias_where(attended):
    return jnp.where(attended, jnp.float32(0), jnp.float32(NEG_FLOOR))


def copy_pieces(pieces, sems):
    copies = [pltpu.make_async_copy(a, b, sems.at[i]) for i, (a, b) in enumerate(pieces)]
    for copy in copies:
        copy.start()
    for copy in copies:
        copy.wait()


def temporal_kernel(plan, table_ref, order_ref, lists_ref, *rest):
    frames, slots = plan.frames, plan.slots
    tiles, outs = rest[:frames], rest[frames : 2 * frames]
    held_ref, result_ref, sems = rest[2 * frames :]
    copy_pieces([(tile, held_ref.at[step]) for step, tile in enumerate(tiles)], sems)
    frame, slot = table_ref[plan.frame_at], table_ref[plan.slot_at]
    held = [lax.rem(frame + frames - step, frames) for step in range(frames)]

    def one(work, _):
        index, step = work // frames, lax.rem(work, frames)
        head = order_ref[index * frames + frame]
        first = (lax.rem(frame + frames - step, frames) * slots + slot) * plan.entries
        listed = jnp.int32(0)
        for entry in range(plan.entries):
            listed |= jnp.int32(1) << (lists_ref[first + entry, head] // slots)
        result_ref[step, index] = attend_tile(
            held_ref[step, index, 0],
            [held_ref[other, index, 1] for other in range(frames)],
            [held_ref[other, index, 2] for other in range(frames)],
            [bias_where((listed >> held[other]) & 1 == 1) for other in range(frames)],
        )
        return 0

    lax.fori_loop(0, plan.heads_in_group(0, table_ref, frame) * frames, one, 0)
    copy_pieces([(result_ref.at[step], out) for step, out in enumerate(outs)], sems)


def spatial_kernel(plan, table_ref, order_ref, lists_ref, *rest):
    slots = plan.slots
    here, frames_kv = rest[:slots], rest[slots : slots + 3]
    outs = rest[slots + 3 : 2 * slots + 3]
    q_ref, kv_ref, result_ref, sems = rest[2 * slots + 3 :]
    copy_pieces(
        [(ref, kv_ref.at[pl.ds(i * slots, slots)]) for i, ref in enumerate(frames_kv)]
        + [(ref.at[:, 0], q_ref.at[step]) for step, ref in enumerate(here)],
        sems,
    )
    frame, slot = table_ref[plan.frame_at], table_ref[plan.slot_at]

    def one(work, _):
        index, step = work // slots, lax.rem(work, slots)
        head = order_ref[plan.kind_stride + index * slots + slot]
        first = (frame * slots + (slot ^ step)) * plan.entries
        listed = jnp.int32(0)
        places, biases = [], []
        for entry in range(plan.entries):
            tile = lists_ref[first + entry, head]
            place = (tile // slots - frame + 1) * slots + (lax.rem(tile, slots) ^ slot)
            places.append(place)
            biases.append(bias_where((listed >> place) & 1 == 0))
            listed |= jnp.int32(1) << place
        result_ref[step, index] = attend_tile(
            q_ref[step, index],
            [kv_ref[place, index, 0] for place in places],
            [kv_ref[place, index, 1] for place in places],
            biases,
        )
        return 0

    lax.fori_loop(0, plan.heads_in_group(1, table_ref, slot) * slots, one, 0)
    copy_pieces([(result_ref.at[step], out) for step, out in enumerate(outs)], sems)


def unpack_kernel(plan, kinds, table_ref, order_ref, *rest):
    pieces, out_ref, sem = list(rest[:-2]), rest[-2], rest[-1]
    for kind in kinds:
        size = plan.sizes(kind)
        for step in range(size):
            piece = pieces.pop(0)
            group = plan.group(kind, table_ref, step)

            def one(index, _, kind=kind, piece=piece, group=group, size=size):
                head = order_ref[kind * plan.kind_stride + index * size + group]
                pltpu.make_async_copy(
                    piece.at[index], out_ref.at[:, head_columns(head)], sem
                ).start()
                return 0

            lax.fori_loop(0, plan.heads_in_group(kind, table_ref, group), one, 0)
    wait_all(out_ref, sem)


SPACES = {"s": pltpu.SMEM, "v": pltpu.VMEM, "a": pl.ANY}


def call(kernel, outs, operands, places, out_place, scratch=(), flops=0):
    nbytes = sum(math.prod(o.shape) * 2 for o in outs) * 2
    return pl.pallas_call(
        kernel,
        out_shape=outs,
        in_specs=[pl.BlockSpec(memory_space=SPACES[c]) for c in places],
        out_specs=[pl.BlockSpec(memory_space=SPACES[c]) for c in out_place],
        scratch_shapes=list(scratch),
        compiler_params=pltpu.CompilerParams(vmem_limit_bytes=VMEM_LIMIT),
        cost_estimate=pl.CostEstimate(flops=flops, bytes_accessed=nbytes, transcendentals=0),
    )(*operands)


def after(arrays, others):
    if not arrays or not others:
        return arrays
    return pl.pallas_call(
        lambda *refs: None,
        out_shape=[jax.ShapeDtypeStruct(a.shape, a.dtype) for a in arrays],
        in_specs=[pl.BlockSpec(memory_space=pltpu.VMEM)] * (len(arrays) + len(others)),
        out_specs=[pl.BlockSpec(memory_space=pltpu.VMEM)] * len(arrays),
        input_output_aliases={i: i for i in range(len(arrays))},
        compiler_params=pltpu.CompilerParams(vmem_limit_bytes=VMEM_LIMIT),
    )(*arrays, *others)


def tiles_of(*lead):
    return jax.ShapeDtypeStruct((*lead, TILE, HEAD_DIM), jnp.bfloat16)


def by_kind(plan, t_count, s_count, queries, keys, values, lists, table):
    frames, slots = plan.frames, plan.slots
    pair_flops = 4 * TILE * TILE * HEAD_DIM

    def to_frame(array, step):
        pairs = [(z, (z + step) % frames) for z in range(frames)]
        return array if step % frames == 0 else lax.ppermute(array, "blk", pairs)

    def to_slot(array, step):
        pairs = [(s, s ^ step) for s in range(slots)]
        return array if step == 0 else lax.ppermute(array, MESH_TAIL, pairs)

    def halo(array, step):
        pairs = [(z, z + step) for z in range(frames) if 0 <= z + step < frames]
        return lax.ppermute(array, "blk", pairs)

    def pack(kind, count, order):
        size = plan.sizes(kind)
        outs, out_places = [tiles_of(count, 3)] * size, "v" * size
        if order is None:
            outs.append(jax.ShapeDtypeStruct((2 * plan.kind_stride,), jnp.int32))
            out_places += "s"
        results = call(
            functools.partial(pack_kernel, plan, kind, count, order is None),
            outs,
            (table, queries, keys, values) + (() if order is None else (order,)),
            "saaa" + ("" if order is None else "s"),
            out_places,
            [pltpu.SemaphoreType.DMA((size,))],
        )
        return (*results, order) if order is not None else results

    pieces, order = [], None
    if t_count:
        *packed, order = pack(0, t_count, order)
        arrived = [to_frame(block, step) for step, block in enumerate(packed)]
    if s_count:
        *packed, order = pack(1, s_count, order)
        here = [to_slot(block, step) for step, block in enumerate(packed)]
        (joined,) = call(
            functools.partial(join_kernel, plan),
            [tiles_of(slots, s_count, 2)],
            here,
            "v" * slots,
            "v",
            [pltpu.SemaphoreType.DMA((slots,))],
        )
        below, above = halo(joined, 1), halo(joined, -1)
    if t_count:
        attended = call(
            functools.partial(temporal_kernel, plan),
            [tiles_of(t_count)] * frames,
            (table, order, lists, *arrived),
            "sss" + "v" * frames,
            "v" * frames,
            [
                pltpu.VMEM((frames, t_count, 3, TILE, HEAD_DIM), jnp.bfloat16),
                pltpu.VMEM((frames, t_count, TILE, HEAD_DIM), jnp.bfloat16),
                pltpu.SemaphoreType.DMA((frames,)),
            ],
            flops=TEMPORAL_WEIGHT * t_count * frames * frames * pair_flops,
        )
        if s_count:
            attended = [attended[0], *after(attended[1:], (below, above))]
        pieces += [to_frame(block, -step) for step, block in enumerate(attended)]
    if s_count:
        attended = call(
            functools.partial(spatial_kernel, plan),
            [tiles_of(s_count)] * slots,
            (table, order, lists, *here, below, joined, above),
            "sss" + "v" * (slots + 3),
            "v" * slots,
            [
                pltpu.VMEM((slots, s_count, TILE, HEAD_DIM), jnp.bfloat16),
                pltpu.VMEM((3 * slots, s_count, 2, TILE, HEAD_DIM), jnp.bfloat16),
                pltpu.VMEM((slots, s_count, TILE, HEAD_DIM), jnp.bfloat16),
                pltpu.SemaphoreType.DMA((3 + slots,)),
            ],
            flops=s_count * slots * plan.entries * pair_flops,
        )
        attended = [attended[0], *after(attended[1:2], pieces[1:]), *attended[2:]]
        pieces += [to_slot(block, step) for step, block in enumerate(attended)]
    kinds = [kind for kind, count in enumerate((t_count, s_count)) if count]
    (out,) = call(
        functools.partial(unpack_kernel, plan, kinds),
        [jax.ShapeDtypeStruct((TILE, plan.heads * HEAD_DIM), jnp.bfloat16)],
        (table, order, *pieces),
        "ss" + "v" * len(pieces),
        "a",
        [pltpu.SemaphoreType.DMA],
    )
    return out


def kind_plan(queries, keys, values, block_lists):
    heads, tiles, entries = block_lists.shape
    frames = lax.axis_size("blk")
    slots = lax.axis_size(MESH_TAIL)
    plan = Plan(heads, frames, slots, entries)
    head_ids = jnp.arange(heads, dtype=jnp.int32)
    tile_slot = jnp.arange(tiles, dtype=jnp.int32) % slots
    temporal = jnp.all(block_lists % slots == tile_slot[None, :, None], axis=(1, 2))
    before = head_ids[None, :] < head_ids[:, None]
    rank_t = jnp.sum((before & temporal[None, :]).astype(jnp.int32), axis=1)
    total_t = jnp.sum(temporal.astype(jnp.int32))
    table = jnp.concatenate(
        [
            jnp.where(temporal, rank_t, heads),
            jnp.where(temporal, heads, head_ids - rank_t),
            jnp.stack(
                [
                    total_t,
                    heads - total_t,
                    lax.axis_index("blk").astype(jnp.int32),
                    lax.axis_index(MESH_TAIL).astype(jnp.int32),
                ]
            ),
        ]
    )
    lists = jnp.transpose(block_lists, (1, 2, 0)).reshape(tiles * entries, heads)
    pairs = []
    for chunks in range(-(-heads // frames) + 1):
        fewest = 0 if chunks == 0 else (chunks - 1) * frames + 1
        pairs.append((chunks, -(-(heads - fewest) // slots)))
    branches = [functools.partial(by_kind, plan, t, s) for t, s in pairs]
    return lax.switch(
        (total_t + frames - 1) // frames, branches, queries, keys, values, lists, table
    )


def per_device(queries, keys, values, block_lists):
    slots = lax.axis_size(MESH_TAIL)
    whole_tiles = queries.shape[0] == TILE and slots == FRAME_TILES
    if whole_tiles and lax.axis_size("blk") * slots == block_lists.shape[1]:
        return kind_plan(queries, keys, values, block_lists)
    return gathered_plan(queries, keys, values, block_lists)


def solution(mesh):
    in_specs = (
        P(("grp", "blk", "head", "sub"), None),
        P(("grp", "blk", "head", "sub"), None),
        P(("grp", "blk", "head", "sub"), None),
        P(),
    )
    out_specs = P(("grp", "blk", "head", "sub"), None)
    return jax.shard_map(
        per_device, mesh=mesh, in_specs=in_specs, out_specs=out_specs, check_vma=False
    )
```

```python
import functools
import math

import jax
import jax.numpy as jnp
from jax import lax
from jax.experimental import pallas as pl
from jax.experimental.pallas import tpu as pltpu
from jax.sharding import PartitionSpec as P

HEADS = 32
HEAD_DIM = 128
TILE = 128
FRAME_TILES = 4


NEG_FLOOR = -1e30


def query_rows(block_lists, first_head, heads_here, query_tokens):
    tile_ids = jnp.arange(block_lists.shape[1], dtype=jnp.int32)
    lists_local = lax.dynamic_slice_in_dim(block_lists, first_head, heads_here, 0)
    tile_mask = jnp.any(lists_local[:, :, :, None] == tile_ids, axis=2).astype(jnp.bfloat16)
    query_onehot = ((query_tokens // TILE)[:, None] == tile_ids[None, :]).astype(jnp.bfloat16)
    listed = jnp.einsum("qi,hij->hqj", query_onehot, tile_mask, preferred_element_type=jnp.float32)
    return listed.astype(jnp.bfloat16)


def attend_block(state_now, key_block, value_block, allowed, query_local, score_scale):
    top_old, total_old, accum_old = state_now
    scores = (
        jnp.einsum("qhd,khd->hqk", query_local, key_block, preferred_element_type=jnp.float32)
        * score_scale
    )
    top_new = jnp.maximum(top_old, jnp.max(jnp.where(allowed, scores, NEG_FLOOR), axis=2))
    factor = jnp.exp(top_old - top_new)
    weights = jnp.where(allowed, jnp.exp(scores - top_new[:, :, None]), 0.0)
    total_new = total_old * factor + jnp.sum(weights, axis=2)
    product = jnp.einsum(
        "hqk,khd->qhd",
        weights.astype(jnp.bfloat16),
        value_block,
        preferred_element_type=jnp.float32,
    )
    accum_new = accum_old * jnp.transpose(factor)[:, :, None] + product
    return (top_new, total_new, accum_new)


def make_step(query_local, listed_rows, key_token, block_len, tile_total):
    score_scale = 1.0 / math.sqrt(HEAD_DIM)
    tile_ids = jnp.arange(tile_total, dtype=jnp.int32)

    def fold_step(state_now, piece, first_row):
        key_piece, value_piece = piece
        block_count = key_piece.shape[0] // block_len

        def one_block(block_index, state_in):
            key_block = lax.dynamic_slice_in_dim(key_piece, block_index * block_len, block_len, 0)
            value_block = lax.dynamic_slice_in_dim(
                value_piece, block_index * block_len, block_len, 0
            )
            positions = block_index * block_len + jnp.arange(block_len, dtype=jnp.int32)
            key_tiles = key_token(positions) // TILE
            key_onehot = (tile_ids[:, None] == key_tiles[None, :]).astype(jnp.bfloat16)
            allowed = (
                jnp.einsum(
                    "hqj,jk->hqk", listed_rows, key_onehot, preferred_element_type=jnp.float32
                )
                > 0.5
            )
            result = attend_block(
                state_in, key_block, value_block, allowed, query_local, score_scale
            )
            return result

        return lax.fori_loop(0, block_count, one_block, state_now)

    return fold_step


def start_state(heads_here, block_len):
    top_all = jnp.full((heads_here, block_len), NEG_FLOOR, jnp.float32)
    total_all = jnp.zeros((heads_here, block_len), jnp.float32)
    accum_all = jnp.zeros((block_len, heads_here, HEAD_DIM), jnp.float32)
    return (top_all, total_all, accum_all)


def normalize(state_end):
    top_all, total_all, accum_all = state_end
    return (accum_all / jnp.transpose(total_all)[:, :, None]).astype(jnp.bfloat16)


def gathered_plan(queries, keys, values, block_lists):
    row_count, col_count = queries.shape
    n_head = lax.axis_size("head")
    n_sub = lax.axis_size("sub")
    blk_index = lax.axis_index("blk")
    head_index = lax.axis_index("head")
    sub_index = lax.axis_index("sub")
    tile_total = block_lists.shape[1]
    heads_here = HEADS // (n_head * n_sub)
    block_len = row_count * n_head * n_sub

    def inward(tensor):
        return tensor.reshape(1, 1, row_count, n_head, n_sub, heads_here * HEAD_DIM)

    query_six, keys_six, values_six = (
        lax.all_to_all(
            lax.all_to_all(inward(queries), "head", split_axis=3, concat_axis=1, tiled=True),
            "sub",
            split_axis=4,
            concat_axis=0,
            tiled=True,
        ),
        lax.all_to_all(
            lax.all_to_all(inward(keys), "head", split_axis=3, concat_axis=1, tiled=True),
            "sub",
            split_axis=4,
            concat_axis=0,
            tiled=True,
        ),
        lax.all_to_all(
            lax.all_to_all(inward(values), "head", split_axis=3, concat_axis=1, tiled=True),
            "sub",
            split_axis=4,
            concat_axis=0,
            tiled=True,
        ),
    )
    query_local = query_six.reshape(block_len, heads_here, HEAD_DIM)
    keys_local = keys_six.reshape(block_len, heads_here, HEAD_DIM)
    values_local = values_six.reshape(block_len, heads_here, HEAD_DIM)

    def key_token(positions):
        source_dev = positions // block_len
        within = positions % block_len
        sub_source = within // (n_head * row_count)
        head_source = within // row_count % n_head
        offset = within % row_count
        return ((source_dev * n_head + head_source) * n_sub + sub_source) * row_count + offset

    query_tokens = key_token(blk_index * block_len + jnp.arange(block_len, dtype=jnp.int32))
    first_head = (head_index * n_sub + sub_index) * heads_here
    listed_rows = query_rows(block_lists, first_head, heads_here, query_tokens)
    fold_step = make_step(query_local, listed_rows, key_token, block_len, tile_total)
    state_end = fold_step(
        start_state(heads_here, block_len),
        (
            lax.all_gather(keys_local, "blk", axis=0, tiled=True),
            lax.all_gather(values_local, "blk", axis=0, tiled=True),
        ),
        jnp.int32(0),
    )
    result_rows = normalize(state_end)
    attended = result_rows.reshape(n_sub, n_head, row_count, 1, 1, heads_here * HEAD_DIM)
    returned = lax.all_to_all(
        lax.all_to_all(attended, "head", split_axis=1, concat_axis=3, tiled=True),
        "sub",
        split_axis=0,
        concat_axis=4,
        tiled=True,
    )
    return returned.reshape(row_count, col_count)


MESH_TAIL = ("head", "sub")
EXP2_SCALE = math.log2(math.e) / math.sqrt(HEAD_DIM)
TEMPORAL_WEIGHT = 100
TILES_A_BODY = 2
VMEM_LIMIT = 16 * 1024 * 1024


class Plan:
    def __init__(self, heads, frames, slots, entries):
        self.heads, self.frames, self.slots, self.entries = heads, frames, slots, entries
        self.count_at = 2 * heads
        self.frame_at = 2 * heads + 2
        self.slot_at = 2 * heads + 3
        self.kind_stride = heads + 1

    def sizes(self, kind):
        return (self.frames, self.slots)[kind]

    def own(self, kind, table_ref):
        return table_ref[(self.frame_at, self.slot_at)[kind]]

    def group(self, kind, table_ref, step):
        return self.own(kind, table_ref) ^ step

    def heads_in_group(self, kind, table_ref, group):
        size = self.sizes(kind)
        return (table_ref[self.count_at + kind] - group + size - 1) // size


def head_columns(head):
    return pl.ds(pl.multiple_of(head * HEAD_DIM, HEAD_DIM), HEAD_DIM)


def fill_order(plan, table_ref, order_ref):
    def clear(p, _):
        order_ref[p] = 0
        return 0

    def place(h, _):
        order_ref[table_ref[h]] = h
        order_ref[plan.kind_stride + table_ref[plan.heads + h]] = h
        return 0

    lax.fori_loop(0, 2 * plan.kind_stride, clear, 0)
    lax.fori_loop(0, plan.heads, place, 0)


def wait_all(ref, sem):
    pltpu.make_async_copy(ref, ref, sem).wait()


def pack_kernel(plan, kind, count, first, table_ref, q_ref, k_ref, v_ref, *rest):
    size = plan.sizes(kind)
    if first:
        outs, order_ref = rest[:size], rest[size]
    else:
        order_ref, outs = rest[0], rest[1 : 1 + size]
    sems = rest[-1]
    if first:
        fill_order(plan, table_ref, order_ref)
    for step in range(size):
        out_ref = outs[step]
        group = plan.group(kind, table_ref, step)

        def one(index, _, group=group, out_ref=out_ref, step=step):
            head = order_ref[kind * plan.kind_stride + index * size + group]
            for place, ref in enumerate((q_ref, k_ref, v_ref)):
                pltpu.make_async_copy(
                    ref.at[:, head_columns(head)], out_ref.at[index, place], sems.at[step]
                ).start()
            return 0

        lax.fori_loop(0, count, one, 0)
    for step, out_ref in enumerate(outs):
        wait_all(out_ref, sems.at[step])


def join_kernel(plan, *refs):
    pieces, out_ref, sems = refs[: plan.slots], refs[-2], refs[-1]
    copies = [
        pltpu.make_async_copy(piece.at[:, pl.ds(1, 2)], out_ref.at[step], sems.at[step])
        for step, piece in enumerate(pieces)
    ]
    for copy in copies:
        copy.start()
    for copy in copies:
        copy.wait()


def attend_tile(query, keys, values, biases):
    scores = lax.dot_general(
        query,
        jnp.concatenate(keys, 0),
        (((1,), (1,)), ((), ())),
        preferred_element_type=jnp.float32,
    )
    tiles = [scores[:, b * TILE : (b + 1) * TILE] + bias for b, bias in enumerate(biases)]
    top = jnp.max(functools.reduce(jnp.maximum, tiles), axis=1, keepdims=True)
    weights = [jnp.exp2((tile - top) * EXP2_SCALE) for tile in tiles]
    total = jnp.sum(functools.reduce(jnp.add, weights), axis=1, keepdims=True)
    accum = jnp.dot(
        jnp.concatenate([w.astype(jnp.bfloat16) for w in weights], 1),
        jnp.concatenate(values, 0),
        preferred_element_type=jnp.float32,
    )
    return (accum / total).astype(jnp.bfloat16)


def bias_where(attended):
    return jnp.where(attended, jnp.float32(0), jnp.float32(NEG_FLOOR))


def copy_pieces(pieces, sems):
    copies = [pltpu.make_async_copy(a, b, sems.at[i]) for i, (a, b) in enumerate(pieces)]
    for copy in copies:
        copy.start()
    for copy in copies:
        copy.wait()


def by_tiles(one, heads_here, steps):
    bodies = steps // TILES_A_BODY

    def body(work, _):
        index, first = work // bodies, lax.rem(work, bodies) * TILES_A_BODY
        for more in range(TILES_A_BODY):
            one(index, first + more)
        return 0

    lax.fori_loop(0, heads_here * bodies, body, 0)


def temporal_kernel(plan, table_ref, order_ref, lists_ref, *rest):
    frames, slots = plan.frames, plan.slots
    tiles, outs = rest[:frames], rest[frames : 2 * frames]
    held_ref, result_ref, sems = rest[2 * frames :]
    copy_pieces([(tile, held_ref.at[step]) for step, tile in enumerate(tiles)], sems)
    frame, slot = table_ref[plan.frame_at], table_ref[plan.slot_at]

    def one(index, step):
        head = order_ref[index * frames + frame]
        first = ((frame ^ step) * slots + slot) * plan.entries
        listed = jnp.int32(0)
        for entry in range(plan.entries):
            listed |= jnp.int32(1) << (lists_ref[first + entry, head] // slots)
        result_ref[step, index] = attend_tile(
            held_ref[step, index, 0],
            [held_ref[other, index, 1] for other in range(frames)],
            [held_ref[other, index, 2] for other in range(frames)],
            [bias_where((listed >> (frame ^ other)) & 1 == 1) for other in range(frames)],
        )

    by_tiles(one, plan.heads_in_group(0, table_ref, frame), frames)
    copy_pieces([(result_ref.at[step], out) for step, out in enumerate(outs)], sems)


def spatial_kernel(plan, table_ref, order_ref, lists_ref, *rest):
    slots = plan.slots
    here, frames_kv = rest[:slots], rest[slots : slots + 3]
    outs = rest[slots + 3 : 2 * slots + 3]
    q_ref, kv_ref, result_ref, sems = rest[2 * slots + 3 :]
    copy_pieces(
        [(ref, kv_ref.at[pl.ds(i * slots, slots)]) for i, ref in enumerate(frames_kv)]
        + [(ref.at[:, 0], q_ref.at[step]) for step, ref in enumerate(here)],
        sems,
    )
    frame, slot = table_ref[plan.frame_at], table_ref[plan.slot_at]

    def one(index, step):
        head = order_ref[plan.kind_stride + index * slots + slot]
        first = (frame * slots + (slot ^ step)) * plan.entries
        listed = jnp.int32(0)
        places, biases = [], []
        for entry in range(plan.entries):
            tile = lists_ref[first + entry, head]
            place = (tile // slots - frame + 1) * slots + (lax.rem(tile, slots) ^ slot)
            places.append(place)
            biases.append(bias_where((listed >> place) & 1 == 0))
            listed |= jnp.int32(1) << place
        result_ref[step, index] = attend_tile(
            q_ref[step, index],
            [kv_ref[place, index, 0] for place in places],
            [kv_ref[place, index, 1] for place in places],
            biases,
        )

    by_tiles(one, plan.heads_in_group(1, table_ref, slot), slots)
    copy_pieces([(result_ref.at[step], out) for step, out in enumerate(outs)], sems)


def unpack_kernel(plan, kinds, table_ref, order_ref, *rest):
    pieces, out_ref, sem = list(rest[:-2]), rest[-2], rest[-1]
    for kind in kinds:
        size = plan.sizes(kind)
        for step in range(size):
            piece = pieces.pop(0)
            group = plan.group(kind, table_ref, step)

            def one(index, _, kind=kind, piece=piece, group=group, size=size):
                head = order_ref[kind * plan.kind_stride + index * size + group]
                pltpu.make_async_copy(
                    piece.at[index], out_ref.at[:, head_columns(head)], sem
                ).start()
                return 0

            lax.fori_loop(0, plan.heads_in_group(kind, table_ref, group), one, 0)
    wait_all(out_ref, sem)


SPACES = {"s": pltpu.SMEM, "v": pltpu.VMEM, "a": pl.ANY, "h": pltpu.HBM}


def call(kernel, outs, operands, places, out_place, scratch=(), flops=0):
    nbytes = sum(math.prod(o.shape) * 2 for o in outs) * 2
    return pl.pallas_call(
        kernel,
        out_shape=outs,
        in_specs=[pl.BlockSpec(memory_space=SPACES[c]) for c in places],
        out_specs=[pl.BlockSpec(memory_space=SPACES[c]) for c in out_place],
        scratch_shapes=list(scratch),
        compiler_params=pltpu.CompilerParams(vmem_limit_bytes=VMEM_LIMIT),
        cost_estimate=pl.CostEstimate(flops=flops, bytes_accessed=nbytes, transcendentals=0),
    )(*operands)


def after(arrays, others):
    if not arrays or not others:
        return arrays
    return pl.pallas_call(
        lambda *refs: None,
        out_shape=[jax.ShapeDtypeStruct(a.shape, a.dtype) for a in arrays],
        in_specs=[pl.BlockSpec(memory_space=pltpu.VMEM)] * (len(arrays) + len(others)),
        out_specs=[pl.BlockSpec(memory_space=pltpu.VMEM)] * len(arrays),
        input_output_aliases={i: i for i in range(len(arrays))},
        compiler_params=pltpu.CompilerParams(vmem_limit_bytes=VMEM_LIMIT),
    )(*arrays, *others)


def tiles_of(*lead):
    return jax.ShapeDtypeStruct((*lead, TILE, HEAD_DIM), jnp.bfloat16)


def by_kind(plan, t_count, s_count, queries, keys, values, lists, table):
    frames, slots = plan.frames, plan.slots
    pair_flops = 4 * TILE * TILE * HEAD_DIM

    def to_frame(array, step):
        pairs = [(z, z ^ step) for z in range(frames)]
        return array if step == 0 else lax.ppermute(array, "blk", pairs)

    def to_slot(array, step):
        pairs = [(s, s ^ step) for s in range(slots)]
        return array if step == 0 else lax.ppermute(array, MESH_TAIL, pairs)

    def halo(array, step):
        pairs = [(z, z + step) for z in range(frames) if 0 <= z + step < frames]
        return lax.ppermute(array, "blk", pairs)

    def pack(kind, count, order):
        size = plan.sizes(kind)
        outs, out_places = [tiles_of(count, 3)] * size, "v" * size
        if order is None:
            outs.append(jax.ShapeDtypeStruct((2 * plan.kind_stride,), jnp.int32))
            out_places += "s"
        results = call(
            functools.partial(pack_kernel, plan, kind, count, order is None),
            outs,
            (table, queries, keys, values) + (() if order is None else (order,)),
            "saaa" + ("" if order is None else "s"),
            out_places,
            [pltpu.SemaphoreType.DMA((size,))],
        )
        return (*results, order) if order is not None else results

    pieces, order = [], None
    if t_count:
        *packed, order = pack(0, t_count, order)
        arrived = [to_frame(packed[step], step) for step in reversed(range(frames))][::-1]
    if s_count:
        *packed, order = pack(1, s_count, order)
        here = [to_slot(block, step) for step, block in enumerate(packed)]
        (joined,) = call(
            functools.partial(join_kernel, plan),
            [tiles_of(slots, s_count, 2)],
            here,
            "v" * slots,
            "v",
            [pltpu.SemaphoreType.DMA((slots,))],
        )
        below, above = halo(joined, 1), halo(joined, -1)
    if t_count:
        attended = call(
            functools.partial(temporal_kernel, plan),
            [tiles_of(t_count)] * frames,
            (table, order, lists, *arrived),
            "sss" + "v" * frames,
            "v" * frames,
            [
                pltpu.VMEM((frames, t_count, 3, TILE, HEAD_DIM), jnp.bfloat16),
                pltpu.VMEM((frames, t_count, TILE, HEAD_DIM), jnp.bfloat16),
                pltpu.SemaphoreType.DMA((frames,)),
            ],
            flops=TEMPORAL_WEIGHT * t_count * frames * frames * pair_flops,
        )
        if s_count:
            attended = [attended[0], *after(attended[1:], (below, above))]
        pieces += [to_frame(block, step) for step, block in enumerate(attended)]
    if s_count:
        attended = call(
            functools.partial(spatial_kernel, plan),
            [tiles_of(s_count)] * slots,
            (table, order, lists, *here, below, joined, above),
            "sss" + "v" * (slots + 3),
            "v" * slots,
            [
                pltpu.VMEM((slots, s_count, TILE, HEAD_DIM), jnp.bfloat16),
                pltpu.VMEM((3 * slots, s_count, 2, TILE, HEAD_DIM), jnp.bfloat16),
                pltpu.VMEM((slots, s_count, TILE, HEAD_DIM), jnp.bfloat16),
                pltpu.SemaphoreType.DMA((3 + slots,)),
            ],
            flops=s_count * slots * plan.entries * pair_flops,
        )
        attended = [attended[0], *after(attended[1:2], pieces[1:]), *attended[2:]]
        pieces += [to_slot(block, step) for step, block in enumerate(attended)]
    kinds = [kind for kind, count in enumerate((t_count, s_count)) if count]
    (out,) = call(
        functools.partial(unpack_kernel, plan, kinds),
        [jax.ShapeDtypeStruct((TILE, plan.heads * HEAD_DIM), jnp.bfloat16)],
        (table, order, *pieces),
        "ss" + "v" * len(pieces),
        "h",
        [pltpu.SemaphoreType.DMA],
    )
    return out


def kind_plan(queries, keys, values, block_lists):
    heads, tiles, entries = block_lists.shape
    frames = lax.axis_size("blk")
    slots = lax.axis_size(MESH_TAIL)
    plan = Plan(heads, frames, slots, entries)
    head_ids = jnp.arange(heads, dtype=jnp.int32)
    tile_slot = jnp.arange(tiles, dtype=jnp.int32) % slots
    temporal = jnp.all(block_lists % slots == tile_slot[None, :, None], axis=(1, 2))
    before = head_ids[None, :] < head_ids[:, None]
    rank_t = jnp.sum((before & temporal[None, :]).astype(jnp.int32), axis=1)
    total_t = jnp.sum(temporal.astype(jnp.int32))
    table = jnp.concatenate(
        [
            jnp.where(temporal, rank_t, heads),
            jnp.where(temporal, heads, head_ids - rank_t),
            jnp.stack(
                [
                    total_t,
                    heads - total_t,
                    lax.axis_index("blk").astype(jnp.int32),
                    lax.axis_index(MESH_TAIL).astype(jnp.int32),
                ]
            ),
        ]
    )
    lists = jnp.transpose(block_lists, (1, 2, 0)).reshape(tiles * entries, heads)
    needed = [(-(-t // frames), -(-(heads - t) // slots)) for t in range(heads + 1)]
    pairs = sorted(set(needed), key=needed.index)
    firsts = jnp.array([needed.index(pair) for pair in pairs[1:]], jnp.int32)
    branch = jnp.sum((total_t >= firsts).astype(jnp.int32))
    branches = [functools.partial(by_kind, plan, t, s) for t, s in pairs]
    return lax.switch(branch, branches, queries, keys, values, lists, table)


def per_device(queries, keys, values, block_lists):
    slots = lax.axis_size(MESH_TAIL)
    whole_tiles = queries.shape[0] == TILE and slots == FRAME_TILES
    frames = lax.axis_size("blk")
    if whole_tiles and frames & (frames - 1) == 0 and frames * slots == block_lists.shape[1]:
        return kind_plan(queries, keys, values, block_lists)
    return gathered_plan(queries, keys, values, block_lists)


def solution(mesh):
    in_specs = (
        P(("grp", "blk", "head", "sub"), None),
        P(("grp", "blk", "head", "sub"), None),
        P(("grp", "blk", "head", "sub"), None),
        P(),
    )
    out_specs = P(("grp", "blk", "head", "sub"), None)
    return jax.shard_map(
        per_device, mesh=mesh, in_specs=in_specs, out_specs=out_specs, check_vma=False
    )
```

```python
import functools
import math

import jax
import jax.numpy as jnp
from jax import lax
from jax.experimental import pallas as pl
from jax.experimental.pallas import tpu as pltpu
from jax.sharding import PartitionSpec as P

HEADS = 32
HEAD_DIM = 128
TILE = 128
FRAME_TILES = 4


NEG_FLOOR = -1e30


def query_rows(block_lists, first_head, heads_here, query_tokens):
    tile_ids = jnp.arange(block_lists.shape[1], dtype=jnp.int32)
    lists_local = lax.dynamic_slice_in_dim(block_lists, first_head, heads_here, 0)
    tile_mask = jnp.any(lists_local[:, :, :, None] == tile_ids, axis=2).astype(jnp.bfloat16)
    query_onehot = ((query_tokens // TILE)[:, None] == tile_ids[None, :]).astype(jnp.bfloat16)
    listed = jnp.einsum("qi,hij->hqj", query_onehot, tile_mask, preferred_element_type=jnp.float32)
    return listed.astype(jnp.bfloat16)


def attend_block(state_now, key_block, value_block, allowed, query_local, score_scale):
    top_old, total_old, accum_old = state_now
    scores = (
        jnp.einsum("qhd,khd->hqk", query_local, key_block, preferred_element_type=jnp.float32)
        * score_scale
    )
    top_new = jnp.maximum(top_old, jnp.max(jnp.where(allowed, scores, NEG_FLOOR), axis=2))
    factor = jnp.exp(top_old - top_new)
    weights = jnp.where(allowed, jnp.exp(scores - top_new[:, :, None]), 0.0)
    total_new = total_old * factor + jnp.sum(weights, axis=2)
    product = jnp.einsum(
        "hqk,khd->qhd",
        weights.astype(jnp.bfloat16),
        value_block,
        preferred_element_type=jnp.float32,
    )
    accum_new = accum_old * jnp.transpose(factor)[:, :, None] + product
    return (top_new, total_new, accum_new)


def make_step(query_local, listed_rows, key_token, block_len, tile_total):
    score_scale = 1.0 / math.sqrt(HEAD_DIM)
    tile_ids = jnp.arange(tile_total, dtype=jnp.int32)

    def fold_step(state_now, piece, first_row):
        key_piece, value_piece = piece
        block_count = key_piece.shape[0] // block_len

        def one_block(block_index, state_in):
            key_block = lax.dynamic_slice_in_dim(key_piece, block_index * block_len, block_len, 0)
            value_block = lax.dynamic_slice_in_dim(
                value_piece, block_index * block_len, block_len, 0
            )
            positions = block_index * block_len + jnp.arange(block_len, dtype=jnp.int32)
            key_tiles = key_token(positions) // TILE
            key_onehot = (tile_ids[:, None] == key_tiles[None, :]).astype(jnp.bfloat16)
            allowed = (
                jnp.einsum(
                    "hqj,jk->hqk", listed_rows, key_onehot, preferred_element_type=jnp.float32
                )
                > 0.5
            )
            result = attend_block(
                state_in, key_block, value_block, allowed, query_local, score_scale
            )
            return result

        return lax.fori_loop(0, block_count, one_block, state_now)

    return fold_step


def start_state(heads_here, block_len):
    top_all = jnp.full((heads_here, block_len), NEG_FLOOR, jnp.float32)
    total_all = jnp.zeros((heads_here, block_len), jnp.float32)
    accum_all = jnp.zeros((block_len, heads_here, HEAD_DIM), jnp.float32)
    return (top_all, total_all, accum_all)


def normalize(state_end):
    top_all, total_all, accum_all = state_end
    return (accum_all / jnp.transpose(total_all)[:, :, None]).astype(jnp.bfloat16)


def gathered_plan(queries, keys, values, block_lists):
    row_count, col_count = queries.shape
    n_head = lax.axis_size("head")
    n_sub = lax.axis_size("sub")
    blk_index = lax.axis_index("blk")
    head_index = lax.axis_index("head")
    sub_index = lax.axis_index("sub")
    tile_total = block_lists.shape[1]
    heads_here = HEADS // (n_head * n_sub)
    block_len = row_count * n_head * n_sub

    def inward(tensor):
        return tensor.reshape(1, 1, row_count, n_head, n_sub, heads_here * HEAD_DIM)

    query_six, keys_six, values_six = (
        lax.all_to_all(
            lax.all_to_all(inward(queries), "head", split_axis=3, concat_axis=1, tiled=True),
            "sub",
            split_axis=4,
            concat_axis=0,
            tiled=True,
        ),
        lax.all_to_all(
            lax.all_to_all(inward(keys), "head", split_axis=3, concat_axis=1, tiled=True),
            "sub",
            split_axis=4,
            concat_axis=0,
            tiled=True,
        ),
        lax.all_to_all(
            lax.all_to_all(inward(values), "head", split_axis=3, concat_axis=1, tiled=True),
            "sub",
            split_axis=4,
            concat_axis=0,
            tiled=True,
        ),
    )
    query_local = query_six.reshape(block_len, heads_here, HEAD_DIM)
    keys_local = keys_six.reshape(block_len, heads_here, HEAD_DIM)
    values_local = values_six.reshape(block_len, heads_here, HEAD_DIM)

    def key_token(positions):
        source_dev = positions // block_len
        within = positions % block_len
        sub_source = within // (n_head * row_count)
        head_source = within // row_count % n_head
        offset = within % row_count
        return ((source_dev * n_head + head_source) * n_sub + sub_source) * row_count + offset

    query_tokens = key_token(blk_index * block_len + jnp.arange(block_len, dtype=jnp.int32))
    first_head = (head_index * n_sub + sub_index) * heads_here
    listed_rows = query_rows(block_lists, first_head, heads_here, query_tokens)
    fold_step = make_step(query_local, listed_rows, key_token, block_len, tile_total)
    state_end = fold_step(
        start_state(heads_here, block_len),
        (
            lax.all_gather(keys_local, "blk", axis=0, tiled=True),
            lax.all_gather(values_local, "blk", axis=0, tiled=True),
        ),
        jnp.int32(0),
    )
    result_rows = normalize(state_end)
    attended = result_rows.reshape(n_sub, n_head, row_count, 1, 1, heads_here * HEAD_DIM)
    returned = lax.all_to_all(
        lax.all_to_all(attended, "head", split_axis=1, concat_axis=3, tiled=True),
        "sub",
        split_axis=0,
        concat_axis=4,
        tiled=True,
    )
    return returned.reshape(row_count, col_count)


MESH_TAIL = ("head", "sub")
EXP2_SCALE = math.log2(math.e) / math.sqrt(HEAD_DIM)
TEMPORAL_WEIGHT = 100
VMEM_LIMIT = 16 * 1024 * 1024


class Plan:
    def __init__(self, heads, frames, slots, entries):
        self.heads, self.frames, self.slots, self.entries = heads, frames, slots, entries
        self.count_at = 2 * heads
        self.frame_at = 2 * heads + 2
        self.slot_at = 2 * heads + 3
        self.kind_stride = heads + 1

    def sizes(self, kind):
        return (self.frames, self.slots)[kind]

    def own(self, kind, table_ref):
        return table_ref[(self.frame_at, self.slot_at)[kind]]

    def group(self, kind, table_ref, step):
        return self.own(kind, table_ref) ^ step

    def heads_in_group(self, kind, table_ref, group):
        size = self.sizes(kind)
        return (table_ref[self.count_at + kind] - group + size - 1) // size


def head_columns(head):
    return pl.ds(pl.multiple_of(head * HEAD_DIM, HEAD_DIM), HEAD_DIM)


def fill_order(plan, table_ref, order_ref):
    def clear(p, _):
        order_ref[p] = 0
        return 0

    def place(h, _):
        order_ref[table_ref[h]] = h
        order_ref[plan.kind_stride + table_ref[plan.heads + h]] = h
        return 0

    lax.fori_loop(0, 2 * plan.kind_stride, clear, 0)
    lax.fori_loop(0, plan.heads, place, 0)


def wait_all(ref, sem):
    pltpu.make_async_copy(ref, ref, sem).wait()


def pack_kernel(plan, kind, count, first, table_ref, q_ref, k_ref, v_ref, *rest):
    size = plan.sizes(kind)
    if first:
        outs, order_ref = rest[:size], rest[size]
    else:
        order_ref, outs = rest[0], rest[1 : 1 + size]
    sems = rest[-1]
    if first:
        fill_order(plan, table_ref, order_ref)
    for step in range(size):
        out_ref = outs[step]
        group = plan.group(kind, table_ref, step)

        def one(index, _, group=group, out_ref=out_ref, step=step):
            head = order_ref[kind * plan.kind_stride + index * size + group]
            for place, ref in enumerate((q_ref, k_ref, v_ref)):
                pltpu.make_async_copy(
                    ref.at[:, head_columns(head)], out_ref.at[index, place], sems.at[step]
                ).start()
            return 0

        lax.fori_loop(0, count, one, 0)
    for step, out_ref in enumerate(outs):
        wait_all(out_ref, sems.at[step])


def turn_keys(kv_ref, place, count):
    def turn(work, _):
        step, index = work // count, lax.rem(work, count)
        kv_ref[step, index, place] = kv_ref[step, index, place].T
        return 0

    lax.fori_loop(0, kv_ref.shape[0] * count, turn, 0)


def join_kernel(plan, count, *refs):
    pieces, out_ref, sems = refs[: plan.slots], refs[-2], refs[-1]
    copy_pieces(
        [(piece.at[:, pl.ds(1, 2)], out_ref.at[step]) for step, piece in enumerate(pieces)], sems
    )
    turn_keys(out_ref, 0, count)


def attend_tile(query, keys, values, biases):
    scores = jnp.dot(query, jnp.concatenate(keys, 1), preferred_element_type=jnp.float32)
    tiles = [scores[:, b * TILE : (b + 1) * TILE] + bias for b, bias in enumerate(biases)]
    top = jnp.max(functools.reduce(jnp.maximum, tiles), axis=1, keepdims=True)
    weights = [jnp.exp2((tile - top) * EXP2_SCALE) for tile in tiles]
    total = jnp.sum(functools.reduce(jnp.add, weights), axis=1, keepdims=True)
    accum = jnp.dot(
        jnp.concatenate([w.astype(jnp.bfloat16) for w in weights], 1),
        jnp.concatenate(values, 0),
        preferred_element_type=jnp.float32,
    )
    return (accum / total).astype(jnp.bfloat16)


def bias_where(attended):
    return jnp.where(attended, jnp.float32(0), jnp.float32(NEG_FLOOR))


def copy_pieces(pieces, sems):
    copies = [pltpu.make_async_copy(a, b, sems.at[i]) for i, (a, b) in enumerate(pieces)]
    for copy in copies:
        copy.start()
    for copy in copies:
        copy.wait()


def by_tiles(one, heads_here, steps, at_once):
    bodies = steps // at_once

    def body(work, _):
        index, first = work // bodies, lax.rem(work, bodies) * at_once
        for more in range(at_once):
            one(index, first + more)
        return 0

    lax.fori_loop(0, heads_here * bodies, body, 0)


def temporal_kernel(plan, count, table_ref, order_ref, lists_ref, *rest):
    frames, slots = plan.frames, plan.slots
    tiles, outs = rest[:frames], rest[frames : 2 * frames]
    held_ref, result_ref, sems = rest[2 * frames :]
    copy_pieces([(tile, held_ref.at[step]) for step, tile in enumerate(tiles)], sems)
    frame, slot = table_ref[plan.frame_at], table_ref[plan.slot_at]
    turn_keys(held_ref, 1, count)

    def one(index, step):
        head = order_ref[index * frames + frame]
        first = ((frame ^ step) * slots + slot) * plan.entries
        listed = jnp.int32(0)
        for entry in range(plan.entries):
            listed |= jnp.int32(1) << (lists_ref[first + entry, head] // slots)
        result_ref[step, index] = attend_tile(
            held_ref[step, index, 0],
            [held_ref[other, index, 1] for other in range(frames)],
            [held_ref[other, index, 2] for other in range(frames)],
            [bias_where((listed >> (frame ^ other)) & 1 == 1) for other in range(frames)],
        )

    by_tiles(one, plan.heads_in_group(0, table_ref, frame), frames, 1)
    copy_pieces([(result_ref.at[step], out) for step, out in enumerate(outs)], sems)


def spatial_kernel(plan, table_ref, order_ref, lists_ref, *rest):
    slots = plan.slots
    here, frames_kv = rest[:slots], rest[slots : slots + 3]
    outs = rest[slots + 3 : 2 * slots + 3]
    q_ref, kv_ref, result_ref, sems = rest[2 * slots + 3 :]
    copy_pieces(
        [(ref, kv_ref.at[pl.ds(i * slots, slots)]) for i, ref in enumerate(frames_kv)]
        + [(ref.at[:, 0], q_ref.at[step]) for step, ref in enumerate(here)],
        sems,
    )
    frame, slot = table_ref[plan.frame_at], table_ref[plan.slot_at]

    def one(index, step):
        head = order_ref[plan.kind_stride + index * slots + slot]
        first = (frame * slots + (slot ^ step)) * plan.entries
        listed = jnp.int32(0)
        places, biases = [], []
        for entry in range(plan.entries):
            tile = lists_ref[first + entry, head]
            place = (tile // slots - frame + 1) * slots + (lax.rem(tile, slots) ^ slot)
            places.append(place)
            biases.append(bias_where((listed >> place) & 1 == 0))
            listed |= jnp.int32(1) << place
        result_ref[step, index] = attend_tile(
            q_ref[step, index],
            [kv_ref[place, index, 0] for place in places],
            [kv_ref[place, index, 1] for place in places],
            biases,
        )

    by_tiles(one, plan.heads_in_group(1, table_ref, slot), slots, 2)
    copy_pieces([(result_ref.at[step], out) for step, out in enumerate(outs)], sems)


def unpack_kernel(plan, kinds, table_ref, order_ref, *rest):
    pieces, out_ref, sem = list(rest[:-2]), rest[-2], rest[-1]
    for kind in kinds:
        size = plan.sizes(kind)
        for step in range(size):
            piece = pieces.pop(0)
            group = plan.group(kind, table_ref, step)

            def one(index, _, kind=kind, piece=piece, group=group, size=size):
                head = order_ref[kind * plan.kind_stride + index * size + group]
                pltpu.make_async_copy(
                    piece.at[index], out_ref.at[:, head_columns(head)], sem
                ).start()
                return 0

            lax.fori_loop(0, plan.heads_in_group(kind, table_ref, group), one, 0)
    wait_all(out_ref, sem)


SPACES = {"s": pltpu.SMEM, "v": pltpu.VMEM, "a": pl.ANY, "h": pltpu.HBM}


def call(kernel, outs, operands, places, out_place, scratch=(), flops=0):
    nbytes = sum(math.prod(o.shape) * 2 for o in outs) * 2
    return pl.pallas_call(
        kernel,
        out_shape=outs,
        in_specs=[pl.BlockSpec(memory_space=SPACES[c]) for c in places],
        out_specs=[pl.BlockSpec(memory_space=SPACES[c]) for c in out_place],
        scratch_shapes=list(scratch),
        compiler_params=pltpu.CompilerParams(vmem_limit_bytes=VMEM_LIMIT),
        cost_estimate=pl.CostEstimate(flops=flops, bytes_accessed=nbytes, transcendentals=0),
    )(*operands)


def after(arrays, others):
    if not arrays or not others:
        return arrays
    return pl.pallas_call(
        lambda *refs: None,
        out_shape=[jax.ShapeDtypeStruct(a.shape, a.dtype) for a in arrays],
        in_specs=[pl.BlockSpec(memory_space=pltpu.VMEM)] * (len(arrays) + len(others)),
        out_specs=[pl.BlockSpec(memory_space=pltpu.VMEM)] * len(arrays),
        input_output_aliases={i: i for i in range(len(arrays))},
        compiler_params=pltpu.CompilerParams(vmem_limit_bytes=VMEM_LIMIT),
    )(*arrays, *others)


def tiles_of(*lead):
    return jax.ShapeDtypeStruct((*lead, TILE, HEAD_DIM), jnp.bfloat16)


def by_kind(plan, t_count, s_count, queries, keys, values, lists, table):
    frames, slots = plan.frames, plan.slots
    pair_flops = 4 * TILE * TILE * HEAD_DIM

    def to_frame(array, step):
        pairs = [(z, z ^ step) for z in range(frames)]
        return array if step == 0 else lax.ppermute(array, "blk", pairs)

    def to_slot(array, step):
        pairs = [(s, s ^ step) for s in range(slots)]
        return array if step == 0 else lax.ppermute(array, MESH_TAIL, pairs)

    def halo(array, step):
        pairs = [(z, z + step) for z in range(frames) if 0 <= z + step < frames]
        return lax.ppermute(array, "blk", pairs)

    def pack(kind, count, order):
        size = plan.sizes(kind)
        outs, out_places = [tiles_of(count, 3)] * size, "v" * size
        if order is None:
            outs.append(jax.ShapeDtypeStruct((2 * plan.kind_stride,), jnp.int32))
            out_places += "s"
        results = call(
            functools.partial(pack_kernel, plan, kind, count, order is None),
            outs,
            (table, queries, keys, values) + (() if order is None else (order,)),
            "saaa" + ("" if order is None else "s"),
            out_places,
            [pltpu.SemaphoreType.DMA((size,))],
        )
        return (*results, order) if order is not None else results

    pieces, order = [], None
    if t_count:
        *packed, order = pack(0, t_count, order)
        arrived = [to_frame(packed[step], step) for step in reversed(range(frames))][::-1]
    if s_count:
        *packed, order = pack(1, s_count, order)
        here = [to_slot(block, step) for step, block in enumerate(packed)]
        (joined,) = call(
            functools.partial(join_kernel, plan, s_count),
            [tiles_of(slots, s_count, 2)],
            here,
            "v" * slots,
            "v",
            [pltpu.SemaphoreType.DMA((slots,))],
        )
        below, above = halo(joined, 1), halo(joined, -1)
    if t_count:
        attended = call(
            functools.partial(temporal_kernel, plan, t_count),
            [tiles_of(t_count)] * frames,
            (table, order, lists, *arrived),
            "sss" + "v" * frames,
            "v" * frames,
            [
                pltpu.VMEM((frames, t_count, 3, TILE, HEAD_DIM), jnp.bfloat16),
                pltpu.VMEM((frames, t_count, TILE, HEAD_DIM), jnp.bfloat16),
                pltpu.SemaphoreType.DMA((frames,)),
            ],
            flops=TEMPORAL_WEIGHT * t_count * frames * frames * pair_flops,
        )
        if s_count:
            attended = [attended[0], *after(attended[1:], (below, above))]
        pieces += [to_frame(block, step) for step, block in enumerate(attended)]
    if s_count:
        attended = call(
            functools.partial(spatial_kernel, plan),
            [tiles_of(s_count)] * slots,
            (table, order, lists, *here, below, joined, above),
            "sss" + "v" * (slots + 3),
            "v" * slots,
            [
                pltpu.VMEM((slots, s_count, TILE, HEAD_DIM), jnp.bfloat16),
                pltpu.VMEM((3 * slots, s_count, 2, TILE, HEAD_DIM), jnp.bfloat16),
                pltpu.VMEM((slots, s_count, TILE, HEAD_DIM), jnp.bfloat16),
                pltpu.SemaphoreType.DMA((3 + slots,)),
            ],
            flops=s_count * slots * plan.entries * pair_flops,
        )
        attended = [attended[0], *after(attended[1:2], pieces[1:]), *attended[2:]]
        pieces += [to_slot(block, step) for step, block in enumerate(attended)]
    kinds = [kind for kind, count in enumerate((t_count, s_count)) if count]
    (out,) = call(
        functools.partial(unpack_kernel, plan, kinds),
        [jax.ShapeDtypeStruct((TILE, plan.heads * HEAD_DIM), jnp.bfloat16)],
        (table, order, *pieces),
        "ss" + "v" * len(pieces),
        "h",
        [pltpu.SemaphoreType.DMA],
    )
    return out


def capacities(heads, frames, slots):
    needed = [(-(-t // frames), -(-(heads - t) // slots)) for t in range(heads + 1)]
    low, high = heads // 4 + 1, heads - heads // 4 - 1
    pairs = [(needed[low - 1][0], needed[0][1])]
    firsts = []
    for t in range(low, high + 1):
        if needed[t] != pairs[-1]:
            pairs.append(needed[t])
            firsts.append(t)
    pairs.append((needed[heads][0], needed[high + 1][1]))
    firsts.append(high + 1)
    return pairs, firsts


def kind_plan(queries, keys, values, block_lists):
    heads, tiles, entries = block_lists.shape
    frames = lax.axis_size("blk")
    slots = lax.axis_size(MESH_TAIL)
    plan = Plan(heads, frames, slots, entries)
    head_ids = jnp.arange(heads, dtype=jnp.int32)
    tile_slot = jnp.arange(tiles, dtype=jnp.int32) % slots
    temporal = jnp.all(block_lists % slots == tile_slot[None, :, None], axis=(1, 2))
    before = head_ids[None, :] < head_ids[:, None]
    rank_t = jnp.sum((before & temporal[None, :]).astype(jnp.int32), axis=1)
    total_t = jnp.sum(temporal.astype(jnp.int32))
    table = jnp.concatenate(
        [
            jnp.where(temporal, rank_t, heads),
            jnp.where(temporal, heads, head_ids - rank_t),
            jnp.stack(
                [
                    total_t,
                    heads - total_t,
                    lax.axis_index("blk").astype(jnp.int32),
                    lax.axis_index(MESH_TAIL).astype(jnp.int32),
                ]
            ),
        ]
    )
    lists = jnp.transpose(block_lists, (1, 2, 0)).reshape(tiles * entries, heads)
    pairs, firsts = capacities(heads, frames, slots)
    branch = sum((total_t >= first).astype(jnp.int32) for first in firsts)
    branches = [functools.partial(by_kind, plan, t, s) for t, s in pairs]
    return lax.switch(branch, branches, queries, keys, values, lists, table)


def per_device(queries, keys, values, block_lists):
    slots = lax.axis_size(MESH_TAIL)
    whole_tiles = queries.shape[0] == TILE and slots == FRAME_TILES
    frames = lax.axis_size("blk")
    if whole_tiles and frames & (frames - 1) == 0 and frames * slots == block_lists.shape[1]:
        return kind_plan(queries, keys, values, block_lists)
    return gathered_plan(queries, keys, values, block_lists)


def solution(mesh):
    in_specs = (
        P(("grp", "blk", "head", "sub"), None),
        P(("grp", "blk", "head", "sub"), None),
        P(("grp", "blk", "head", "sub"), None),
        P(),
    )
    out_specs = P(("grp", "blk", "head", "sub"), None)
    return jax.shard_map(
        per_device, mesh=mesh, in_specs=in_specs, out_specs=out_specs, check_vma=False
    )
```

```python
import functools
import math

import jax
import jax.numpy as jnp
from jax import lax
from jax.experimental import pallas as pl
from jax.experimental.pallas import tpu as pltpu
from jax.sharding import PartitionSpec as P

HEADS = 32
HEAD_DIM = 128
TILE = 128
FRAME_TILES = 4


NEG_FLOOR = -1e30


def query_rows(block_lists, first_head, heads_here, query_tokens):
    tile_ids = jnp.arange(block_lists.shape[1], dtype=jnp.int32)
    lists_local = lax.dynamic_slice_in_dim(block_lists, first_head, heads_here, 0)
    tile_mask = jnp.any(lists_local[:, :, :, None] == tile_ids, axis=2).astype(jnp.bfloat16)
    query_onehot = ((query_tokens // TILE)[:, None] == tile_ids[None, :]).astype(jnp.bfloat16)
    listed = jnp.einsum("qi,hij->hqj", query_onehot, tile_mask, preferred_element_type=jnp.float32)
    return listed.astype(jnp.bfloat16)


def attend_block(state_now, key_block, value_block, allowed, query_local, score_scale):
    top_old, total_old, accum_old = state_now
    scores = (
        jnp.einsum("qhd,khd->hqk", query_local, key_block, preferred_element_type=jnp.float32)
        * score_scale
    )
    top_new = jnp.maximum(top_old, jnp.max(jnp.where(allowed, scores, NEG_FLOOR), axis=2))
    factor = jnp.exp(top_old - top_new)
    weights = jnp.where(allowed, jnp.exp(scores - top_new[:, :, None]), 0.0)
    total_new = total_old * factor + jnp.sum(weights, axis=2)
    product = jnp.einsum(
        "hqk,khd->qhd",
        weights.astype(jnp.bfloat16),
        value_block,
        preferred_element_type=jnp.float32,
    )
    accum_new = accum_old * jnp.transpose(factor)[:, :, None] + product
    return (top_new, total_new, accum_new)


def make_step(query_local, listed_rows, key_token, block_len, tile_total):
    score_scale = 1.0 / math.sqrt(HEAD_DIM)
    tile_ids = jnp.arange(tile_total, dtype=jnp.int32)

    def fold_step(state_now, piece, first_row):
        key_piece, value_piece = piece
        block_count = key_piece.shape[0] // block_len

        def one_block(block_index, state_in):
            key_block = lax.dynamic_slice_in_dim(key_piece, block_index * block_len, block_len, 0)
            value_block = lax.dynamic_slice_in_dim(
                value_piece, block_index * block_len, block_len, 0
            )
            positions = block_index * block_len + jnp.arange(block_len, dtype=jnp.int32)
            key_tiles = key_token(positions) // TILE
            key_onehot = (tile_ids[:, None] == key_tiles[None, :]).astype(jnp.bfloat16)
            allowed = (
                jnp.einsum(
                    "hqj,jk->hqk", listed_rows, key_onehot, preferred_element_type=jnp.float32
                )
                > 0.5
            )
            result = attend_block(
                state_in, key_block, value_block, allowed, query_local, score_scale
            )
            return result

        return lax.fori_loop(0, block_count, one_block, state_now)

    return fold_step


def start_state(heads_here, block_len):
    top_all = jnp.full((heads_here, block_len), NEG_FLOOR, jnp.float32)
    total_all = jnp.zeros((heads_here, block_len), jnp.float32)
    accum_all = jnp.zeros((block_len, heads_here, HEAD_DIM), jnp.float32)
    return (top_all, total_all, accum_all)


def normalize(state_end):
    top_all, total_all, accum_all = state_end
    return (accum_all / jnp.transpose(total_all)[:, :, None]).astype(jnp.bfloat16)


def gathered_plan(queries, keys, values, block_lists):
    row_count, col_count = queries.shape
    n_head = lax.axis_size("head")
    n_sub = lax.axis_size("sub")
    blk_index = lax.axis_index("blk")
    head_index = lax.axis_index("head")
    sub_index = lax.axis_index("sub")
    tile_total = block_lists.shape[1]
    heads_here = HEADS // (n_head * n_sub)
    block_len = row_count * n_head * n_sub

    def inward(tensor):
        return tensor.reshape(1, 1, row_count, n_head, n_sub, heads_here * HEAD_DIM)

    query_six, keys_six, values_six = (
        lax.all_to_all(
            lax.all_to_all(inward(queries), "head", split_axis=3, concat_axis=1, tiled=True),
            "sub",
            split_axis=4,
            concat_axis=0,
            tiled=True,
        ),
        lax.all_to_all(
            lax.all_to_all(inward(keys), "head", split_axis=3, concat_axis=1, tiled=True),
            "sub",
            split_axis=4,
            concat_axis=0,
            tiled=True,
        ),
        lax.all_to_all(
            lax.all_to_all(inward(values), "head", split_axis=3, concat_axis=1, tiled=True),
            "sub",
            split_axis=4,
            concat_axis=0,
            tiled=True,
        ),
    )
    query_local = query_six.reshape(block_len, heads_here, HEAD_DIM)
    keys_local = keys_six.reshape(block_len, heads_here, HEAD_DIM)
    values_local = values_six.reshape(block_len, heads_here, HEAD_DIM)

    def key_token(positions):
        source_dev = positions // block_len
        within = positions % block_len
        sub_source = within // (n_head * row_count)
        head_source = within // row_count % n_head
        offset = within % row_count
        return ((source_dev * n_head + head_source) * n_sub + sub_source) * row_count + offset

    query_tokens = key_token(blk_index * block_len + jnp.arange(block_len, dtype=jnp.int32))
    first_head = (head_index * n_sub + sub_index) * heads_here
    listed_rows = query_rows(block_lists, first_head, heads_here, query_tokens)
    fold_step = make_step(query_local, listed_rows, key_token, block_len, tile_total)
    state_end = fold_step(
        start_state(heads_here, block_len),
        (
            lax.all_gather(keys_local, "blk", axis=0, tiled=True),
            lax.all_gather(values_local, "blk", axis=0, tiled=True),
        ),
        jnp.int32(0),
    )
    result_rows = normalize(state_end)
    attended = result_rows.reshape(n_sub, n_head, row_count, 1, 1, heads_here * HEAD_DIM)
    returned = lax.all_to_all(
        lax.all_to_all(attended, "head", split_axis=1, concat_axis=3, tiled=True),
        "sub",
        split_axis=0,
        concat_axis=4,
        tiled=True,
    )
    return returned.reshape(row_count, col_count)


MESH_TAIL = ("head", "sub")
EXP2_SCALE = math.log2(math.e) / math.sqrt(HEAD_DIM)
TEMPORAL_WEIGHT = 100
VMEM_LIMIT = 16 * 1024 * 1024


class Plan:
    def __init__(self, heads, frames, slots, entries):
        self.heads, self.frames, self.slots, self.entries = heads, frames, slots, entries
        self.kind_stride = heads
        self.count_at = 2 * heads
        self.frame_at = 2 * heads + 2
        self.slot_at = 2 * heads + 3
        self.table_size = 2 * heads + 4

    def sizes(self, kind):
        return (self.frames, self.slots)[kind]

    def own(self, kind, table_ref):
        return table_ref[(self.frame_at, self.slot_at)[kind]]

    def head_at(self, kind, table_ref, group, index):
        return table_ref[kind * self.kind_stride + index * self.sizes(kind) + group]

    def group(self, kind, table_ref, step):
        return self.own(kind, table_ref) ^ step

    def heads_in_group(self, kind, table_ref, group):
        size = self.sizes(kind)
        return (table_ref[self.count_at + kind] - group + size - 1) // size

    def steps(self, kind):
        others = range(1, self.sizes(kind))
        return [0, *others] if kind else [0, *reversed(others)]


def head_columns(head):
    return pl.ds(pl.multiple_of(head * HEAD_DIM, HEAD_DIM), HEAD_DIM)


def table_kernel(plan, firsts, lists_ref, table_ref, branch_ref, mask_ref):
    lists = lists_ref[...]
    tiles = lax.broadcasted_iota(jnp.int32, lists.shape, 0)
    other_slot = ((lists ^ tiles) & (plan.slots - 1)).astype(jnp.float32)
    spatial = jnp.sum(jnp.sum(other_slot, axis=0), axis=0, keepdims=True) > 0
    lanes = lax.broadcasted_iota(jnp.int32, spatial.shape, 1)
    for place in range(plan.heads // 16):
        bit = jnp.where(lanes // 16 == place, jnp.int32(1) << (lanes % 16), 0)
        bits = jnp.where(spatial, bit, 0).astype(jnp.float32)
        mask_ref[place] = jnp.sum(bits).astype(jnp.int32)

    def clear(p, _):
        table_ref[p] = 0
        return 0

    def place_head(h, counts):
        kind = (mask_ref[h // 16] >> (h % 16)) & 1
        t_count, s_count = counts
        table_ref[jnp.where(kind == 1, plan.kind_stride + s_count, t_count)] = h
        return t_count + 1 - kind, s_count + kind

    lax.fori_loop(0, 2 * plan.heads, clear, 0)
    counts = lax.fori_loop(0, plan.heads, place_head, (jnp.int32(0), jnp.int32(0)))
    table_ref[plan.count_at], table_ref[plan.count_at + 1] = counts
    table_ref[plan.frame_at] = lax.axis_index("blk")
    n_sub = lax.axis_size("sub")
    table_ref[plan.slot_at] = lax.axis_index("head") * n_sub + lax.axis_index("sub")
    branch_ref[0] = sum((counts[0] >= first).astype(jnp.int32) for first in firsts)


def wait_all(ref, sem):
    pltpu.make_async_copy(ref, ref, sem).wait()


def pack_kernel(plan, kind, count, table_ref, q_ref, k_ref, v_ref, *rest):
    outs, sems = rest[-1 - plan.sizes(kind) : -1], rest[-1]
    for step, out_ref, sem in zip(plan.steps(kind), outs, range(len(outs))):
        group = plan.group(kind, table_ref, step)

        def one(index, _, group=group, out_ref=out_ref, sem=sem):
            columns = head_columns(plan.head_at(kind, table_ref, group, index))
            for place, ref in enumerate((q_ref, k_ref, v_ref)):
                pltpu.make_async_copy(
                    ref.at[:, columns], out_ref.at[index, place], sems.at[sem]
                ).start()
            return 0

        lax.fori_loop(0, count, one, 0)
    for sem, out_ref in enumerate(outs):
        wait_all(out_ref, sems.at[sem])


def turn_keys(kv_ref, place, count):
    def turn(work, _):
        step, index = work // count, lax.rem(work, count)
        kv_ref[step, index, place] = kv_ref[step, index, place].T
        return 0

    lax.fori_loop(0, kv_ref.shape[0] * count, turn, 0)


def join_kernel(plan, count, *refs):
    pieces, out_ref, sems = refs[: plan.slots], refs[-2], refs[-1]
    copy_pieces(
        [(piece.at[:, pl.ds(1, 2)], out_ref.at[step]) for step, piece in enumerate(pieces)], sems
    )
    turn_keys(out_ref, 0, count)


def attend_tile(query, keys, values, biases):
    scores = jnp.dot(query, jnp.concatenate(keys, 1), preferred_element_type=jnp.float32)
    tiles = [scores[:, b * TILE : (b + 1) * TILE] + bias for b, bias in enumerate(biases)]
    top = jnp.max(functools.reduce(jnp.maximum, tiles), axis=1, keepdims=True)
    weights = [jnp.exp2((tile - top) * EXP2_SCALE) for tile in tiles]
    total = jnp.sum(functools.reduce(jnp.add, weights), axis=1, keepdims=True)
    accum = jnp.dot(
        jnp.concatenate([w.astype(jnp.bfloat16) for w in weights], 1),
        jnp.concatenate(values, 0),
        preferred_element_type=jnp.float32,
    )
    return (accum / total).astype(jnp.bfloat16)


def bias_where(attended):
    return jnp.where(attended, jnp.float32(0), jnp.float32(NEG_FLOOR))


def copy_pieces(pieces, sems):
    copies = [pltpu.make_async_copy(a, b, sems.at[i]) for i, (a, b) in enumerate(pieces)]
    for copy in copies:
        copy.start()
    for copy in copies:
        copy.wait()


def by_tiles(one, heads_here, steps, at_once):
    bodies = steps // at_once

    def body(work, _):
        index, first = work // bodies, lax.rem(work, bodies) * at_once
        for more in range(at_once):
            one(index, first + more)
        return 0

    lax.fori_loop(0, heads_here * bodies, body, 0)


def temporal_kernel(plan, count, table_ref, lists_ref, *rest):
    frames, slots = plan.frames, plan.slots
    tiles, outs = rest[:frames], rest[frames : 2 * frames]
    held_ref, result_ref, sems = rest[2 * frames :]
    copy_pieces([(tile, held_ref.at[step]) for step, tile in zip(plan.steps(0), tiles)], sems)
    frame, slot = table_ref[plan.frame_at], table_ref[plan.slot_at]
    turn_keys(held_ref, 1, count)

    def one(index, step):
        head = plan.head_at(0, table_ref, frame, index)
        first = ((frame ^ step) * slots + slot) * plan.entries
        listed = jnp.int32(0)
        for entry in range(plan.entries):
            listed |= jnp.int32(1) << (lists_ref[first + entry, head] // slots)
        result_ref[step, index] = attend_tile(
            held_ref[step, index, 0],
            [held_ref[other, index, 1] for other in range(frames)],
            [held_ref[other, index, 2] for other in range(frames)],
            [bias_where((listed >> (frame ^ other)) & 1 == 1) for other in range(frames)],
        )

    by_tiles(one, plan.heads_in_group(0, table_ref, frame), frames, 1)
    copy_pieces([(result_ref.at[step], out) for step, out in zip(plan.steps(0), outs)], sems)


def spatial_kernel(plan, table_ref, lists_ref, *rest):
    slots = plan.slots
    here, frames_kv = rest[:slots], rest[slots : slots + 3]
    outs = rest[slots + 3 : 2 * slots + 3]
    q_ref, kv_ref, result_ref, sems = rest[2 * slots + 3 :]
    copy_pieces(
        [(ref, kv_ref.at[pl.ds(i * slots, slots)]) for i, ref in enumerate(frames_kv)]
        + [(ref.at[:, 0], q_ref.at[step]) for step, ref in enumerate(here)],
        sems,
    )
    frame, slot = table_ref[plan.frame_at], table_ref[plan.slot_at]

    def one(index, step):
        head = plan.head_at(1, table_ref, slot, index)
        first = (frame * slots + (slot ^ step)) * plan.entries
        listed = jnp.int32(0)
        places, biases = [], []
        for entry in range(plan.entries):
            tile = lists_ref[first + entry, head]
            place = (tile // slots - frame + 1) * slots + (lax.rem(tile, slots) ^ slot)
            places.append(place)
            biases.append(bias_where((listed >> place) & 1 == 0))
            listed |= jnp.int32(1) << place
        result_ref[step, index] = attend_tile(
            q_ref[step, index],
            [kv_ref[place, index, 0] for place in places],
            [kv_ref[place, index, 1] for place in places],
            biases,
        )

    by_tiles(one, plan.heads_in_group(1, table_ref, slot), slots, 2)
    copy_pieces([(result_ref.at[step], out) for step, out in enumerate(outs)], sems)


def unpack_kernel(plan, kinds, table_ref, *rest):
    pieces, out_ref, sem = list(rest[:-2]), rest[-2], rest[-1]
    for kind in kinds:
        for step in plan.steps(kind):
            piece = pieces.pop(0)
            group = plan.group(kind, table_ref, step)

            def one(index, _, kind=kind, piece=piece, group=group):
                columns = head_columns(plan.head_at(kind, table_ref, group, index))
                pltpu.make_async_copy(piece.at[index], out_ref.at[:, columns], sem).start()
                return 0

            lax.fori_loop(0, plan.heads_in_group(kind, table_ref, group), one, 0)
    wait_all(out_ref, sem)


SPACES = {"s": pltpu.SMEM, "v": pltpu.VMEM, "a": pl.ANY, "h": pltpu.HBM}


def call(kernel, outs, operands, places, out_place, scratch=(), flops=0):
    nbytes = sum(math.prod(o.shape) * 2 for o in outs) * 2
    return pl.pallas_call(
        kernel,
        out_shape=outs,
        in_specs=[pl.BlockSpec(memory_space=SPACES[c]) for c in places],
        out_specs=[pl.BlockSpec(memory_space=SPACES[c]) for c in out_place],
        scratch_shapes=list(scratch),
        compiler_params=pltpu.CompilerParams(vmem_limit_bytes=VMEM_LIMIT),
        cost_estimate=pl.CostEstimate(flops=flops, bytes_accessed=nbytes, transcendentals=0),
    )(*operands)


def after(arrays, others):
    if not arrays or not others:
        return arrays
    return pl.pallas_call(
        lambda *refs: None,
        out_shape=[jax.ShapeDtypeStruct(a.shape, a.dtype) for a in arrays],
        in_specs=[pl.BlockSpec(memory_space=pltpu.VMEM)] * (len(arrays) + len(others)),
        out_specs=[pl.BlockSpec(memory_space=pltpu.VMEM)] * len(arrays),
        input_output_aliases={i: i for i in range(len(arrays))},
        compiler_params=pltpu.CompilerParams(vmem_limit_bytes=VMEM_LIMIT),
    )(*arrays, *others)


def tiles_of(*lead):
    return jax.ShapeDtypeStruct((*lead, TILE, HEAD_DIM), jnp.bfloat16)


def by_kind(plan, t_count, s_count, queries, keys, values, lists, table):
    frames, slots = plan.frames, plan.slots
    pair_flops = 4 * TILE * TILE * HEAD_DIM

    def to_frame(array, step):
        pairs = [(z, z ^ step) for z in range(frames)]
        return array if step == 0 else lax.ppermute(array, "blk", pairs)

    def to_slot(array, step):
        pairs = [(s, s ^ step) for s in range(slots)]
        return array if step == 0 else lax.ppermute(array, MESH_TAIL, pairs)

    def halo(array, step):
        pairs = [(z, z + step) for z in range(frames) if 0 <= z + step < frames]
        return lax.ppermute(array, "blk", pairs)

    def pack(kind, count, earlier=()):
        size = plan.sizes(kind)
        return call(
            functools.partial(pack_kernel, plan, kind, count),
            [tiles_of(count, 3)] * size,
            (table, queries, keys, values, *earlier),
            "saaa" + "v" * len(earlier),
            "v" * size,
            [pltpu.SemaphoreType.DMA((size,))],
        )

    pieces, packed = [], ()
    if t_count:
        packed = pack(0, t_count)
        arrived = [to_frame(block, step) for step, block in zip(plan.steps(0), packed)]
    if s_count:
        packed = pack(1, s_count, packed[:1])
        here = [to_slot(block, step) for step, block in enumerate(packed)]
        (joined,) = call(
            functools.partial(join_kernel, plan, s_count),
            [tiles_of(slots, s_count, 2)],
            here,
            "v" * slots,
            "v",
            [pltpu.SemaphoreType.DMA((slots,))],
        )
        below, above = halo(joined, 1), halo(joined, -1)
    if t_count:
        attended = call(
            functools.partial(temporal_kernel, plan, t_count),
            [tiles_of(t_count)] * frames,
            (table, lists, *arrived),
            "ss" + "v" * frames,
            "v" * frames,
            [
                pltpu.VMEM((frames, t_count, 3, TILE, HEAD_DIM), jnp.bfloat16),
                pltpu.VMEM((frames, t_count, TILE, HEAD_DIM), jnp.bfloat16),
                pltpu.SemaphoreType.DMA((frames,)),
            ],
            flops=TEMPORAL_WEIGHT * t_count * frames * frames * pair_flops,
        )
        if s_count:
            attended = [attended[0], *after(attended[1:], (below, above))]
        pieces += [to_frame(block, step) for step, block in zip(plan.steps(0), attended)]
    if s_count:
        attended = call(
            functools.partial(spatial_kernel, plan),
            [tiles_of(s_count)] * slots,
            (table, lists, *here, below, joined, above),
            "ss" + "v" * (slots + 3),
            "v" * slots,
            [
                pltpu.VMEM((slots, s_count, TILE, HEAD_DIM), jnp.bfloat16),
                pltpu.VMEM((3 * slots, s_count, 2, TILE, HEAD_DIM), jnp.bfloat16),
                pltpu.VMEM((slots, s_count, TILE, HEAD_DIM), jnp.bfloat16),
                pltpu.SemaphoreType.DMA((3 + slots,)),
            ],
            flops=s_count * slots * plan.entries * pair_flops,
        )
        attended = [attended[0], *after(attended[1:2], pieces[1:]), *attended[2:]]
        pieces += [to_slot(block, step) for step, block in enumerate(attended)]
    kinds = [kind for kind, count in enumerate((t_count, s_count)) if count]
    (out,) = call(
        functools.partial(unpack_kernel, plan, kinds),
        [jax.ShapeDtypeStruct((TILE, plan.heads * HEAD_DIM), jnp.bfloat16)],
        (table, *pieces),
        "s" + "v" * len(pieces),
        "h",
        [pltpu.SemaphoreType.DMA],
    )
    return out


def capacities(heads, frames, slots):
    needed = [(-(-t // frames), -(-(heads - t) // slots)) for t in range(heads + 1)]
    low, high = heads // 4 + 1, heads - heads // 4 - 1
    pairs = [(needed[low - 1][0], needed[0][1])]
    firsts = []
    for t in range(low, high + 1):
        if needed[t] != pairs[-1]:
            pairs.append(needed[t])
            firsts.append(t)
    pairs.append((needed[heads][0], needed[high + 1][1]))
    firsts.append(high + 1)
    return pairs, firsts


def kind_plan(queries, keys, values, block_lists):
    heads, tiles, entries = block_lists.shape
    frames = lax.axis_size("blk")
    slots = lax.axis_size(MESH_TAIL)
    plan = Plan(heads, frames, slots, entries)
    pairs, firsts = capacities(heads, frames, slots)
    by_tile = jnp.transpose(block_lists, (1, 2, 0))
    table, branch = call(
        functools.partial(table_kernel, plan, firsts),
        [jax.ShapeDtypeStruct((size,), jnp.int32) for size in (plan.table_size, 1)],
        (by_tile,),
        "v",
        "ss",
        [pltpu.SMEM((heads // 16,), jnp.int32)],
    )
    lists = by_tile.reshape(tiles * entries, heads)
    branches = [functools.partial(by_kind, plan, t, s) for t, s in pairs]
    return lax.switch(branch[0], branches, queries, keys, values, lists, table)


def per_device(queries, keys, values, block_lists):
    slots = lax.axis_size(MESH_TAIL)
    whole_tiles = queries.shape[0] == TILE and slots == FRAME_TILES
    frames = lax.axis_size("blk")
    if whole_tiles and frames & (frames - 1) == 0 and frames * slots == block_lists.shape[1]:
        return kind_plan(queries, keys, values, block_lists)
    return gathered_plan(queries, keys, values, block_lists)


def solution(mesh):
    in_specs = (
        P(("grp", "blk", "head", "sub"), None),
        P(("grp", "blk", "head", "sub"), None),
        P(("grp", "blk", "head", "sub"), None),
        P(),
    )
    out_specs = P(("grp", "blk", "head", "sub"), None)
    return jax.shard_map(
        per_device, mesh=mesh, in_specs=in_specs, out_specs=out_specs, check_vma=False
    )
```

```python
import functools
import math

import jax
import jax.numpy as jnp
from jax import lax
from jax.experimental import pallas as pl
from jax.experimental.pallas import tpu as pltpu
from jax.sharding import PartitionSpec as P

HEADS = 32
HEAD_DIM = 128
TILE = 128
FRAME_TILES = 4


NEG_FLOOR = -1e30


def query_rows(block_lists, first_head, heads_here, query_tokens):
    tile_ids = jnp.arange(block_lists.shape[1], dtype=jnp.int32)
    lists_local = lax.dynamic_slice_in_dim(block_lists, first_head, heads_here, 0)
    tile_mask = jnp.any(lists_local[:, :, :, None] == tile_ids, axis=2).astype(jnp.bfloat16)
    query_onehot = ((query_tokens // TILE)[:, None] == tile_ids[None, :]).astype(jnp.bfloat16)
    listed = jnp.einsum("qi,hij->hqj", query_onehot, tile_mask, preferred_element_type=jnp.float32)
    return listed.astype(jnp.bfloat16)


def attend_block(state_now, key_block, value_block, allowed, query_local, score_scale):
    top_old, total_old, accum_old = state_now
    scores = (
        jnp.einsum("qhd,khd->hqk", query_local, key_block, preferred_element_type=jnp.float32)
        * score_scale
    )
    top_new = jnp.maximum(top_old, jnp.max(jnp.where(allowed, scores, NEG_FLOOR), axis=2))
    factor = jnp.exp(top_old - top_new)
    weights = jnp.where(allowed, jnp.exp(scores - top_new[:, :, None]), 0.0)
    total_new = total_old * factor + jnp.sum(weights, axis=2)
    product = jnp.einsum(
        "hqk,khd->qhd",
        weights.astype(jnp.bfloat16),
        value_block,
        preferred_element_type=jnp.float32,
    )
    accum_new = accum_old * jnp.transpose(factor)[:, :, None] + product
    return (top_new, total_new, accum_new)


def make_step(query_local, listed_rows, key_token, block_len, tile_total):
    score_scale = 1.0 / math.sqrt(HEAD_DIM)
    tile_ids = jnp.arange(tile_total, dtype=jnp.int32)

    def fold_step(state_now, piece, first_row):
        key_piece, value_piece = piece
        block_count = key_piece.shape[0] // block_len

        def one_block(block_index, state_in):
            key_block = lax.dynamic_slice_in_dim(key_piece, block_index * block_len, block_len, 0)
            value_block = lax.dynamic_slice_in_dim(
                value_piece, block_index * block_len, block_len, 0
            )
            positions = block_index * block_len + jnp.arange(block_len, dtype=jnp.int32)
            key_tiles = key_token(positions) // TILE
            key_onehot = (tile_ids[:, None] == key_tiles[None, :]).astype(jnp.bfloat16)
            allowed = (
                jnp.einsum(
                    "hqj,jk->hqk", listed_rows, key_onehot, preferred_element_type=jnp.float32
                )
                > 0.5
            )
            result = attend_block(
                state_in, key_block, value_block, allowed, query_local, score_scale
            )
            return result

        return lax.fori_loop(0, block_count, one_block, state_now)

    return fold_step


def start_state(heads_here, block_len):
    top_all = jnp.full((heads_here, block_len), NEG_FLOOR, jnp.float32)
    total_all = jnp.zeros((heads_here, block_len), jnp.float32)
    accum_all = jnp.zeros((block_len, heads_here, HEAD_DIM), jnp.float32)
    return (top_all, total_all, accum_all)


def normalize(state_end):
    top_all, total_all, accum_all = state_end
    return (accum_all / jnp.transpose(total_all)[:, :, None]).astype(jnp.bfloat16)


def gathered_plan(queries, keys, values, block_lists):
    row_count, col_count = queries.shape
    n_head = lax.axis_size("head")
    n_sub = lax.axis_size("sub")
    blk_index = lax.axis_index("blk")
    head_index = lax.axis_index("head")
    sub_index = lax.axis_index("sub")
    tile_total = block_lists.shape[1]
    heads_here = HEADS // (n_head * n_sub)
    block_len = row_count * n_head * n_sub

    def inward(tensor):
        return tensor.reshape(1, 1, row_count, n_head, n_sub, heads_here * HEAD_DIM)

    query_six, keys_six, values_six = (
        lax.all_to_all(
            lax.all_to_all(inward(queries), "head", split_axis=3, concat_axis=1, tiled=True),
            "sub",
            split_axis=4,
            concat_axis=0,
            tiled=True,
        ),
        lax.all_to_all(
            lax.all_to_all(inward(keys), "head", split_axis=3, concat_axis=1, tiled=True),
            "sub",
            split_axis=4,
            concat_axis=0,
            tiled=True,
        ),
        lax.all_to_all(
            lax.all_to_all(inward(values), "head", split_axis=3, concat_axis=1, tiled=True),
            "sub",
            split_axis=4,
            concat_axis=0,
            tiled=True,
        ),
    )
    query_local = query_six.reshape(block_len, heads_here, HEAD_DIM)
    keys_local = keys_six.reshape(block_len, heads_here, HEAD_DIM)
    values_local = values_six.reshape(block_len, heads_here, HEAD_DIM)

    def key_token(positions):
        source_dev = positions // block_len
        within = positions % block_len
        sub_source = within // (n_head * row_count)
        head_source = within // row_count % n_head
        offset = within % row_count
        return ((source_dev * n_head + head_source) * n_sub + sub_source) * row_count + offset

    query_tokens = key_token(blk_index * block_len + jnp.arange(block_len, dtype=jnp.int32))
    first_head = (head_index * n_sub + sub_index) * heads_here
    listed_rows = query_rows(block_lists, first_head, heads_here, query_tokens)
    fold_step = make_step(query_local, listed_rows, key_token, block_len, tile_total)
    state_end = fold_step(
        start_state(heads_here, block_len),
        (
            lax.all_gather(keys_local, "blk", axis=0, tiled=True),
            lax.all_gather(values_local, "blk", axis=0, tiled=True),
        ),
        jnp.int32(0),
    )
    result_rows = normalize(state_end)
    attended = result_rows.reshape(n_sub, n_head, row_count, 1, 1, heads_here * HEAD_DIM)
    returned = lax.all_to_all(
        lax.all_to_all(attended, "head", split_axis=1, concat_axis=3, tiled=True),
        "sub",
        split_axis=0,
        concat_axis=4,
        tiled=True,
    )
    return returned.reshape(row_count, col_count)


MESH_TAIL = ("head", "sub")
EXP2_SCALE = math.log2(math.e) / math.sqrt(HEAD_DIM)
VMEM_LIMIT = 16 * 1024 * 1024


class Plan:
    def __init__(self, heads, frames, slots, entries):
        self.heads, self.frames, self.slots, self.entries = heads, frames, slots, entries
        self.over_slots_at = heads
        self.pure_at = 2 * heads
        self.mixed_at = 2 * heads + 1
        self.spatial_at = 2 * heads + 2
        self.frame_at = 2 * heads + 3
        self.slot_at = 2 * heads + 4
        self.table_size = 2 * heads + 5

    def sizes(self, kind):
        return (self.frames, self.slots)[kind]

    def head_at(self, kind, table_ref, group, index):
        return table_ref[(0, self.over_slots_at)[kind] + index * self.sizes(kind) + group]

    def group(self, kind, table_ref, step):
        return table_ref[(self.frame_at, self.slot_at)[kind]] ^ step

    def heads_in_group(self, kind, table_ref, group):
        size = self.sizes(kind)
        return (table_ref[(self.pure_at, self.spatial_at)[kind]] - group + size - 1) // size

    def steps(self, kind):
        others = range(1, self.sizes(kind))
        return [0, *others] if kind else [0, *reversed(others)]


def head_columns(head):
    return pl.ds(pl.multiple_of(head * HEAD_DIM, HEAD_DIM), HEAD_DIM)


def table_kernel(plan, pairs, firsts, lists_ref, table_ref, branch_ref, mask_ref):
    lists = lists_ref[...]
    tiles = lax.broadcasted_iota(jnp.int32, lists.shape, 0)
    other_slot = ((lists ^ tiles) & (plan.slots - 1)).astype(jnp.float32)
    spatial = jnp.sum(jnp.sum(other_slot, axis=0), axis=0, keepdims=True) > 0
    lanes = lax.broadcasted_iota(jnp.int32, spatial.shape, 1)
    for place in range(plan.heads // 16):
        bit = jnp.where(lanes // 16 == place, jnp.int32(1) << (lanes % 16), 0)
        bits = jnp.where(spatial, bit, 0).astype(jnp.float32)
        mask_ref[place] = jnp.sum(bits).astype(jnp.int32)
    spatial_total = jnp.sum(spatial.astype(jnp.float32)).astype(jnp.int32)
    temporal_total = plan.heads - spatial_total
    branch = sum((temporal_total >= first).astype(jnp.int32) for first in firsts)
    chunks = pairs[0][0] + sum(
        (temporal_total >= first).astype(jnp.int32) * (pairs[i + 1][0] - pairs[i][0])
        for i, first in enumerate(firsts)
    )
    mixed = (chunks - 1) * plan.frames
    shared = lax.max(temporal_total, mixed)
    room = chunks * plan.frames - shared

    def clear(p, _):
        table_ref[p] = 0
        return 0

    def place_head(h, counts):
        kind = (mask_ref[h // 16] >> (h % 16)) & 1
        t_rank, s_rank = counts
        s_place = jnp.where(s_rank < room, shared + s_rank, plan.over_slots_at + s_rank - room)
        table_ref[jnp.where(kind == 1, s_place, t_rank)] = h
        return t_rank + 1 - kind, s_rank + kind

    lax.fori_loop(0, 2 * plan.heads, clear, 0)
    lax.fori_loop(0, plan.heads, place_head, (jnp.int32(0), jnp.int32(0)))
    table_ref[plan.pure_at] = lax.min(temporal_total, mixed)
    table_ref[plan.mixed_at] = shared + lax.min(spatial_total, room)
    table_ref[plan.spatial_at] = lax.max(spatial_total - room, 0)
    table_ref[plan.frame_at] = lax.axis_index("blk")
    n_sub = lax.axis_size("sub")
    table_ref[plan.slot_at] = lax.axis_index("head") * n_sub + lax.axis_index("sub")
    branch_ref[0] = branch


def wait_all(ref, sem):
    pltpu.make_async_copy(ref, ref, sem).wait()


def pack_kernel(plan, kind, count, table_ref, q_ref, k_ref, v_ref, *rest):
    outs, sems = rest[-1 - plan.sizes(kind) : -1], rest[-1]
    for step, out_ref, sem in zip(plan.steps(kind), outs, range(len(outs))):
        group = plan.group(kind, table_ref, step)

        def one(index, _, group=group, out_ref=out_ref, sem=sem):
            columns = head_columns(plan.head_at(kind, table_ref, group, index))
            for place, ref in enumerate((q_ref, k_ref, v_ref)):
                pltpu.make_async_copy(
                    ref.at[:, columns], out_ref.at[index, place], sems.at[sem]
                ).start()
            return 0

        lax.fori_loop(0, count, one, 0)
    for sem, out_ref in enumerate(outs):
        wait_all(out_ref, sems.at[sem])


def turn_keys(kv_ref, place, count):
    def turn(work, _):
        step, index = work // count, lax.rem(work, count)
        kv_ref[step, index, place] = kv_ref[step, index, place].T
        return 0

    lax.fori_loop(0, kv_ref.shape[0] * count, turn, 0)


def join_kernel(plan, count, *refs):
    pieces, out_ref, sems = refs[: plan.slots], refs[-2], refs[-1]
    copy_pieces(
        [(piece.at[:, pl.ds(1, 2)], out_ref.at[step]) for step, piece in enumerate(pieces)], sems
    )
    turn_keys(out_ref, 0, count)


def join_mixed_kernel(plan, count, *refs):
    pieces, out_ref, sems = refs[: plan.frames], refs[-2], refs[-1]
    copy_pieces(
        [
            (piece.at[count - 1, pl.ds(1, 2)], out_ref.at[step, 0])
            for step, piece in zip(plan.steps(0), pieces)
        ],
        sems,
    )
    turn_keys(out_ref, 0, 1)


def attend_tiles(queries, keys, values, biases):
    scores = jnp.dot(
        jnp.concatenate(queries, 0), jnp.concatenate(keys, 1), preferred_element_type=jnp.float32
    )
    rows, totals = [], []
    for a, bias in enumerate(biases):
        tiles = [
            scores[a * TILE : (a + 1) * TILE, b * TILE : (b + 1) * TILE] + bias[b]
            for b in range(len(keys))
        ]
        top = jnp.max(functools.reduce(jnp.maximum, tiles), axis=1, keepdims=True)
        weights = [jnp.exp2((tile - top) * EXP2_SCALE) for tile in tiles]
        totals.append(jnp.sum(functools.reduce(jnp.add, weights), axis=1, keepdims=True))
        rows.append(jnp.concatenate([w.astype(jnp.bfloat16) for w in weights], 1))
    accum = jnp.dot(
        jnp.concatenate(rows, 0), jnp.concatenate(values, 0), preferred_element_type=jnp.float32
    )
    return [
        (accum[a * TILE : (a + 1) * TILE] / total).astype(jnp.bfloat16)
        for a, total in enumerate(totals)
    ]


def bias_where(attended):
    return jnp.where(attended, jnp.float32(0), jnp.float32(NEG_FLOOR))


def copy_pieces(pieces, sems):
    copies = [pltpu.make_async_copy(a, b, sems.at[i]) for i, (a, b) in enumerate(pieces)]
    for copy in copies:
        copy.start()
    for copy in copies:
        copy.wait()


def listed_places(plan, lists_ref, head, query_tile, place_of):
    first = query_tile * plan.entries
    listed = jnp.int32(0)
    places, biases = [], []
    for entry in range(plan.entries):
        place = place_of(lists_ref[first + entry, head])
        places.append(place)
        biases.append(bias_where((listed >> place) & 1 == 0))
        listed |= jnp.int32(1) << place
    return places, biases


def temporal_kernel(plan, count, table_ref, lists_ref, *rest):
    frames, slots = plan.frames, plan.slots
    tiles, gathered = rest[:frames], rest[frames : frames + slots]
    outs = rest[frames + slots : 2 * frames + slots]
    held_ref, mixed_ref, result_ref, sems = rest[2 * frames + slots :]
    copy_pieces(
        [(tile, held_ref.at[step]) for step, tile in zip(plan.steps(0), tiles)]
        + [(block, mixed_ref.at[step]) for step, block in enumerate(gathered)],
        sems,
    )
    frame, slot = table_ref[plan.frame_at], table_ref[plan.slot_at]
    turn_keys(held_ref, 1, count)

    def one_head(index, _):
        head = plan.head_at(0, table_ref, frame, index)
        biases = []
        for step in range(frames):
            first = ((frame ^ step) * slots + slot) * plan.entries
            listed = jnp.int32(0)
            for entry in range(plan.entries):
                listed |= jnp.int32(1) << (lists_ref[first + entry, head] // slots)
            biases.append(
                [bias_where((listed >> (frame ^ other)) & 1 == 1) for other in range(frames)]
            )
        results = attend_tiles(
            *([held_ref[step, index, i] for step in range(frames)] for i in range(3)), biases
        )
        for step, result in enumerate(results):
            result_ref[step, index] = result
        return 0

    lax.fori_loop(0, plan.heads_in_group(0, table_ref, frame), one_head, 0)

    def one_mixed(step, _):
        places, biases = listed_places(
            plan,
            lists_ref,
            plan.head_at(0, table_ref, frame, count - 1),
            (frame ^ step) * slots + slot,
            lambda tile: (lax.rem(tile, slots) ^ slot) * frames + (tile // slots ^ frame),
        )
        (result_ref[step, count - 1],) = attend_tiles(
            [held_ref[step, count - 1, 0]],
            [mixed_ref[place // frames, lax.rem(place, frames), 0, 0] for place in places],
            [mixed_ref[place // frames, lax.rem(place, frames), 0, 1] for place in places],
            [biases],
        )
        return 0

    lax.fori_loop(0, frames, one_mixed, 0)
    copy_pieces([(result_ref.at[step], out) for step, out in zip(plan.steps(0), outs)], sems)


def spatial_kernel(plan, table_ref, lists_ref, *rest):
    slots = plan.slots
    here, frames_kv = rest[:slots], rest[slots : slots + 3]
    outs = rest[slots + 3 : 2 * slots + 3]
    kv_ref, sems = rest[2 * slots + 3 :]
    copy_pieces(
        [(ref, kv_ref.at[pl.ds(i * slots, slots)]) for i, ref in enumerate(frames_kv)], sems
    )
    frame, slot = table_ref[plan.frame_at], table_ref[plan.slot_at]

    def one_head(index, _):
        head = plan.head_at(1, table_ref, slot, index)
        for step in range(slots):
            places, biases = listed_places(
                plan,
                lists_ref,
                head,
                frame * slots + (slot ^ step),
                lambda tile: (tile // slots - frame + 1) * slots + (lax.rem(tile, slots) ^ slot),
            )
            (outs[step][index],) = attend_tiles(
                [here[step][index, 0]],
                [kv_ref[place, index, 0] for place in places],
                [kv_ref[place, index, 1] for place in places],
                [biases],
            )
        return 0

    lax.fori_loop(0, plan.heads_in_group(1, table_ref, slot), one_head, 0)


def unpack_kernel(plan, counts, table_ref, *rest):
    pieces, out_ref, sem = list(rest[:-2]), rest[-2], rest[-1]
    for kind, count in enumerate(counts):
        for step in plan.steps(kind):
            piece = pieces.pop(0)
            group = plan.group(kind, table_ref, step)

            def one(index, _, kind=kind, piece=piece, group=group):
                columns = head_columns(plan.head_at(kind, table_ref, group, index))
                pltpu.make_async_copy(piece.at[index], out_ref.at[:, columns], sem).start()
                return 0

            lax.fori_loop(0, plan.heads_in_group(kind, table_ref, group), one, 0)
            if kind == 0:
                filled = (count - 1) * plan.frames + group < table_ref[plan.mixed_at]
                lax.fori_loop(count - 1, count - 1 + filled.astype(jnp.int32), one, 0)
    wait_all(out_ref, sem)


SPACES = {"s": pltpu.SMEM, "v": pltpu.VMEM, "a": pl.ANY, "h": pltpu.HBM}


def call(kernel, outs, operands, places, out_place, scratch=(), flops=0):
    nbytes = sum(math.prod(o.shape) * 2 for o in outs) * 2
    return pl.pallas_call(
        kernel,
        out_shape=outs,
        in_specs=[pl.BlockSpec(memory_space=SPACES[c]) for c in places],
        out_specs=[pl.BlockSpec(memory_space=SPACES[c]) for c in out_place],
        scratch_shapes=list(scratch),
        compiler_params=pltpu.CompilerParams(vmem_limit_bytes=VMEM_LIMIT),
        cost_estimate=pl.CostEstimate(flops=flops, bytes_accessed=nbytes, transcendentals=0),
    )(*operands)


def after(arrays, others):
    if not arrays or not others:
        return arrays
    return pl.pallas_call(
        lambda *refs: None,
        out_shape=[jax.ShapeDtypeStruct(a.shape, a.dtype) for a in arrays],
        in_specs=[pl.BlockSpec(memory_space=pltpu.VMEM)] * (len(arrays) + len(others)),
        out_specs=[pl.BlockSpec(memory_space=pltpu.VMEM)] * len(arrays),
        input_output_aliases={i: i for i in range(len(arrays))},
        compiler_params=pltpu.CompilerParams(vmem_limit_bytes=VMEM_LIMIT),
    )(*arrays, *others)


def tiles_of(*lead):
    return jax.ShapeDtypeStruct((*lead, TILE, HEAD_DIM), jnp.bfloat16)


def by_kind(plan, t_count, s_count, queries, keys, values, lists, table):
    frames, slots = plan.frames, plan.slots
    pair_flops = 4 * TILE * TILE * HEAD_DIM

    def to_frame(array, step):
        pairs = [(z, z ^ step) for z in range(frames)]
        return array if step == 0 else lax.ppermute(array, "blk", pairs)

    def to_slot(array, step):
        pairs = [(s, s ^ step) for s in range(slots)]
        return array if step == 0 else lax.ppermute(array, MESH_TAIL, pairs)

    def halo(array, step):
        pairs = [(z, z + step) for z in range(frames) if 0 <= z + step < frames]
        return lax.ppermute(array, "blk", pairs)

    def pack(kind, count, earlier=()):
        size = plan.sizes(kind)
        return call(
            functools.partial(pack_kernel, plan, kind, count),
            [tiles_of(count, 3)] * size,
            (table, queries, keys, values, *earlier),
            "saaa" + "v" * len(earlier),
            "v" * size,
            [pltpu.SemaphoreType.DMA((size,))],
        )

    packed = pack(0, t_count)
    arrived = [to_frame(block, step) for step, block in zip(plan.steps(0), packed)]
    packed = pack(1, s_count, packed[:1])
    here = [to_slot(block, step) for step, block in enumerate(packed)]
    (joined,) = call(
        functools.partial(join_kernel, plan, s_count),
        [tiles_of(slots, s_count, 2)],
        here,
        "v" * slots,
        "v",
        [pltpu.SemaphoreType.DMA((slots,))],
    )
    below, above = halo(joined, 1), halo(joined, -1)
    (mixed,) = call(
        functools.partial(join_mixed_kernel, plan, t_count),
        [tiles_of(frames, 1, 2)],
        (*arrived, joined),
        "v" * (frames + 1),
        "v",
        [pltpu.SemaphoreType.DMA((frames,))],
    )
    gathered = [to_slot(mixed, step) for step in range(slots)]
    tiles_ahead = 2 * slots * s_count - 2 * frames - 3 * t_count // 2
    flops_ahead = max(tiles_ahead, 1) * 42 * pair_flops
    attended = call(
        functools.partial(temporal_kernel, plan, t_count),
        [tiles_of(t_count)] * frames,
        (table, lists, *arrived, *gathered),
        "ss" + "v" * (frames + slots),
        "v" * frames,
        [
            pltpu.VMEM((frames, t_count, 3, TILE, HEAD_DIM), jnp.bfloat16),
            pltpu.VMEM((slots, frames, 1, 2, TILE, HEAD_DIM), jnp.bfloat16),
            pltpu.VMEM((frames, t_count, TILE, HEAD_DIM), jnp.bfloat16),
            pltpu.SemaphoreType.DMA((frames + slots,)),
        ],
        flops=flops_ahead,
    )
    attended = [attended[0], *after(attended[1:], (below, above))]
    pieces = [to_frame(block, step) for step, block in zip(plan.steps(0), attended)]
    attended = call(
        functools.partial(spatial_kernel, plan),
        [tiles_of(s_count)] * slots,
        (table, lists, *here, below, joined, above),
        "ss" + "v" * (slots + 3),
        "v" * slots,
        [
            pltpu.VMEM((3 * slots, s_count, 2, TILE, HEAD_DIM), jnp.bfloat16),
            pltpu.SemaphoreType.DMA((3,)),
        ],
        flops=s_count * slots * plan.entries * pair_flops,
    )
    attended = [attended[0], *after(attended[1:2], pieces[1:]), *attended[2:]]
    pieces += [to_slot(block, step) for step, block in enumerate(attended)]
    (out,) = call(
        functools.partial(unpack_kernel, plan, (t_count, s_count)),
        [jax.ShapeDtypeStruct((TILE, plan.heads * HEAD_DIM), jnp.bfloat16)],
        (table, *pieces),
        "s" + "v" * len(pieces),
        "h",
        [pltpu.SemaphoreType.DMA],
    )
    return out


def capacities(heads, frames, slots):
    low, high = heads // 4, heads - heads // 4

    def chunks_for(fewest, most):
        over_frames = max(-(-most // frames), 1)
        shared = max(fewest, (over_frames - 1) * frames)
        left = heads - fewest - (over_frames * frames - shared)
        return over_frames, max(-(-left // slots), 1)

    pairs, firsts = [chunks_for(0, low)], []
    for t in range(low + 1, high + 1):
        if t % frames == 1 or t == low + 1:
            pairs.append(chunks_for(t, min(-(-t // frames) * frames, high)))
            firsts.append(t)
    return pairs + [chunks_for(high + 1, heads)], firsts + [high + 1]


def kind_plan(queries, keys, values, block_lists):
    heads, tiles, entries = block_lists.shape
    frames = lax.axis_size("blk")
    slots = lax.axis_size(MESH_TAIL)
    plan = Plan(heads, frames, slots, entries)
    pairs, firsts = capacities(heads, frames, slots)
    by_tile = jnp.transpose(block_lists, (1, 2, 0))
    table, branch = call(
        functools.partial(table_kernel, plan, pairs, firsts),
        [jax.ShapeDtypeStruct((size,), jnp.int32) for size in (plan.table_size, 1)],
        (by_tile,),
        "v",
        "ss",
        [pltpu.SMEM((heads // 16,), jnp.int32)],
    )
    lists = by_tile.reshape(tiles * entries, heads)
    branches = [functools.partial(by_kind, plan, t, s) for t, s in pairs]
    return lax.switch(branch[0], branches, queries, keys, values, lists, table)


def per_device(queries, keys, values, block_lists):
    slots = lax.axis_size(MESH_TAIL)
    whole_tiles = queries.shape[0] == TILE and slots == FRAME_TILES
    frames = lax.axis_size("blk")
    if whole_tiles and frames & (frames - 1) == 0 and frames * slots == block_lists.shape[1]:
        return kind_plan(queries, keys, values, block_lists)
    return gathered_plan(queries, keys, values, block_lists)


def solution(mesh):
    in_specs = (
        P(("grp", "blk", "head", "sub"), None),
        P(("grp", "blk", "head", "sub"), None),
        P(("grp", "blk", "head", "sub"), None),
        P(),
    )
    out_specs = P(("grp", "blk", "head", "sub"), None)
    return jax.shard_map(
        per_device, mesh=mesh, in_specs=in_specs, out_specs=out_specs, check_vma=False
    )
```

```python
import functools
import math

import jax
import jax.numpy as jnp
from jax import lax
from jax.experimental import pallas as pl
from jax.experimental.pallas import tpu as pltpu
from jax.sharding import PartitionSpec as P

HEADS = 32
HEAD_DIM = 128
TILE = 128
FRAME_TILES = 4


NEG_FLOOR = -1e30


def query_rows(block_lists, first_head, heads_here, query_tokens):
    tile_ids = jnp.arange(block_lists.shape[1], dtype=jnp.int32)
    lists_local = lax.dynamic_slice_in_dim(block_lists, first_head, heads_here, 0)
    tile_mask = jnp.any(lists_local[:, :, :, None] == tile_ids, axis=2).astype(jnp.bfloat16)
    query_onehot = ((query_tokens // TILE)[:, None] == tile_ids[None, :]).astype(jnp.bfloat16)
    listed = jnp.einsum("qi,hij->hqj", query_onehot, tile_mask, preferred_element_type=jnp.float32)
    return listed.astype(jnp.bfloat16)


def attend_block(state_now, key_block, value_block, allowed, query_local, score_scale):
    top_old, total_old, accum_old = state_now
    scores = (
        jnp.einsum("qhd,khd->hqk", query_local, key_block, preferred_element_type=jnp.float32)
        * score_scale
    )
    top_new = jnp.maximum(top_old, jnp.max(jnp.where(allowed, scores, NEG_FLOOR), axis=2))
    factor = jnp.exp(top_old - top_new)
    weights = jnp.where(allowed, jnp.exp(scores - top_new[:, :, None]), 0.0)
    total_new = total_old * factor + jnp.sum(weights, axis=2)
    product = jnp.einsum(
        "hqk,khd->qhd",
        weights.astype(jnp.bfloat16),
        value_block,
        preferred_element_type=jnp.float32,
    )
    accum_new = accum_old * jnp.transpose(factor)[:, :, None] + product
    return (top_new, total_new, accum_new)


def make_step(query_local, listed_rows, key_token, block_len, tile_total):
    score_scale = 1.0 / math.sqrt(HEAD_DIM)
    tile_ids = jnp.arange(tile_total, dtype=jnp.int32)

    def fold_step(state_now, piece, first_row):
        key_piece, value_piece = piece
        block_count = key_piece.shape[0] // block_len

        def one_block(block_index, state_in):
            key_block = lax.dynamic_slice_in_dim(key_piece, block_index * block_len, block_len, 0)
            value_block = lax.dynamic_slice_in_dim(
                value_piece, block_index * block_len, block_len, 0
            )
            positions = block_index * block_len + jnp.arange(block_len, dtype=jnp.int32)
            key_tiles = key_token(positions) // TILE
            key_onehot = (tile_ids[:, None] == key_tiles[None, :]).astype(jnp.bfloat16)
            allowed = (
                jnp.einsum(
                    "hqj,jk->hqk", listed_rows, key_onehot, preferred_element_type=jnp.float32
                )
                > 0.5
            )
            result = attend_block(
                state_in, key_block, value_block, allowed, query_local, score_scale
            )
            return result

        return lax.fori_loop(0, block_count, one_block, state_now)

    return fold_step


def start_state(heads_here, block_len):
    top_all = jnp.full((heads_here, block_len), NEG_FLOOR, jnp.float32)
    total_all = jnp.zeros((heads_here, block_len), jnp.float32)
    accum_all = jnp.zeros((block_len, heads_here, HEAD_DIM), jnp.float32)
    return (top_all, total_all, accum_all)


def normalize(state_end):
    top_all, total_all, accum_all = state_end
    return (accum_all / jnp.transpose(total_all)[:, :, None]).astype(jnp.bfloat16)


def gathered_plan(queries, keys, values, block_lists):
    row_count, col_count = queries.shape
    n_head = lax.axis_size("head")
    n_sub = lax.axis_size("sub")
    blk_index = lax.axis_index("blk")
    head_index = lax.axis_index("head")
    sub_index = lax.axis_index("sub")
    tile_total = block_lists.shape[1]
    heads_here = HEADS // (n_head * n_sub)
    block_len = row_count * n_head * n_sub

    def inward(tensor):
        return tensor.reshape(1, 1, row_count, n_head, n_sub, heads_here * HEAD_DIM)

    query_six, keys_six, values_six = (
        lax.all_to_all(
            lax.all_to_all(inward(queries), "head", split_axis=3, concat_axis=1, tiled=True),
            "sub",
            split_axis=4,
            concat_axis=0,
            tiled=True,
        ),
        lax.all_to_all(
            lax.all_to_all(inward(keys), "head", split_axis=3, concat_axis=1, tiled=True),
            "sub",
            split_axis=4,
            concat_axis=0,
            tiled=True,
        ),
        lax.all_to_all(
            lax.all_to_all(inward(values), "head", split_axis=3, concat_axis=1, tiled=True),
            "sub",
            split_axis=4,
            concat_axis=0,
            tiled=True,
        ),
    )
    query_local = query_six.reshape(block_len, heads_here, HEAD_DIM)
    keys_local = keys_six.reshape(block_len, heads_here, HEAD_DIM)
    values_local = values_six.reshape(block_len, heads_here, HEAD_DIM)

    def key_token(positions):
        source_dev = positions // block_len
        within = positions % block_len
        sub_source = within // (n_head * row_count)
        head_source = within // row_count % n_head
        offset = within % row_count
        return ((source_dev * n_head + head_source) * n_sub + sub_source) * row_count + offset

    query_tokens = key_token(blk_index * block_len + jnp.arange(block_len, dtype=jnp.int32))
    first_head = (head_index * n_sub + sub_index) * heads_here
    listed_rows = query_rows(block_lists, first_head, heads_here, query_tokens)
    fold_step = make_step(query_local, listed_rows, key_token, block_len, tile_total)
    state_end = fold_step(
        start_state(heads_here, block_len),
        (
            lax.all_gather(keys_local, "blk", axis=0, tiled=True),
            lax.all_gather(values_local, "blk", axis=0, tiled=True),
        ),
        jnp.int32(0),
    )
    result_rows = normalize(state_end)
    attended = result_rows.reshape(n_sub, n_head, row_count, 1, 1, heads_here * HEAD_DIM)
    returned = lax.all_to_all(
        lax.all_to_all(attended, "head", split_axis=1, concat_axis=3, tiled=True),
        "sub",
        split_axis=0,
        concat_axis=4,
        tiled=True,
    )
    return returned.reshape(row_count, col_count)


MESH_TAIL = ("head", "sub")
EXP2_SCALE = math.log2(math.e) / math.sqrt(HEAD_DIM)
VMEM_LIMIT = 16 * 1024 * 1024


class Plan:
    def __init__(self, heads, frames, slots, entries):
        self.heads, self.frames, self.slots, self.entries = heads, frames, slots, entries
        self.over_slots_at = heads
        self.pure_at = 2 * heads
        self.mixed_at = 2 * heads + 1
        self.spatial_at = 2 * heads + 2
        self.frame_at = 2 * heads + 3
        self.slot_at = 2 * heads + 4
        self.table_size = 2 * heads + 5

    def sizes(self, kind):
        return (self.frames, self.slots)[kind]

    def head_at(self, kind, table_ref, group, index):
        return table_ref[(0, self.over_slots_at)[kind] + index * self.sizes(kind) + group]

    def group(self, kind, table_ref, step):
        return table_ref[(self.frame_at, self.slot_at)[kind]] ^ step

    def heads_in_group(self, kind, table_ref, group):
        size = self.sizes(kind)
        return (table_ref[(self.pure_at, self.spatial_at)[kind]] - group + size - 1) // size

    def steps(self, kind):
        others = range(1, self.sizes(kind))
        return [0, *others] if kind else [0, *reversed(others)]


def head_columns(head):
    return pl.ds(pl.multiple_of(head * HEAD_DIM, HEAD_DIM), HEAD_DIM)


def table_kernel(plan, pairs, firsts, lists_ref, table_ref, branch_ref, mask_ref):
    lists = lists_ref[...]
    tiles = lax.broadcasted_iota(jnp.int32, lists.shape, 0)
    other_slot = ((lists ^ tiles) & (plan.slots - 1)).astype(jnp.float32)
    spatial = jnp.sum(jnp.sum(other_slot, axis=0), axis=0, keepdims=True) > 0
    lanes = lax.broadcasted_iota(jnp.int32, spatial.shape, 1)
    for place in range(plan.heads // 16):
        bit = jnp.where(lanes // 16 == place, jnp.int32(1) << (lanes % 16), 0)
        bits = jnp.where(spatial, bit, 0).astype(jnp.float32)
        mask_ref[place] = jnp.sum(bits).astype(jnp.int32)
    spatial_total = jnp.sum(spatial.astype(jnp.float32)).astype(jnp.int32)
    temporal_total = plan.heads - spatial_total
    branch = sum((temporal_total >= first).astype(jnp.int32) for first in firsts)
    chunks = pairs[0][0] + sum(
        (temporal_total >= first).astype(jnp.int32) * (pairs[i + 1][0] - pairs[i][0])
        for i, first in enumerate(firsts)
    )
    mixed = (chunks - 1) * plan.frames
    shared = lax.max(temporal_total, mixed)
    room = chunks * plan.frames - shared

    def clear(p, _):
        table_ref[p] = 0
        return 0

    def place_head(h, counts):
        kind = (mask_ref[h // 16] >> (h % 16)) & 1
        t_rank, s_rank = counts
        s_place = jnp.where(s_rank < room, shared + s_rank, plan.over_slots_at + s_rank - room)
        table_ref[jnp.where(kind == 1, s_place, t_rank)] = h
        return t_rank + 1 - kind, s_rank + kind

    lax.fori_loop(0, 2 * plan.heads, clear, 0)
    lax.fori_loop(0, plan.heads, place_head, (jnp.int32(0), jnp.int32(0)))
    table_ref[plan.pure_at] = lax.min(temporal_total, mixed)
    table_ref[plan.mixed_at] = shared + lax.min(spatial_total, room)
    table_ref[plan.spatial_at] = lax.max(spatial_total - room, 0)
    table_ref[plan.frame_at] = lax.axis_index("blk")
    n_sub = lax.axis_size("sub")
    table_ref[plan.slot_at] = lax.axis_index("head") * n_sub + lax.axis_index("sub")
    branch_ref[0] = branch


def wait_all(ref, sem):
    pltpu.make_async_copy(ref, ref, sem).wait()


def pack_kernel(plan, kind, count, table_ref, q_ref, k_ref, v_ref, *rest):
    outs, sems = rest[-1 - plan.sizes(kind) : -1], rest[-1]
    for step, out_ref, sem in zip(plan.steps(kind), outs, range(len(outs))):
        group = plan.group(kind, table_ref, step)

        def one(index, _, group=group, out_ref=out_ref, sem=sem):
            columns = head_columns(plan.head_at(kind, table_ref, group, index))
            for place, ref in enumerate((q_ref, k_ref, v_ref)):
                pltpu.make_async_copy(
                    ref.at[:, columns], out_ref.at[index, place], sems.at[sem]
                ).start()
            return 0

        lax.fori_loop(0, count, one, 0)
    for sem, out_ref in enumerate(outs):
        wait_all(out_ref, sems.at[sem])


def turn_keys(kv_ref, place, count):
    def turn(work, _):
        step, index = work // count, lax.rem(work, count)
        kv_ref[step, index, place] = kv_ref[step, index, place].T
        return 0

    lax.fori_loop(0, kv_ref.shape[0] * count, turn, 0)


def join_kernel(plan, count, *refs):
    pieces, out_ref, sems = refs[: plan.slots], refs[-2], refs[-1]
    copy_pieces(
        [(piece.at[:, pl.ds(1, 2)], out_ref.at[step]) for step, piece in enumerate(pieces)], sems
    )
    turn_keys(out_ref, 0, count)


def join_mixed_kernel(plan, count, *refs):
    pieces, out_ref, sems = refs[: plan.frames], refs[-2], refs[-1]
    copy_pieces(
        [
            (piece.at[count - 1, pl.ds(1, 2)], out_ref.at[step, 0])
            for step, piece in zip(plan.steps(0), pieces)
        ],
        sems,
    )
    turn_keys(out_ref, 0, 1)


def attend_tiles(queries, keys, values, biases):
    scores = jnp.dot(
        jnp.concatenate(queries, 0), jnp.concatenate(keys, 1), preferred_element_type=jnp.float32
    )
    rows, totals = [], []
    for a, bias in enumerate(biases):
        tiles = [
            scores[a * TILE : (a + 1) * TILE, b * TILE : (b + 1) * TILE] + bias[b]
            for b in range(len(keys))
        ]
        top = jnp.max(functools.reduce(jnp.maximum, tiles), axis=1, keepdims=True)
        weights = [jnp.exp2((tile - top) * EXP2_SCALE) for tile in tiles]
        totals.append(jnp.sum(functools.reduce(jnp.add, weights), axis=1, keepdims=True))
        rows.append(jnp.concatenate([w.astype(jnp.bfloat16) for w in weights], 1))
    accum = jnp.dot(
        jnp.concatenate(rows, 0), jnp.concatenate(values, 0), preferred_element_type=jnp.float32
    )
    return [
        (accum[a * TILE : (a + 1) * TILE] / total).astype(jnp.bfloat16)
        for a, total in enumerate(totals)
    ]


def bias_where(attended):
    return jnp.where(attended, jnp.float32(0), jnp.float32(NEG_FLOOR))


def copy_pieces(pieces, sems):
    copies = [pltpu.make_async_copy(a, b, sems.at[i]) for i, (a, b) in enumerate(pieces)]
    for copy in copies:
        copy.start()
    for copy in copies:
        copy.wait()


def listed_places(plan, lists_ref, head, query_tile, place_of):
    first = query_tile * plan.entries
    listed = jnp.int32(0)
    places, biases = [], []
    for entry in range(plan.entries):
        place = place_of(lists_ref[first + entry, head])
        places.append(place)
        biases.append(bias_where((listed >> place) & 1 == 0))
        listed |= jnp.int32(1) << place
    return places, biases


def temporal_kernel(plan, count, table_ref, lists_ref, *rest):
    frames, slots = plan.frames, plan.slots
    tiles, outs = rest[:frames], rest[frames : 2 * frames]
    held_ref, result_ref, sems = rest[2 * frames :]
    copy_pieces([(tile, held_ref.at[step]) for step, tile in zip(plan.steps(0), tiles)], sems)
    frame, slot = table_ref[plan.frame_at], table_ref[plan.slot_at]
    turn_keys(held_ref, 1, count)

    def one_head(index, _):
        head = plan.head_at(0, table_ref, frame, index)
        biases = []
        for step in range(frames):
            first = ((frame ^ step) * slots + slot) * plan.entries
            listed = jnp.int32(0)
            for entry in range(plan.entries):
                listed |= jnp.int32(1) << (lists_ref[first + entry, head] // slots)
            biases.append(
                [bias_where((listed >> (frame ^ other)) & 1 == 1) for other in range(frames)]
            )
        results = attend_tiles(
            *([held_ref[step, index, i] for step in range(frames)] for i in range(3)), biases
        )
        for step, result in enumerate(results):
            result_ref[step, index] = result
        return 0

    lax.fori_loop(0, plan.heads_in_group(0, table_ref, frame), one_head, 0)
    copy_pieces([(result_ref.at[step], out) for step, out in zip(plan.steps(0), outs)], sems)


def mixed_kernel(plan, count, table_ref, lists_ref, *rest):
    frames, slots = plan.frames, plan.slots
    tiles, gathered = rest[:frames], rest[frames : frames + slots]
    outs = rest[2 * frames + slots : 3 * frames + slots]
    q_ref, kv_ref, result_ref, sems = rest[3 * frames + slots :]
    copy_pieces(
        [(tile.at[count - 1, 0], q_ref.at[step]) for step, tile in zip(plan.steps(0), tiles)]
        + [
            (block, kv_ref.at[pl.ds(step * frames, frames)])
            for step, block in enumerate(gathered)
        ],
        sems,
    )
    frame, slot = table_ref[plan.frame_at], table_ref[plan.slot_at]
    head = plan.head_at(0, table_ref, frame, count - 1)

    def one_tile(step, _):
        places, biases = listed_places(
            plan,
            lists_ref,
            head,
            (frame ^ step) * slots + slot,
            lambda tile: (lax.rem(tile, slots) ^ slot) * frames + (tile // slots ^ frame),
        )
        (result_ref[step],) = attend_tiles(
            [q_ref[step]],
            [kv_ref[place, 0, 0] for place in places],
            [kv_ref[place, 0, 1] for place in places],
            [biases],
        )
        return 0

    lax.fori_loop(0, frames, one_tile, 0)
    copy_pieces(
        [(result_ref.at[step], out.at[count - 1]) for step, out in zip(plan.steps(0), outs)], sems
    )


def spatial_kernel(plan, steps, table_ref, lists_ref, *rest):
    slots, ways = plan.slots, len(steps)
    queries, frames_kv = rest[:ways], rest[ways : ways + 3]
    outs = rest[-2 - ways : -2]
    kv_ref, sems = rest[-2:]
    copy_pieces(
        [(ref, kv_ref.at[pl.ds(i * slots, slots)]) for i, ref in enumerate(frames_kv)], sems
    )
    frame, slot = table_ref[plan.frame_at], table_ref[plan.slot_at]

    def one_head(index, _):
        head = plan.head_at(1, table_ref, slot, index)
        for step, query_ref, out_ref in zip(steps, queries, outs):
            places, biases = listed_places(
                plan,
                lists_ref,
                head,
                frame * slots + (slot ^ step),
                lambda tile: (tile // slots - frame + 1) * slots + (lax.rem(tile, slots) ^ slot),
            )
            (out_ref[index],) = attend_tiles(
                [query_ref[index, 0]],
                [kv_ref[place, index, 0] for place in places],
                [kv_ref[place, index, 1] for place in places],
                [biases],
            )
        return 0

    lax.fori_loop(0, plan.heads_in_group(1, table_ref, slot), one_head, 0)


def unpack_kernel(plan, counts, table_ref, *rest):
    pieces, out_ref, sem = list(rest[:-2]), rest[-2], rest[-1]
    for kind, count in enumerate(counts):
        for step in plan.steps(kind):
            piece = pieces.pop(0)
            group = plan.group(kind, table_ref, step)

            def one(index, _, kind=kind, piece=piece, group=group):
                columns = head_columns(plan.head_at(kind, table_ref, group, index))
                pltpu.make_async_copy(piece.at[index], out_ref.at[:, columns], sem).start()
                return 0

            lax.fori_loop(0, plan.heads_in_group(kind, table_ref, group), one, 0)
            if kind == 0:
                filled = (count - 1) * plan.frames + group < table_ref[plan.mixed_at]
                lax.fori_loop(count - 1, count - 1 + filled.astype(jnp.int32), one, 0)
    wait_all(out_ref, sem)


SPACES = {"s": pltpu.SMEM, "v": pltpu.VMEM, "a": pl.ANY}


def call(kernel, outs, operands, places, out_place, scratch=(), flops=0, in_place=None):
    nbytes = sum(math.prod(o.shape) * 2 for o in outs) * 2
    return pl.pallas_call(
        kernel,
        out_shape=outs,
        in_specs=[pl.BlockSpec(memory_space=SPACES[c]) for c in places],
        out_specs=[pl.BlockSpec(memory_space=SPACES[c]) for c in out_place],
        scratch_shapes=list(scratch),
        input_output_aliases=in_place or {},
        compiler_params=pltpu.CompilerParams(vmem_limit_bytes=VMEM_LIMIT),
        cost_estimate=pl.CostEstimate(flops=flops, bytes_accessed=nbytes, transcendentals=0),
    )(*operands)


def after(arrays, others):
    if not arrays or not others:
        return arrays
    return pl.pallas_call(
        lambda *refs: None,
        out_shape=[jax.ShapeDtypeStruct(a.shape, a.dtype) for a in arrays],
        in_specs=[pl.BlockSpec(memory_space=pltpu.VMEM)] * (len(arrays) + len(others)),
        out_specs=[pl.BlockSpec(memory_space=pltpu.VMEM)] * len(arrays),
        input_output_aliases={i: i for i in range(len(arrays))},
        compiler_params=pltpu.CompilerParams(vmem_limit_bytes=VMEM_LIMIT),
    )(*arrays, *others)


def tiles_of(*lead):
    return jax.ShapeDtypeStruct((*lead, TILE, HEAD_DIM), jnp.bfloat16)


def by_kind(plan, t_count, s_count, queries, keys, values, lists, table):
    frames, slots = plan.frames, plan.slots
    pair_flops = 4 * TILE * TILE * HEAD_DIM

    def to_frame(array, step):
        pairs = [(z, z ^ step) for z in range(frames)]
        return array if step == 0 else lax.ppermute(array, "blk", pairs)

    def to_slot(array, step):
        pairs = [(s, s ^ step) for s in range(slots)]
        return array if step == 0 else lax.ppermute(array, MESH_TAIL, pairs)

    def halo(array, step):
        pairs = [(z, z + step) for z in range(frames) if 0 <= z + step < frames]
        return lax.ppermute(array, "blk", pairs)

    def pack(kind, count, earlier=()):
        size = plan.sizes(kind)
        return call(
            functools.partial(pack_kernel, plan, kind, count),
            [tiles_of(count, 3)] * size,
            (table, queries, keys, values, *earlier),
            "saaa" + "v" * len(earlier),
            "v" * size,
            [pltpu.SemaphoreType.DMA((size,))],
        )

    packed = pack(0, t_count)
    arrived = [to_frame(block, step) for step, block in zip(plan.steps(0), packed)]
    packed = pack(1, s_count, packed[:1])
    here = [to_slot(block, step) for step, block in enumerate(packed)]
    (joined,) = call(
        functools.partial(join_kernel, plan, s_count),
        [tiles_of(slots, s_count, 2)],
        here,
        "v" * slots,
        "v",
        [pltpu.SemaphoreType.DMA((slots,))],
    )
    below, above = halo(joined, 1), halo(joined, -1)
    (mixed,) = call(
        functools.partial(join_mixed_kernel, plan, t_count),
        [tiles_of(frames, 1, 2)],
        (*arrived, joined),
        "v" * (frames + 1),
        "v",
        [pltpu.SemaphoreType.DMA((frames,))],
    )
    gathered = [to_slot(mixed, step) for step in range(slots)]
    tiles_ahead = 2 * slots * s_count - 2 * frames - 3 * t_count // 2
    flops_ahead = max(tiles_ahead, 1) * 42 * pair_flops
    attended = call(
        functools.partial(temporal_kernel, plan, t_count),
        [tiles_of(t_count)] * frames,
        (table, lists, *arrived),
        "ss" + "v" * frames,
        "v" * frames,
        [
            pltpu.VMEM((frames, t_count, 3, TILE, HEAD_DIM), jnp.bfloat16),
            pltpu.VMEM((frames, t_count, TILE, HEAD_DIM), jnp.bfloat16),
            pltpu.SemaphoreType.DMA((frames,)),
        ],
        flops=t_count * frames * frames * pair_flops,
    )
    attended = call(
        functools.partial(mixed_kernel, plan, t_count),
        [tiles_of(t_count)] * frames,
        (table, lists, *arrived, *gathered, *attended),
        "ss" + "v" * (2 * frames + slots),
        "v" * frames,
        [
            pltpu.VMEM((frames, TILE, HEAD_DIM), jnp.bfloat16),
            pltpu.VMEM((slots * frames, 1, 2, TILE, HEAD_DIM), jnp.bfloat16),
            pltpu.VMEM((frames, TILE, HEAD_DIM), jnp.bfloat16),
            pltpu.SemaphoreType.DMA((frames + slots,)),
        ],
        flops=flops_ahead,
        in_place={2 + frames + slots + i: i for i in range(frames)},
    )
    attended = [attended[0], *after(attended[1:], (below, above))]
    pieces = [to_frame(block, step) for step, block in zip(plan.steps(0), attended)]

    def attend_slots(steps, *earlier):
        return call(
            functools.partial(spatial_kernel, plan, steps),
            [tiles_of(s_count)] * len(steps),
            (table, lists, *(here[step] for step in steps), below, joined, above, *earlier),
            "ss" + "v" * (len(steps) + 3 + len(earlier)),
            "v" * len(steps),
            [
                pltpu.VMEM((3 * slots, s_count, 2, TILE, HEAD_DIM), jnp.bfloat16),
                pltpu.SemaphoreType.DMA((3,)),
            ],
            flops=s_count * len(steps) * plan.entries * pair_flops,
        )

    half = slots // 2
    away = attend_slots(range(half, slots))
    near = attend_slots(range(half), away[0])
    attended = [near[0], *after(near[1:], pieces[1:]), *away]
    pieces += [to_slot(block, step) for step, block in enumerate(attended)]
    (out,) = call(
        functools.partial(unpack_kernel, plan, (t_count, s_count)),
        [jax.ShapeDtypeStruct((TILE, plan.heads * HEAD_DIM), jnp.bfloat16)],
        (table, *pieces),
        "s" + "v" * len(pieces),
        "v",
        [pltpu.SemaphoreType.DMA],
    )
    return out


def capacities(heads, frames, slots):
    low, high = heads // 4, heads - heads // 4

    def chunks_for(fewest, most):
        over_frames = max(-(-most // frames), 1)
        shared = max(fewest, (over_frames - 1) * frames)
        left = heads - fewest - (over_frames * frames - shared)
        return over_frames, max(-(-left // slots), 1)

    pairs, firsts = [chunks_for(0, low)], []
    for t in range(low + 1, high + 1):
        if t % frames == 1 or t == low + 1:
            pairs.append(chunks_for(t, min(-(-t // frames) * frames, high)))
            firsts.append(t)
    return pairs + [chunks_for(high + 1, heads)], firsts + [high + 1]


def kind_plan(queries, keys, values, block_lists):
    heads, tiles, entries = block_lists.shape
    frames = lax.axis_size("blk")
    slots = lax.axis_size(MESH_TAIL)
    plan = Plan(heads, frames, slots, entries)
    pairs, firsts = capacities(heads, frames, slots)
    by_tile = jnp.transpose(block_lists, (1, 2, 0))
    table, branch = call(
        functools.partial(table_kernel, plan, pairs, firsts),
        [jax.ShapeDtypeStruct((size,), jnp.int32) for size in (plan.table_size, 1)],
        (by_tile,),
        "v",
        "ss",
        [pltpu.SMEM((heads // 16,), jnp.int32)],
    )
    lists = by_tile.reshape(tiles * entries, heads)
    branches = [functools.partial(by_kind, plan, t, s) for t, s in pairs]
    return lax.switch(branch[0], branches, queries, keys, values, lists, table)


def per_device(queries, keys, values, block_lists):
    slots = lax.axis_size(MESH_TAIL)
    whole_tiles = queries.shape[0] == TILE and slots == FRAME_TILES
    frames = lax.axis_size("blk")
    if whole_tiles and frames & (frames - 1) == 0 and frames * slots == block_lists.shape[1]:
        return kind_plan(queries, keys, values, block_lists)
    return gathered_plan(queries, keys, values, block_lists)


def solution(mesh):
    in_specs = (
        P(("grp", "blk", "head", "sub"), None),
        P(("grp", "blk", "head", "sub"), None),
        P(("grp", "blk", "head", "sub"), None),
        P(),
    )
    out_specs = P(("grp", "blk", "head", "sub"), None)
    return jax.shard_map(
        per_device, mesh=mesh, in_specs=in_specs, out_specs=out_specs, check_vma=False
    )
```

```python
import functools
import math

import jax
import jax.numpy as jnp
from jax import lax
from jax.experimental import pallas as pl
from jax.experimental.pallas import tpu as pltpu
from jax.sharding import PartitionSpec as P

HEADS = 32
HEAD_DIM = 128
TILE = 128
FRAME_TILES = 4


NEG_FLOOR = -1e30


def query_rows(block_lists, first_head, heads_here, query_tokens):
    tile_ids = jnp.arange(block_lists.shape[1], dtype=jnp.int32)
    lists_local = lax.dynamic_slice_in_dim(block_lists, first_head, heads_here, 0)
    tile_mask = jnp.any(lists_local[:, :, :, None] == tile_ids, axis=2).astype(jnp.bfloat16)
    query_onehot = ((query_tokens // TILE)[:, None] == tile_ids[None, :]).astype(jnp.bfloat16)
    listed = jnp.einsum("qi,hij->hqj", query_onehot, tile_mask, preferred_element_type=jnp.float32)
    return listed.astype(jnp.bfloat16)


def attend_block(state_now, key_block, value_block, allowed, query_local, score_scale):
    top_old, total_old, accum_old = state_now
    scores = (
        jnp.einsum("qhd,khd->hqk", query_local, key_block, preferred_element_type=jnp.float32)
        * score_scale
    )
    top_new = jnp.maximum(top_old, jnp.max(jnp.where(allowed, scores, NEG_FLOOR), axis=2))
    factor = jnp.exp(top_old - top_new)
    weights = jnp.where(allowed, jnp.exp(scores - top_new[:, :, None]), 0.0)
    total_new = total_old * factor + jnp.sum(weights, axis=2)
    product = jnp.einsum(
        "hqk,khd->qhd",
        weights.astype(jnp.bfloat16),
        value_block,
        preferred_element_type=jnp.float32,
    )
    accum_new = accum_old * jnp.transpose(factor)[:, :, None] + product
    return (top_new, total_new, accum_new)


def make_step(query_local, listed_rows, key_token, block_len, tile_total):
    score_scale = 1.0 / math.sqrt(HEAD_DIM)
    tile_ids = jnp.arange(tile_total, dtype=jnp.int32)

    def fold_step(state_now, piece, first_row):
        key_piece, value_piece = piece
        block_count = key_piece.shape[0] // block_len

        def one_block(block_index, state_in):
            key_block = lax.dynamic_slice_in_dim(key_piece, block_index * block_len, block_len, 0)
            value_block = lax.dynamic_slice_in_dim(
                value_piece, block_index * block_len, block_len, 0
            )
            positions = block_index * block_len + jnp.arange(block_len, dtype=jnp.int32)
            key_tiles = key_token(positions) // TILE
            key_onehot = (tile_ids[:, None] == key_tiles[None, :]).astype(jnp.bfloat16)
            allowed = (
                jnp.einsum(
                    "hqj,jk->hqk", listed_rows, key_onehot, preferred_element_type=jnp.float32
                )
                > 0.5
            )
            result = attend_block(
                state_in, key_block, value_block, allowed, query_local, score_scale
            )
            return result

        return lax.fori_loop(0, block_count, one_block, state_now)

    return fold_step


def start_state(heads_here, block_len):
    top_all = jnp.full((heads_here, block_len), NEG_FLOOR, jnp.float32)
    total_all = jnp.zeros((heads_here, block_len), jnp.float32)
    accum_all = jnp.zeros((block_len, heads_here, HEAD_DIM), jnp.float32)
    return (top_all, total_all, accum_all)


def normalize(state_end):
    top_all, total_all, accum_all = state_end
    return (accum_all / jnp.transpose(total_all)[:, :, None]).astype(jnp.bfloat16)


def gathered_plan(queries, keys, values, block_lists):
    row_count, col_count = queries.shape
    n_head = lax.axis_size("head")
    n_sub = lax.axis_size("sub")
    blk_index = lax.axis_index("blk")
    head_index = lax.axis_index("head")
    sub_index = lax.axis_index("sub")
    tile_total = block_lists.shape[1]
    heads_here = HEADS // (n_head * n_sub)
    block_len = row_count * n_head * n_sub

    def inward(tensor):
        return tensor.reshape(1, 1, row_count, n_head, n_sub, heads_here * HEAD_DIM)

    query_six, keys_six, values_six = (
        lax.all_to_all(
            lax.all_to_all(inward(queries), "head", split_axis=3, concat_axis=1, tiled=True),
            "sub",
            split_axis=4,
            concat_axis=0,
            tiled=True,
        ),
        lax.all_to_all(
            lax.all_to_all(inward(keys), "head", split_axis=3, concat_axis=1, tiled=True),
            "sub",
            split_axis=4,
            concat_axis=0,
            tiled=True,
        ),
        lax.all_to_all(
            lax.all_to_all(inward(values), "head", split_axis=3, concat_axis=1, tiled=True),
            "sub",
            split_axis=4,
            concat_axis=0,
            tiled=True,
        ),
    )
    query_local = query_six.reshape(block_len, heads_here, HEAD_DIM)
    keys_local = keys_six.reshape(block_len, heads_here, HEAD_DIM)
    values_local = values_six.reshape(block_len, heads_here, HEAD_DIM)

    def key_token(positions):
        source_dev = positions // block_len
        within = positions % block_len
        sub_source = within // (n_head * row_count)
        head_source = within // row_count % n_head
        offset = within % row_count
        return ((source_dev * n_head + head_source) * n_sub + sub_source) * row_count + offset

    query_tokens = key_token(blk_index * block_len + jnp.arange(block_len, dtype=jnp.int32))
    first_head = (head_index * n_sub + sub_index) * heads_here
    listed_rows = query_rows(block_lists, first_head, heads_here, query_tokens)
    fold_step = make_step(query_local, listed_rows, key_token, block_len, tile_total)
    state_end = fold_step(
        start_state(heads_here, block_len),
        (
            lax.all_gather(keys_local, "blk", axis=0, tiled=True),
            lax.all_gather(values_local, "blk", axis=0, tiled=True),
        ),
        jnp.int32(0),
    )
    result_rows = normalize(state_end)
    attended = result_rows.reshape(n_sub, n_head, row_count, 1, 1, heads_here * HEAD_DIM)
    returned = lax.all_to_all(
        lax.all_to_all(attended, "head", split_axis=1, concat_axis=3, tiled=True),
        "sub",
        split_axis=0,
        concat_axis=4,
        tiled=True,
    )
    return returned.reshape(row_count, col_count)


MESH_TAIL = ("head", "sub")
EXP2_SCALE = math.log2(math.e) / math.sqrt(HEAD_DIM)
VMEM_LIMIT = 16 * 1024 * 1024


class Plan:
    def __init__(self, heads, frames, slots, entries):
        self.heads, self.frames, self.slots, self.entries = heads, frames, slots, entries
        self.over_slots_at = heads
        self.pure_at = 2 * heads
        self.mixed_at = 2 * heads + 1
        self.spatial_at = 2 * heads + 2
        self.frame_at = 2 * heads + 3
        self.slot_at = 2 * heads + 4
        self.table_size = 2 * heads + 5

    def sizes(self, kind):
        return (self.frames, self.slots)[kind]

    def head_at(self, kind, table_ref, group, index):
        return table_ref[(0, self.over_slots_at)[kind] + index * self.sizes(kind) + group]

    def group(self, kind, table_ref, step):
        return table_ref[(self.frame_at, self.slot_at)[kind]] ^ step

    def heads_in_group(self, kind, table_ref, group):
        size = self.sizes(kind)
        return (table_ref[(self.pure_at, self.spatial_at)[kind]] - group + size - 1) // size

    def steps(self, kind):
        others = range(1, self.sizes(kind))
        return [0, *others] if kind else [0, *reversed(others)]


def head_columns(head):
    return pl.ds(pl.multiple_of(head * HEAD_DIM, HEAD_DIM), HEAD_DIM)


def table_kernel(plan, pairs, begins, lists_ref, table_ref, branch_ref, mask_ref):
    lists = lists_ref[...]
    tiles = lax.broadcasted_iota(jnp.int32, lists.shape, 0)
    other_slot = ((lists ^ tiles) & (plan.slots - 1)).astype(jnp.float32)
    spatial = jnp.sum(jnp.sum(other_slot, axis=0), axis=0, keepdims=True) > 0
    lanes = lax.broadcasted_iota(jnp.int32, spatial.shape, 1)
    for place in range(plan.heads // 16):
        bit = jnp.where(lanes // 16 == place, jnp.int32(1) << (lanes % 16), 0)
        bits = jnp.where(spatial, bit, 0).astype(jnp.float32)
        mask_ref[place] = jnp.sum(bits).astype(jnp.int32)
    spatial_total = jnp.sum(spatial.astype(jnp.float32)).astype(jnp.int32)
    temporal_total = plan.heads - spatial_total
    branch, chunks, last = 0, pairs[0][0], 0
    for first, place in begins:
        reached = (temporal_total >= first).astype(jnp.int32)
        branch += reached * (place - last)
        chunks += reached * (pairs[place][0] - pairs[last][0])
        last = place
    mixed = (chunks - 1) * plan.frames
    shared = lax.max(temporal_total, mixed)
    room = chunks * plan.frames - shared

    def clear(p, _):
        table_ref[p] = 0
        return 0

    def place_head(h, counts):
        kind = (mask_ref[h // 16] >> (h % 16)) & 1
        t_rank, s_rank = counts
        s_place = jnp.where(s_rank < room, shared + s_rank, plan.over_slots_at + s_rank - room)
        table_ref[jnp.where(kind == 1, s_place, t_rank)] = h
        return t_rank + 1 - kind, s_rank + kind

    lax.fori_loop(0, 2 * plan.heads, clear, 0)
    lax.fori_loop(0, plan.heads, place_head, (jnp.int32(0), jnp.int32(0)))
    table_ref[plan.pure_at] = lax.min(temporal_total, mixed)
    table_ref[plan.mixed_at] = shared + lax.min(spatial_total, room)
    table_ref[plan.spatial_at] = lax.max(spatial_total - room, 0)
    table_ref[plan.frame_at] = lax.axis_index("blk")
    n_sub = lax.axis_size("sub")
    table_ref[plan.slot_at] = lax.axis_index("head") * n_sub + lax.axis_index("sub")
    branch_ref[0] = branch


def wait_all(ref, sem):
    pltpu.make_async_copy(ref, ref, sem).wait()


def pack_kernel(plan, counts, table_ref, q_ref, k_ref, v_ref, *rest):
    outs, sems = rest[:-1], rest[-1]
    steps = [(kind, step) for kind in range(2) for step in plan.steps(kind)]
    for sem, (kind, step) in enumerate(steps):
        group = plan.group(kind, table_ref, step)

        def one(index, _, kind=kind, group=group, sem=sem):
            columns = head_columns(plan.head_at(kind, table_ref, group, index))
            for place, ref in enumerate((q_ref, k_ref, v_ref)):
                pltpu.make_async_copy(
                    ref.at[:, columns], outs[sem].at[index, place], sems.at[sem]
                ).start()
            return 0

        lax.fori_loop(0, counts[kind], one, 0)
    for sem, out_ref in enumerate(outs):
        wait_all(out_ref, sems.at[sem])


def turn_keys(kv_ref, place, count):
    def turn(work, _):
        step, index = work // count, lax.rem(work, count)
        kv_ref[step, index, place] = kv_ref[step, index, place].T
        return 0

    lax.fori_loop(0, kv_ref.shape[0] * count, turn, 0)


def join_kernel(plan, count, *refs):
    pieces, out_ref, sems = refs[: plan.slots], refs[-2], refs[-1]
    copy_pieces(
        [(piece.at[:, pl.ds(1, 2)], out_ref.at[step]) for step, piece in enumerate(pieces)], sems
    )
    turn_keys(out_ref, 0, count)


def join_mixed_kernel(plan, count, *refs):
    pieces, out_ref, sems = refs[: plan.frames], refs[-2], refs[-1]
    copy_pieces(
        [
            (piece.at[count - 1, pl.ds(1, 2)], out_ref.at[step, 0])
            for step, piece in zip(plan.steps(0), pieces)
        ],
        sems,
    )
    turn_keys(out_ref, 0, 1)


def attend_tiles(queries, keys, values, biases, before=None):
    scores = jnp.dot(
        jnp.concatenate(queries, 0), jnp.concatenate(keys, 1), preferred_element_type=jnp.float32
    )
    rows, tops, totals = [], [], []
    for a, bias in enumerate(biases):
        tiles = [
            scores[a * TILE : (a + 1) * TILE, b * TILE : (b + 1) * TILE] + bias[b]
            for b in range(len(keys))
        ]
        top = jnp.max(functools.reduce(jnp.maximum, tiles), axis=1, keepdims=True)
        if before is not None:
            top = jnp.maximum(top, before[a][0])
        weights = [jnp.exp2((tile - top) * EXP2_SCALE) for tile in tiles]
        tops.append(top)
        totals.append(jnp.sum(functools.reduce(jnp.add, weights), axis=1, keepdims=True))
        rows.append(jnp.concatenate([w.astype(jnp.bfloat16) for w in weights], 1))
    accum = jnp.dot(
        jnp.concatenate(rows, 0), jnp.concatenate(values, 0), preferred_element_type=jnp.float32
    )
    states = []
    for a, (top, total) in enumerate(zip(tops, totals)):
        part = accum[a * TILE : (a + 1) * TILE]
        if before is not None:
            factor = jnp.exp2((before[a][0] - top) * EXP2_SCALE)
            total, part = total + before[a][1] * factor, part + before[a][2] * factor
        states.append((top, total, part))
    return states


def normalized(state):
    return (state[2] / state[1]).astype(jnp.bfloat16)


def bias_where(attended):
    return jnp.where(attended, jnp.float32(0), jnp.float32(NEG_FLOOR))


def copy_pieces(pieces, sems):
    copies = [pltpu.make_async_copy(a, b, sems.at[i]) for i, (a, b) in enumerate(pieces)]
    for copy in copies:
        copy.start()
    for copy in copies:
        copy.wait()


def listed_places(plan, lists_ref, head, query_tile, place_of):
    first = query_tile * plan.entries
    listed = jnp.int32(0)
    places, biases = [], []
    for entry in range(plan.entries):
        place = place_of(lists_ref[first + entry, head])
        places.append(place)
        biases.append(bias_where((listed >> place) & 1 == 0))
        listed |= jnp.int32(1) << place
    return places, biases


def temporal_kernel(plan, count, table_ref, lists_ref, *rest):
    frames, slots = plan.frames, plan.slots
    tiles, outs = rest[:frames], rest[frames : 2 * frames]
    held_ref, result_ref, sems = rest[2 * frames :]
    copy_pieces([(tile, held_ref.at[step]) for step, tile in zip(plan.steps(0), tiles)], sems)
    frame, slot = table_ref[plan.frame_at], table_ref[plan.slot_at]
    turn_keys(held_ref, 1, count)

    def one_head(index, _):
        head = plan.head_at(0, table_ref, frame, index)
        biases = []
        for step in range(frames):
            first = ((frame ^ step) * slots + slot) * plan.entries
            listed = jnp.int32(0)
            for entry in range(plan.entries):
                listed |= jnp.int32(1) << (lists_ref[first + entry, head] // slots)
            biases.append(
                [bias_where((listed >> (frame ^ other)) & 1 == 1) for other in range(frames)]
            )
        states = attend_tiles(
            *([held_ref[step, index, i] for step in range(frames)] for i in range(3)), biases
        )
        for step, state in enumerate(states):
            result_ref[step, index] = normalized(state)
        return 0

    lax.fori_loop(0, plan.heads_in_group(0, table_ref, frame), one_head, 0)
    copy_pieces([(result_ref.at[step], out) for step, out in zip(plan.steps(0), outs)], sems)


def mixed_kernel(plan, count, table_ref, lists_ref, *rest):
    frames, slots = plan.frames, plan.slots
    tiles, gathered = rest[:frames], rest[frames : frames + slots]
    outs = rest[-4 - frames : -4]
    q_ref, kv_ref, result_ref, sems = rest[-4:]
    copy_pieces(
        [(tile.at[count - 1, 0], q_ref.at[step]) for step, tile in zip(plan.steps(0), tiles)]
        + [
            (block, kv_ref.at[pl.ds(step * frames, frames)])
            for step, block in enumerate(gathered)
        ],
        sems,
    )
    frame, slot = table_ref[plan.frame_at], table_ref[plan.slot_at]
    head = plan.head_at(0, table_ref, frame, count - 1)

    def one_tile(step, _):
        places, biases = listed_places(
            plan,
            lists_ref,
            head,
            (frame ^ step) * slots + slot,
            lambda tile: (lax.rem(tile, slots) ^ slot) * frames + (tile // slots ^ frame),
        )
        (state,) = attend_tiles(
            [q_ref[step]],
            [kv_ref[place, 0, 0] for place in places],
            [kv_ref[place, 0, 1] for place in places],
            [biases],
        )
        result_ref[step] = normalized(state)
        return 0

    lax.fori_loop(0, frames, one_tile, 0)
    copy_pieces(
        [(result_ref.at[step], out.at[count - 1]) for step, out in zip(plan.steps(0), outs)], sems
    )


def spatial_biases(plan, table_ref, lists_ref, head, step, places):
    slots = plan.slots
    frame, slot = table_ref[plan.frame_at], table_ref[plan.slot_at]
    first = (frame * slots + (slot ^ step)) * plan.entries
    listed = jnp.int32(0)
    for entry in range(plan.entries):
        tile = lists_ref[first + entry, head]
        place = (tile // slots - frame + 1) * slots + (lax.rem(tile, slots) ^ slot)
        listed |= jnp.int32(1) << place
    return [bias_where((listed >> place) & 1 == 1) for place in places]


def own_frame_kernel(plan, table_ref, lists_ref, *rest):
    slots = plan.slots
    here, joined, outs = rest[:slots], rest[slots], rest[slots + 1 :]
    slot = table_ref[plan.slot_at]

    def one_head(index, _):
        head = plan.head_at(1, table_ref, slot, index)
        states = attend_tiles(
            [tile[index, 0] for tile in here],
            [joined[step, index, 0] for step in range(slots)],
            [joined[step, index, 1] for step in range(slots)],
            [
                spatial_biases(plan, table_ref, lists_ref, head, step, range(slots, 2 * slots))
                for step in range(slots)
            ],
        )
        for step, state in enumerate(states):
            for out_ref, value in zip(outs, state):
                out_ref[step, index] = jnp.broadcast_to(value, (TILE, HEAD_DIM))
        return 0

    lax.fori_loop(0, plan.heads_in_group(1, table_ref, slot), one_head, 0)


def halo_kernel(plan, steps, table_ref, lists_ref, *rest):
    slots, ways = plan.slots, len(steps)
    queries, (below, above) = rest[:ways], rest[ways : ways + 2]
    top_ref, total_ref, sum_ref = rest[ways + 2 : ways + 5]
    outs = rest[-ways:]
    slot = table_ref[plan.slot_at]
    places = [*range(slots), *range(2 * slots, 3 * slots)]

    def one_head(index, _):
        head = plan.head_at(1, table_ref, slot, index)
        states = attend_tiles(
            [query_ref[index, 0] for query_ref in queries],
            [ref[step, index, 0] for ref in (below, above) for step in range(slots)],
            [ref[step, index, 1] for ref in (below, above) for step in range(slots)],
            [spatial_biases(plan, table_ref, lists_ref, head, step, places) for step in steps],
            [
                (
                    top_ref[step, index][:, :1],
                    total_ref[step, index][:, :1],
                    sum_ref[step, index],
                )
                for step in steps
            ],
        )
        for out_ref, state in zip(outs, states):
            out_ref[index] = normalized(state)
        return 0

    lax.fori_loop(0, plan.heads_in_group(1, table_ref, slot), one_head, 0)


def unpack_kernel(plan, counts, table_ref, *rest):
    pieces, out_ref, sem = list(rest[:-2]), rest[-2], rest[-1]
    for kind, count in enumerate(counts):
        for step in plan.steps(kind):
            piece = pieces.pop(0)
            group = plan.group(kind, table_ref, step)

            def one(index, _, kind=kind, piece=piece, group=group):
                columns = head_columns(plan.head_at(kind, table_ref, group, index))
                pltpu.make_async_copy(piece.at[index], out_ref.at[:, columns], sem).start()
                return 0

            lax.fori_loop(0, plan.heads_in_group(kind, table_ref, group), one, 0)
            if kind == 0:
                filled = (count - 1) * plan.frames + group < table_ref[plan.mixed_at]
                lax.fori_loop(count - 1, count - 1 + filled.astype(jnp.int32), one, 0)
    wait_all(out_ref, sem)


SPACES = {"s": pltpu.SMEM, "v": pltpu.VMEM, "a": pl.ANY}


def call(kernel, outs, operands, places, out_place, scratch=(), flops=0, in_place=None):
    nbytes = sum(math.prod(o.shape) * 2 for o in outs) * 2
    return pl.pallas_call(
        kernel,
        out_shape=outs,
        in_specs=[pl.BlockSpec(memory_space=SPACES[c]) for c in places],
        out_specs=[pl.BlockSpec(memory_space=SPACES[c]) for c in out_place],
        scratch_shapes=list(scratch),
        input_output_aliases=in_place or {},
        compiler_params=pltpu.CompilerParams(vmem_limit_bytes=VMEM_LIMIT),
        cost_estimate=pl.CostEstimate(flops=flops, bytes_accessed=nbytes, transcendentals=0),
    )(*operands)


def after(arrays, others):
    if not arrays or not others:
        return arrays
    return pl.pallas_call(
        lambda *refs: None,
        out_shape=[jax.ShapeDtypeStruct(a.shape, a.dtype) for a in arrays],
        in_specs=[pl.BlockSpec(memory_space=pltpu.VMEM)] * (len(arrays) + len(others)),
        out_specs=[pl.BlockSpec(memory_space=pltpu.VMEM)] * len(arrays),
        input_output_aliases={i: i for i in range(len(arrays))},
        compiler_params=pltpu.CompilerParams(vmem_limit_bytes=VMEM_LIMIT),
    )(*arrays, *others)


def tiles_of(*lead):
    return jax.ShapeDtypeStruct((*lead, TILE, HEAD_DIM), jnp.bfloat16)


def by_kind(plan, t_count, s_count, queries, keys, values, lists, table):
    frames, slots = plan.frames, plan.slots
    pair_flops = 4 * TILE * TILE * HEAD_DIM

    def to_frame(array, step):
        pairs = [(z, z ^ step) for z in range(frames)]
        return array if step == 0 else lax.ppermute(array, "blk", pairs)

    def to_slot(array, step):
        pairs = [(s, s ^ step) for s in range(slots)]
        return array if step == 0 else lax.ppermute(array, MESH_TAIL, pairs)

    def halo(array, step):
        pairs = [(z, z + step) for z in range(frames) if 0 <= z + step < frames]
        return lax.ppermute(array, "blk", pairs)

    packed = call(
        functools.partial(pack_kernel, plan, (t_count, s_count)),
        [tiles_of(t_count, 3)] * frames + [tiles_of(s_count, 3)] * slots,
        (table, queries, keys, values),
        "saaa",
        "v" * (frames + slots),
        [pltpu.SemaphoreType.DMA((frames + slots,))],
    )
    arrived = [to_frame(block, step) for step, block in zip(plan.steps(0), packed[:frames])]
    here = [to_slot(block, step) for step, block in enumerate(packed[frames:])]
    (joined,) = call(
        functools.partial(join_kernel, plan, s_count),
        [tiles_of(slots, s_count, 2)],
        here,
        "v" * slots,
        "v",
        [pltpu.SemaphoreType.DMA((slots,))],
    )
    below, above = halo(joined, 1), halo(joined, -1)
    (mixed,) = call(
        functools.partial(join_mixed_kernel, plan, t_count),
        [tiles_of(frames, 1, 2)],
        (*arrived, joined),
        "v" * (frames + 1),
        "v",
        [pltpu.SemaphoreType.DMA((frames,))],
    )
    gathered = [to_slot(mixed, step) for step in range(slots)]
    tiles_ahead = 2 * slots * s_count - 2 * frames - 3 * t_count // 2
    flops_ahead = max(tiles_ahead, 1) * 42 * pair_flops
    attended = call(
        functools.partial(temporal_kernel, plan, t_count),
        [tiles_of(t_count)] * frames,
        (table, lists, *arrived),
        "ss" + "v" * frames,
        "v" * frames,
        [
            pltpu.VMEM((frames, t_count, 3, TILE, HEAD_DIM), jnp.bfloat16),
            pltpu.VMEM((frames, t_count, TILE, HEAD_DIM), jnp.bfloat16),
            pltpu.SemaphoreType.DMA((frames,)),
        ],
        flops=t_count * frames * frames * pair_flops,
    )
    own_state = call(
        functools.partial(own_frame_kernel, plan),
        [jax.ShapeDtypeStruct((slots, s_count, TILE, HEAD_DIM), jnp.float32)] * 3,
        (table, lists, *here, joined),
        "ss" + "v" * (slots + 1),
        "vvv",
        flops=s_count * slots * slots * pair_flops,
    )
    attended = call(
        functools.partial(mixed_kernel, plan, t_count),
        [tiles_of(t_count)] * frames,
        (table, lists, *arrived, *gathered, *attended, own_state[0]),
        "ss" + "v" * (2 * frames + slots + 1),
        "v" * frames,
        [
            pltpu.VMEM((frames, TILE, HEAD_DIM), jnp.bfloat16),
            pltpu.VMEM((slots * frames, 1, 2, TILE, HEAD_DIM), jnp.bfloat16),
            pltpu.VMEM((frames, TILE, HEAD_DIM), jnp.bfloat16),
            pltpu.SemaphoreType.DMA((frames + slots,)),
        ],
        flops=flops_ahead,
        in_place={2 + frames + slots + i: i for i in range(frames)},
    )
    attended = [attended[0], *after(attended[1:], (below, above))]
    pieces = [to_frame(block, step) for step, block in zip(plan.steps(0), attended)]

    def attend_slots(steps, *earlier):
        return call(
            functools.partial(halo_kernel, plan, steps),
            [tiles_of(s_count)] * len(steps),
            (table, lists, *(here[step] for step in steps), below, above, *own_state, *earlier),
            "ss" + "v" * (len(steps) + 5 + len(earlier)),
            "v" * len(steps),
            flops=s_count * len(steps) * 2 * slots * pair_flops,
        )

    half = slots // 2
    away = attend_slots(range(half, slots))
    near = attend_slots(range(half), away[0])
    attended = [near[0], *after(near[1:], pieces[1:]), *away]
    pieces += [to_slot(block, step) for step, block in enumerate(attended)]
    (out,) = call(
        functools.partial(unpack_kernel, plan, (t_count, s_count)),
        [jax.ShapeDtypeStruct((TILE, plan.heads * HEAD_DIM), jnp.bfloat16)],
        (table, *pieces),
        "s" + "v" * len(pieces),
        "v",
        [pltpu.SemaphoreType.DMA],
    )
    return out


def capacities(heads, frames, slots):
    low, high = heads // 4, heads - heads // 4

    def chunks_for(fewest, most):
        over_frames = max(-(-most // frames), 1)
        shared = max(fewest, (over_frames - 1) * frames)
        left = heads - fewest - (over_frames * frames - shared)
        return over_frames, max(-(-left // slots), 1)

    pairs, begins = [(chunks_for(high + 1, heads)[0], chunks_for(0, low)[1])], []
    for t in range(low + 1, high + 1):
        if t % frames == 1 or t == low + 1:
            begins.append((t, len(pairs)))
            pairs.append(chunks_for(t, min(-(-t // frames) * frames, high)))
    return pairs, begins + [(high + 1, 0)]


def kind_plan(queries, keys, values, block_lists):
    heads, tiles, entries = block_lists.shape
    frames = lax.axis_size("blk")
    slots = lax.axis_size(MESH_TAIL)
    plan = Plan(heads, frames, slots, entries)
    pairs, begins = capacities(heads, frames, slots)
    by_tile = jnp.transpose(block_lists, (1, 2, 0))
    table, branch = call(
        functools.partial(table_kernel, plan, pairs, begins),
        [jax.ShapeDtypeStruct((size,), jnp.int32) for size in (plan.table_size, 1)],
        (by_tile,),
        "v",
        "ss",
        [pltpu.SMEM((heads // 16,), jnp.int32)],
    )
    lists = by_tile.reshape(tiles * entries, heads)
    branches = [functools.partial(by_kind, plan, t, s) for t, s in pairs]
    return lax.switch(branch[0], branches, queries, keys, values, lists, table)


def per_device(queries, keys, values, block_lists):
    slots = lax.axis_size(MESH_TAIL)
    whole_tiles = queries.shape[0] == TILE and slots == FRAME_TILES
    frames = lax.axis_size("blk")
    if whole_tiles and frames & (frames - 1) == 0 and frames * slots == block_lists.shape[1]:
        return kind_plan(queries, keys, values, block_lists)
    return gathered_plan(queries, keys, values, block_lists)


def solution(mesh):
    in_specs = (
        P(("grp", "blk", "head", "sub"), None),
        P(("grp", "blk", "head", "sub"), None),
        P(("grp", "blk", "head", "sub"), None),
        P(),
    )
    out_specs = P(("grp", "blk", "head", "sub"), None)
    return jax.shard_map(
        per_device, mesh=mesh, in_specs=in_specs, out_specs=out_specs, check_vma=False
    )
```

```python
import functools
import math

import jax
import jax.numpy as jnp
from jax import lax
from jax.experimental import pallas as pl
from jax.experimental.pallas import tpu as pltpu
from jax.sharding import PartitionSpec as P

HEADS = 32
HEAD_DIM = 128
TILE = 128
FRAME_TILES = 4


NEG_FLOOR = -1e30


def query_rows(block_lists, first_head, heads_here, query_tokens):
    tile_ids = jnp.arange(block_lists.shape[1], dtype=jnp.int32)
    lists_local = lax.dynamic_slice_in_dim(block_lists, first_head, heads_here, 0)
    tile_mask = jnp.any(lists_local[:, :, :, None] == tile_ids, axis=2).astype(jnp.bfloat16)
    query_onehot = ((query_tokens // TILE)[:, None] == tile_ids[None, :]).astype(jnp.bfloat16)
    listed = jnp.einsum("qi,hij->hqj", query_onehot, tile_mask, preferred_element_type=jnp.float32)
    return listed.astype(jnp.bfloat16)


def attend_block(state_now, key_block, value_block, allowed, query_local, score_scale):
    top_old, total_old, accum_old = state_now
    scores = (
        jnp.einsum("qhd,khd->hqk", query_local, key_block, preferred_element_type=jnp.float32)
        * score_scale
    )
    top_new = jnp.maximum(top_old, jnp.max(jnp.where(allowed, scores, NEG_FLOOR), axis=2))
    factor = jnp.exp(top_old - top_new)
    weights = jnp.where(allowed, jnp.exp(scores - top_new[:, :, None]), 0.0)
    total_new = total_old * factor + jnp.sum(weights, axis=2)
    product = jnp.einsum(
        "hqk,khd->qhd",
        weights.astype(jnp.bfloat16),
        value_block,
        preferred_element_type=jnp.float32,
    )
    accum_new = accum_old * jnp.transpose(factor)[:, :, None] + product
    return (top_new, total_new, accum_new)


def make_step(query_local, listed_rows, key_token, block_len, tile_total):
    score_scale = 1.0 / math.sqrt(HEAD_DIM)
    tile_ids = jnp.arange(tile_total, dtype=jnp.int32)

    def fold_step(state_now, piece, first_row):
        key_piece, value_piece = piece
        block_count = key_piece.shape[0] // block_len

        def one_block(block_index, state_in):
            key_block = lax.dynamic_slice_in_dim(key_piece, block_index * block_len, block_len, 0)
            value_block = lax.dynamic_slice_in_dim(
                value_piece, block_index * block_len, block_len, 0
            )
            positions = block_index * block_len + jnp.arange(block_len, dtype=jnp.int32)
            key_tiles = key_token(positions) // TILE
            key_onehot = (tile_ids[:, None] == key_tiles[None, :]).astype(jnp.bfloat16)
            allowed = (
                jnp.einsum(
                    "hqj,jk->hqk", listed_rows, key_onehot, preferred_element_type=jnp.float32
                )
                > 0.5
            )
            result = attend_block(
                state_in, key_block, value_block, allowed, query_local, score_scale
            )
            return result

        return lax.fori_loop(0, block_count, one_block, state_now)

    return fold_step


def start_state(heads_here, block_len):
    top_all = jnp.full((heads_here, block_len), NEG_FLOOR, jnp.float32)
    total_all = jnp.zeros((heads_here, block_len), jnp.float32)
    accum_all = jnp.zeros((block_len, heads_here, HEAD_DIM), jnp.float32)
    return (top_all, total_all, accum_all)


def normalize(state_end):
    top_all, total_all, accum_all = state_end
    return (accum_all / jnp.transpose(total_all)[:, :, None]).astype(jnp.bfloat16)


def gathered_plan(queries, keys, values, block_lists):
    row_count, col_count = queries.shape
    n_head = lax.axis_size("head")
    n_sub = lax.axis_size("sub")
    blk_index = lax.axis_index("blk")
    head_index = lax.axis_index("head")
    sub_index = lax.axis_index("sub")
    tile_total = block_lists.shape[1]
    heads_here = HEADS // (n_head * n_sub)
    block_len = row_count * n_head * n_sub

    def inward(tensor):
        return tensor.reshape(1, 1, row_count, n_head, n_sub, heads_here * HEAD_DIM)

    query_six, keys_six, values_six = (
        lax.all_to_all(
            lax.all_to_all(inward(queries), "head", split_axis=3, concat_axis=1, tiled=True),
            "sub",
            split_axis=4,
            concat_axis=0,
            tiled=True,
        ),
        lax.all_to_all(
            lax.all_to_all(inward(keys), "head", split_axis=3, concat_axis=1, tiled=True),
            "sub",
            split_axis=4,
            concat_axis=0,
            tiled=True,
        ),
        lax.all_to_all(
            lax.all_to_all(inward(values), "head", split_axis=3, concat_axis=1, tiled=True),
            "sub",
            split_axis=4,
            concat_axis=0,
            tiled=True,
        ),
    )
    query_local = query_six.reshape(block_len, heads_here, HEAD_DIM)
    keys_local = keys_six.reshape(block_len, heads_here, HEAD_DIM)
    values_local = values_six.reshape(block_len, heads_here, HEAD_DIM)

    def key_token(positions):
        source_dev = positions // block_len
        within = positions % block_len
        sub_source = within // (n_head * row_count)
        head_source = within // row_count % n_head
        offset = within % row_count
        return ((source_dev * n_head + head_source) * n_sub + sub_source) * row_count + offset

    query_tokens = key_token(blk_index * block_len + jnp.arange(block_len, dtype=jnp.int32))
    first_head = (head_index * n_sub + sub_index) * heads_here
    listed_rows = query_rows(block_lists, first_head, heads_here, query_tokens)
    fold_step = make_step(query_local, listed_rows, key_token, block_len, tile_total)
    state_end = fold_step(
        start_state(heads_here, block_len),
        (
            lax.all_gather(keys_local, "blk", axis=0, tiled=True),
            lax.all_gather(values_local, "blk", axis=0, tiled=True),
        ),
        jnp.int32(0),
    )
    result_rows = normalize(state_end)
    attended = result_rows.reshape(n_sub, n_head, row_count, 1, 1, heads_here * HEAD_DIM)
    returned = lax.all_to_all(
        lax.all_to_all(attended, "head", split_axis=1, concat_axis=3, tiled=True),
        "sub",
        split_axis=0,
        concat_axis=4,
        tiled=True,
    )
    return returned.reshape(row_count, col_count)


MESH_TAIL = ("head", "sub")
EXP2_SCALE = math.log2(math.e) / math.sqrt(HEAD_DIM)
VMEM_LIMIT = 16 * 1024 * 1024
MIXED_TILES = 2


class Plan:
    def __init__(self, heads, frames, slots, entries):
        self.heads, self.frames, self.slots, self.entries = heads, frames, slots, entries
        self.over_slots_at = heads
        self.pure_at = 2 * heads
        self.mixed_at = 2 * heads + 1
        self.spatial_at = 2 * heads + 2
        self.frame_at = 2 * heads + 3
        self.slot_at = 2 * heads + 4
        self.table_size = 2 * heads + 5

    def sizes(self, kind):
        return (self.frames, self.slots)[kind]

    def head_at(self, kind, table_ref, group, index):
        return table_ref[(0, self.over_slots_at)[kind] + index * self.sizes(kind) + group]

    def group(self, kind, table_ref, step):
        return table_ref[(self.frame_at, self.slot_at)[kind]] ^ step

    def heads_in_group(self, kind, table_ref, group):
        size = self.sizes(kind)
        return (table_ref[(self.pure_at, self.spatial_at)[kind]] - group + size - 1) // size

    def steps(self, kind):
        others = range(1, self.sizes(kind))
        return [0, *others] if kind else [0, *reversed(others)]


def head_columns(head):
    return pl.ds(pl.multiple_of(head * HEAD_DIM, HEAD_DIM), HEAD_DIM)


def table_kernel(plan, pairs, begins, lists_ref, table_ref, branch_ref, mask_ref):
    lists = lists_ref[...]
    tiles = lax.broadcasted_iota(jnp.int32, lists.shape, 0)
    other_slot = ((lists ^ tiles) & (plan.slots - 1)).astype(jnp.float32)
    spatial = jnp.sum(jnp.sum(other_slot, axis=0), axis=0, keepdims=True) > 0
    lanes = lax.broadcasted_iota(jnp.int32, spatial.shape, 1)
    for place in range(plan.heads // 16):
        bit = jnp.where(lanes // 16 == place, jnp.int32(1) << (lanes % 16), 0)
        bits = jnp.where(spatial, bit, 0).astype(jnp.float32)
        mask_ref[place] = jnp.sum(bits).astype(jnp.int32)
    spatial_total = jnp.sum(spatial.astype(jnp.float32)).astype(jnp.int32)
    temporal_total = plan.heads - spatial_total
    branch, chunks, last = 0, pairs[0][0], 0
    for first, place in begins:
        reached = (temporal_total >= first).astype(jnp.int32)
        branch += reached * (place - last)
        chunks += reached * (pairs[place][0] - pairs[last][0])
        last = place
    mixed = (chunks - 1) * plan.frames
    shared = lax.max(temporal_total, mixed)
    room = chunks * plan.frames - shared

    def clear(p, _):
        table_ref[p] = 0
        return 0

    def place_head(h, counts):
        kind = (mask_ref[h // 16] >> (h % 16)) & 1
        t_rank, s_rank = counts
        s_place = jnp.where(s_rank < room, shared + s_rank, plan.over_slots_at + s_rank - room)
        table_ref[jnp.where(kind == 1, s_place, t_rank)] = h
        return t_rank + 1 - kind, s_rank + kind

    lax.fori_loop(0, 2 * plan.heads, clear, 0)
    lax.fori_loop(0, plan.heads, place_head, (jnp.int32(0), jnp.int32(0)))
    table_ref[plan.pure_at] = lax.min(temporal_total, mixed)
    table_ref[plan.mixed_at] = shared + lax.min(spatial_total, room)
    table_ref[plan.spatial_at] = lax.max(spatial_total - room, 0)
    table_ref[plan.frame_at] = lax.axis_index("blk")
    n_sub = lax.axis_size("sub")
    table_ref[plan.slot_at] = lax.axis_index("head") * n_sub + lax.axis_index("sub")
    branch_ref[0] = branch


def wait_all(ref, sem):
    pltpu.make_async_copy(ref, ref, sem).wait()


def pack_kernel(plan, counts, table_ref, q_ref, k_ref, v_ref, *rest):
    outs, sems = rest[:-1], rest[-1]
    steps = [(kind, step) for kind in range(2) for step in plan.steps(kind)]
    for sem, (kind, step) in enumerate(steps):
        group = plan.group(kind, table_ref, step)

        def one(index, _, kind=kind, group=group, sem=sem):
            columns = head_columns(plan.head_at(kind, table_ref, group, index))
            for place, ref in enumerate((q_ref, k_ref, v_ref)):
                pltpu.make_async_copy(
                    ref.at[:, columns], outs[sem].at[index, place], sems.at[sem]
                ).start()
            return 0

        lax.fori_loop(0, counts[kind], one, 0)
    for sem, out_ref in enumerate(outs):
        wait_all(out_ref, sems.at[sem])


def turn_keys(kv_ref, place, count):
    def turn(work, _):
        step, index = work // count, lax.rem(work, count)
        kv_ref[step, index, place] = kv_ref[step, index, place].T
        return 0

    lax.fori_loop(0, kv_ref.shape[0] * count, turn, 0)


def join_kernel(plan, count, *refs):
    pieces, out_ref, sems = refs[: plan.slots], refs[-2], refs[-1]
    copy_pieces(
        [(piece.at[:, pl.ds(1, 2)], out_ref.at[step]) for step, piece in enumerate(pieces)], sems
    )
    turn_keys(out_ref, 0, count)


def join_mixed_kernel(plan, count, *refs):
    pieces, out_ref, sems = refs[: plan.frames], refs[-2], refs[-1]
    copy_pieces(
        [
            (piece.at[count - 1, pl.ds(1, 2)], out_ref.at[step, 0])
            for step, piece in zip(plan.steps(0), pieces)
        ],
        sems,
    )
    turn_keys(out_ref, 0, 1)


def attend_tiles(queries, keys, values, biases, before=None, turned=True):
    scores = lax.dot_general(
        jnp.concatenate(queries, 0),
        jnp.concatenate(keys, 1 if turned else 0),
        (((1,), (0 if turned else 1,)), ((), ())),
        preferred_element_type=jnp.float32,
    )
    rows, tops, totals = [], [], []
    for a, bias in enumerate(biases):
        tiles = [
            scores[a * TILE : (a + 1) * TILE, b * TILE : (b + 1) * TILE] + bias[b]
            for b in range(len(keys))
        ]
        top = jnp.max(functools.reduce(jnp.maximum, tiles), axis=1, keepdims=True)
        if before is not None:
            top = jnp.maximum(top, before[a][0])
        weights = [jnp.exp2((tile - top) * EXP2_SCALE) for tile in tiles]
        tops.append(top)
        totals.append(jnp.sum(functools.reduce(jnp.add, weights), axis=1, keepdims=True))
        rows.append(jnp.concatenate([w.astype(jnp.bfloat16) for w in weights], 1))
    accum = jnp.dot(
        jnp.concatenate(rows, 0), jnp.concatenate(values, 0), preferred_element_type=jnp.float32
    )
    states = []
    for a, (top, total) in enumerate(zip(tops, totals)):
        part = accum[a * TILE : (a + 1) * TILE]
        if before is not None:
            factor = jnp.exp2((before[a][0] - top) * EXP2_SCALE)
            total, part = total + before[a][1] * factor, part + before[a][2] * factor
        states.append((top, total, part))
    return states


def normalized(state):
    return (state[2] / state[1]).astype(jnp.bfloat16)


def bias_where(attended):
    return jnp.where(attended, jnp.float32(0), jnp.float32(NEG_FLOOR))


def copy_pieces(pieces, sems):
    copies = [pltpu.make_async_copy(a, b, sems.at[i]) for i, (a, b) in enumerate(pieces)]
    for copy in copies:
        copy.start()
    for copy in copies:
        copy.wait()


def listed_places(plan, lists_ref, head, query_tile, place_of):
    first = query_tile * plan.entries
    listed = jnp.int32(0)
    places, biases = [], []
    for entry in range(plan.entries):
        place = place_of(lists_ref[first + entry, head])
        places.append(place)
        biases.append(bias_where((listed >> place) & 1 == 0))
        listed |= jnp.int32(1) << place
    return places, biases


def temporal_kernel(plan, table_ref, lists_ref, *rest):
    frames, slots = plan.frames, plan.slots
    by_step = [plan.steps(0).index(step) for step in range(frames)]
    tiles = [rest[i] for i in by_step]
    outs = [rest[frames + i] for i in by_step]
    frame, slot = table_ref[plan.frame_at], table_ref[plan.slot_at]

    def one_head(index, _):
        head = plan.head_at(0, table_ref, frame, index)
        biases = []
        for step in range(frames):
            first = ((frame ^ step) * slots + slot) * plan.entries
            listed = jnp.int32(0)
            for entry in range(plan.entries):
                listed |= jnp.int32(1) << (lists_ref[first + entry, head] // slots)
            biases.append(
                [bias_where((listed >> (frame ^ other)) & 1 == 1) for other in range(frames)]
            )
        states = attend_tiles(
            *([tile[index, i] for tile in tiles] for i in range(3)), biases, turned=False
        )
        for out_ref, state in zip(outs, states):
            out_ref[index] = normalized(state)
        return 0

    lax.fori_loop(0, plan.heads_in_group(0, table_ref, frame), one_head, 0)


def mixed_kernel(plan, count, table_ref, lists_ref, *rest):
    frames, slots = plan.frames, plan.slots
    tiles, gathered = rest[:frames], rest[frames : frames + slots]
    outs = rest[-4 - frames : -4]
    q_ref, kv_ref, result_ref, sems = rest[-4:]
    copy_pieces(
        [(tile.at[count - 1, 0], q_ref.at[step]) for step, tile in zip(plan.steps(0), tiles)]
        + [
            (block, kv_ref.at[pl.ds(step * frames, frames)])
            for step, block in zip((0, *reversed(range(1, slots))), gathered)
        ],
        sems,
    )
    frame, slot = table_ref[plan.frame_at], table_ref[plan.slot_at]
    head = plan.head_at(0, table_ref, frame, count - 1)

    def some_tiles(body, _):
        for step in (body * MIXED_TILES + more for more in range(MIXED_TILES)):
            places, biases = listed_places(
                plan,
                lists_ref,
                head,
                (frame ^ step) * slots + slot,
                lambda tile: (lax.rem(tile, slots) ^ slot) * frames + (tile // slots ^ frame),
            )
            (state,) = attend_tiles(
                [q_ref[step]],
                [kv_ref[place, 0, 0] for place in places],
                [kv_ref[place, 0, 1] for place in places],
                [biases],
            )
            result_ref[step] = normalized(state)
        return 0

    lax.fori_loop(0, frames // MIXED_TILES, some_tiles, 0)
    copy_pieces(
        [(result_ref.at[step], out.at[count - 1]) for step, out in zip(plan.steps(0), outs)], sems
    )


def spatial_biases(plan, table_ref, lists_ref, head, step, places):
    slots = plan.slots
    frame, slot = table_ref[plan.frame_at], table_ref[plan.slot_at]
    first = (frame * slots + (slot ^ step)) * plan.entries
    listed = jnp.int32(0)
    for entry in range(plan.entries):
        tile = lists_ref[first + entry, head]
        place = (tile // slots - frame + 1) * slots + (lax.rem(tile, slots) ^ slot)
        listed |= jnp.int32(1) << place
    return [bias_where((listed >> place) & 1 == 1) for place in places]


def own_frame_kernel(plan, table_ref, lists_ref, *rest):
    slots = plan.slots
    here, joined, outs = rest[:slots], rest[slots], rest[slots + 1 :]
    slot = table_ref[plan.slot_at]

    def one_head(index, _):
        head = plan.head_at(1, table_ref, slot, index)
        states = attend_tiles(
            [tile[index, 0] for tile in here],
            [joined[step, index, 0] for step in range(slots)],
            [joined[step, index, 1] for step in range(slots)],
            [
                spatial_biases(plan, table_ref, lists_ref, head, step, range(slots, 2 * slots))
                for step in range(slots)
            ],
        )
        for step, state in enumerate(states):
            for out_ref, value in zip(outs, state):
                out_ref[step, index] = jnp.broadcast_to(value, (TILE, HEAD_DIM))
        return 0

    lax.fori_loop(0, plan.heads_in_group(1, table_ref, slot), one_head, 0)


def halo_kernel(plan, steps, table_ref, lists_ref, *rest):
    slots, ways = plan.slots, len(steps)
    queries, (below, above) = rest[:ways], rest[ways : ways + 2]
    top_ref, total_ref, sum_ref = rest[ways + 2 : ways + 5]
    outs = rest[-ways:]
    slot = table_ref[plan.slot_at]
    places = [*range(slots), *range(2 * slots, 3 * slots)]

    def one_head(index, _):
        head = plan.head_at(1, table_ref, slot, index)
        states = attend_tiles(
            [query_ref[index, 0] for query_ref in queries],
            [ref[step, index, 0] for ref in (below, above) for step in range(slots)],
            [ref[step, index, 1] for ref in (below, above) for step in range(slots)],
            [spatial_biases(plan, table_ref, lists_ref, head, step, places) for step in steps],
            [
                (
                    top_ref[step, index][:, :1],
                    total_ref[step, index][:, :1],
                    sum_ref[step, index],
                )
                for step in steps
            ],
        )
        for out_ref, state in zip(outs, states):
            out_ref[index] = normalized(state)
        return 0

    lax.fori_loop(0, plan.heads_in_group(1, table_ref, slot), one_head, 0)


def unpack_kernel(plan, counts, table_ref, *rest):
    pieces, out_ref, sem = list(rest[:-2]), rest[-2], rest[-1]
    for kind, count in enumerate(counts):
        for step in plan.steps(kind):
            piece = pieces.pop(0)
            group = plan.group(kind, table_ref, step)

            def one(index, _, kind=kind, piece=piece, group=group):
                columns = head_columns(plan.head_at(kind, table_ref, group, index))
                pltpu.make_async_copy(piece.at[index], out_ref.at[:, columns], sem).start()
                return 0

            lax.fori_loop(0, plan.heads_in_group(kind, table_ref, group), one, 0)
            if kind == 0:
                filled = (count - 1) * plan.frames + group < table_ref[plan.mixed_at]
                lax.fori_loop(count - 1, count - 1 + filled.astype(jnp.int32), one, 0)
    wait_all(out_ref, sem)


SPACES = {"s": pltpu.SMEM, "v": pltpu.VMEM, "a": pl.ANY}


def call(kernel, outs, operands, places, out_place, scratch=(), flops=0, in_place=None):
    nbytes = sum(math.prod(o.shape) * 2 for o in outs) * 2
    return pl.pallas_call(
        kernel,
        out_shape=outs,
        in_specs=[pl.BlockSpec(memory_space=SPACES[c]) for c in places],
        out_specs=[pl.BlockSpec(memory_space=SPACES[c]) for c in out_place],
        scratch_shapes=list(scratch),
        input_output_aliases=in_place or {},
        compiler_params=pltpu.CompilerParams(vmem_limit_bytes=VMEM_LIMIT),
        cost_estimate=pl.CostEstimate(flops=flops, bytes_accessed=nbytes, transcendentals=0),
    )(*operands)


def after(arrays, others):
    if not arrays or not others:
        return arrays
    return pl.pallas_call(
        lambda *refs: None,
        out_shape=[jax.ShapeDtypeStruct(a.shape, a.dtype) for a in arrays],
        in_specs=[pl.BlockSpec(memory_space=pltpu.VMEM)] * (len(arrays) + len(others)),
        out_specs=[pl.BlockSpec(memory_space=pltpu.VMEM)] * len(arrays),
        input_output_aliases={i: i for i in range(len(arrays))},
        compiler_params=pltpu.CompilerParams(vmem_limit_bytes=VMEM_LIMIT),
    )(*arrays, *others)


def tiles_of(*lead):
    return jax.ShapeDtypeStruct((*lead, TILE, HEAD_DIM), jnp.bfloat16)


def by_kind(plan, t_count, s_count, queries, keys, values, lists, table):
    frames, slots = plan.frames, plan.slots
    pair_flops = 4 * TILE * TILE * HEAD_DIM

    def to_frame(array, step):
        pairs = [(z, z ^ step) for z in range(frames)]
        return array if step == 0 else lax.ppermute(array, "blk", pairs)

    def to_slot(array, step):
        pairs = [(s, s ^ step) for s in range(slots)]
        return array if step == 0 else lax.ppermute(array, MESH_TAIL, pairs)

    def halo(array, step):
        pairs = [(z, z + step) for z in range(frames) if 0 <= z + step < frames]
        return lax.ppermute(array, "blk", pairs)

    packed = call(
        functools.partial(pack_kernel, plan, (t_count, s_count)),
        [tiles_of(t_count, 3)] * frames + [tiles_of(s_count, 3)] * slots,
        (table, queries, keys, values),
        "saaa",
        "v" * (frames + slots),
        [pltpu.SemaphoreType.DMA((frames + slots,))],
    )
    arrived = [to_frame(block, step) for step, block in zip(plan.steps(0), packed[:frames])]
    here = [to_slot(block, step) for step, block in enumerate(packed[frames:])]
    (joined,) = call(
        functools.partial(join_kernel, plan, s_count),
        [tiles_of(slots, s_count, 2)],
        here,
        "v" * slots,
        "v",
        [pltpu.SemaphoreType.DMA((slots,))],
    )
    below, above = halo(joined, 1), halo(joined, -1)
    (mixed,) = call(
        functools.partial(join_mixed_kernel, plan, t_count),
        [tiles_of(frames, 1, 2)],
        (*arrived, joined),
        "v" * (frames + 1),
        "v",
        [pltpu.SemaphoreType.DMA((frames,))],
    )
    gathered = [to_slot(mixed, step) for step in (0, *reversed(range(1, slots)))]
    tiles_ahead = 2 * slots * s_count - 2 * frames - 3 * t_count // 2
    flops_ahead = max(tiles_ahead, 1) * 42 * pair_flops
    attended = call(
        functools.partial(temporal_kernel, plan),
        [tiles_of(t_count)] * frames,
        (table, lists, *arrived),
        "ss" + "v" * frames,
        "v" * frames,
        flops=t_count * frames * frames * pair_flops,
    )
    own_state = call(
        functools.partial(own_frame_kernel, plan),
        [jax.ShapeDtypeStruct((slots, s_count, TILE, HEAD_DIM), jnp.float32)] * 3,
        (table, lists, *here, joined),
        "ss" + "v" * (slots + 1),
        "vvv",
        flops=s_count * slots * slots * pair_flops,
    )
    attended = call(
        functools.partial(mixed_kernel, plan, t_count),
        [tiles_of(t_count)] * frames,
        (table, lists, *arrived, *gathered, *attended, own_state[0]),
        "ss" + "v" * (2 * frames + slots + 1),
        "v" * frames,
        [
            pltpu.VMEM((frames, TILE, HEAD_DIM), jnp.bfloat16),
            pltpu.VMEM((slots * frames, 1, 2, TILE, HEAD_DIM), jnp.bfloat16),
            pltpu.VMEM((frames, TILE, HEAD_DIM), jnp.bfloat16),
            pltpu.SemaphoreType.DMA((frames + slots,)),
        ],
        flops=flops_ahead,
        in_place={2 + frames + slots + i: i for i in range(frames)},
    )
    attended = [attended[0], *after(attended[1:], (below, above))]
    pieces = [to_frame(block, step) for step, block in zip(plan.steps(0), attended)]

    def attend_slots(steps, *earlier):
        return call(
            functools.partial(halo_kernel, plan, steps),
            [tiles_of(s_count)] * len(steps),
            (table, lists, *(here[step] for step in steps), below, above, *own_state, *earlier),
            "ss" + "v" * (len(steps) + 5 + len(earlier)),
            "v" * len(steps),
            flops=s_count * len(steps) * 2 * slots * pair_flops,
        )

    half = slots // 2
    away = attend_slots(range(half, slots))
    near = attend_slots(range(half), away[0])
    attended = [near[0], *after(near[1:], pieces[1:]), *away]
    pieces += [to_slot(block, step) for step, block in enumerate(attended)]
    (out,) = call(
        functools.partial(unpack_kernel, plan, (t_count, s_count)),
        [pltpu.HBM((TILE, plan.heads * HEAD_DIM), jnp.bfloat16)],
        (table, *pieces),
        "s" + "v" * len(pieces),
        "v",
        [pltpu.SemaphoreType.DMA],
    )
    return out


def capacities(heads, frames, slots):
    low, high = heads // 4, heads - heads // 4

    def chunks_for(fewest, most):
        over_frames = max(-(-most // frames), 1)
        shared = max(fewest, (over_frames - 1) * frames)
        left = heads - fewest - (over_frames * frames - shared)
        return over_frames, max(-(-left // slots), 1)

    pairs, begins = [(chunks_for(high + 1, heads)[0], chunks_for(0, low)[1])], []
    for t in range(low + 1, high + 1):
        if t % frames == 1 or t == low + 1:
            begins.append((t, len(pairs)))
            pairs.append(chunks_for(t, min(-(-t // frames) * frames, high)))
    return pairs, begins + [(high + 1, 0)]


def kind_plan(queries, keys, values, block_lists):
    heads, tiles, entries = block_lists.shape
    frames = lax.axis_size("blk")
    slots = lax.axis_size(MESH_TAIL)
    plan = Plan(heads, frames, slots, entries)
    pairs, begins = capacities(heads, frames, slots)
    by_tile = jnp.transpose(block_lists, (1, 2, 0))
    table, branch = call(
        functools.partial(table_kernel, plan, pairs, begins),
        [jax.ShapeDtypeStruct((size,), jnp.int32) for size in (plan.table_size, 1)],
        (by_tile,),
        "v",
        "ss",
        [pltpu.SMEM((heads // 16,), jnp.int32)],
    )
    lists = by_tile.reshape(tiles * entries, heads)
    branches = [functools.partial(by_kind, plan, t, s) for t, s in pairs]
    return lax.switch(branch[0], branches, queries, keys, values, lists, table)


def per_device(queries, keys, values, block_lists):
    slots = lax.axis_size(MESH_TAIL)
    whole_tiles = queries.shape[0] == TILE and slots == FRAME_TILES
    frames = lax.axis_size("blk")
    if whole_tiles and frames & (frames - 1) == 0 and frames * slots == block_lists.shape[1]:
        return kind_plan(queries, keys, values, block_lists)
    return gathered_plan(queries, keys, values, block_lists)


def solution(mesh):
    in_specs = (
        P(("grp", "blk", "head", "sub"), None),
        P(("grp", "blk", "head", "sub"), None),
        P(("grp", "blk", "head", "sub"), None),
        P(),
    )
    out_specs = P(("grp", "blk", "head", "sub"), None)
    return jax.shard_map(
        per_device, mesh=mesh, in_specs=in_specs, out_specs=out_specs, check_vma=False
    )
```

```python
import functools
import math

import jax
import jax.numpy as jnp
from jax import lax
from jax.experimental import pallas as pl
from jax.experimental.pallas import tpu as pltpu
from jax.sharding import PartitionSpec as P

HEADS = 32
HEAD_DIM = 128
TILE = 128
FRAME_TILES = 4


NEG_FLOOR = -1e30


def query_rows(block_lists, first_head, heads_here, query_tokens):
    tile_ids = jnp.arange(block_lists.shape[1], dtype=jnp.int32)
    lists_local = lax.dynamic_slice_in_dim(block_lists, first_head, heads_here, 0)
    tile_mask = jnp.any(lists_local[:, :, :, None] == tile_ids, axis=2).astype(jnp.bfloat16)
    query_onehot = ((query_tokens // TILE)[:, None] == tile_ids[None, :]).astype(jnp.bfloat16)
    listed = jnp.einsum("qi,hij->hqj", query_onehot, tile_mask, preferred_element_type=jnp.float32)
    return listed.astype(jnp.bfloat16)


def attend_block(state_now, key_block, value_block, allowed, query_local, score_scale):
    top_old, total_old, accum_old = state_now
    scores = (
        jnp.einsum("qhd,khd->hqk", query_local, key_block, preferred_element_type=jnp.float32)
        * score_scale
    )
    top_new = jnp.maximum(top_old, jnp.max(jnp.where(allowed, scores, NEG_FLOOR), axis=2))
    factor = jnp.exp(top_old - top_new)
    weights = jnp.where(allowed, jnp.exp(scores - top_new[:, :, None]), 0.0)
    total_new = total_old * factor + jnp.sum(weights, axis=2)
    product = jnp.einsum(
        "hqk,khd->qhd",
        weights.astype(jnp.bfloat16),
        value_block,
        preferred_element_type=jnp.float32,
    )
    accum_new = accum_old * jnp.transpose(factor)[:, :, None] + product
    return (top_new, total_new, accum_new)


def make_step(query_local, listed_rows, key_token, block_len, tile_total):
    score_scale = 1.0 / math.sqrt(HEAD_DIM)
    tile_ids = jnp.arange(tile_total, dtype=jnp.int32)

    def fold_step(state_now, piece, first_row):
        key_piece, value_piece = piece
        block_count = key_piece.shape[0] // block_len

        def one_block(block_index, state_in):
            key_block = lax.dynamic_slice_in_dim(key_piece, block_index * block_len, block_len, 0)
            value_block = lax.dynamic_slice_in_dim(
                value_piece, block_index * block_len, block_len, 0
            )
            positions = block_index * block_len + jnp.arange(block_len, dtype=jnp.int32)
            key_tiles = key_token(positions) // TILE
            key_onehot = (tile_ids[:, None] == key_tiles[None, :]).astype(jnp.bfloat16)
            allowed = (
                jnp.einsum(
                    "hqj,jk->hqk", listed_rows, key_onehot, preferred_element_type=jnp.float32
                )
                > 0.5
            )
            result = attend_block(
                state_in, key_block, value_block, allowed, query_local, score_scale
            )
            return result

        return lax.fori_loop(0, block_count, one_block, state_now)

    return fold_step


def start_state(heads_here, block_len):
    top_all = jnp.full((heads_here, block_len), NEG_FLOOR, jnp.float32)
    total_all = jnp.zeros((heads_here, block_len), jnp.float32)
    accum_all = jnp.zeros((block_len, heads_here, HEAD_DIM), jnp.float32)
    return (top_all, total_all, accum_all)


def normalize(state_end):
    top_all, total_all, accum_all = state_end
    return (accum_all / jnp.transpose(total_all)[:, :, None]).astype(jnp.bfloat16)


def gathered_plan(queries, keys, values, block_lists):
    row_count, col_count = queries.shape
    n_head = lax.axis_size("head")
    n_sub = lax.axis_size("sub")
    blk_index = lax.axis_index("blk")
    head_index = lax.axis_index("head")
    sub_index = lax.axis_index("sub")
    tile_total = block_lists.shape[1]
    heads_here = HEADS // (n_head * n_sub)
    block_len = row_count * n_head * n_sub

    def inward(tensor):
        return tensor.reshape(1, 1, row_count, n_head, n_sub, heads_here * HEAD_DIM)

    query_six, keys_six, values_six = (
        lax.all_to_all(
            lax.all_to_all(inward(queries), "head", split_axis=3, concat_axis=1, tiled=True),
            "sub",
            split_axis=4,
            concat_axis=0,
            tiled=True,
        ),
        lax.all_to_all(
            lax.all_to_all(inward(keys), "head", split_axis=3, concat_axis=1, tiled=True),
            "sub",
            split_axis=4,
            concat_axis=0,
            tiled=True,
        ),
        lax.all_to_all(
            lax.all_to_all(inward(values), "head", split_axis=3, concat_axis=1, tiled=True),
            "sub",
            split_axis=4,
            concat_axis=0,
            tiled=True,
        ),
    )
    query_local = query_six.reshape(block_len, heads_here, HEAD_DIM)
    keys_local = keys_six.reshape(block_len, heads_here, HEAD_DIM)
    values_local = values_six.reshape(block_len, heads_here, HEAD_DIM)

    def key_token(positions):
        source_dev = positions // block_len
        within = positions % block_len
        sub_source = within // (n_head * row_count)
        head_source = within // row_count % n_head
        offset = within % row_count
        return ((source_dev * n_head + head_source) * n_sub + sub_source) * row_count + offset

    query_tokens = key_token(blk_index * block_len + jnp.arange(block_len, dtype=jnp.int32))
    first_head = (head_index * n_sub + sub_index) * heads_here
    listed_rows = query_rows(block_lists, first_head, heads_here, query_tokens)
    fold_step = make_step(query_local, listed_rows, key_token, block_len, tile_total)
    state_end = fold_step(
        start_state(heads_here, block_len),
        (
            lax.all_gather(keys_local, "blk", axis=0, tiled=True),
            lax.all_gather(values_local, "blk", axis=0, tiled=True),
        ),
        jnp.int32(0),
    )
    result_rows = normalize(state_end)
    attended = result_rows.reshape(n_sub, n_head, row_count, 1, 1, heads_here * HEAD_DIM)
    returned = lax.all_to_all(
        lax.all_to_all(attended, "head", split_axis=1, concat_axis=3, tiled=True),
        "sub",
        split_axis=0,
        concat_axis=4,
        tiled=True,
    )
    return returned.reshape(row_count, col_count)


MESH_TAIL = ("head", "sub")
EXP2_SCALE = math.log2(math.e) / math.sqrt(HEAD_DIM)
VMEM_LIMIT = 16 * 1024 * 1024
MIXED_TILES = 2


class Plan:
    def __init__(self, heads, frames, slots, entries):
        self.heads, self.frames, self.slots, self.entries = heads, frames, slots, entries
        self.over_slots_at = heads
        self.pure_at = 2 * heads
        self.mixed_at = 2 * heads + 1
        self.spatial_at = 2 * heads + 2
        self.frame_at = 2 * heads + 3
        self.slot_at = 2 * heads + 4
        self.table_size = 2 * heads + 5

    def sizes(self, kind):
        return (self.frames, self.slots)[kind]

    def head_at(self, kind, table_ref, group, index):
        return table_ref[(0, self.over_slots_at)[kind] + index * self.sizes(kind) + group]

    def group(self, kind, table_ref, step):
        return table_ref[(self.frame_at, self.slot_at)[kind]] ^ step

    def heads_in_group(self, kind, table_ref, group):
        size = self.sizes(kind)
        return (table_ref[(self.pure_at, self.spatial_at)[kind]] - group + size - 1) // size

    def steps(self, kind):
        others = range(1, self.sizes(kind))
        return [0, *others] if kind else [0, *reversed(others)]


def head_columns(head):
    return pl.ds(pl.multiple_of(head * HEAD_DIM, HEAD_DIM), HEAD_DIM)


def table_kernel(plan, pairs, begins, lists_ref, table_ref, branch_ref, mask_ref):
    lists = lists_ref[...]
    tiles = lax.broadcasted_iota(jnp.int32, lists.shape, 0)
    other_slot = ((lists ^ tiles) & (plan.slots - 1)).astype(jnp.float32)
    spatial = jnp.sum(jnp.sum(other_slot, axis=0), axis=0, keepdims=True) > 0
    lanes = lax.broadcasted_iota(jnp.int32, spatial.shape, 1)
    for place in range(plan.heads // 16):
        bit = jnp.where(lanes // 16 == place, jnp.int32(1) << (lanes % 16), 0)
        bits = jnp.where(spatial, bit, 0).astype(jnp.float32)
        mask_ref[place] = jnp.sum(bits).astype(jnp.int32)
    spatial_total = jnp.sum(spatial.astype(jnp.float32)).astype(jnp.int32)
    temporal_total = plan.heads - spatial_total
    branch, chunks, last = 0, pairs[0][0], 0
    for first, place in begins:
        reached = (temporal_total >= first).astype(jnp.int32)
        branch += reached * (place - last)
        chunks += reached * (pairs[place][0] - pairs[last][0])
        last = place
    mixed = (chunks - 1) * plan.frames
    shared = lax.max(temporal_total, mixed)
    room = chunks * plan.frames - shared

    def clear(p, _):
        table_ref[p] = 0
        return 0

    def place_head(h, counts):
        kind = (mask_ref[h // 16] >> (h % 16)) & 1
        t_rank, s_rank = counts
        s_place = jnp.where(s_rank < room, shared + s_rank, plan.over_slots_at + s_rank - room)
        table_ref[jnp.where(kind == 1, s_place, t_rank)] = h
        return t_rank + 1 - kind, s_rank + kind

    lax.fori_loop(0, 2 * plan.heads, clear, 0)
    lax.fori_loop(0, plan.heads, place_head, (jnp.int32(0), jnp.int32(0)))
    table_ref[plan.pure_at] = lax.min(temporal_total, mixed)
    table_ref[plan.mixed_at] = shared + lax.min(spatial_total, room)
    table_ref[plan.spatial_at] = lax.max(spatial_total - room, 0)
    table_ref[plan.frame_at] = lax.axis_index("blk")
    n_sub = lax.axis_size("sub")
    table_ref[plan.slot_at] = lax.axis_index("head") * n_sub + lax.axis_index("sub")
    branch_ref[0] = branch


def wait_all(ref, sem):
    pltpu.make_async_copy(ref, ref, sem).wait()


def pack_kernel(plan, counts, table_ref, q_ref, k_ref, v_ref, *rest):
    outs, sems = rest[:-1], rest[-1]
    steps = [(kind, step) for kind in range(2) for step in plan.steps(kind)]
    for sem, (kind, step) in enumerate(steps):
        group = plan.group(kind, table_ref, step)

        def one(index, _, kind=kind, group=group, sem=sem):
            columns = head_columns(plan.head_at(kind, table_ref, group, index))
            for place, ref in enumerate((q_ref, k_ref, v_ref)):
                pltpu.make_async_copy(
                    ref.at[:, columns], outs[sem].at[index, place], sems.at[sem]
                ).start()
            return 0

        lax.fori_loop(0, counts[kind], one, 0)
    for sem, out_ref in enumerate(outs):
        wait_all(out_ref, sems.at[sem])


def turn_keys(kv_ref, place, count):
    def turn(work, _):
        step, index = work // count, lax.rem(work, count)
        kv_ref[step, index, place] = kv_ref[step, index, place].T
        return 0

    lax.fori_loop(0, kv_ref.shape[0] * count, turn, 0)


def join_kernel(plan, count, *refs):
    pieces, out_ref, sems = refs[: plan.slots], refs[-2], refs[-1]
    copy_pieces(
        [(piece.at[:, pl.ds(1, 2)], out_ref.at[step]) for step, piece in enumerate(pieces)], sems
    )
    turn_keys(out_ref, 0, count)


def join_mixed_kernel(plan, count, *refs):
    pieces, out_ref, sems = refs[: plan.frames], refs[-2], refs[-1]
    copy_pieces(
        [
            (piece.at[count - 1, pl.ds(1, 2)], out_ref.at[step, 0])
            for step, piece in zip(plan.steps(0), pieces)
        ],
        sems,
    )
    turn_keys(out_ref, 0, 1)


def attend_tiles(queries, keys, values, biases, before=None, turned=True):
    scores = lax.dot_general(
        jnp.concatenate(queries, 0),
        jnp.concatenate(keys, 1 if turned else 0),
        (((1,), (0 if turned else 1,)), ((), ())),
        preferred_element_type=jnp.float32,
    )
    rows, tops, totals = [], [], []
    for a, bias in enumerate(biases):
        tiles = [
            scores[a * TILE : (a + 1) * TILE, b * TILE : (b + 1) * TILE] + bias[b]
            for b in range(len(keys))
        ]
        top = jnp.max(functools.reduce(jnp.maximum, tiles), axis=1, keepdims=True)
        if before is not None:
            top = jnp.maximum(top, before[a][0])
        weights = [jnp.exp2((tile - top) * EXP2_SCALE) for tile in tiles]
        tops.append(top)
        totals.append(jnp.sum(functools.reduce(jnp.add, weights), axis=1, keepdims=True))
        rows.append(jnp.concatenate([w.astype(jnp.bfloat16) for w in weights], 1))
    accum = jnp.dot(
        jnp.concatenate(rows, 0), jnp.concatenate(values, 0), preferred_element_type=jnp.float32
    )
    states = []
    for a, (top, total) in enumerate(zip(tops, totals)):
        part = accum[a * TILE : (a + 1) * TILE]
        if before is not None:
            factor = jnp.exp2((before[a][0] - top) * EXP2_SCALE)
            total, part = total + before[a][1] * factor, part + before[a][2] * factor
        states.append((top, total, part))
    return states


def normalized(state):
    return (state[2] / state[1]).astype(jnp.bfloat16)


def bias_where(attended):
    return jnp.where(attended, jnp.float32(0), jnp.float32(NEG_FLOOR))


def copy_pieces(pieces, sems):
    copies = [pltpu.make_async_copy(a, b, sems.at[i]) for i, (a, b) in enumerate(pieces)]
    for copy in copies:
        copy.start()
    for copy in copies:
        copy.wait()


def listed_places(plan, lists_ref, head, query_tile, place_of):
    first = query_tile * plan.entries
    listed = jnp.int32(0)
    places, biases = [], []
    for entry in range(plan.entries):
        place = place_of(lists_ref[first + entry, head])
        places.append(place)
        biases.append(bias_where((listed >> place) & 1 == 0))
        listed |= jnp.int32(1) << place
    return places, biases


def temporal_kernel(plan, table_ref, lists_ref, *rest):
    frames, slots = plan.frames, plan.slots
    by_step = [plan.steps(0).index(step) for step in range(frames)]
    tiles = [rest[i] for i in by_step]
    outs = [rest[frames + i] for i in by_step]
    frame, slot = table_ref[plan.frame_at], table_ref[plan.slot_at]

    def one_head(index, _):
        head = plan.head_at(0, table_ref, frame, index)
        biases = []
        for step in range(frames):
            first = ((frame ^ step) * slots + slot) * plan.entries
            listed = jnp.int32(0)
            for entry in range(plan.entries):
                listed |= jnp.int32(1) << (lists_ref[first + entry, head] // slots)
            biases.append(
                [bias_where((listed >> (frame ^ other)) & 1 == 1) for other in range(frames)]
            )
        states = attend_tiles(
            *([tile[index, i] for tile in tiles] for i in range(3)), biases, turned=False
        )
        for out_ref, state in zip(outs, states):
            out_ref[index] = normalized(state)
        return 0

    lax.fori_loop(0, plan.heads_in_group(0, table_ref, frame), one_head, 0)


def mixed_kernel(plan, count, table_ref, lists_ref, *rest):
    frames, slots = plan.frames, plan.slots
    tiles, gathered = rest[:frames], rest[frames : frames + slots]
    outs = rest[-4 - frames : -4]
    q_ref, kv_ref, result_ref, sems = rest[-4:]
    copy_pieces(
        [(tile.at[count - 1, 0], q_ref.at[step]) for step, tile in zip(plan.steps(0), tiles)]
        + [
            (block, kv_ref.at[pl.ds(step * frames, frames)])
            for step, block in zip((0, *reversed(range(1, slots))), gathered)
        ],
        sems,
    )
    frame, slot = table_ref[plan.frame_at], table_ref[plan.slot_at]
    head = plan.head_at(0, table_ref, frame, count - 1)

    def some_tiles(body, _):
        for step in (body * MIXED_TILES + more for more in range(MIXED_TILES)):
            places, biases = listed_places(
                plan,
                lists_ref,
                head,
                (frame ^ step) * slots + slot,
                lambda tile: (lax.rem(tile, slots) ^ slot) * frames + (tile // slots ^ frame),
            )
            (state,) = attend_tiles(
                [q_ref[step]],
                [kv_ref[place, 0, 0] for place in places],
                [kv_ref[place, 0, 1] for place in places],
                [biases],
            )
            result_ref[step] = normalized(state)
        return 0

    lax.fori_loop(0, frames // MIXED_TILES, some_tiles, 0)
    copy_pieces(
        [(result_ref.at[step], out.at[count - 1]) for step, out in zip(plan.steps(0), outs)], sems
    )


def spatial_biases(plan, table_ref, lists_ref, head, step, places):
    slots = plan.slots
    frame, slot = table_ref[plan.frame_at], table_ref[plan.slot_at]
    first = (frame * slots + (slot ^ step)) * plan.entries
    listed = jnp.int32(0)
    for entry in range(plan.entries):
        tile = lists_ref[first + entry, head]
        place = (tile // slots - frame + 1) * slots + (lax.rem(tile, slots) ^ slot)
        listed |= jnp.int32(1) << place
    return [bias_where((listed >> place) & 1 == 1) for place in places]


def own_frame_kernel(plan, table_ref, lists_ref, *rest):
    slots = plan.slots
    here, joined, outs = rest[:slots], rest[slots], rest[slots + 1 :]
    slot = table_ref[plan.slot_at]

    def one_head(index, _):
        head = plan.head_at(1, table_ref, slot, index)
        states = attend_tiles(
            [tile[index, 0] for tile in here],
            [joined[step, index, 0] for step in range(slots)],
            [joined[step, index, 1] for step in range(slots)],
            [
                spatial_biases(plan, table_ref, lists_ref, head, step, range(slots, 2 * slots))
                for step in range(slots)
            ],
        )
        for step, state in enumerate(states):
            for out_ref, value in zip(outs, state):
                out_ref[step, index] = jnp.broadcast_to(value, (TILE, HEAD_DIM))
        return 0

    lax.fori_loop(0, plan.heads_in_group(1, table_ref, slot), one_head, 0)


def halo_kernel(plan, steps, table_ref, lists_ref, *rest):
    slots, ways = plan.slots, len(steps)
    queries, (below, above) = rest[:ways], rest[ways : ways + 2]
    top_ref, total_ref, sum_ref = rest[ways + 2 : ways + 5]
    outs = rest[-ways:]
    slot = table_ref[plan.slot_at]
    places = [*range(slots), *range(2 * slots, 3 * slots)]

    def one_head(index, _):
        head = plan.head_at(1, table_ref, slot, index)
        states = attend_tiles(
            [query_ref[index, 0] for query_ref in queries],
            [ref[step, index, 0] for ref in (below, above) for step in range(slots)],
            [ref[step, index, 1] for ref in (below, above) for step in range(slots)],
            [spatial_biases(plan, table_ref, lists_ref, head, step, places) for step in steps],
            [
                (
                    top_ref[step, index][:, :1],
                    total_ref[step, index][:, :1],
                    sum_ref[step, index],
                )
                for step in steps
            ],
        )
        for out_ref, state in zip(outs, states):
            out_ref[index] = normalized(state)
        return 0

    lax.fori_loop(0, plan.heads_in_group(1, table_ref, slot), one_head, 0)


def unpack_kernel(plan, counts, table_ref, *rest):
    pieces, out_ref, sem = list(rest[:-2]), rest[-2], rest[-1]
    for kind, count in enumerate(counts):
        for step in plan.steps(kind):
            piece = pieces.pop(0)
            group = plan.group(kind, table_ref, step)

            def one(index, _, kind=kind, piece=piece, group=group):
                columns = head_columns(plan.head_at(kind, table_ref, group, index))
                pltpu.make_async_copy(piece.at[index], out_ref.at[:, columns], sem).start()
                return 0

            lax.fori_loop(0, plan.heads_in_group(kind, table_ref, group), one, 0)
            if kind == 0:
                filled = (count - 1) * plan.frames + group < table_ref[plan.mixed_at]
                lax.fori_loop(count - 1, count - 1 + filled.astype(jnp.int32), one, 0)
    wait_all(out_ref, sem)


SPACES = {"s": pltpu.SMEM, "v": pltpu.VMEM, "a": pl.ANY}


def call(kernel, outs, operands, places, out_place, scratch=(), flops=0, in_place=None):
    nbytes = sum(math.prod(o.shape) * 2 for o in outs) * 2
    return pl.pallas_call(
        kernel,
        out_shape=outs,
        in_specs=[pl.BlockSpec(memory_space=SPACES[c]) for c in places],
        out_specs=[pl.BlockSpec(memory_space=SPACES[c]) for c in out_place],
        scratch_shapes=list(scratch),
        input_output_aliases=in_place or {},
        compiler_params=pltpu.CompilerParams(vmem_limit_bytes=VMEM_LIMIT),
        cost_estimate=pl.CostEstimate(flops=flops, bytes_accessed=nbytes, transcendentals=0),
    )(*operands)


def after(arrays, others):
    if not arrays or not others:
        return arrays
    return pl.pallas_call(
        lambda *refs: None,
        out_shape=[jax.ShapeDtypeStruct(a.shape, a.dtype) for a in arrays],
        in_specs=[pl.BlockSpec(memory_space=pltpu.VMEM)] * (len(arrays) + len(others)),
        out_specs=[pl.BlockSpec(memory_space=pltpu.VMEM)] * len(arrays),
        input_output_aliases={i: i for i in range(len(arrays))},
        compiler_params=pltpu.CompilerParams(vmem_limit_bytes=VMEM_LIMIT),
    )(*arrays, *others)


def tiles_of(*lead):
    return jax.ShapeDtypeStruct((*lead, TILE, HEAD_DIM), jnp.bfloat16)


def by_kind(plan, t_count, s_count, queries, keys, values, lists, table):
    frames, slots = plan.frames, plan.slots
    pair_flops = 4 * TILE * TILE * HEAD_DIM

    def to_frame(array, step):
        pairs = [(z, z ^ step) for z in range(frames)]
        return array if step == 0 else lax.ppermute(array, "blk", pairs)

    def to_slot(array, step):
        pairs = [(s, s ^ step) for s in range(slots)]
        return array if step == 0 else lax.ppermute(array, MESH_TAIL, pairs)

    def halo(array, step):
        pairs = [(z, z + step) for z in range(frames) if 0 <= z + step < frames]
        return lax.ppermute(array, "blk", pairs)

    packed = call(
        functools.partial(pack_kernel, plan, (t_count, s_count)),
        [tiles_of(t_count, 3)] * frames + [tiles_of(s_count, 3)] * slots,
        (table, queries, keys, values),
        "saaa",
        "v" * (frames + slots),
        [pltpu.SemaphoreType.DMA((frames + slots,))],
    )
    arrived = [to_frame(block, step) for step, block in zip(plan.steps(0), packed[:frames])]
    here = [to_slot(block, step) for step, block in enumerate(packed[frames:])]
    (joined,) = call(
        functools.partial(join_kernel, plan, s_count),
        [tiles_of(slots, s_count, 2)],
        here,
        "v" * slots,
        "v",
        [pltpu.SemaphoreType.DMA((slots,))],
    )
    below, above = halo(joined, 1), halo(joined, -1)
    own_state = call(
        functools.partial(own_frame_kernel, plan),
        [jax.ShapeDtypeStruct((slots, s_count, TILE, HEAD_DIM), jnp.float32)] * 3,
        (table, lists, *here, joined),
        "ss" + "v" * (slots + 1),
        "vvv",
        flops=s_count * slots * slots * pair_flops,
    )
    (mixed,) = call(
        functools.partial(join_mixed_kernel, plan, t_count),
        [tiles_of(frames, 1, 2)],
        (*arrived, own_state[0]),
        "v" * (frames + 1),
        "v",
        [pltpu.SemaphoreType.DMA((frames,))],
    )
    attended = call(
        functools.partial(temporal_kernel, plan),
        [tiles_of(t_count)] * frames,
        (table, lists, *arrived),
        "ss" + "v" * frames,
        "v" * frames,
        flops=t_count * frames * frames * pair_flops,
    )
    gathered = {0: mixed}
    for bit in sorted((1 << n for n in range(slots.bit_length() - 1)), reverse=True):
        for step in list(gathered):
            block = after([gathered[step]], attended[:1])[0] if step else mixed
            gathered[step | bit] = to_slot(block, bit)
    gathered = [gathered[step] for step in (0, *reversed(range(1, slots)))]
    tiles_ahead = 2 * slots * s_count - 4 * frames - 3 * t_count // 2
    flops_ahead = max(tiles_ahead, 1) * 42 * pair_flops
    attended = call(
        functools.partial(mixed_kernel, plan, t_count),
        [tiles_of(t_count)] * frames,
        (table, lists, *arrived, *gathered, *attended),
        "ss" + "v" * (2 * frames + slots),
        "v" * frames,
        [
            pltpu.VMEM((frames, TILE, HEAD_DIM), jnp.bfloat16),
            pltpu.VMEM((slots * frames, 1, 2, TILE, HEAD_DIM), jnp.bfloat16),
            pltpu.VMEM((frames, TILE, HEAD_DIM), jnp.bfloat16),
            pltpu.SemaphoreType.DMA((frames + slots,)),
        ],
        flops=flops_ahead,
        in_place={2 + frames + slots + i: i for i in range(frames)},
    )
    attended = [attended[0], *after(attended[1:], (below, above))]
    pieces = [to_frame(block, step) for step, block in zip(plan.steps(0), attended)]

    def attend_slots(steps, *earlier):
        return call(
            functools.partial(halo_kernel, plan, steps),
            [tiles_of(s_count)] * len(steps),
            (table, lists, *(here[step] for step in steps), below, above, *own_state, *earlier),
            "ss" + "v" * (len(steps) + 5 + len(earlier)),
            "v" * len(steps),
            flops=s_count * len(steps) * 2 * slots * pair_flops,
        )

    half = slots // 2
    away = attend_slots(range(half, slots))
    near = attend_slots(range(half), away[0])
    attended = [near[0], *after(near[1:], pieces[1:]), *away]
    pieces += [to_slot(block, step) for step, block in enumerate(attended)]
    (out,) = call(
        functools.partial(unpack_kernel, plan, (t_count, s_count)),
        [pltpu.HBM((TILE, plan.heads * HEAD_DIM), jnp.bfloat16)],
        (table, *pieces),
        "s" + "v" * len(pieces),
        "v",
        [pltpu.SemaphoreType.DMA],
    )
    return out


def capacities(heads, frames, slots):
    low, high = heads // 4, heads - heads // 4

    def chunks_for(fewest, most):
        over_frames = max(-(-most // frames), 1)
        shared = max(fewest, (over_frames - 1) * frames)
        left = heads - fewest - (over_frames * frames - shared)
        return over_frames, max(-(-left // slots), 1)

    pairs, begins = [(chunks_for(high + 1, heads)[0], chunks_for(0, low)[1])], []
    for t in range(low + 1, high + 1):
        if t % frames == 1 or t == low + 1:
            begins.append((t, len(pairs)))
            pairs.append(chunks_for(t, min(-(-t // frames) * frames, high)))
    return pairs, begins + [(high + 1, 0)]


def kind_plan(queries, keys, values, block_lists):
    heads, tiles, entries = block_lists.shape
    frames = lax.axis_size("blk")
    slots = lax.axis_size(MESH_TAIL)
    plan = Plan(heads, frames, slots, entries)
    pairs, begins = capacities(heads, frames, slots)
    by_tile = jnp.transpose(block_lists, (1, 2, 0))
    table, branch = call(
        functools.partial(table_kernel, plan, pairs, begins),
        [jax.ShapeDtypeStruct((size,), jnp.int32) for size in (plan.table_size, 1)],
        (by_tile,),
        "v",
        "ss",
        [pltpu.SMEM((heads // 16,), jnp.int32)],
    )
    lists = by_tile.reshape(tiles * entries, heads)
    branches = [functools.partial(by_kind, plan, t, s) for t, s in pairs]
    return lax.switch(branch[0], branches, queries, keys, values, lists, table)


def per_device(queries, keys, values, block_lists):
    slots = lax.axis_size(MESH_TAIL)
    whole_tiles = queries.shape[0] == TILE and slots == FRAME_TILES
    frames = lax.axis_size("blk")
    if whole_tiles and frames & (frames - 1) == 0 and frames * slots == block_lists.shape[1]:
        return kind_plan(queries, keys, values, block_lists)
    return gathered_plan(queries, keys, values, block_lists)


def solution(mesh):
    in_specs = (
        P(("grp", "blk", "head", "sub"), None),
        P(("grp", "blk", "head", "sub"), None),
        P(("grp", "blk", "head", "sub"), None),
        P(),
    )
    out_specs = P(("grp", "blk", "head", "sub"), None)
    return jax.shard_map(
        per_device, mesh=mesh, in_specs=in_specs, out_specs=out_specs, check_vma=False
    )
```

```python
import functools
import math

import jax
import jax.numpy as jnp
from jax import lax
from jax.experimental import pallas as pl
from jax.experimental.pallas import tpu as pltpu
from jax.sharding import PartitionSpec as P

HEADS = 32
HEAD_DIM = 128
TILE = 128
FRAME_TILES = 4


NEG_FLOOR = -1e30


def query_rows(block_lists, first_head, heads_here, query_tokens):
    tile_ids = jnp.arange(block_lists.shape[1], dtype=jnp.int32)
    lists_local = lax.dynamic_slice_in_dim(block_lists, first_head, heads_here, 0)
    tile_mask = jnp.any(lists_local[:, :, :, None] == tile_ids, axis=2).astype(jnp.bfloat16)
    query_onehot = ((query_tokens // TILE)[:, None] == tile_ids[None, :]).astype(jnp.bfloat16)
    listed = jnp.einsum("qi,hij->hqj", query_onehot, tile_mask, preferred_element_type=jnp.float32)
    return listed.astype(jnp.bfloat16)


def attend_block(state_now, key_block, value_block, allowed, query_local, score_scale):
    top_old, total_old, accum_old = state_now
    scores = (
        jnp.einsum("qhd,khd->hqk", query_local, key_block, preferred_element_type=jnp.float32)
        * score_scale
    )
    top_new = jnp.maximum(top_old, jnp.max(jnp.where(allowed, scores, NEG_FLOOR), axis=2))
    factor = jnp.exp(top_old - top_new)
    weights = jnp.where(allowed, jnp.exp(scores - top_new[:, :, None]), 0.0)
    total_new = total_old * factor + jnp.sum(weights, axis=2)
    product = jnp.einsum(
        "hqk,khd->qhd",
        weights.astype(jnp.bfloat16),
        value_block,
        preferred_element_type=jnp.float32,
    )
    accum_new = accum_old * jnp.transpose(factor)[:, :, None] + product
    return (top_new, total_new, accum_new)


def make_step(query_local, listed_rows, key_token, block_len, tile_total):
    score_scale = 1.0 / math.sqrt(HEAD_DIM)
    tile_ids = jnp.arange(tile_total, dtype=jnp.int32)

    def fold_step(state_now, piece, first_row):
        key_piece, value_piece = piece
        block_count = key_piece.shape[0] // block_len

        def one_block(block_index, state_in):
            key_block = lax.dynamic_slice_in_dim(key_piece, block_index * block_len, block_len, 0)
            value_block = lax.dynamic_slice_in_dim(
                value_piece, block_index * block_len, block_len, 0
            )
            positions = block_index * block_len + jnp.arange(block_len, dtype=jnp.int32)
            key_tiles = key_token(positions) // TILE
            key_onehot = (tile_ids[:, None] == key_tiles[None, :]).astype(jnp.bfloat16)
            allowed = (
                jnp.einsum(
                    "hqj,jk->hqk", listed_rows, key_onehot, preferred_element_type=jnp.float32
                )
                > 0.5
            )
            result = attend_block(
                state_in, key_block, value_block, allowed, query_local, score_scale
            )
            return result

        return lax.fori_loop(0, block_count, one_block, state_now)

    return fold_step


def start_state(heads_here, block_len):
    top_all = jnp.full((heads_here, block_len), NEG_FLOOR, jnp.float32)
    total_all = jnp.zeros((heads_here, block_len), jnp.float32)
    accum_all = jnp.zeros((block_len, heads_here, HEAD_DIM), jnp.float32)
    return (top_all, total_all, accum_all)


def normalize(state_end):
    top_all, total_all, accum_all = state_end
    return (accum_all / jnp.transpose(total_all)[:, :, None]).astype(jnp.bfloat16)


def gathered_plan(queries, keys, values, block_lists):
    row_count, col_count = queries.shape
    n_head = lax.axis_size("head")
    n_sub = lax.axis_size("sub")
    blk_index = lax.axis_index("blk")
    head_index = lax.axis_index("head")
    sub_index = lax.axis_index("sub")
    tile_total = block_lists.shape[1]
    heads_here = HEADS // (n_head * n_sub)
    block_len = row_count * n_head * n_sub

    def inward(tensor):
        return tensor.reshape(1, 1, row_count, n_head, n_sub, heads_here * HEAD_DIM)

    query_six, keys_six, values_six = (
        lax.all_to_all(
            lax.all_to_all(inward(queries), "head", split_axis=3, concat_axis=1, tiled=True),
            "sub",
            split_axis=4,
            concat_axis=0,
            tiled=True,
        ),
        lax.all_to_all(
            lax.all_to_all(inward(keys), "head", split_axis=3, concat_axis=1, tiled=True),
            "sub",
            split_axis=4,
            concat_axis=0,
            tiled=True,
        ),
        lax.all_to_all(
            lax.all_to_all(inward(values), "head", split_axis=3, concat_axis=1, tiled=True),
            "sub",
            split_axis=4,
            concat_axis=0,
            tiled=True,
        ),
    )
    query_local = query_six.reshape(block_len, heads_here, HEAD_DIM)
    keys_local = keys_six.reshape(block_len, heads_here, HEAD_DIM)
    values_local = values_six.reshape(block_len, heads_here, HEAD_DIM)

    def key_token(positions):
        source_dev = positions // block_len
        within = positions % block_len
        sub_source = within // (n_head * row_count)
        head_source = within // row_count % n_head
        offset = within % row_count
        return ((source_dev * n_head + head_source) * n_sub + sub_source) * row_count + offset

    query_tokens = key_token(blk_index * block_len + jnp.arange(block_len, dtype=jnp.int32))
    first_head = (head_index * n_sub + sub_index) * heads_here
    listed_rows = query_rows(block_lists, first_head, heads_here, query_tokens)
    fold_step = make_step(query_local, listed_rows, key_token, block_len, tile_total)
    state_end = fold_step(
        start_state(heads_here, block_len),
        (
            lax.all_gather(keys_local, "blk", axis=0, tiled=True),
            lax.all_gather(values_local, "blk", axis=0, tiled=True),
        ),
        jnp.int32(0),
    )
    result_rows = normalize(state_end)
    attended = result_rows.reshape(n_sub, n_head, row_count, 1, 1, heads_here * HEAD_DIM)
    returned = lax.all_to_all(
        lax.all_to_all(attended, "head", split_axis=1, concat_axis=3, tiled=True),
        "sub",
        split_axis=0,
        concat_axis=4,
        tiled=True,
    )
    return returned.reshape(row_count, col_count)


MESH_TAIL = ("head", "sub")
EXP2_SCALE = math.log2(math.e) / math.sqrt(HEAD_DIM)
VMEM_LIMIT = 16 * 1024 * 1024
MIXED_TILES = 2


class Plan:
    def __init__(self, heads, frames, slots, entries):
        self.heads, self.frames, self.slots, self.entries = heads, frames, slots, entries
        self.over_slots_at = heads
        self.pure_at = 2 * heads
        self.mixed_at = 2 * heads + 1
        self.spatial_at = 2 * heads + 2
        self.frame_at = 2 * heads + 3
        self.slot_at = 2 * heads + 4
        self.table_size = 2 * heads + 5

    def sizes(self, kind):
        return (self.frames, self.slots)[kind]

    def head_at(self, kind, table_ref, group, index):
        return table_ref[(0, self.over_slots_at)[kind] + index * self.sizes(kind) + group]

    def group(self, kind, table_ref, step):
        return table_ref[(self.frame_at, self.slot_at)[kind]] ^ step

    def heads_in_group(self, kind, table_ref, group):
        size = self.sizes(kind)
        return (table_ref[(self.pure_at, self.spatial_at)[kind]] - group + size - 1) // size

    def steps(self, kind):
        others = range(1, self.sizes(kind))
        return [0, *others] if kind else [0, *reversed(others)]


def head_columns(head):
    return pl.ds(pl.multiple_of(head * HEAD_DIM, HEAD_DIM), HEAD_DIM)


def table_kernel(plan, pairs, begins, lists_ref, table_ref, branch_ref, mask_ref):
    lists = lists_ref[...]
    tiles = lax.broadcasted_iota(jnp.int32, lists.shape, 0)
    other_slot = ((lists ^ tiles) & (plan.slots - 1)).astype(jnp.float32)
    spatial = jnp.sum(jnp.sum(other_slot, axis=0), axis=0, keepdims=True) > 0
    lanes = lax.broadcasted_iota(jnp.int32, spatial.shape, 1)
    for place in range(plan.heads // 16):
        bit = jnp.where(lanes // 16 == place, jnp.int32(1) << (lanes % 16), 0)
        bits = jnp.where(spatial, bit, 0).astype(jnp.float32)
        mask_ref[place] = jnp.sum(bits).astype(jnp.int32)
    spatial_total = jnp.sum(spatial.astype(jnp.float32)).astype(jnp.int32)
    temporal_total = plan.heads - spatial_total
    branch, chunks, last = 0, pairs[0][0], 0
    for first, place in begins:
        reached = (temporal_total >= first).astype(jnp.int32)
        branch += reached * (place - last)
        chunks += reached * (pairs[place][0] - pairs[last][0])
        last = place
    mixed = (chunks - 1) * plan.frames
    shared = lax.max(temporal_total, mixed)
    room = chunks * plan.frames - shared

    def clear(p, _):
        table_ref[p] = 0
        return 0

    def place_head(h, counts):
        kind = (mask_ref[h // 16] >> (h % 16)) & 1
        t_rank, s_rank = counts
        s_place = jnp.where(s_rank < room, shared + s_rank, plan.over_slots_at + s_rank - room)
        table_ref[jnp.where(kind == 1, s_place, t_rank)] = h
        return t_rank + 1 - kind, s_rank + kind

    lax.fori_loop(0, 2 * plan.heads, clear, 0)
    lax.fori_loop(0, plan.heads, place_head, (jnp.int32(0), jnp.int32(0)))
    table_ref[plan.pure_at] = lax.min(temporal_total, mixed)
    table_ref[plan.mixed_at] = shared + lax.min(spatial_total, room)
    table_ref[plan.spatial_at] = lax.max(spatial_total - room, 0)
    table_ref[plan.frame_at] = lax.axis_index("blk")
    n_sub = lax.axis_size("sub")
    table_ref[plan.slot_at] = lax.axis_index("head") * n_sub + lax.axis_index("sub")
    branch_ref[0] = branch


def wait_all(ref, sem):
    pltpu.make_async_copy(ref, ref, sem).wait()


def pack_kernel(plan, counts, table_ref, q_ref, k_ref, v_ref, *rest):
    outs, sems = rest[:-1], rest[-1]
    steps = [(kind, step) for kind in range(2) for step in plan.steps(kind)]
    for sem, (kind, step) in enumerate(steps):
        group = plan.group(kind, table_ref, step)

        def one(index, _, kind=kind, group=group, sem=sem):
            columns = head_columns(plan.head_at(kind, table_ref, group, index))
            for place, ref in enumerate((q_ref, k_ref, v_ref)):
                pltpu.make_async_copy(
                    ref.at[:, columns], outs[sem].at[index, place], sems.at[sem]
                ).start()
            return 0

        lax.fori_loop(0, counts[kind], one, 0)
    for sem, out_ref in enumerate(outs):
        wait_all(out_ref, sems.at[sem])


def turn_keys(kv_ref, place, count):
    def turn(work, _):
        step, index = work // count, lax.rem(work, count)
        kv_ref[step, index, place] = kv_ref[step, index, place].T
        return 0

    lax.fori_loop(0, kv_ref.shape[0] * count, turn, 0)


def join_kernel(plan, count, *refs):
    pieces, out_ref, sems = refs[: plan.slots], refs[-2], refs[-1]
    copy_pieces(
        [(piece.at[:, pl.ds(1, 2)], out_ref.at[step]) for step, piece in enumerate(pieces)], sems
    )
    turn_keys(out_ref, 0, count)


def join_mixed_kernel(plan, count, *refs):
    pieces, out_ref, sems = refs[: plan.frames], refs[-2], refs[-1]
    copy_pieces(
        [
            (piece.at[count - 1, pl.ds(1, 2)], out_ref.at[step, 0])
            for step, piece in zip(plan.steps(0), pieces)
        ],
        sems,
    )
    turn_keys(out_ref, 0, 1)


def attend_tiles(queries, keys, values, biases, before=None, turned=True):
    scores = lax.dot_general(
        jnp.concatenate(queries, 0),
        jnp.concatenate(keys, 1 if turned else 0),
        (((1,), (0 if turned else 1,)), ((), ())),
        preferred_element_type=jnp.float32,
    )
    rows, tops, totals = [], [], []
    for a, bias in enumerate(biases):
        tiles = [
            scores[a * TILE : (a + 1) * TILE, b * TILE : (b + 1) * TILE] + bias[b]
            for b in range(len(keys))
        ]
        top = jnp.max(functools.reduce(jnp.maximum, tiles), axis=1, keepdims=True)
        if before is not None:
            top = jnp.maximum(top, before[a][0])
        weights = [jnp.exp2((tile - top) * EXP2_SCALE) for tile in tiles]
        tops.append(top)
        totals.append(jnp.sum(functools.reduce(jnp.add, weights), axis=1, keepdims=True))
        rows.append(jnp.concatenate([w.astype(jnp.bfloat16) for w in weights], 1))
    accum = jnp.dot(
        jnp.concatenate(rows, 0), jnp.concatenate(values, 0), preferred_element_type=jnp.float32
    )
    states = []
    for a, (top, total) in enumerate(zip(tops, totals)):
        part = accum[a * TILE : (a + 1) * TILE]
        if before is not None:
            factor = jnp.exp2((before[a][0] - top) * EXP2_SCALE)
            total, part = total + before[a][1] * factor, part + before[a][2] * factor
        states.append((top, total, part))
    return states


def normalized(state):
    return (state[2] / state[1]).astype(jnp.bfloat16)


def bias_where(attended):
    return jnp.where(attended, jnp.float32(0), jnp.float32(NEG_FLOOR))


def copy_pieces(pieces, sems):
    copies = [pltpu.make_async_copy(a, b, sems.at[i]) for i, (a, b) in enumerate(pieces)]
    for copy in copies:
        copy.start()
    for copy in copies:
        copy.wait()


def listed_places(plan, lists_ref, head, query_tile, place_of):
    first = query_tile * plan.entries
    listed = jnp.int32(0)
    places, biases = [], []
    for entry in range(plan.entries):
        place = place_of(lists_ref[first + entry, head])
        places.append(place)
        biases.append(bias_where((listed >> place) & 1 == 0))
        listed |= jnp.int32(1) << place
    return places, biases


def temporal_kernel(plan, table_ref, lists_ref, *rest):
    frames, slots = plan.frames, plan.slots
    by_step = [plan.steps(0).index(step) for step in range(frames)]
    tiles = [rest[i] for i in by_step]
    outs = [rest[frames + i] for i in by_step]
    frame, slot = table_ref[plan.frame_at], table_ref[plan.slot_at]

    def one_head(index, _):
        head = plan.head_at(0, table_ref, frame, index)
        biases = []
        for step in range(frames):
            first = ((frame ^ step) * slots + slot) * plan.entries
            listed = jnp.int32(0)
            for entry in range(plan.entries):
                listed |= jnp.int32(1) << (lists_ref[first + entry, head] // slots)
            biases.append(
                [bias_where((listed >> (frame ^ other)) & 1 == 1) for other in range(frames)]
            )
        states = attend_tiles(
            *([tile[index, i] for tile in tiles] for i in range(3)), biases, turned=False
        )
        for out_ref, state in zip(outs, states):
            out_ref[index] = normalized(state)
        return 0

    lax.fori_loop(0, plan.heads_in_group(0, table_ref, frame), one_head, 0)


def mixed_kernel(plan, count, table_ref, lists_ref, *rest):
    frames, slots = plan.frames, plan.slots
    tiles, gathered = rest[:frames], rest[frames : frames + slots]
    outs = rest[-4 - frames : -4]
    q_ref, kv_ref, result_ref, sems = rest[-4:]
    copy_pieces(
        [(tile.at[count - 1, 0], q_ref.at[step]) for step, tile in zip(plan.steps(0), tiles)]
        + [
            (block, kv_ref.at[pl.ds(step * frames, frames)])
            for step, block in zip((0, *reversed(range(1, slots))), gathered)
        ],
        sems,
    )
    frame, slot = table_ref[plan.frame_at], table_ref[plan.slot_at]
    head = plan.head_at(0, table_ref, frame, count - 1)

    def some_tiles(body, _):
        for step in (body * MIXED_TILES + more for more in range(MIXED_TILES)):
            places, biases = listed_places(
                plan,
                lists_ref,
                head,
                (frame ^ step) * slots + slot,
                lambda tile: (lax.rem(tile, slots) ^ slot) * frames + (tile // slots ^ frame),
            )
            (state,) = attend_tiles(
                [q_ref[step]],
                [kv_ref[place, 0, 0] for place in places],
                [kv_ref[place, 0, 1] for place in places],
                [biases],
            )
            result_ref[step] = normalized(state)
        return 0

    lax.fori_loop(0, frames // MIXED_TILES, some_tiles, 0)
    copy_pieces(
        [(result_ref.at[step], out.at[count - 1]) for step, out in zip(plan.steps(0), outs)], sems
    )


def spatial_biases(plan, table_ref, lists_ref, head, step, places):
    slots = plan.slots
    frame, slot = table_ref[plan.frame_at], table_ref[plan.slot_at]
    first = (frame * slots + (slot ^ step)) * plan.entries
    listed = jnp.int32(0)
    for entry in range(plan.entries):
        tile = lists_ref[first + entry, head]
        place = (tile // slots - frame + 1) * slots + (lax.rem(tile, slots) ^ slot)
        listed |= jnp.int32(1) << place
    return [bias_where((listed >> place) & 1 == 1) for place in places]


def own_frame_kernel(plan, table_ref, lists_ref, *rest):
    slots = plan.slots
    here, joined, outs = rest[:slots], rest[slots], rest[slots + 1 :]
    slot = table_ref[plan.slot_at]

    def one_head(index, _):
        head = plan.head_at(1, table_ref, slot, index)
        states = attend_tiles(
            [tile[index, 0] for tile in here],
            [joined[step, index, 0] for step in range(slots)],
            [joined[step, index, 1] for step in range(slots)],
            [
                spatial_biases(plan, table_ref, lists_ref, head, step, range(slots, 2 * slots))
                for step in range(slots)
            ],
        )
        for step, state in enumerate(states):
            for out_ref, value in zip(outs, state):
                out_ref[step, index] = jnp.broadcast_to(value, (TILE, HEAD_DIM))
        return 0

    lax.fori_loop(0, plan.heads_in_group(1, table_ref, slot), one_head, 0)


def halo_kernel(plan, steps, table_ref, lists_ref, *rest):
    slots, ways = plan.slots, len(steps)
    queries, (below, above) = rest[:ways], rest[ways : ways + 2]
    top_ref, total_ref, sum_ref = rest[ways + 2 : ways + 5]
    outs = rest[-ways:]
    slot = table_ref[plan.slot_at]
    places = [*range(slots), *range(2 * slots, 3 * slots)]

    def one_head(index, _):
        head = plan.head_at(1, table_ref, slot, index)
        states = attend_tiles(
            [query_ref[index, 0] for query_ref in queries],
            [ref[step, index, 0] for ref in (below, above) for step in range(slots)],
            [ref[step, index, 1] for ref in (below, above) for step in range(slots)],
            [spatial_biases(plan, table_ref, lists_ref, head, step, places) for step in steps],
            [
                (
                    top_ref[step, index][:, :1],
                    total_ref[step, index][:, :1],
                    sum_ref[step, index],
                )
                for step in steps
            ],
        )
        for out_ref, state in zip(outs, states):
            out_ref[index] = normalized(state)
        return 0

    lax.fori_loop(0, plan.heads_in_group(1, table_ref, slot), one_head, 0)


def unpack_kernel(plan, counts, table_ref, *rest):
    pieces, out_ref, sem = list(rest[:-2]), rest[-2], rest[-1]
    for kind, count in enumerate(counts):
        for step in plan.steps(kind):
            piece = pieces.pop(0)
            group = plan.group(kind, table_ref, step)

            def one(index, _, kind=kind, piece=piece, group=group):
                columns = head_columns(plan.head_at(kind, table_ref, group, index))
                pltpu.make_async_copy(piece.at[index], out_ref.at[:, columns], sem).start()
                return 0

            lax.fori_loop(0, plan.heads_in_group(kind, table_ref, group), one, 0)
            if kind == 0:
                filled = (count - 1) * plan.frames + group < table_ref[plan.mixed_at]
                lax.fori_loop(count - 1, count - 1 + filled.astype(jnp.int32), one, 0)
    wait_all(out_ref, sem)


SPACES = {"s": pltpu.SMEM, "v": pltpu.VMEM, "a": pl.ANY}


def call(kernel, outs, operands, places, out_place, scratch=(), flops=0, in_place=None):
    nbytes = sum(math.prod(o.shape) * 2 for o in outs) * 2
    return pl.pallas_call(
        kernel,
        out_shape=outs,
        in_specs=[pl.BlockSpec(memory_space=SPACES[c]) for c in places],
        out_specs=[pl.BlockSpec(memory_space=SPACES[c]) for c in out_place],
        scratch_shapes=list(scratch),
        input_output_aliases=in_place or {},
        compiler_params=pltpu.CompilerParams(vmem_limit_bytes=VMEM_LIMIT),
        cost_estimate=pl.CostEstimate(flops=flops, bytes_accessed=nbytes, transcendentals=0),
    )(*operands)


def after(arrays, others):
    if not arrays or not others:
        return arrays
    return pl.pallas_call(
        lambda *refs: None,
        out_shape=[jax.ShapeDtypeStruct(a.shape, a.dtype) for a in arrays],
        in_specs=[pl.BlockSpec(memory_space=pltpu.VMEM)] * (len(arrays) + len(others)),
        out_specs=[pl.BlockSpec(memory_space=pltpu.VMEM)] * len(arrays),
        input_output_aliases={i: i for i in range(len(arrays))},
        compiler_params=pltpu.CompilerParams(vmem_limit_bytes=VMEM_LIMIT),
    )(*arrays, *others)


def tiles_of(*lead):
    return jax.ShapeDtypeStruct((*lead, TILE, HEAD_DIM), jnp.bfloat16)


def by_kind(plan, t_count, s_count, queries, keys, values, lists, table):
    frames, slots = plan.frames, plan.slots
    pair_flops = 4 * TILE * TILE * HEAD_DIM

    def to_frame(array, step):
        pairs = [(z, z ^ step) for z in range(frames)]
        return array if step == 0 else lax.ppermute(array, "blk", pairs)

    def to_slot(array, step):
        pairs = [(s, s ^ step) for s in range(slots)]
        return array if step == 0 else lax.ppermute(array, MESH_TAIL, pairs)

    def halo(array, step):
        pairs = [(z, z + step) for z in range(frames) if 0 <= z + step < frames]
        return lax.ppermute(array, "blk", pairs)

    packed = call(
        functools.partial(pack_kernel, plan, (t_count, s_count)),
        [tiles_of(t_count, 3)] * frames + [tiles_of(s_count, 3)] * slots,
        (table, queries, keys, values),
        "saaa",
        "v" * (frames + slots),
        [pltpu.SemaphoreType.DMA((frames + slots,))],
    )
    arrived = [to_frame(block, step) for step, block in zip(plan.steps(0), packed[:frames])]
    here = [to_slot(block, step) for step, block in enumerate(packed[frames:])]
    (joined,) = call(
        functools.partial(join_kernel, plan, s_count),
        [tiles_of(slots, s_count, 2)],
        here,
        "v" * slots,
        "v",
        [pltpu.SemaphoreType.DMA((slots,))],
    )
    below, above = halo(joined, 1), halo(joined, -1)
    own_state = call(
        functools.partial(own_frame_kernel, plan),
        [jax.ShapeDtypeStruct((slots, s_count, TILE, HEAD_DIM), jnp.float32)] * 3,
        (table, lists, *here, joined),
        "ss" + "v" * (slots + 1),
        "vvv",
        flops=s_count * slots * slots * pair_flops,
    )
    (mixed,) = call(
        functools.partial(join_mixed_kernel, plan, t_count),
        [tiles_of(frames, 1, 2)],
        (*arrived, own_state[0]),
        "v" * (frames + 1),
        "v",
        [pltpu.SemaphoreType.DMA((frames,))],
    )
    attended = call(
        functools.partial(temporal_kernel, plan),
        [tiles_of(t_count)] * frames,
        (table, lists, *arrived),
        "ss" + "v" * frames,
        "v" * frames,
        flops=t_count * frames * frames * pair_flops,
    )
    gathered = {0: mixed}
    for bit in sorted((1 << n for n in range(slots.bit_length() - 1)), reverse=True):
        for step in list(gathered):
            block = after([gathered[step]], attended[:1])[0] if step else mixed
            gathered[step | bit] = to_slot(block, bit)
    gathered = [gathered[step] for step in (0, *reversed(range(1, slots)))]
    tiles_ahead = 2 * slots * s_count - 4 * frames - 3 * t_count // 2
    flops_ahead = max(tiles_ahead, 1) * 42 * pair_flops
    attended = call(
        functools.partial(mixed_kernel, plan, t_count),
        [tiles_of(t_count)] * frames,
        (table, lists, *arrived, *gathered, *attended),
        "ss" + "v" * (2 * frames + slots),
        "v" * frames,
        [
            pltpu.VMEM((frames, TILE, HEAD_DIM), jnp.bfloat16),
            pltpu.VMEM((slots * frames, 1, 2, TILE, HEAD_DIM), jnp.bfloat16),
            pltpu.VMEM((frames, TILE, HEAD_DIM), jnp.bfloat16),
            pltpu.SemaphoreType.DMA((frames + slots,)),
        ],
        flops=flops_ahead,
        in_place={2 + frames + slots + i: i for i in range(frames)},
    )
    attended = [attended[0], *after(attended[1:-1], (below, above)), attended[-1]]
    pieces = [to_frame(block, step) for step, block in zip(plan.steps(0), attended)]

    def attend_slots(steps, *earlier):
        return call(
            functools.partial(halo_kernel, plan, steps),
            [tiles_of(s_count)] * len(steps),
            (table, lists, *(here[step] for step in steps), below, above, *own_state, *earlier),
            "ss" + "v" * (len(steps) + 5 + len(earlier)),
            "v" * len(steps),
            flops=s_count * len(steps) * 2 * slots * pair_flops,
        )

    half = slots // 2
    away = attend_slots(range(half, slots))
    near = attend_slots(range(half), away[0])
    attended = [near[0], *after(near[1:], pieces[1:]), *away]
    pieces += [to_slot(block, step) for step, block in enumerate(attended)]
    (out,) = call(
        functools.partial(unpack_kernel, plan, (t_count, s_count)),
        [pltpu.HBM((TILE, plan.heads * HEAD_DIM), jnp.bfloat16)],
        (table, *pieces),
        "s" + "v" * len(pieces),
        "v",
        [pltpu.SemaphoreType.DMA],
    )
    return out


def capacities(heads, frames, slots):
    low, high = heads // 4, heads - heads // 4

    def chunks_for(fewest, most):
        over_frames = max(-(-most // frames), 1)
        shared = max(fewest, (over_frames - 1) * frames)
        left = heads - fewest - (over_frames * frames - shared)
        return over_frames, max(-(-left // slots), 1)

    pairs, begins = [(chunks_for(high + 1, heads)[0], chunks_for(0, low)[1])], []
    for t in range(low + 1, high + 1):
        if t % frames == 1 or t == low + 1:
            begins.append((t, len(pairs)))
            pairs.append(chunks_for(t, min(-(-t // frames) * frames, high)))
    return pairs, begins + [(high + 1, 0)]


def kind_plan(queries, keys, values, block_lists):
    heads, tiles, entries = block_lists.shape
    frames = lax.axis_size("blk")
    slots = lax.axis_size(MESH_TAIL)
    plan = Plan(heads, frames, slots, entries)
    pairs, begins = capacities(heads, frames, slots)
    by_tile = jnp.transpose(block_lists, (1, 2, 0))
    table, branch = call(
        functools.partial(table_kernel, plan, pairs, begins),
        [jax.ShapeDtypeStruct((size,), jnp.int32) for size in (plan.table_size, 1)],
        (by_tile,),
        "v",
        "ss",
        [pltpu.SMEM((heads // 16,), jnp.int32)],
    )
    lists = by_tile.reshape(tiles * entries, heads)
    branches = [functools.partial(by_kind, plan, t, s) for t, s in pairs]
    return lax.switch(branch[0], branches, queries, keys, values, lists, table)


def per_device(queries, keys, values, block_lists):
    slots = lax.axis_size(MESH_TAIL)
    whole_tiles = queries.shape[0] == TILE and slots == FRAME_TILES
    frames = lax.axis_size("blk")
    if whole_tiles and frames & (frames - 1) == 0 and frames * slots == block_lists.shape[1]:
        return kind_plan(queries, keys, values, block_lists)
    return gathered_plan(queries, keys, values, block_lists)


def solution(mesh):
    in_specs = (
        P(("grp", "blk", "head", "sub"), None),
        P(("grp", "blk", "head", "sub"), None),
        P(("grp", "blk", "head", "sub"), None),
        P(),
    )
    out_specs = P(("grp", "blk", "head", "sub"), None)
    return jax.shard_map(
        per_device, mesh=mesh, in_specs=in_specs, out_specs=out_specs, check_vma=False
    )
```

```python
import functools
import math

import jax
import jax.numpy as jnp
from jax import lax
from jax.experimental import pallas as pl
from jax.experimental.pallas import tpu as pltpu
from jax.sharding import PartitionSpec as P

HEADS = 32
HEAD_DIM = 128
TILE = 128
FRAME_TILES = 4


NEG_FLOOR = -1e30


def query_rows(block_lists, first_head, heads_here, query_tokens):
    tile_ids = jnp.arange(block_lists.shape[1], dtype=jnp.int32)
    lists_local = lax.dynamic_slice_in_dim(block_lists, first_head, heads_here, 0)
    tile_mask = jnp.any(lists_local[:, :, :, None] == tile_ids, axis=2).astype(jnp.bfloat16)
    query_onehot = ((query_tokens // TILE)[:, None] == tile_ids[None, :]).astype(jnp.bfloat16)
    listed = jnp.einsum("qi,hij->hqj", query_onehot, tile_mask, preferred_element_type=jnp.float32)
    return listed.astype(jnp.bfloat16)


def attend_block(state_now, key_block, value_block, allowed, query_local, score_scale):
    top_old, total_old, accum_old = state_now
    scores = (
        jnp.einsum("qhd,khd->hqk", query_local, key_block, preferred_element_type=jnp.float32)
        * score_scale
    )
    top_new = jnp.maximum(top_old, jnp.max(jnp.where(allowed, scores, NEG_FLOOR), axis=2))
    factor = jnp.exp(top_old - top_new)
    weights = jnp.where(allowed, jnp.exp(scores - top_new[:, :, None]), 0.0)
    total_new = total_old * factor + jnp.sum(weights, axis=2)
    product = jnp.einsum(
        "hqk,khd->qhd",
        weights.astype(jnp.bfloat16),
        value_block,
        preferred_element_type=jnp.float32,
    )
    accum_new = accum_old * jnp.transpose(factor)[:, :, None] + product
    return (top_new, total_new, accum_new)


def make_step(query_local, listed_rows, key_token, block_len, tile_total):
    score_scale = 1.0 / math.sqrt(HEAD_DIM)
    tile_ids = jnp.arange(tile_total, dtype=jnp.int32)

    def fold_step(state_now, piece, first_row):
        key_piece, value_piece = piece
        block_count = key_piece.shape[0] // block_len

        def one_block(block_index, state_in):
            key_block = lax.dynamic_slice_in_dim(key_piece, block_index * block_len, block_len, 0)
            value_block = lax.dynamic_slice_in_dim(
                value_piece, block_index * block_len, block_len, 0
            )
            positions = block_index * block_len + jnp.arange(block_len, dtype=jnp.int32)
            key_tiles = key_token(positions) // TILE
            key_onehot = (tile_ids[:, None] == key_tiles[None, :]).astype(jnp.bfloat16)
            allowed = (
                jnp.einsum(
                    "hqj,jk->hqk", listed_rows, key_onehot, preferred_element_type=jnp.float32
                )
                > 0.5
            )
            result = attend_block(
                state_in, key_block, value_block, allowed, query_local, score_scale
            )
            return result

        return lax.fori_loop(0, block_count, one_block, state_now)

    return fold_step


def start_state(heads_here, block_len):
    top_all = jnp.full((heads_here, block_len), NEG_FLOOR, jnp.float32)
    total_all = jnp.zeros((heads_here, block_len), jnp.float32)
    accum_all = jnp.zeros((block_len, heads_here, HEAD_DIM), jnp.float32)
    return (top_all, total_all, accum_all)


def normalize(state_end):
    top_all, total_all, accum_all = state_end
    return (accum_all / jnp.transpose(total_all)[:, :, None]).astype(jnp.bfloat16)


def gathered_plan(queries, keys, values, block_lists):
    row_count, col_count = queries.shape
    n_head = lax.axis_size("head")
    n_sub = lax.axis_size("sub")
    blk_index = lax.axis_index("blk")
    head_index = lax.axis_index("head")
    sub_index = lax.axis_index("sub")
    tile_total = block_lists.shape[1]
    heads_here = HEADS // (n_head * n_sub)
    block_len = row_count * n_head * n_sub

    def inward(tensor):
        return tensor.reshape(1, 1, row_count, n_head, n_sub, heads_here * HEAD_DIM)

    query_six, keys_six, values_six = (
        lax.all_to_all(
            lax.all_to_all(inward(queries), "head", split_axis=3, concat_axis=1, tiled=True),
            "sub",
            split_axis=4,
            concat_axis=0,
            tiled=True,
        ),
        lax.all_to_all(
            lax.all_to_all(inward(keys), "head", split_axis=3, concat_axis=1, tiled=True),
            "sub",
            split_axis=4,
            concat_axis=0,
            tiled=True,
        ),
        lax.all_to_all(
            lax.all_to_all(inward(values), "head", split_axis=3, concat_axis=1, tiled=True),
            "sub",
            split_axis=4,
            concat_axis=0,
            tiled=True,
        ),
    )
    query_local = query_six.reshape(block_len, heads_here, HEAD_DIM)
    keys_local = keys_six.reshape(block_len, heads_here, HEAD_DIM)
    values_local = values_six.reshape(block_len, heads_here, HEAD_DIM)

    def key_token(positions):
        source_dev = positions // block_len
        within = positions % block_len
        sub_source = within // (n_head * row_count)
        head_source = within // row_count % n_head
        offset = within % row_count
        return ((source_dev * n_head + head_source) * n_sub + sub_source) * row_count + offset

    query_tokens = key_token(blk_index * block_len + jnp.arange(block_len, dtype=jnp.int32))
    first_head = (head_index * n_sub + sub_index) * heads_here
    listed_rows = query_rows(block_lists, first_head, heads_here, query_tokens)
    fold_step = make_step(query_local, listed_rows, key_token, block_len, tile_total)
    state_end = fold_step(
        start_state(heads_here, block_len),
        (
            lax.all_gather(keys_local, "blk", axis=0, tiled=True),
            lax.all_gather(values_local, "blk", axis=0, tiled=True),
        ),
        jnp.int32(0),
    )
    result_rows = normalize(state_end)
    attended = result_rows.reshape(n_sub, n_head, row_count, 1, 1, heads_here * HEAD_DIM)
    returned = lax.all_to_all(
        lax.all_to_all(attended, "head", split_axis=1, concat_axis=3, tiled=True),
        "sub",
        split_axis=0,
        concat_axis=4,
        tiled=True,
    )
    return returned.reshape(row_count, col_count)


MESH_TAIL = ("head", "sub")
EXP2_SCALE = math.log2(math.e) / math.sqrt(HEAD_DIM)
VMEM_LIMIT = 16 * 1024 * 1024
MIXED_TILES = 2


class Plan:
    def __init__(self, heads, frames, slots, entries):
        self.heads, self.frames, self.slots, self.entries = heads, frames, slots, entries
        self.over_slots_at = heads
        self.pure_at = 2 * heads
        self.mixed_at = 2 * heads + 1
        self.spatial_at = 2 * heads + 2
        self.frame_at = 2 * heads + 3
        self.slot_at = 2 * heads + 4
        self.table_size = 2 * heads + 5

    def sizes(self, kind):
        return (self.frames, self.slots)[kind]

    def head_at(self, kind, table_ref, group, index):
        return table_ref[(0, self.over_slots_at)[kind] + index * self.sizes(kind) + group]

    def group(self, kind, table_ref, step):
        return table_ref[(self.frame_at, self.slot_at)[kind]] ^ step

    def heads_in_group(self, kind, table_ref, group):
        size = self.sizes(kind)
        return (table_ref[(self.pure_at, self.spatial_at)[kind]] - group + size - 1) // size

    def steps(self, kind):
        others = range(1, self.sizes(kind))
        return [0, *others] if kind else [0, *reversed(others)]


def head_columns(head):
    return pl.ds(pl.multiple_of(head * HEAD_DIM, HEAD_DIM), HEAD_DIM)


def table_kernel(plan, pairs, begins, lists_ref, *rest):
    table_ref, branch_ref, mask_ref, sems = rest[3], rest[4], rest[-2], rest[-1]
    copies = [pltpu.make_async_copy(rest[i], rest[5 + i], sems.at[i]) for i in range(3)]
    for copy in copies:
        copy.start()
    lists = lists_ref[...]
    tiles = lax.broadcasted_iota(jnp.int32, lists.shape, 0)
    other_slot = ((lists ^ tiles) & (plan.slots - 1)).astype(jnp.float32)
    spatial = jnp.sum(jnp.sum(other_slot, axis=0), axis=0, keepdims=True) > 0
    lanes = lax.broadcasted_iota(jnp.int32, spatial.shape, 1)
    for place in range(plan.heads // 16):
        bit = jnp.where(lanes // 16 == place, jnp.int32(1) << (lanes % 16), 0)
        bits = jnp.where(spatial, bit, 0).astype(jnp.float32)
        mask_ref[place] = jnp.sum(bits).astype(jnp.int32)
    spatial_total = jnp.sum(spatial.astype(jnp.float32)).astype(jnp.int32)
    temporal_total = plan.heads - spatial_total
    branch, chunks, last = 0, pairs[0][0], 0
    for first, place in begins:
        reached = (temporal_total >= first).astype(jnp.int32)
        branch += reached * (place - last)
        chunks += reached * (pairs[place][0] - pairs[last][0])
        last = place
    mixed = (chunks - 1) * plan.frames
    shared = lax.max(temporal_total, mixed)
    room = chunks * plan.frames - shared

    def clear(p, _):
        table_ref[p] = 0
        return 0

    def place_head(h, counts):
        kind = (mask_ref[h // 16] >> (h % 16)) & 1
        t_rank, s_rank = counts
        s_place = jnp.where(s_rank < room, shared + s_rank, plan.over_slots_at + s_rank - room)
        table_ref[jnp.where(kind == 1, s_place, t_rank)] = h
        return t_rank + 1 - kind, s_rank + kind

    lax.fori_loop(0, 2 * plan.heads, clear, 0)
    lax.fori_loop(0, plan.heads, place_head, (jnp.int32(0), jnp.int32(0)))
    table_ref[plan.pure_at] = lax.min(temporal_total, mixed)
    table_ref[plan.mixed_at] = shared + lax.min(spatial_total, room)
    table_ref[plan.spatial_at] = lax.max(spatial_total - room, 0)
    table_ref[plan.frame_at] = lax.axis_index("blk")
    n_sub = lax.axis_size("sub")
    table_ref[plan.slot_at] = lax.axis_index("head") * n_sub + lax.axis_index("sub")
    branch_ref[0] = branch
    for copy in copies:
        copy.wait()


def wait_all(ref, sem):
    pltpu.make_async_copy(ref, ref, sem).wait()


def pack_kernel(plan, counts, table_ref, q_ref, k_ref, v_ref, *rest):
    outs, sems = rest[:-1], rest[-1]
    steps = [(kind, step) for kind in range(2) for step in plan.steps(kind)]
    for sem, (kind, step) in enumerate(steps):
        group = plan.group(kind, table_ref, step)

        def one(index, _, kind=kind, group=group, sem=sem):
            columns = head_columns(plan.head_at(kind, table_ref, group, index))
            for place, ref in enumerate((q_ref, k_ref, v_ref)):
                pltpu.make_async_copy(
                    ref.at[:, columns], outs[sem].at[index, place], sems.at[sem]
                ).start()
            return 0

        lax.fori_loop(0, counts[kind], one, 0)
    for sem, out_ref in enumerate(outs):
        wait_all(out_ref, sems.at[sem])


def turn_keys(kv_ref, place, count):
    def turn(work, _):
        step, index = work // count, lax.rem(work, count)
        kv_ref[step, index, place] = kv_ref[step, index, place].T
        return 0

    lax.fori_loop(0, kv_ref.shape[0] * count, turn, 0)


def join_kernel(plan, count, *refs):
    pieces, out_ref, sems = refs[: plan.slots], refs[-2], refs[-1]
    copy_pieces(
        [(piece.at[:, pl.ds(1, 2)], out_ref.at[step]) for step, piece in enumerate(pieces)], sems
    )
    turn_keys(out_ref, 0, count)


def join_mixed_kernel(plan, count, *refs):
    pieces, out_ref, sems = refs[: plan.frames], refs[-2], refs[-1]
    copy_pieces(
        [
            (piece.at[count - 1, pl.ds(1, 2)], out_ref.at[step, 0])
            for step, piece in zip(plan.steps(0), pieces)
        ],
        sems,
    )
    turn_keys(out_ref, 0, 1)


def attend_tiles(queries, keys, values, biases, before=None, turned=True):
    scores = lax.dot_general(
        jnp.concatenate(queries, 0),
        jnp.concatenate(keys, 1 if turned else 0),
        (((1,), (0 if turned else 1,)), ((), ())),
        preferred_element_type=jnp.float32,
    )
    rows, tops, totals = [], [], []
    for a, bias in enumerate(biases):
        tiles = [
            scores[a * TILE : (a + 1) * TILE, b * TILE : (b + 1) * TILE] + bias[b]
            for b in range(len(keys))
        ]
        top = jnp.max(functools.reduce(jnp.maximum, tiles), axis=1, keepdims=True)
        if before is not None:
            top = jnp.maximum(top, before[a][0])
        weights = [jnp.exp2((tile - top) * EXP2_SCALE) for tile in tiles]
        tops.append(top)
        totals.append(jnp.sum(functools.reduce(jnp.add, weights), axis=1, keepdims=True))
        rows.append(jnp.concatenate([w.astype(jnp.bfloat16) for w in weights], 1))
    accum = jnp.dot(
        jnp.concatenate(rows, 0), jnp.concatenate(values, 0), preferred_element_type=jnp.float32
    )
    states = []
    for a, (top, total) in enumerate(zip(tops, totals)):
        part = accum[a * TILE : (a + 1) * TILE]
        if before is not None:
            factor = jnp.exp2((before[a][0] - top) * EXP2_SCALE)
            total, part = total + before[a][1] * factor, part + before[a][2] * factor
        states.append((top, total, part))
    return states


def normalized(state):
    return (state[2] / state[1]).astype(jnp.bfloat16)


def bias_where(attended):
    return jnp.where(attended, jnp.float32(0), jnp.float32(NEG_FLOOR))


def copy_pieces(pieces, sems):
    copies = [pltpu.make_async_copy(a, b, sems.at[i]) for i, (a, b) in enumerate(pieces)]
    for copy in copies:
        copy.start()
    for copy in copies:
        copy.wait()


def listed_places(plan, lists_ref, head, query_tile, place_of):
    first = query_tile * plan.entries
    listed = jnp.int32(0)
    places, biases = [], []
    for entry in range(plan.entries):
        place = place_of(lists_ref[first + entry, head])
        places.append(place)
        biases.append(bias_where((listed >> place) & 1 == 0))
        listed |= jnp.int32(1) << place
    return places, biases


def temporal_kernel(plan, table_ref, lists_ref, *rest):
    frames, slots = plan.frames, plan.slots
    by_step = [plan.steps(0).index(step) for step in range(frames)]
    tiles = [rest[i] for i in by_step]
    outs = [rest[frames + i] for i in by_step]
    frame, slot = table_ref[plan.frame_at], table_ref[plan.slot_at]

    def one_head(index, _):
        head = plan.head_at(0, table_ref, frame, index)
        biases = []
        for step in range(frames):
            first = ((frame ^ step) * slots + slot) * plan.entries
            listed = jnp.int32(0)
            for entry in range(plan.entries):
                listed |= jnp.int32(1) << (lists_ref[first + entry, head] // slots)
            biases.append(
                [bias_where((listed >> (frame ^ other)) & 1 == 1) for other in range(frames)]
            )
        states = attend_tiles(
            *([tile[index, i] for tile in tiles] for i in range(3)), biases, turned=False
        )
        for out_ref, state in zip(outs, states):
            out_ref[index] = normalized(state)
        return 0

    lax.fori_loop(0, plan.heads_in_group(0, table_ref, frame), one_head, 0)


def mixed_kernel(plan, count, table_ref, lists_ref, *rest):
    frames, slots = plan.frames, plan.slots
    tiles, gathered = rest[:frames], rest[frames : frames + slots]
    outs = rest[-4 - frames : -4]
    q_ref, kv_ref, result_ref, sems = rest[-4:]
    copy_pieces(
        [(tile.at[count - 1, 0], q_ref.at[step]) for step, tile in zip(plan.steps(0), tiles)]
        + [
            (block, kv_ref.at[pl.ds(step * frames, frames)])
            for step, block in zip((0, *reversed(range(1, slots))), gathered)
        ],
        sems,
    )
    frame, slot = table_ref[plan.frame_at], table_ref[plan.slot_at]
    head = plan.head_at(0, table_ref, frame, count - 1)

    def some_tiles(body, _):
        for step in (body * MIXED_TILES + more for more in range(MIXED_TILES)):
            places, biases = listed_places(
                plan,
                lists_ref,
                head,
                (frame ^ step) * slots + slot,
                lambda tile: (lax.rem(tile, slots) ^ slot) * frames + (tile // slots ^ frame),
            )
            (state,) = attend_tiles(
                [q_ref[step]],
                [kv_ref[place, 0, 0] for place in places],
                [kv_ref[place, 0, 1] for place in places],
                [biases],
            )
            result_ref[step] = normalized(state)
        return 0

    lax.fori_loop(0, frames // MIXED_TILES, some_tiles, 0)
    copy_pieces(
        [(result_ref.at[step], out.at[count - 1]) for step, out in zip(plan.steps(0), outs)], sems
    )


def spatial_biases(plan, table_ref, lists_ref, head, step, places):
    slots = plan.slots
    frame, slot = table_ref[plan.frame_at], table_ref[plan.slot_at]
    first = (frame * slots + (slot ^ step)) * plan.entries
    listed = jnp.int32(0)
    for entry in range(plan.entries):
        tile = lists_ref[first + entry, head]
        place = (tile // slots - frame + 1) * slots + (lax.rem(tile, slots) ^ slot)
        listed |= jnp.int32(1) << place
    return [bias_where((listed >> place) & 1 == 1) for place in places]


def own_frame_kernel(plan, table_ref, lists_ref, *rest):
    slots = plan.slots
    here, joined, outs = rest[:slots], rest[slots], rest[slots + 1 :]
    slot = table_ref[plan.slot_at]

    def one_head(index, _):
        head = plan.head_at(1, table_ref, slot, index)
        states = attend_tiles(
            [tile[index, 0] for tile in here],
            [joined[step, index, 0] for step in range(slots)],
            [joined[step, index, 1] for step in range(slots)],
            [
                spatial_biases(plan, table_ref, lists_ref, head, step, range(slots, 2 * slots))
                for step in range(slots)
            ],
        )
        for step, state in enumerate(states):
            for out_ref, value in zip(outs, state):
                out_ref[step, index] = jnp.broadcast_to(value, (TILE, HEAD_DIM))
        return 0

    lax.fori_loop(0, plan.heads_in_group(1, table_ref, slot), one_head, 0)


def halo_kernel(plan, steps, table_ref, lists_ref, *rest):
    slots, ways = plan.slots, len(steps)
    queries, (below, above) = rest[:ways], rest[ways : ways + 2]
    top_ref, total_ref, sum_ref = rest[ways + 2 : ways + 5]
    outs = rest[-ways:]
    slot = table_ref[plan.slot_at]
    places = [*range(slots), *range(2 * slots, 3 * slots)]

    def one_head(index, _):
        head = plan.head_at(1, table_ref, slot, index)
        states = attend_tiles(
            [query_ref[index, 0] for query_ref in queries],
            [ref[step, index, 0] for ref in (below, above) for step in range(slots)],
            [ref[step, index, 1] for ref in (below, above) for step in range(slots)],
            [spatial_biases(plan, table_ref, lists_ref, head, step, places) for step in steps],
            [
                (
                    top_ref[step, index][:, :1],
                    total_ref[step, index][:, :1],
                    sum_ref[step, index],
                )
                for step in steps
            ],
        )
        for out_ref, state in zip(outs, states):
            out_ref[index] = normalized(state)
        return 0

    lax.fori_loop(0, plan.heads_in_group(1, table_ref, slot), one_head, 0)


def unpack_kernel(plan, counts, table_ref, *rest):
    pieces, out_ref, sem = list(rest[:-2]), rest[-2], rest[-1]
    for kind, count in enumerate(counts):
        for step in plan.steps(kind):
            piece = pieces.pop(0)
            group = plan.group(kind, table_ref, step)

            def one(index, _, kind=kind, piece=piece, group=group):
                columns = head_columns(plan.head_at(kind, table_ref, group, index))
                pltpu.make_async_copy(piece.at[index], out_ref.at[:, columns], sem).start()
                return 0

            lax.fori_loop(0, plan.heads_in_group(kind, table_ref, group), one, 0)
            if kind == 0:
                filled = (count - 1) * plan.frames + group < table_ref[plan.mixed_at]
                lax.fori_loop(count - 1, count - 1 + filled.astype(jnp.int32), one, 0)
    wait_all(out_ref, sem)


SPACES = {"s": pltpu.SMEM, "v": pltpu.VMEM, "a": pl.ANY}


def call(kernel, outs, operands, places, out_place, scratch=(), flops=0, in_place=None):
    nbytes = sum(math.prod(o.shape) * 2 for o in outs) * 2
    return pl.pallas_call(
        kernel,
        out_shape=outs,
        in_specs=[pl.BlockSpec(memory_space=SPACES[c]) for c in places],
        out_specs=[pl.BlockSpec(memory_space=SPACES[c]) for c in out_place],
        scratch_shapes=list(scratch),
        input_output_aliases=in_place or {},
        compiler_params=pltpu.CompilerParams(vmem_limit_bytes=VMEM_LIMIT),
        cost_estimate=pl.CostEstimate(flops=flops, bytes_accessed=nbytes, transcendentals=0),
    )(*operands)


def after(arrays, others):
    if not arrays or not others:
        return arrays
    return pl.pallas_call(
        lambda *refs: None,
        out_shape=[jax.ShapeDtypeStruct(a.shape, a.dtype) for a in arrays],
        in_specs=[pl.BlockSpec(memory_space=pltpu.VMEM)] * (len(arrays) + len(others)),
        out_specs=[pl.BlockSpec(memory_space=pltpu.VMEM)] * len(arrays),
        input_output_aliases={i: i for i in range(len(arrays))},
        compiler_params=pltpu.CompilerParams(vmem_limit_bytes=VMEM_LIMIT),
    )(*arrays, *others)


def tiles_of(*lead):
    return jax.ShapeDtypeStruct((*lead, TILE, HEAD_DIM), jnp.bfloat16)


def by_kind(plan, t_count, s_count, queries, keys, values, lists, table):
    frames, slots = plan.frames, plan.slots
    pair_flops = 4 * TILE * TILE * HEAD_DIM

    def to_frame(array, step):
        pairs = [(z, z ^ step) for z in range(frames)]
        return array if step == 0 else lax.ppermute(array, "blk", pairs)

    def to_slot(array, step):
        pairs = [(s, s ^ step) for s in range(slots)]
        return array if step == 0 else lax.ppermute(array, MESH_TAIL, pairs)

    def halo(array, step):
        pairs = [(z, z + step) for z in range(frames) if 0 <= z + step < frames]
        return lax.ppermute(array, "blk", pairs)

    packed = call(
        functools.partial(pack_kernel, plan, (t_count, s_count)),
        [tiles_of(t_count, 3)] * frames + [tiles_of(s_count, 3)] * slots,
        (table, queries, keys, values),
        "saaa",
        "v" * (frames + slots),
        [pltpu.SemaphoreType.DMA((frames + slots,))],
    )
    arrived = [to_frame(block, step) for step, block in zip(plan.steps(0), packed[:frames])]
    here = [to_slot(block, step) for step, block in enumerate(packed[frames:])]
    (joined,) = call(
        functools.partial(join_kernel, plan, s_count),
        [tiles_of(slots, s_count, 2)],
        here,
        "v" * slots,
        "v",
        [pltpu.SemaphoreType.DMA((slots,))],
    )
    below, above = halo(joined, 1), halo(joined, -1)
    own_state = call(
        functools.partial(own_frame_kernel, plan),
        [jax.ShapeDtypeStruct((slots, s_count, TILE, HEAD_DIM), jnp.float32)] * 3,
        (table, lists, *here, joined),
        "ss" + "v" * (slots + 1),
        "vvv",
        flops=s_count * slots * slots * pair_flops,
    )
    (mixed,) = call(
        functools.partial(join_mixed_kernel, plan, t_count),
        [tiles_of(frames, 1, 2)],
        (*arrived, own_state[0]),
        "v" * (frames + 1),
        "v",
        [pltpu.SemaphoreType.DMA((frames,))],
    )
    attended = call(
        functools.partial(temporal_kernel, plan),
        [tiles_of(t_count)] * frames,
        (table, lists, *arrived),
        "ss" + "v" * frames,
        "v" * frames,
        flops=t_count * frames * frames * pair_flops,
    )
    gathered = {0: mixed}
    for bit in sorted((1 << n for n in range(slots.bit_length() - 1)), reverse=True):
        for step in list(gathered):
            block = after([gathered[step]], attended[:1])[0] if step else mixed
            gathered[step | bit] = to_slot(block, bit)
    gathered = [gathered[step] for step in (0, *reversed(range(1, slots)))]
    tiles_ahead = 2 * slots * s_count - 4 * frames - 3 * t_count // 2
    flops_ahead = max(tiles_ahead, 1) * 42 * pair_flops
    attended = call(
        functools.partial(mixed_kernel, plan, t_count),
        [tiles_of(t_count)] * frames,
        (table, lists, *arrived, *gathered, *attended),
        "ss" + "v" * (2 * frames + slots),
        "v" * frames,
        [
            pltpu.VMEM((frames, TILE, HEAD_DIM), jnp.bfloat16),
            pltpu.VMEM((slots * frames, 1, 2, TILE, HEAD_DIM), jnp.bfloat16),
            pltpu.VMEM((frames, TILE, HEAD_DIM), jnp.bfloat16),
            pltpu.SemaphoreType.DMA((frames + slots,)),
        ],
        flops=flops_ahead,
        in_place={2 + frames + slots + i: i for i in range(frames)},
    )
    attended = [attended[0], *after(attended[1:-1], (below, above)), attended[-1]]
    pieces = [to_frame(block, step) for step, block in zip(plan.steps(0), attended)]

    def attend_slots(steps, *earlier):
        return call(
            functools.partial(halo_kernel, plan, steps),
            [tiles_of(s_count)] * len(steps),
            (table, lists, *(here[step] for step in steps), below, above, *own_state, *earlier),
            "ss" + "v" * (len(steps) + 5 + len(earlier)),
            "v" * len(steps),
            flops=s_count * len(steps) * 2 * slots * pair_flops,
        )

    half = slots // 2
    away = attend_slots(range(half, slots))
    near = attend_slots(range(half), away[0])
    ahead = pieces[-1:] if t_count > s_count else pieces[1:]
    attended = [near[0], *after(near[1:], ahead), *away]
    pieces += [to_slot(block, step) for step, block in enumerate(attended)]
    (out,) = call(
        functools.partial(unpack_kernel, plan, (t_count, s_count)),
        [pltpu.HBM((TILE, plan.heads * HEAD_DIM), jnp.bfloat16)],
        (table, *pieces),
        "s" + "v" * len(pieces),
        "v",
        [pltpu.SemaphoreType.DMA],
    )
    return out


def capacities(heads, frames, slots):
    low, high = heads // 4, heads - heads // 4

    def chunks_for(fewest, most):
        over_frames = max(-(-most // frames), 1)
        shared = max(fewest, (over_frames - 1) * frames)
        left = heads - fewest - (over_frames * frames - shared)
        return over_frames, max(-(-left // slots), 1)

    pairs, begins = [(chunks_for(high + 1, heads)[0], chunks_for(0, low)[1])], []
    for t in range(low + 1, high + 1):
        if t % frames == 1 or t == low + 1:
            begins.append((t, len(pairs)))
            pairs.append(chunks_for(t, min(-(-t // frames) * frames, high)))
    return pairs, begins + [(high + 1, 0)]


def kind_plan(queries, keys, values, block_lists):
    heads, tiles, entries = block_lists.shape
    frames = lax.axis_size("blk")
    slots = lax.axis_size(MESH_TAIL)
    plan = Plan(heads, frames, slots, entries)
    pairs, begins = capacities(heads, frames, slots)
    by_tile = jnp.transpose(block_lists, (1, 2, 0))
    table, branch, *tensors = call(
        functools.partial(table_kernel, plan, pairs, begins),
        [jax.ShapeDtypeStruct((size,), jnp.int32) for size in (plan.table_size, 1)]
        + [jax.ShapeDtypeStruct(queries.shape, queries.dtype)] * 3,
        (
            by_tile,
            *(pltpu.with_memory_space_constraint(x, pltpu.HBM) for x in (queries, keys, values)),
        ),
        "vaaa",
        "ssvvv",
        [pltpu.SMEM((heads // 16,), jnp.int32), pltpu.SemaphoreType.DMA((3,))],
    )
    lists = by_tile.reshape(tiles * entries, heads)
    branches = [functools.partial(by_kind, plan, t, s) for t, s in pairs]
    return lax.switch(branch[0], branches, *tensors, lists, table)


def per_device(queries, keys, values, block_lists):
    slots = lax.axis_size(MESH_TAIL)
    whole_tiles = queries.shape[0] == TILE and slots == FRAME_TILES
    frames = lax.axis_size("blk")
    if whole_tiles and frames & (frames - 1) == 0 and frames * slots == block_lists.shape[1]:
        return kind_plan(queries, keys, values, block_lists)
    return gathered_plan(queries, keys, values, block_lists)


def solution(mesh):
    in_specs = (
        P(("grp", "blk", "head", "sub"), None),
        P(("grp", "blk", "head", "sub"), None),
        P(("grp", "blk", "head", "sub"), None),
        P(),
    )
    out_specs = P(("grp", "blk", "head", "sub"), None)
    return jax.shard_map(
        per_device, mesh=mesh, in_specs=in_specs, out_specs=out_specs, check_vma=False
    )
```

```python
import functools
import math

import jax
import jax.numpy as jnp
from jax import lax
from jax.experimental import pallas as pl
from jax.experimental.pallas import tpu as pltpu
from jax.sharding import PartitionSpec as P

HEADS = 32
HEAD_DIM = 128
TILE = 128
FRAME_TILES = 4


NEG_FLOOR = -1e30


def query_rows(block_lists, first_head, heads_here, query_tokens):
    tile_ids = jnp.arange(block_lists.shape[1], dtype=jnp.int32)
    lists_local = lax.dynamic_slice_in_dim(block_lists, first_head, heads_here, 0)
    tile_mask = jnp.any(lists_local[:, :, :, None] == tile_ids, axis=2).astype(jnp.bfloat16)
    query_onehot = ((query_tokens // TILE)[:, None] == tile_ids[None, :]).astype(jnp.bfloat16)
    listed = jnp.einsum("qi,hij->hqj", query_onehot, tile_mask, preferred_element_type=jnp.float32)
    return listed.astype(jnp.bfloat16)


def attend_block(state_now, key_block, value_block, allowed, query_local, score_scale):
    top_old, total_old, accum_old = state_now
    scores = (
        jnp.einsum("qhd,khd->hqk", query_local, key_block, preferred_element_type=jnp.float32)
        * score_scale
    )
    top_new = jnp.maximum(top_old, jnp.max(jnp.where(allowed, scores, NEG_FLOOR), axis=2))
    factor = jnp.exp(top_old - top_new)
    weights = jnp.where(allowed, jnp.exp(scores - top_new[:, :, None]), 0.0)
    total_new = total_old * factor + jnp.sum(weights, axis=2)
    product = jnp.einsum(
        "hqk,khd->qhd",
        weights.astype(jnp.bfloat16),
        value_block,
        preferred_element_type=jnp.float32,
    )
    accum_new = accum_old * jnp.transpose(factor)[:, :, None] + product
    return (top_new, total_new, accum_new)


def make_step(query_local, listed_rows, key_token, block_len, tile_total):
    score_scale = 1.0 / math.sqrt(HEAD_DIM)
    tile_ids = jnp.arange(tile_total, dtype=jnp.int32)

    def fold_step(state_now, piece, first_row):
        key_piece, value_piece = piece
        block_count = key_piece.shape[0] // block_len

        def one_block(block_index, state_in):
            key_block = lax.dynamic_slice_in_dim(key_piece, block_index * block_len, block_len, 0)
            value_block = lax.dynamic_slice_in_dim(
                value_piece, block_index * block_len, block_len, 0
            )
            positions = block_index * block_len + jnp.arange(block_len, dtype=jnp.int32)
            key_tiles = key_token(positions) // TILE
            key_onehot = (tile_ids[:, None] == key_tiles[None, :]).astype(jnp.bfloat16)
            allowed = (
                jnp.einsum(
                    "hqj,jk->hqk", listed_rows, key_onehot, preferred_element_type=jnp.float32
                )
                > 0.5
            )
            result = attend_block(
                state_in, key_block, value_block, allowed, query_local, score_scale
            )
            return result

        return lax.fori_loop(0, block_count, one_block, state_now)

    return fold_step


def start_state(heads_here, block_len):
    top_all = jnp.full((heads_here, block_len), NEG_FLOOR, jnp.float32)
    total_all = jnp.zeros((heads_here, block_len), jnp.float32)
    accum_all = jnp.zeros((block_len, heads_here, HEAD_DIM), jnp.float32)
    return (top_all, total_all, accum_all)


def normalize(state_end):
    top_all, total_all, accum_all = state_end
    return (accum_all / jnp.transpose(total_all)[:, :, None]).astype(jnp.bfloat16)


def gathered_plan(queries, keys, values, block_lists):
    row_count, col_count = queries.shape
    n_head = lax.axis_size("head")
    n_sub = lax.axis_size("sub")
    blk_index = lax.axis_index("blk")
    head_index = lax.axis_index("head")
    sub_index = lax.axis_index("sub")
    tile_total = block_lists.shape[1]
    heads_here = HEADS // (n_head * n_sub)
    block_len = row_count * n_head * n_sub

    def inward(tensor):
        return tensor.reshape(1, 1, row_count, n_head, n_sub, heads_here * HEAD_DIM)

    query_six, keys_six, values_six = (
        lax.all_to_all(
            lax.all_to_all(inward(queries), "head", split_axis=3, concat_axis=1, tiled=True),
            "sub",
            split_axis=4,
            concat_axis=0,
            tiled=True,
        ),
        lax.all_to_all(
            lax.all_to_all(inward(keys), "head", split_axis=3, concat_axis=1, tiled=True),
            "sub",
            split_axis=4,
            concat_axis=0,
            tiled=True,
        ),
        lax.all_to_all(
            lax.all_to_all(inward(values), "head", split_axis=3, concat_axis=1, tiled=True),
            "sub",
            split_axis=4,
            concat_axis=0,
            tiled=True,
        ),
    )
    query_local = query_six.reshape(block_len, heads_here, HEAD_DIM)
    keys_local = keys_six.reshape(block_len, heads_here, HEAD_DIM)
    values_local = values_six.reshape(block_len, heads_here, HEAD_DIM)

    def key_token(positions):
        source_dev = positions // block_len
        within = positions % block_len
        sub_source = within // (n_head * row_count)
        head_source = within // row_count % n_head
        offset = within % row_count
        return ((source_dev * n_head + head_source) * n_sub + sub_source) * row_count + offset

    query_tokens = key_token(blk_index * block_len + jnp.arange(block_len, dtype=jnp.int32))
    first_head = (head_index * n_sub + sub_index) * heads_here
    listed_rows = query_rows(block_lists, first_head, heads_here, query_tokens)
    fold_step = make_step(query_local, listed_rows, key_token, block_len, tile_total)
    state_end = fold_step(
        start_state(heads_here, block_len),
        (
            lax.all_gather(keys_local, "blk", axis=0, tiled=True),
            lax.all_gather(values_local, "blk", axis=0, tiled=True),
        ),
        jnp.int32(0),
    )
    result_rows = normalize(state_end)
    attended = result_rows.reshape(n_sub, n_head, row_count, 1, 1, heads_here * HEAD_DIM)
    returned = lax.all_to_all(
        lax.all_to_all(attended, "head", split_axis=1, concat_axis=3, tiled=True),
        "sub",
        split_axis=0,
        concat_axis=4,
        tiled=True,
    )
    return returned.reshape(row_count, col_count)


MESH_TAIL = ("head", "sub")
EXP2_SCALE = math.log2(math.e) / math.sqrt(HEAD_DIM)
VMEM_LIMIT = 16 * 1024 * 1024
MIXED_TILES = 2


class Plan:
    def __init__(self, heads, frames, slots, entries):
        self.heads, self.frames, self.slots, self.entries = heads, frames, slots, entries
        self.over_slots_at = heads
        self.pure_at = 2 * heads
        self.mixed_at = 2 * heads + 1
        self.spatial_at = 2 * heads + 2
        self.frame_at = 2 * heads + 3
        self.slot_at = 2 * heads + 4
        self.table_size = 2 * heads + 5

    def sizes(self, kind):
        return (self.frames, self.slots)[kind]

    def head_at(self, kind, table_ref, group, index):
        return table_ref[(0, self.over_slots_at)[kind] + index * self.sizes(kind) + group]

    def group(self, kind, table_ref, step):
        return table_ref[(self.frame_at, self.slot_at)[kind]] ^ step

    def heads_in_group(self, kind, table_ref, group):
        size = self.sizes(kind)
        return (table_ref[(self.pure_at, self.spatial_at)[kind]] - group + size - 1) // size

    def steps(self, kind):
        others = range(1, self.sizes(kind))
        return [0, *others] if kind else [0, *reversed(others)]


def head_columns(head):
    return pl.ds(pl.multiple_of(head * HEAD_DIM, HEAD_DIM), HEAD_DIM)


def table_kernel(plan, pairs, begins, lists_ref, *rest):
    table_ref, branch_ref, mask_ref, sems = rest[3], rest[4], rest[-2], rest[-1]
    copies = [pltpu.make_async_copy(rest[i], rest[5 + i], sems.at[i]) for i in range(3)]
    for copy in copies:
        copy.start()
    lists = lists_ref[...]
    tiles = lax.broadcasted_iota(jnp.int32, lists.shape, 0)
    other_slot = ((lists ^ tiles) & (plan.slots - 1)).astype(jnp.float32)
    spatial = jnp.sum(jnp.sum(other_slot, axis=0), axis=0, keepdims=True) > 0
    lanes = lax.broadcasted_iota(jnp.int32, spatial.shape, 1)
    for place in range(plan.heads // 16):
        bit = jnp.where(lanes // 16 == place, jnp.int32(1) << (lanes % 16), 0)
        bits = jnp.where(spatial, bit, 0).astype(jnp.float32)
        mask_ref[place] = jnp.sum(bits).astype(jnp.int32)
    spatial_total = jnp.sum(spatial.astype(jnp.float32)).astype(jnp.int32)
    temporal_total = plan.heads - spatial_total
    branch, chunks, last = 0, pairs[0][0], 0
    for first, place in begins:
        reached = (temporal_total >= first).astype(jnp.int32)
        branch += reached * (place - last)
        chunks += reached * (pairs[place][0] - pairs[last][0])
        last = place
    mixed = (chunks - 1) * plan.frames
    shared = lax.max(temporal_total, mixed)
    room = chunks * plan.frames - shared

    def clear(p, _):
        table_ref[p] = 0
        return 0

    def place_head(h, counts):
        kind = (mask_ref[h // 16] >> (h % 16)) & 1
        t_rank, s_rank = counts
        s_place = jnp.where(s_rank < room, shared + s_rank, plan.over_slots_at + s_rank - room)
        table_ref[jnp.where(kind == 1, s_place, t_rank)] = h
        return t_rank + 1 - kind, s_rank + kind

    lax.fori_loop(0, 2 * plan.heads, clear, 0)
    lax.fori_loop(0, plan.heads, place_head, (jnp.int32(0), jnp.int32(0)))
    table_ref[plan.pure_at] = lax.min(temporal_total, mixed)
    table_ref[plan.mixed_at] = shared + lax.min(spatial_total, room)
    table_ref[plan.spatial_at] = lax.max(spatial_total - room, 0)
    table_ref[plan.frame_at] = lax.axis_index("blk")
    n_sub = lax.axis_size("sub")
    table_ref[plan.slot_at] = lax.axis_index("head") * n_sub + lax.axis_index("sub")
    branch_ref[0] = branch
    for copy in copies:
        copy.wait()


def wait_all(ref, sem):
    pltpu.make_async_copy(ref, ref, sem).wait()


def pack_kernel(plan, counts, table_ref, q_ref, k_ref, v_ref, *rest):
    outs, sems = rest[:-1], rest[-1]
    steps = [(kind, step) for kind in range(2) for step in plan.steps(kind)]
    for sem, (kind, step) in enumerate(steps):
        group = plan.group(kind, table_ref, step)

        def one(index, _, kind=kind, group=group, sem=sem):
            columns = head_columns(plan.head_at(kind, table_ref, group, index))
            for place, ref in enumerate((q_ref, k_ref, v_ref)):
                pltpu.make_async_copy(
                    ref.at[:, columns], outs[sem].at[index, place], sems.at[sem]
                ).start()
            return 0

        lax.fori_loop(0, counts[kind], one, 0)
    for sem, out_ref in enumerate(outs):
        wait_all(out_ref, sems.at[sem])


def turn_keys(kv_ref, place, count):
    def turn(work, _):
        step, index = work // count, lax.rem(work, count)
        kv_ref[step, index, place] = kv_ref[step, index, place].T
        return 0

    lax.fori_loop(0, kv_ref.shape[0] * count, turn, 0)


def join_kernel(plan, count, *refs):
    pieces, out_ref, sems = refs[: plan.slots], refs[-2], refs[-1]
    copy_pieces(
        [(piece.at[:, pl.ds(1, 2)], out_ref.at[step]) for step, piece in enumerate(pieces)], sems
    )
    turn_keys(out_ref, 0, count)


def join_mixed_kernel(plan, count, *refs):
    pieces, out_ref, sems = refs[: plan.frames], refs[-2], refs[-1]
    copy_pieces(
        [
            (piece.at[count - 1, pl.ds(1, 2)], out_ref.at[step, 0])
            for step, piece in zip(plan.steps(0), pieces)
        ],
        sems,
    )
    turn_keys(out_ref, 0, 1)


def attend_tiles(queries, keys, values, biases, before=None, turned=True):
    scores = lax.dot_general(
        jnp.concatenate(queries, 0),
        jnp.concatenate(keys, 1 if turned else 0),
        (((1,), (0 if turned else 1,)), ((), ())),
        preferred_element_type=jnp.float32,
    )
    rows, tops = [], []
    for a, bias in enumerate(biases):
        tiles = [
            scores[a * TILE : (a + 1) * TILE, b * TILE : (b + 1) * TILE] + bias[b]
            for b in range(len(keys))
        ]
        top = jnp.max(functools.reduce(jnp.maximum, tiles), axis=1, keepdims=True)
        if before is not None:
            top = jnp.maximum(top, before[a][0])
        weights = [jnp.exp2((tile - top) * EXP2_SCALE) for tile in tiles]
        tops.append(top)
        rows.append(jnp.concatenate([w.astype(jnp.bfloat16) for w in weights], 1))
    values = jnp.concatenate(values, 0)
    accum = jnp.dot(
        jnp.concatenate(rows, 0),
        jnp.concatenate([values, jnp.ones_like(values)], 1),
        preferred_element_type=jnp.float32,
    )
    states = []
    for a, top in enumerate(tops):
        part = accum[a * TILE : (a + 1) * TILE, :HEAD_DIM]
        total = accum[a * TILE : (a + 1) * TILE, HEAD_DIM:]
        if before is not None:
            factor = jnp.exp2((before[a][0] - top) * EXP2_SCALE)
            total, part = total + before[a][1] * factor, part + before[a][2] * factor
        states.append((top, total, part))
    return states


def normalized(state):
    return (state[2] / state[1]).astype(jnp.bfloat16)


def bias_where(attended):
    return jnp.where(attended, jnp.float32(0), jnp.float32(NEG_FLOOR))


def copy_pieces(pieces, sems):
    copies = [pltpu.make_async_copy(a, b, sems.at[i]) for i, (a, b) in enumerate(pieces)]
    for copy in copies:
        copy.start()
    for copy in copies:
        copy.wait()


def listed_places(plan, lists_ref, head, query_tile, place_of):
    first = query_tile * plan.entries
    listed = jnp.int32(0)
    places, biases = [], []
    for entry in range(plan.entries):
        place = place_of(lists_ref[first + entry, head])
        places.append(place)
        biases.append(bias_where((listed >> place) & 1 == 0))
        listed |= jnp.int32(1) << place
    return places, biases


def temporal_kernel(plan, table_ref, lists_ref, *rest):
    frames, slots = plan.frames, plan.slots
    by_step = [plan.steps(0).index(step) for step in range(frames)]
    tiles = [rest[i] for i in by_step]
    outs = [rest[frames + i] for i in by_step]
    frame, slot = table_ref[plan.frame_at], table_ref[plan.slot_at]

    def one_head(index, _):
        head = plan.head_at(0, table_ref, frame, index)
        biases = []
        for step in range(frames):
            first = ((frame ^ step) * slots + slot) * plan.entries
            listed = jnp.int32(0)
            for entry in range(plan.entries):
                listed |= jnp.int32(1) << (lists_ref[first + entry, head] // slots)
            biases.append(
                [bias_where((listed >> (frame ^ other)) & 1 == 1) for other in range(frames)]
            )
        states = attend_tiles(
            *([tile[index, i] for tile in tiles] for i in range(3)), biases, turned=False
        )
        for out_ref, state in zip(outs, states):
            out_ref[index] = normalized(state)
        return 0

    lax.fori_loop(0, plan.heads_in_group(0, table_ref, frame), one_head, 0)


def mixed_kernel(plan, count, table_ref, lists_ref, *rest):
    frames, slots = plan.frames, plan.slots
    tiles, gathered = rest[:frames], rest[frames : frames + slots]
    outs = rest[-4 - frames : -4]
    q_ref, kv_ref, result_ref, sems = rest[-4:]
    copy_pieces(
        [(tile.at[count - 1, 0], q_ref.at[step]) for step, tile in zip(plan.steps(0), tiles)]
        + [
            (block, kv_ref.at[pl.ds(step * frames, frames)])
            for step, block in zip((0, *reversed(range(1, slots))), gathered)
        ],
        sems,
    )
    frame, slot = table_ref[plan.frame_at], table_ref[plan.slot_at]
    head = plan.head_at(0, table_ref, frame, count - 1)

    def some_tiles(body, _):
        for step in (body * MIXED_TILES + more for more in range(MIXED_TILES)):
            places, biases = listed_places(
                plan,
                lists_ref,
                head,
                (frame ^ step) * slots + slot,
                lambda tile: (lax.rem(tile, slots) ^ slot) * frames + (tile // slots ^ frame),
            )
            (state,) = attend_tiles(
                [q_ref[step]],
                [kv_ref[place, 0, 0] for place in places],
                [kv_ref[place, 0, 1] for place in places],
                [biases],
            )
            result_ref[step] = normalized(state)
        return 0

    lax.fori_loop(0, frames // MIXED_TILES, some_tiles, 0)
    copy_pieces(
        [(result_ref.at[step], out.at[count - 1]) for step, out in zip(plan.steps(0), outs)], sems
    )


def spatial_biases(plan, table_ref, lists_ref, head, step, places):
    slots = plan.slots
    frame, slot = table_ref[plan.frame_at], table_ref[plan.slot_at]
    first = (frame * slots + (slot ^ step)) * plan.entries
    listed = jnp.int32(0)
    for entry in range(plan.entries):
        tile = lists_ref[first + entry, head]
        place = (tile // slots - frame + 1) * slots + (lax.rem(tile, slots) ^ slot)
        listed |= jnp.int32(1) << place
    return [bias_where((listed >> place) & 1 == 1) for place in places]


def own_frame_kernel(plan, table_ref, lists_ref, *rest):
    slots = plan.slots
    here, joined, outs = rest[:slots], rest[slots], rest[slots + 1 :]
    slot = table_ref[plan.slot_at]

    def one_head(index, _):
        head = plan.head_at(1, table_ref, slot, index)
        states = attend_tiles(
            [tile[index, 0] for tile in here],
            [joined[step, index, 0] for step in range(slots)],
            [joined[step, index, 1] for step in range(slots)],
            [
                spatial_biases(plan, table_ref, lists_ref, head, step, range(slots, 2 * slots))
                for step in range(slots)
            ],
        )
        for step, state in enumerate(states):
            for out_ref, value in zip(outs, state):
                out_ref[step, index] = jnp.broadcast_to(value, (TILE, HEAD_DIM))
        return 0

    lax.fori_loop(0, plan.heads_in_group(1, table_ref, slot), one_head, 0)


def halo_kernel(plan, steps, table_ref, lists_ref, *rest):
    slots, ways = plan.slots, len(steps)
    queries, (below, above) = rest[:ways], rest[ways : ways + 2]
    top_ref, total_ref, sum_ref = rest[ways + 2 : ways + 5]
    outs = rest[-ways:]
    slot = table_ref[plan.slot_at]
    places = [*range(slots), *range(2 * slots, 3 * slots)]

    def one_head(index, _):
        head = plan.head_at(1, table_ref, slot, index)
        states = attend_tiles(
            [query_ref[index, 0] for query_ref in queries],
            [ref[step, index, 0] for ref in (below, above) for step in range(slots)],
            [ref[step, index, 1] for ref in (below, above) for step in range(slots)],
            [spatial_biases(plan, table_ref, lists_ref, head, step, places) for step in steps],
            [
                (top_ref[step, index], total_ref[step, index], sum_ref[step, index])
                for step in steps
            ],
        )
        for out_ref, state in zip(outs, states):
            out_ref[index] = normalized(state)
        return 0

    lax.fori_loop(0, plan.heads_in_group(1, table_ref, slot), one_head, 0)


def unpack_kernel(plan, counts, table_ref, *rest):
    pieces, out_ref, sem = list(rest[:-2]), rest[-2], rest[-1]
    for kind, count in enumerate(counts):
        for step in plan.steps(kind):
            piece = pieces.pop(0)
            group = plan.group(kind, table_ref, step)

            def one(index, _, kind=kind, piece=piece, group=group):
                columns = head_columns(plan.head_at(kind, table_ref, group, index))
                pltpu.make_async_copy(piece.at[index], out_ref.at[:, columns], sem).start()
                return 0

            lax.fori_loop(0, plan.heads_in_group(kind, table_ref, group), one, 0)
            if kind == 0:
                filled = (count - 1) * plan.frames + group < table_ref[plan.mixed_at]
                lax.fori_loop(count - 1, count - 1 + filled.astype(jnp.int32), one, 0)
    wait_all(out_ref, sem)


SPACES = {"s": pltpu.SMEM, "v": pltpu.VMEM, "a": pl.ANY}


def call(kernel, outs, operands, places, out_place, scratch=(), flops=0, in_place=None):
    nbytes = sum(math.prod(o.shape) * 2 for o in outs) * 2
    return pl.pallas_call(
        kernel,
        out_shape=outs,
        in_specs=[pl.BlockSpec(memory_space=SPACES[c]) for c in places],
        out_specs=[pl.BlockSpec(memory_space=SPACES[c]) for c in out_place],
        scratch_shapes=list(scratch),
        input_output_aliases=in_place or {},
        compiler_params=pltpu.CompilerParams(vmem_limit_bytes=VMEM_LIMIT),
        cost_estimate=pl.CostEstimate(flops=flops, bytes_accessed=nbytes, transcendentals=0),
    )(*operands)


def after(arrays, others):
    if not arrays or not others:
        return arrays
    return pl.pallas_call(
        lambda *refs: None,
        out_shape=[jax.ShapeDtypeStruct(a.shape, a.dtype) for a in arrays],
        in_specs=[pl.BlockSpec(memory_space=pltpu.VMEM)] * (len(arrays) + len(others)),
        out_specs=[pl.BlockSpec(memory_space=pltpu.VMEM)] * len(arrays),
        input_output_aliases={i: i for i in range(len(arrays))},
        compiler_params=pltpu.CompilerParams(vmem_limit_bytes=VMEM_LIMIT),
    )(*arrays, *others)


def tiles_of(*lead):
    return jax.ShapeDtypeStruct((*lead, TILE, HEAD_DIM), jnp.bfloat16)


def by_kind(plan, t_count, s_count, queries, keys, values, lists, table):
    frames, slots = plan.frames, plan.slots
    pair_flops = 4 * TILE * TILE * HEAD_DIM

    def to_frame(array, step):
        pairs = [(z, z ^ step) for z in range(frames)]
        return array if step == 0 else lax.ppermute(array, "blk", pairs)

    def to_slot(array, step):
        pairs = [(s, s ^ step) for s in range(slots)]
        return array if step == 0 else lax.ppermute(array, MESH_TAIL, pairs)

    def halo(array, step):
        pairs = [(z, z + step) for z in range(frames) if 0 <= z + step < frames]
        return lax.ppermute(array, "blk", pairs)

    packed = call(
        functools.partial(pack_kernel, plan, (t_count, s_count)),
        [tiles_of(t_count, 3)] * frames + [tiles_of(s_count, 3)] * slots,
        (table, queries, keys, values),
        "saaa",
        "v" * (frames + slots),
        [pltpu.SemaphoreType.DMA((frames + slots,))],
    )
    arrived = [to_frame(block, step) for step, block in zip(plan.steps(0), packed[:frames])]
    here = [to_slot(block, step) for step, block in enumerate(packed[frames:])]
    (joined,) = call(
        functools.partial(join_kernel, plan, s_count),
        [tiles_of(slots, s_count, 2)],
        here,
        "v" * slots,
        "v",
        [pltpu.SemaphoreType.DMA((slots,))],
    )
    below, above = halo(joined, 1), halo(joined, -1)
    own_state = call(
        functools.partial(own_frame_kernel, plan),
        [jax.ShapeDtypeStruct((slots, s_count, TILE, HEAD_DIM), jnp.float32)] * 3,
        (table, lists, *here, joined),
        "ss" + "v" * (slots + 1),
        "vvv",
        flops=s_count * slots * slots * pair_flops,
    )
    (mixed,) = call(
        functools.partial(join_mixed_kernel, plan, t_count),
        [tiles_of(frames, 1, 2)],
        (*arrived, own_state[0]),
        "v" * (frames + 1),
        "v",
        [pltpu.SemaphoreType.DMA((frames,))],
    )
    attended = call(
        functools.partial(temporal_kernel, plan),
        [tiles_of(t_count)] * frames,
        (table, lists, *arrived),
        "ss" + "v" * frames,
        "v" * frames,
        flops=t_count * frames * frames * pair_flops,
    )
    gathered = {0: mixed}
    for bit in sorted((1 << n for n in range(slots.bit_length() - 1)), reverse=True):
        for step in list(gathered):
            block = after([gathered[step]], attended[:1])[0] if step else mixed
            gathered[step | bit] = to_slot(block, bit)
    gathered = [gathered[step] for step in (0, *reversed(range(1, slots)))]
    tiles_ahead = 2 * slots * s_count - 4 * frames - 3 * t_count // 2
    flops_ahead = max(tiles_ahead, 1) * 42 * pair_flops
    attended = call(
        functools.partial(mixed_kernel, plan, t_count),
        [tiles_of(t_count)] * frames,
        (table, lists, *arrived, *gathered, *attended),
        "ss" + "v" * (2 * frames + slots),
        "v" * frames,
        [
            pltpu.VMEM((frames, TILE, HEAD_DIM), jnp.bfloat16),
            pltpu.VMEM((slots * frames, 1, 2, TILE, HEAD_DIM), jnp.bfloat16),
            pltpu.VMEM((frames, TILE, HEAD_DIM), jnp.bfloat16),
            pltpu.SemaphoreType.DMA((frames + slots,)),
        ],
        flops=flops_ahead,
        in_place={2 + frames + slots + i: i for i in range(frames)},
    )
    attended = [attended[0], *after(attended[1:-1], (below, above)), attended[-1]]
    pieces = [to_frame(block, step) for step, block in zip(plan.steps(0), attended)]

    def attend_slots(steps, *earlier):
        return call(
            functools.partial(halo_kernel, plan, steps),
            [tiles_of(s_count)] * len(steps),
            (table, lists, *(here[step] for step in steps), below, above, *own_state, *earlier),
            "ss" + "v" * (len(steps) + 5 + len(earlier)),
            "v" * len(steps),
            flops=s_count * len(steps) * 2 * slots * pair_flops,
        )

    half = slots // 2
    away = attend_slots(range(half, slots))
    near = attend_slots(range(half), away[0])
    ahead = pieces[-1:] if t_count > s_count else pieces[1:]
    attended = [near[0], *after(near[1:], ahead), *away]
    pieces += [to_slot(block, step) for step, block in enumerate(attended)]
    (out,) = call(
        functools.partial(unpack_kernel, plan, (t_count, s_count)),
        [pltpu.HBM((TILE, plan.heads * HEAD_DIM), jnp.bfloat16)],
        (table, *pieces),
        "s" + "v" * len(pieces),
        "v",
        [pltpu.SemaphoreType.DMA],
    )
    return out


def capacities(heads, frames, slots):
    low, high = heads // 4, heads - heads // 4

    def chunks_for(fewest, most):
        over_frames = max(-(-most // frames), 1)
        shared = max(fewest, (over_frames - 1) * frames)
        left = heads - fewest - (over_frames * frames - shared)
        return over_frames, max(-(-left // slots), 1)

    pairs, begins = [(chunks_for(high + 1, heads)[0], chunks_for(0, low)[1])], []
    for t in range(low + 1, high + 1):
        if t % frames == 1 or t == low + 1:
            begins.append((t, len(pairs)))
            pairs.append(chunks_for(t, min(-(-t // frames) * frames, high)))
    return pairs, begins + [(high + 1, 0)]


def kind_plan(queries, keys, values, block_lists):
    heads, tiles, entries = block_lists.shape
    frames = lax.axis_size("blk")
    slots = lax.axis_size(MESH_TAIL)
    plan = Plan(heads, frames, slots, entries)
    pairs, begins = capacities(heads, frames, slots)
    by_tile = jnp.transpose(block_lists, (1, 2, 0))
    table, branch, *tensors = call(
        functools.partial(table_kernel, plan, pairs, begins),
        [jax.ShapeDtypeStruct((size,), jnp.int32) for size in (plan.table_size, 1)]
        + [jax.ShapeDtypeStruct(queries.shape, queries.dtype)] * 3,
        (
            by_tile,
            *(pltpu.with_memory_space_constraint(x, pltpu.HBM) for x in (queries, keys, values)),
        ),
        "vaaa",
        "ssvvv",
        [pltpu.SMEM((heads // 16,), jnp.int32), pltpu.SemaphoreType.DMA((3,))],
    )
    lists = by_tile.reshape(tiles * entries, heads)
    branches = [functools.partial(by_kind, plan, t, s) for t, s in pairs]
    return lax.switch(branch[0], branches, *tensors, lists, table)


def per_device(queries, keys, values, block_lists):
    slots = lax.axis_size(MESH_TAIL)
    whole_tiles = queries.shape[0] == TILE and slots == FRAME_TILES
    frames = lax.axis_size("blk")
    if whole_tiles and frames & (frames - 1) == 0 and frames * slots == block_lists.shape[1]:
        return kind_plan(queries, keys, values, block_lists)
    return gathered_plan(queries, keys, values, block_lists)


def solution(mesh):
    in_specs = (
        P(("grp", "blk", "head", "sub"), None),
        P(("grp", "blk", "head", "sub"), None),
        P(("grp", "blk", "head", "sub"), None),
        P(),
    )
    out_specs = P(("grp", "blk", "head", "sub"), None)
    return jax.shard_map(
        per_device, mesh=mesh, in_specs=in_specs, out_specs=out_specs, check_vma=False
    )
```

```python
import functools
import math

import jax
import jax.numpy as jnp
from jax import lax
from jax.experimental import pallas as pl
from jax.experimental.pallas import tpu as pltpu
from jax.sharding import PartitionSpec as P

HEADS = 32
HEAD_DIM = 128
TILE = 128
FRAME_TILES = 4


NEG_FLOOR = -1e30


def query_rows(block_lists, first_head, heads_here, query_tokens):
    tile_ids = jnp.arange(block_lists.shape[1], dtype=jnp.int32)
    lists_local = lax.dynamic_slice_in_dim(block_lists, first_head, heads_here, 0)
    tile_mask = jnp.any(lists_local[:, :, :, None] == tile_ids, axis=2).astype(jnp.bfloat16)
    query_onehot = ((query_tokens // TILE)[:, None] == tile_ids[None, :]).astype(jnp.bfloat16)
    listed = jnp.einsum("qi,hij->hqj", query_onehot, tile_mask, preferred_element_type=jnp.float32)
    return listed.astype(jnp.bfloat16)


def attend_block(state_now, key_block, value_block, allowed, query_local, score_scale):
    top_old, total_old, accum_old = state_now
    scores = (
        jnp.einsum("qhd,khd->hqk", query_local, key_block, preferred_element_type=jnp.float32)
        * score_scale
    )
    top_new = jnp.maximum(top_old, jnp.max(jnp.where(allowed, scores, NEG_FLOOR), axis=2))
    factor = jnp.exp(top_old - top_new)
    weights = jnp.where(allowed, jnp.exp(scores - top_new[:, :, None]), 0.0)
    total_new = total_old * factor + jnp.sum(weights, axis=2)
    product = jnp.einsum(
        "hqk,khd->qhd",
        weights.astype(jnp.bfloat16),
        value_block,
        preferred_element_type=jnp.float32,
    )
    accum_new = accum_old * jnp.transpose(factor)[:, :, None] + product
    return (top_new, total_new, accum_new)


def make_step(query_local, listed_rows, key_token, block_len, tile_total):
    score_scale = 1.0 / math.sqrt(HEAD_DIM)
    tile_ids = jnp.arange(tile_total, dtype=jnp.int32)

    def fold_step(state_now, piece, first_row):
        key_piece, value_piece = piece
        block_count = key_piece.shape[0] // block_len

        def one_block(block_index, state_in):
            key_block = lax.dynamic_slice_in_dim(key_piece, block_index * block_len, block_len, 0)
            value_block = lax.dynamic_slice_in_dim(
                value_piece, block_index * block_len, block_len, 0
            )
            positions = block_index * block_len + jnp.arange(block_len, dtype=jnp.int32)
            key_tiles = key_token(positions) // TILE
            key_onehot = (tile_ids[:, None] == key_tiles[None, :]).astype(jnp.bfloat16)
            allowed = (
                jnp.einsum(
                    "hqj,jk->hqk", listed_rows, key_onehot, preferred_element_type=jnp.float32
                )
                > 0.5
            )
            result = attend_block(
                state_in, key_block, value_block, allowed, query_local, score_scale
            )
            return result

        return lax.fori_loop(0, block_count, one_block, state_now)

    return fold_step


def start_state(heads_here, block_len):
    top_all = jnp.full((heads_here, block_len), NEG_FLOOR, jnp.float32)
    total_all = jnp.zeros((heads_here, block_len), jnp.float32)
    accum_all = jnp.zeros((block_len, heads_here, HEAD_DIM), jnp.float32)
    return (top_all, total_all, accum_all)


def normalize(state_end):
    top_all, total_all, accum_all = state_end
    return (accum_all / jnp.transpose(total_all)[:, :, None]).astype(jnp.bfloat16)


def gathered_plan(queries, keys, values, block_lists):
    row_count, col_count = queries.shape
    n_head = lax.axis_size("head")
    n_sub = lax.axis_size("sub")
    blk_index = lax.axis_index("blk")
    head_index = lax.axis_index("head")
    sub_index = lax.axis_index("sub")
    tile_total = block_lists.shape[1]
    heads_here = HEADS // (n_head * n_sub)
    block_len = row_count * n_head * n_sub

    def inward(tensor):
        return tensor.reshape(1, 1, row_count, n_head, n_sub, heads_here * HEAD_DIM)

    query_six, keys_six, values_six = (
        lax.all_to_all(
            lax.all_to_all(inward(queries), "head", split_axis=3, concat_axis=1, tiled=True),
            "sub",
            split_axis=4,
            concat_axis=0,
            tiled=True,
        ),
        lax.all_to_all(
            lax.all_to_all(inward(keys), "head", split_axis=3, concat_axis=1, tiled=True),
            "sub",
            split_axis=4,
            concat_axis=0,
            tiled=True,
        ),
        lax.all_to_all(
            lax.all_to_all(inward(values), "head", split_axis=3, concat_axis=1, tiled=True),
            "sub",
            split_axis=4,
            concat_axis=0,
            tiled=True,
        ),
    )
    query_local = query_six.reshape(block_len, heads_here, HEAD_DIM)
    keys_local = keys_six.reshape(block_len, heads_here, HEAD_DIM)
    values_local = values_six.reshape(block_len, heads_here, HEAD_DIM)

    def key_token(positions):
        source_dev = positions // block_len
        within = positions % block_len
        sub_source = within // (n_head * row_count)
        head_source = within // row_count % n_head
        offset = within % row_count
        return ((source_dev * n_head + head_source) * n_sub + sub_source) * row_count + offset

    query_tokens = key_token(blk_index * block_len + jnp.arange(block_len, dtype=jnp.int32))
    first_head = (head_index * n_sub + sub_index) * heads_here
    listed_rows = query_rows(block_lists, first_head, heads_here, query_tokens)
    fold_step = make_step(query_local, listed_rows, key_token, block_len, tile_total)
    state_end = fold_step(
        start_state(heads_here, block_len),
        (
            lax.all_gather(keys_local, "blk", axis=0, tiled=True),
            lax.all_gather(values_local, "blk", axis=0, tiled=True),
        ),
        jnp.int32(0),
    )
    result_rows = normalize(state_end)
    attended = result_rows.reshape(n_sub, n_head, row_count, 1, 1, heads_here * HEAD_DIM)
    returned = lax.all_to_all(
        lax.all_to_all(attended, "head", split_axis=1, concat_axis=3, tiled=True),
        "sub",
        split_axis=0,
        concat_axis=4,
        tiled=True,
    )
    return returned.reshape(row_count, col_count)


MESH_TAIL = ("head", "sub")
EXP2_SCALE = math.log2(math.e) / math.sqrt(HEAD_DIM)
VMEM_LIMIT = 16 * 1024 * 1024
MIXED_TILES = 4


class Plan:
    def __init__(self, heads, frames, slots, entries):
        self.heads, self.frames, self.slots, self.entries = heads, frames, slots, entries
        self.over_slots_at = heads
        self.pure_at = 2 * heads
        self.mixed_at = 2 * heads + 1
        self.spatial_at = 2 * heads + 2
        self.frame_at = 2 * heads + 3
        self.slot_at = 2 * heads + 4
        self.table_size = 2 * heads + 5

    def sizes(self, kind):
        return (self.frames, self.slots)[kind]

    def head_at(self, kind, table_ref, group, index):
        return table_ref[(0, self.over_slots_at)[kind] + index * self.sizes(kind) + group]

    def group(self, kind, table_ref, step):
        return table_ref[(self.frame_at, self.slot_at)[kind]] ^ step

    def heads_in_group(self, kind, table_ref, group):
        size = self.sizes(kind)
        return (table_ref[(self.pure_at, self.spatial_at)[kind]] - group + size - 1) // size

    def steps(self, kind):
        others = range(1, self.sizes(kind))
        return [0, *others] if kind else [0, *reversed(others)]


def head_columns(head):
    return pl.ds(pl.multiple_of(head * HEAD_DIM, HEAD_DIM), HEAD_DIM)


def table_kernel(plan, pairs, begins, lists_ref, *rest):
    table_ref, branch_ref, mask_ref, sems = rest[3], rest[4], rest[-2], rest[-1]
    copies = [pltpu.make_async_copy(rest[i], rest[5 + i], sems.at[i]) for i in range(3)]
    for copy in copies:
        copy.start()
    lists = lists_ref[...]
    tiles = lax.broadcasted_iota(jnp.int32, lists.shape, 0)
    other_slot = ((lists ^ tiles) & (plan.slots - 1)).astype(jnp.float32)
    spatial = jnp.sum(jnp.sum(other_slot, axis=0), axis=0, keepdims=True) > 0
    lanes = lax.broadcasted_iota(jnp.int32, spatial.shape, 1)
    for place in range(plan.heads // 16):
        bit = jnp.where(lanes // 16 == place, jnp.int32(1) << (lanes % 16), 0)
        bits = jnp.where(spatial, bit, 0).astype(jnp.float32)
        mask_ref[place] = jnp.sum(bits).astype(jnp.int32)
    spatial_total = jnp.sum(spatial.astype(jnp.float32)).astype(jnp.int32)
    temporal_total = plan.heads - spatial_total
    branch, chunks, last = 0, pairs[0][0], 0
    for first, place in begins:
        reached = (temporal_total >= first).astype(jnp.int32)
        branch += reached * (place - last)
        chunks += reached * (pairs[place][0] - pairs[last][0])
        last = place
    mixed = (chunks - 1) * plan.frames
    shared = lax.max(temporal_total, mixed)
    room = chunks * plan.frames - shared

    def clear(p, _):
        table_ref[p] = 0
        return 0

    def place_head(h, counts):
        kind = (mask_ref[h // 16] >> (h % 16)) & 1
        t_rank, s_rank = counts
        s_place = jnp.where(s_rank < room, shared + s_rank, plan.over_slots_at + s_rank - room)
        table_ref[jnp.where(kind == 1, s_place, t_rank)] = h
        return t_rank + 1 - kind, s_rank + kind

    lax.fori_loop(0, 2 * plan.heads, clear, 0)
    lax.fori_loop(0, plan.heads, place_head, (jnp.int32(0), jnp.int32(0)))
    table_ref[plan.pure_at] = lax.min(temporal_total, mixed)
    table_ref[plan.mixed_at] = shared + lax.min(spatial_total, room)
    table_ref[plan.spatial_at] = lax.max(spatial_total - room, 0)
    table_ref[plan.frame_at] = lax.axis_index("blk")
    n_sub = lax.axis_size("sub")
    table_ref[plan.slot_at] = lax.axis_index("head") * n_sub + lax.axis_index("sub")
    branch_ref[0] = branch
    for copy in copies:
        copy.wait()


def wait_all(ref, sem):
    pltpu.make_async_copy(ref, ref, sem).wait()


def pack_kernel(plan, counts, table_ref, q_ref, k_ref, v_ref, *rest):
    outs, sems = rest[:-1], rest[-1]
    steps = [(kind, step) for kind in range(2) for step in plan.steps(kind)]
    for sem, (kind, step) in enumerate(steps):
        group = plan.group(kind, table_ref, step)

        def one(index, _, kind=kind, group=group, sem=sem):
            columns = head_columns(plan.head_at(kind, table_ref, group, index))
            for place, ref in enumerate((q_ref, k_ref, v_ref)):
                pltpu.make_async_copy(
                    ref.at[:, columns], outs[sem].at[index, place], sems.at[sem]
                ).start()
            return 0

        lax.fori_loop(0, counts[kind], one, 0)
    for sem, out_ref in enumerate(outs):
        wait_all(out_ref, sems.at[sem])


def turn_keys(kv_ref, place, count):
    def turn(work, _):
        step, index = work // count, lax.rem(work, count)
        kv_ref[step, index, place] = kv_ref[step, index, place].T
        return 0

    lax.fori_loop(0, kv_ref.shape[0] * count, turn, 0)


def join_kernel(plan, count, *refs):
    pieces, out_ref, sems = refs[: plan.slots], refs[-2], refs[-1]
    copy_pieces(
        [(piece.at[:, pl.ds(1, 2)], out_ref.at[step]) for step, piece in enumerate(pieces)], sems
    )
    turn_keys(out_ref, 0, count)


def join_mixed_kernel(plan, count, *refs):
    pieces, out_ref, sems = refs[: plan.frames], refs[-2], refs[-1]
    copy_pieces(
        [
            (piece.at[count - 1, pl.ds(1, 2)], out_ref.at[step, 0])
            for step, piece in zip(plan.steps(0), pieces)
        ],
        sems,
    )
    turn_keys(out_ref, 0, 1)


def attend_tiles(queries, keys, values, biases, before=None, turned=True):
    scores = lax.dot_general(
        jnp.concatenate(queries, 0),
        jnp.concatenate(keys, 1 if turned else 0),
        (((1,), (0 if turned else 1,)), ((), ())),
        preferred_element_type=jnp.float32,
    )
    rows, tops = [], []
    for a, bias in enumerate(biases):
        tiles = [
            scores[a * TILE : (a + 1) * TILE, b * TILE : (b + 1) * TILE] + bias[b]
            for b in range(len(keys))
        ]
        top = jnp.max(functools.reduce(jnp.maximum, tiles), axis=1, keepdims=True)
        if before is not None:
            top = jnp.maximum(top, before[a][0])
        weights = [jnp.exp2((tile - top) * EXP2_SCALE) for tile in tiles]
        tops.append(top)
        rows.append(jnp.concatenate([w.astype(jnp.bfloat16) for w in weights], 1))
    values = jnp.concatenate(values, 0)
    accum = jnp.dot(
        jnp.concatenate(rows, 0),
        jnp.concatenate([values, jnp.ones_like(values)], 1),
        preferred_element_type=jnp.float32,
    )
    states = []
    for a, top in enumerate(tops):
        part = accum[a * TILE : (a + 1) * TILE, :HEAD_DIM]
        total = accum[a * TILE : (a + 1) * TILE, HEAD_DIM:]
        if before is not None:
            factor = jnp.exp2((before[a][0] - top) * EXP2_SCALE)
            total, part = total + before[a][1] * factor, part + before[a][2] * factor
        states.append((top, total, part))
    return states


def normalized(state):
    return (state[2] / state[1]).astype(jnp.bfloat16)


def bias_where(attended):
    return jnp.where(attended, jnp.float32(0), jnp.float32(NEG_FLOOR))


def copy_pieces(pieces, sems):
    copies = [pltpu.make_async_copy(a, b, sems.at[i]) for i, (a, b) in enumerate(pieces)]
    for copy in copies:
        copy.start()
    for copy in copies:
        copy.wait()


def listed_places(plan, lists_ref, head, query_tile, place_of):
    first = query_tile * plan.entries
    listed = jnp.int32(0)
    places, biases = [], []
    for entry in range(plan.entries):
        place = place_of(lists_ref[first + entry, head])
        places.append(place)
        biases.append(bias_where((listed >> place) & 1 == 0))
        listed |= jnp.int32(1) << place
    return places, biases


def temporal_kernel(plan, table_ref, lists_ref, *rest):
    frames, slots = plan.frames, plan.slots
    by_step = [plan.steps(0).index(step) for step in range(frames)]
    tiles = [rest[i] for i in by_step]
    outs = [rest[frames + i] for i in by_step]
    frame, slot = table_ref[plan.frame_at], table_ref[plan.slot_at]

    def one_head(index, _):
        head = plan.head_at(0, table_ref, frame, index)
        biases = []
        for step in range(frames):
            first = ((frame ^ step) * slots + slot) * plan.entries
            listed = jnp.int32(0)
            for entry in range(plan.entries):
                listed |= jnp.int32(1) << (lists_ref[first + entry, head] // slots)
            biases.append(
                [bias_where((listed >> (frame ^ other)) & 1 == 1) for other in range(frames)]
            )
        states = attend_tiles(
            *([tile[index, i] for tile in tiles] for i in range(3)), biases, turned=False
        )
        for out_ref, state in zip(outs, states):
            out_ref[index] = normalized(state)
        return 0

    lax.fori_loop(0, plan.heads_in_group(0, table_ref, frame), one_head, 0)


def mixed_kernel(plan, count, table_ref, lists_ref, *rest):
    frames, slots = plan.frames, plan.slots
    tiles, gathered = rest[:frames], rest[frames : frames + slots]
    outs = rest[-4 - frames : -4]
    q_ref, kv_ref, result_ref, sems = rest[-4:]
    copy_pieces(
        [(tile.at[count - 1, 0], q_ref.at[step]) for step, tile in zip(plan.steps(0), tiles)]
        + [
            (block, kv_ref.at[pl.ds(step * frames, frames)])
            for step, block in zip((0, *reversed(range(1, slots))), gathered)
        ],
        sems,
    )
    frame, slot = table_ref[plan.frame_at], table_ref[plan.slot_at]
    head = plan.head_at(0, table_ref, frame, count - 1)

    def some_tiles(body, _):
        for step in (body * MIXED_TILES + more for more in range(MIXED_TILES)):
            places, biases = listed_places(
                plan,
                lists_ref,
                head,
                (frame ^ step) * slots + slot,
                lambda tile: (lax.rem(tile, slots) ^ slot) * frames + (tile // slots ^ frame),
            )
            (state,) = attend_tiles(
                [q_ref[step]],
                [kv_ref[place, 0, 0] for place in places],
                [kv_ref[place, 0, 1] for place in places],
                [biases],
            )
            result_ref[step] = normalized(state)
        return 0

    lax.fori_loop(0, frames // MIXED_TILES, some_tiles, 0)
    copy_pieces(
        [(result_ref.at[step], out.at[count - 1]) for step, out in zip(plan.steps(0), outs)], sems
    )


def spatial_biases(plan, table_ref, lists_ref, head, step, places):
    slots = plan.slots
    frame, slot = table_ref[plan.frame_at], table_ref[plan.slot_at]
    first = (frame * slots + (slot ^ step)) * plan.entries
    listed = jnp.int32(0)
    for entry in range(plan.entries):
        tile = lists_ref[first + entry, head]
        place = (tile // slots - frame + 1) * slots + (lax.rem(tile, slots) ^ slot)
        listed |= jnp.int32(1) << place
    return [bias_where((listed >> place) & 1 == 1) for place in places]


def own_frame_kernel(plan, table_ref, lists_ref, *rest):
    slots = plan.slots
    here, joined, outs = rest[:slots], rest[slots], rest[slots + 1 :]
    slot = table_ref[plan.slot_at]

    def one_head(index, _):
        head = plan.head_at(1, table_ref, slot, index)
        states = attend_tiles(
            [tile[index, 0] for tile in here],
            [joined[step, index, 0] for step in range(slots)],
            [joined[step, index, 1] for step in range(slots)],
            [
                spatial_biases(plan, table_ref, lists_ref, head, step, range(slots, 2 * slots))
                for step in range(slots)
            ],
        )
        for step, state in enumerate(states):
            for out_ref, value in zip(outs, state):
                out_ref[step, index] = jnp.broadcast_to(value, (TILE, HEAD_DIM))
        return 0

    lax.fori_loop(0, plan.heads_in_group(1, table_ref, slot), one_head, 0)


def halo_kernel(plan, steps, table_ref, lists_ref, *rest):
    slots, ways = plan.slots, len(steps)
    queries, (below, above) = rest[:ways], rest[ways : ways + 2]
    top_ref, total_ref, sum_ref = rest[ways + 2 : ways + 5]
    outs = rest[-ways:]
    slot = table_ref[plan.slot_at]
    places = [*range(slots), *range(2 * slots, 3 * slots)]

    def one_head(index, _):
        head = plan.head_at(1, table_ref, slot, index)
        states = attend_tiles(
            [query_ref[index, 0] for query_ref in queries],
            [ref[step, index, 0] for ref in (below, above) for step in range(slots)],
            [ref[step, index, 1] for ref in (below, above) for step in range(slots)],
            [spatial_biases(plan, table_ref, lists_ref, head, step, places) for step in steps],
            [
                (top_ref[step, index], total_ref[step, index], sum_ref[step, index])
                for step in steps
            ],
        )
        for out_ref, state in zip(outs, states):
            out_ref[index] = normalized(state)
        return 0

    lax.fori_loop(0, plan.heads_in_group(1, table_ref, slot), one_head, 0)


def unpack_kernel(plan, counts, table_ref, *rest):
    pieces, out_ref, sem = list(rest[:-2]), rest[-2], rest[-1]
    for kind, count in enumerate(counts):
        for step in plan.steps(kind):
            piece = pieces.pop(0)
            group = plan.group(kind, table_ref, step)

            def one(index, _, kind=kind, piece=piece, group=group):
                columns = head_columns(plan.head_at(kind, table_ref, group, index))
                pltpu.make_async_copy(piece.at[index], out_ref.at[:, columns], sem).start()
                return 0

            lax.fori_loop(0, plan.heads_in_group(kind, table_ref, group), one, 0)
            if kind == 0:
                filled = (count - 1) * plan.frames + group < table_ref[plan.mixed_at]
                lax.fori_loop(count - 1, count - 1 + filled.astype(jnp.int32), one, 0)
    wait_all(out_ref, sem)


SPACES = {"s": pltpu.SMEM, "v": pltpu.VMEM, "a": pl.ANY}


def call(kernel, outs, operands, places, out_place, scratch=(), flops=0, in_place=None):
    nbytes = sum(math.prod(o.shape) * 2 for o in outs) * 2
    return pl.pallas_call(
        kernel,
        out_shape=outs,
        in_specs=[pl.BlockSpec(memory_space=SPACES[c]) for c in places],
        out_specs=[pl.BlockSpec(memory_space=SPACES[c]) for c in out_place],
        scratch_shapes=list(scratch),
        input_output_aliases=in_place or {},
        compiler_params=pltpu.CompilerParams(vmem_limit_bytes=VMEM_LIMIT),
        cost_estimate=pl.CostEstimate(flops=flops, bytes_accessed=nbytes, transcendentals=0),
    )(*operands)


def after(arrays, others):
    if not arrays or not others:
        return arrays
    return pl.pallas_call(
        lambda *refs: None,
        out_shape=[jax.ShapeDtypeStruct(a.shape, a.dtype) for a in arrays],
        in_specs=[pl.BlockSpec(memory_space=pltpu.VMEM)] * (len(arrays) + len(others)),
        out_specs=[pl.BlockSpec(memory_space=pltpu.VMEM)] * len(arrays),
        input_output_aliases={i: i for i in range(len(arrays))},
        compiler_params=pltpu.CompilerParams(vmem_limit_bytes=VMEM_LIMIT),
    )(*arrays, *others)


def tiles_of(*lead):
    return jax.ShapeDtypeStruct((*lead, TILE, HEAD_DIM), jnp.bfloat16)


def by_kind(plan, t_count, s_count, queries, keys, values, lists, table):
    frames, slots = plan.frames, plan.slots
    pair_flops = 4 * TILE * TILE * HEAD_DIM

    def to_frame(array, step):
        pairs = [(z, z ^ step) for z in range(frames)]
        return array if step == 0 else lax.ppermute(array, "blk", pairs)

    def to_slot(array, step):
        pairs = [(s, s ^ step) for s in range(slots)]
        return array if step == 0 else lax.ppermute(array, MESH_TAIL, pairs)

    def halo(array, step):
        pairs = [(z, z + step) for z in range(frames) if 0 <= z + step < frames]
        return lax.ppermute(array, "blk", pairs)

    packed = call(
        functools.partial(pack_kernel, plan, (t_count, s_count)),
        [tiles_of(t_count, 3)] * frames + [tiles_of(s_count, 3)] * slots,
        (table, queries, keys, values),
        "saaa",
        "v" * (frames + slots),
        [pltpu.SemaphoreType.DMA((frames + slots,))],
    )
    arrived = [to_frame(block, step) for step, block in zip(plan.steps(0), packed[:frames])]
    here = [to_slot(block, step) for step, block in enumerate(packed[frames:])]
    (joined,) = call(
        functools.partial(join_kernel, plan, s_count),
        [tiles_of(slots, s_count, 2)],
        here,
        "v" * slots,
        "v",
        [pltpu.SemaphoreType.DMA((slots,))],
    )
    below, above = halo(joined, 1), halo(joined, -1)
    own_state = call(
        functools.partial(own_frame_kernel, plan),
        [jax.ShapeDtypeStruct((slots, s_count, TILE, HEAD_DIM), jnp.float32)] * 3,
        (table, lists, *here, joined),
        "ss" + "v" * (slots + 1),
        "vvv",
        flops=s_count * slots * slots * pair_flops,
    )
    (mixed,) = call(
        functools.partial(join_mixed_kernel, plan, t_count),
        [tiles_of(frames, 1, 2)],
        (*arrived, own_state[0]),
        "v" * (frames + 1),
        "v",
        [pltpu.SemaphoreType.DMA((frames,))],
    )
    attended = call(
        functools.partial(temporal_kernel, plan),
        [tiles_of(t_count)] * frames,
        (table, lists, *arrived),
        "ss" + "v" * frames,
        "v" * frames,
        flops=t_count * frames * frames * pair_flops,
    )
    gathered = {0: mixed}
    for bit in sorted((1 << n for n in range(slots.bit_length() - 1)), reverse=True):
        for step in list(gathered):
            block = after([gathered[step]], attended[:1])[0] if step else mixed
            gathered[step | bit] = to_slot(block, bit)
    gathered = [gathered[step] for step in (0, *reversed(range(1, slots)))]
    tiles_ahead = 2 * slots * s_count - 4 * frames - 3 * t_count // 2
    flops_ahead = max(tiles_ahead, 1) * 42 * pair_flops
    attended = call(
        functools.partial(mixed_kernel, plan, t_count),
        [tiles_of(t_count)] * frames,
        (table, lists, *arrived, *gathered, *attended),
        "ss" + "v" * (2 * frames + slots),
        "v" * frames,
        [
            pltpu.VMEM((frames, TILE, HEAD_DIM), jnp.bfloat16),
            pltpu.VMEM((slots * frames, 1, 2, TILE, HEAD_DIM), jnp.bfloat16),
            pltpu.VMEM((frames, TILE, HEAD_DIM), jnp.bfloat16),
            pltpu.SemaphoreType.DMA((frames + slots,)),
        ],
        flops=flops_ahead,
        in_place={2 + frames + slots + i: i for i in range(frames)},
    )
    attended = [attended[0], *after(attended[1:-1], (below, above)), attended[-1]]
    pieces = [to_frame(block, step) for step, block in zip(plan.steps(0), attended)]

    def attend_slots(steps, *earlier):
        return call(
            functools.partial(halo_kernel, plan, steps),
            [tiles_of(s_count)] * len(steps),
            (table, lists, *(here[step] for step in steps), below, above, *own_state, *earlier),
            "ss" + "v" * (len(steps) + 5 + len(earlier)),
            "v" * len(steps),
            flops=s_count * len(steps) * 2 * slots * pair_flops,
        )

    half = slots // 2
    away = attend_slots(range(half, slots))
    near = attend_slots(range(half), away[0])
    ahead = pieces[-1:] if t_count > s_count else pieces[1:]
    attended = [near[0], *after(near[1:], ahead), *away]
    pieces += [to_slot(block, step) for step, block in enumerate(attended)]
    (out,) = call(
        functools.partial(unpack_kernel, plan, (t_count, s_count)),
        [pltpu.HBM((TILE, plan.heads * HEAD_DIM), jnp.bfloat16)],
        (table, *pieces),
        "s" + "v" * len(pieces),
        "v",
        [pltpu.SemaphoreType.DMA],
    )
    return out


def capacities(heads, frames, slots):
    low, high = heads // 4, heads - heads // 4

    def chunks_for(fewest, most):
        over_frames = max(-(-most // frames), 1)
        shared = max(fewest, (over_frames - 1) * frames)
        left = heads - fewest - (over_frames * frames - shared)
        return over_frames, max(-(-left // slots), 1)

    pairs, begins = [(chunks_for(high + 1, heads)[0], chunks_for(0, low)[1])], []
    for t in range(low + 1, high + 1):
        if t % frames == 1 or t == low + 1:
            begins.append((t, len(pairs)))
            pairs.append(chunks_for(t, min(-(-t // frames) * frames, high)))
    return pairs, begins + [(high + 1, 0)]


def kind_plan(queries, keys, values, block_lists):
    heads, tiles, entries = block_lists.shape
    frames = lax.axis_size("blk")
    slots = lax.axis_size(MESH_TAIL)
    plan = Plan(heads, frames, slots, entries)
    pairs, begins = capacities(heads, frames, slots)
    by_tile = jnp.transpose(block_lists, (1, 2, 0))
    table, branch, *tensors = call(
        functools.partial(table_kernel, plan, pairs, begins),
        [jax.ShapeDtypeStruct((size,), jnp.int32) for size in (plan.table_size, 1)]
        + [jax.ShapeDtypeStruct(queries.shape, queries.dtype)] * 3,
        (
            by_tile,
            *(pltpu.with_memory_space_constraint(x, pltpu.HBM) for x in (queries, keys, values)),
        ),
        "vaaa",
        "ssvvv",
        [pltpu.SMEM((heads // 16,), jnp.int32), pltpu.SemaphoreType.DMA((3,))],
    )
    lists = by_tile.reshape(tiles * entries, heads)
    branches = [functools.partial(by_kind, plan, t, s) for t, s in pairs]
    return lax.switch(branch[0], branches, *tensors, lists, table)


def per_device(queries, keys, values, block_lists):
    slots = lax.axis_size(MESH_TAIL)
    whole_tiles = queries.shape[0] == TILE and slots == FRAME_TILES
    frames = lax.axis_size("blk")
    if whole_tiles and frames & (frames - 1) == 0 and frames * slots == block_lists.shape[1]:
        return kind_plan(queries, keys, values, block_lists)
    return gathered_plan(queries, keys, values, block_lists)


def solution(mesh):
    in_specs = (
        P(("grp", "blk", "head", "sub"), None),
        P(("grp", "blk", "head", "sub"), None),
        P(("grp", "blk", "head", "sub"), None),
        P(),
    )
    out_specs = P(("grp", "blk", "head", "sub"), None)
    return jax.shard_map(
        per_device, mesh=mesh, in_specs=in_specs, out_specs=out_specs, check_vma=False
    )
```

```python
import functools
import math

import jax
import jax.numpy as jnp
from jax import lax
from jax.experimental import pallas as pl
from jax.experimental.pallas import tpu as pltpu
from jax.sharding import PartitionSpec as P

HEADS = 32
HEAD_DIM = 128
TILE = 128
FRAME_TILES = 4


NEG_FLOOR = -1e30


def query_rows(block_lists, first_head, heads_here, query_tokens):
    tile_ids = jnp.arange(block_lists.shape[1], dtype=jnp.int32)
    lists_local = lax.dynamic_slice_in_dim(block_lists, first_head, heads_here, 0)
    tile_mask = jnp.any(lists_local[:, :, :, None] == tile_ids, axis=2).astype(jnp.bfloat16)
    query_onehot = ((query_tokens // TILE)[:, None] == tile_ids[None, :]).astype(jnp.bfloat16)
    listed = jnp.einsum("qi,hij->hqj", query_onehot, tile_mask, preferred_element_type=jnp.float32)
    return listed.astype(jnp.bfloat16)


def attend_block(state_now, key_block, value_block, allowed, query_local, score_scale):
    top_old, total_old, accum_old = state_now
    scores = (
        jnp.einsum("qhd,khd->hqk", query_local, key_block, preferred_element_type=jnp.float32)
        * score_scale
    )
    top_new = jnp.maximum(top_old, jnp.max(jnp.where(allowed, scores, NEG_FLOOR), axis=2))
    factor = jnp.exp(top_old - top_new)
    weights = jnp.where(allowed, jnp.exp(scores - top_new[:, :, None]), 0.0)
    total_new = total_old * factor + jnp.sum(weights, axis=2)
    product = jnp.einsum(
        "hqk,khd->qhd",
        weights.astype(jnp.bfloat16),
        value_block,
        preferred_element_type=jnp.float32,
    )
    accum_new = accum_old * jnp.transpose(factor)[:, :, None] + product
    return (top_new, total_new, accum_new)


def make_step(query_local, listed_rows, key_token, block_len, tile_total):
    score_scale = 1.0 / math.sqrt(HEAD_DIM)
    tile_ids = jnp.arange(tile_total, dtype=jnp.int32)

    def fold_step(state_now, piece, first_row):
        key_piece, value_piece = piece
        block_count = key_piece.shape[0] // block_len

        def one_block(block_index, state_in):
            key_block = lax.dynamic_slice_in_dim(key_piece, block_index * block_len, block_len, 0)
            value_block = lax.dynamic_slice_in_dim(
                value_piece, block_index * block_len, block_len, 0
            )
            positions = block_index * block_len + jnp.arange(block_len, dtype=jnp.int32)
            key_tiles = key_token(positions) // TILE
            key_onehot = (tile_ids[:, None] == key_tiles[None, :]).astype(jnp.bfloat16)
            allowed = (
                jnp.einsum(
                    "hqj,jk->hqk", listed_rows, key_onehot, preferred_element_type=jnp.float32
                )
                > 0.5
            )
            result = attend_block(
                state_in, key_block, value_block, allowed, query_local, score_scale
            )
            return result

        return lax.fori_loop(0, block_count, one_block, state_now)

    return fold_step


def start_state(heads_here, block_len):
    top_all = jnp.full((heads_here, block_len), NEG_FLOOR, jnp.float32)
    total_all = jnp.zeros((heads_here, block_len), jnp.float32)
    accum_all = jnp.zeros((block_len, heads_here, HEAD_DIM), jnp.float32)
    return (top_all, total_all, accum_all)


def normalize(state_end):
    top_all, total_all, accum_all = state_end
    return (accum_all / jnp.transpose(total_all)[:, :, None]).astype(jnp.bfloat16)


def gathered_plan(queries, keys, values, block_lists):
    row_count, col_count = queries.shape
    n_head = lax.axis_size("head")
    n_sub = lax.axis_size("sub")
    blk_index = lax.axis_index("blk")
    head_index = lax.axis_index("head")
    sub_index = lax.axis_index("sub")
    tile_total = block_lists.shape[1]
    heads_here = HEADS // (n_head * n_sub)
    block_len = row_count * n_head * n_sub

    def inward(tensor):
        return tensor.reshape(1, 1, row_count, n_head, n_sub, heads_here * HEAD_DIM)

    query_six, keys_six, values_six = (
        lax.all_to_all(
            lax.all_to_all(inward(queries), "head", split_axis=3, concat_axis=1, tiled=True),
            "sub",
            split_axis=4,
            concat_axis=0,
            tiled=True,
        ),
        lax.all_to_all(
            lax.all_to_all(inward(keys), "head", split_axis=3, concat_axis=1, tiled=True),
            "sub",
            split_axis=4,
            concat_axis=0,
            tiled=True,
        ),
        lax.all_to_all(
            lax.all_to_all(inward(values), "head", split_axis=3, concat_axis=1, tiled=True),
            "sub",
            split_axis=4,
            concat_axis=0,
            tiled=True,
        ),
    )
    query_local = query_six.reshape(block_len, heads_here, HEAD_DIM)
    keys_local = keys_six.reshape(block_len, heads_here, HEAD_DIM)
    values_local = values_six.reshape(block_len, heads_here, HEAD_DIM)

    def key_token(positions):
        source_dev = positions // block_len
        within = positions % block_len
        sub_source = within // (n_head * row_count)
        head_source = within // row_count % n_head
        offset = within % row_count
        return ((source_dev * n_head + head_source) * n_sub + sub_source) * row_count + offset

    query_tokens = key_token(blk_index * block_len + jnp.arange(block_len, dtype=jnp.int32))
    first_head = (head_index * n_sub + sub_index) * heads_here
    listed_rows = query_rows(block_lists, first_head, heads_here, query_tokens)
    fold_step = make_step(query_local, listed_rows, key_token, block_len, tile_total)
    state_end = fold_step(
        start_state(heads_here, block_len),
        (
            lax.all_gather(keys_local, "blk", axis=0, tiled=True),
            lax.all_gather(values_local, "blk", axis=0, tiled=True),
        ),
        jnp.int32(0),
    )
    result_rows = normalize(state_end)
    attended = result_rows.reshape(n_sub, n_head, row_count, 1, 1, heads_here * HEAD_DIM)
    returned = lax.all_to_all(
        lax.all_to_all(attended, "head", split_axis=1, concat_axis=3, tiled=True),
        "sub",
        split_axis=0,
        concat_axis=4,
        tiled=True,
    )
    return returned.reshape(row_count, col_count)


MESH_TAIL = ("head", "sub")
EXP2_SCALE = math.log2(math.e) / math.sqrt(HEAD_DIM)
VMEM_LIMIT = 16 * 1024 * 1024
MIXED_TILES = 2


class Plan:
    def __init__(self, heads, frames, slots, entries):
        self.heads, self.frames, self.slots, self.entries = heads, frames, slots, entries
        self.over_slots_at = heads
        self.pure_at = 2 * heads
        self.mixed_at = 2 * heads + 1
        self.spatial_at = 2 * heads + 2
        self.frame_at = 2 * heads + 3
        self.slot_at = 2 * heads + 4
        self.table_size = 2 * heads + 5

    def sizes(self, kind):
        return (self.frames, self.slots)[kind]

    def head_at(self, kind, table_ref, group, index):
        return table_ref[(0, self.over_slots_at)[kind] + index * self.sizes(kind) + group]

    def group(self, kind, table_ref, step):
        return table_ref[(self.frame_at, self.slot_at)[kind]] ^ step

    def heads_in_group(self, kind, table_ref, group):
        size = self.sizes(kind)
        return (table_ref[(self.pure_at, self.spatial_at)[kind]] - group + size - 1) // size

    def steps(self, kind):
        others = range(1, self.sizes(kind))
        return [0, *others] if kind else [0, *reversed(others)]


def head_columns(head):
    return pl.ds(pl.multiple_of(head * HEAD_DIM, HEAD_DIM), HEAD_DIM)


def table_kernel(plan, pairs, begins, lists_ref, *rest):
    table_ref, branch_ref, mask_ref, sems = rest[3], rest[4], rest[-2], rest[-1]
    copies = [pltpu.make_async_copy(rest[i], rest[5 + i], sems.at[i]) for i in range(3)]
    for copy in copies:
        copy.start()
    lists = lists_ref[...]
    tiles = lax.broadcasted_iota(jnp.int32, lists.shape, 0)
    other_slot = ((lists ^ tiles) & (plan.slots - 1)).astype(jnp.float32)
    spatial = jnp.sum(jnp.sum(other_slot, axis=0), axis=0, keepdims=True) > 0
    lanes = lax.broadcasted_iota(jnp.int32, spatial.shape, 1)
    for place in range(plan.heads // 16):
        bit = jnp.where(lanes // 16 == place, jnp.int32(1) << (lanes % 16), 0)
        bits = jnp.where(spatial, bit, 0).astype(jnp.float32)
        mask_ref[place] = jnp.sum(bits).astype(jnp.int32)
    spatial_total = jnp.sum(spatial.astype(jnp.float32)).astype(jnp.int32)
    temporal_total = plan.heads - spatial_total
    branch, chunks, last = 0, pairs[0][0], 0
    for first, place in begins:
        reached = (temporal_total >= first).astype(jnp.int32)
        branch += reached * (place - last)
        chunks += reached * (pairs[place][0] - pairs[last][0])
        last = place
    mixed = (chunks - 1) * plan.frames
    shared = lax.max(temporal_total, mixed)
    room = chunks * plan.frames - shared

    def clear(p, _):
        table_ref[p] = 0
        return 0

    def place_head(h, counts):
        kind = (mask_ref[h // 16] >> (h % 16)) & 1
        t_rank, s_rank = counts
        s_place = jnp.where(s_rank < room, shared + s_rank, plan.over_slots_at + s_rank - room)
        table_ref[jnp.where(kind == 1, s_place, t_rank)] = h
        return t_rank + 1 - kind, s_rank + kind

    lax.fori_loop(0, 2 * plan.heads, clear, 0)
    lax.fori_loop(0, plan.heads, place_head, (jnp.int32(0), jnp.int32(0)))
    table_ref[plan.pure_at] = lax.min(temporal_total, mixed)
    table_ref[plan.mixed_at] = shared + lax.min(spatial_total, room)
    table_ref[plan.spatial_at] = lax.max(spatial_total - room, 0)
    table_ref[plan.frame_at] = lax.axis_index("blk")
    n_sub = lax.axis_size("sub")
    table_ref[plan.slot_at] = lax.axis_index("head") * n_sub + lax.axis_index("sub")
    branch_ref[0] = branch
    for copy in copies:
        copy.wait()


def wait_all(ref, sem):
    pltpu.make_async_copy(ref, ref, sem).wait()


def pack_kernel(plan, counts, table_ref, q_ref, k_ref, v_ref, *rest):
    outs, sems = rest[:-1], rest[-1]
    steps = [(kind, step) for kind in range(2) for step in plan.steps(kind)]
    for sem, (kind, step) in enumerate(steps):
        group = plan.group(kind, table_ref, step)

        def one(index, _, kind=kind, group=group, sem=sem):
            columns = head_columns(plan.head_at(kind, table_ref, group, index))
            for place, ref in enumerate((q_ref, k_ref, v_ref)):
                pltpu.make_async_copy(
                    ref.at[:, columns], outs[sem].at[index, place], sems.at[sem]
                ).start()
            return 0

        lax.fori_loop(0, counts[kind], one, 0)
    for sem, out_ref in enumerate(outs):
        wait_all(out_ref, sems.at[sem])


def turn_keys(kv_ref, place, count):
    def turn(work, _):
        step, index = work // count, lax.rem(work, count)
        kv_ref[step, index, place] = kv_ref[step, index, place].T
        return 0

    lax.fori_loop(0, kv_ref.shape[0] * count, turn, 0)


def join_kernel(plan, count, *refs):
    pieces, out_ref, sems = refs[: plan.slots], refs[-2], refs[-1]
    copy_pieces(
        [(piece.at[:, pl.ds(1, 2)], out_ref.at[step]) for step, piece in enumerate(pieces)], sems
    )
    turn_keys(out_ref, 0, count)


def join_mixed_kernel(plan, count, *refs):
    pieces, out_ref, sems = refs[: plan.frames], refs[-2], refs[-1]
    copy_pieces(
        [
            (piece.at[count - 1, pl.ds(1, 2)], out_ref.at[step, 0])
            for step, piece in zip(plan.steps(0), pieces)
        ],
        sems,
    )
    turn_keys(out_ref, 0, 1)


def attend_tiles(queries, keys, values, biases, before=None, turned=True):
    scores = lax.dot_general(
        jnp.concatenate(queries, 0),
        jnp.concatenate(keys, 1 if turned else 0),
        (((1,), (0 if turned else 1,)), ((), ())),
        preferred_element_type=jnp.float32,
    )
    rows, tops = [], []
    for a, bias in enumerate(biases):
        tiles = [
            scores[a * TILE : (a + 1) * TILE, b * TILE : (b + 1) * TILE] + bias[b]
            for b in range(len(keys))
        ]
        top = jnp.max(functools.reduce(jnp.maximum, tiles), axis=1, keepdims=True)
        if before is not None:
            top = jnp.maximum(top, before[a][0])
        weights = [jnp.exp2((tile - top) * EXP2_SCALE) for tile in tiles]
        tops.append(top)
        rows.append(jnp.concatenate([w.astype(jnp.bfloat16) for w in weights], 1))
    values = jnp.concatenate(values, 0)
    accum = jnp.dot(
        jnp.concatenate(rows, 0),
        jnp.concatenate([values, jnp.ones_like(values)], 1),
        preferred_element_type=jnp.float32,
    )
    states = []
    for a, top in enumerate(tops):
        part = accum[a * TILE : (a + 1) * TILE, :HEAD_DIM]
        total = accum[a * TILE : (a + 1) * TILE, HEAD_DIM:]
        if before is not None:
            factor = jnp.exp2((before[a][0] - top) * EXP2_SCALE)
            total, part = total + before[a][1] * factor, part + before[a][2] * factor
        states.append((top, total, part))
    return states


def normalized(state):
    return (state[2] / state[1]).astype(jnp.bfloat16)


def bias_where(attended):
    return jnp.where(attended, jnp.float32(0), jnp.float32(NEG_FLOOR))


def copy_pieces(pieces, sems):
    copies = [pltpu.make_async_copy(a, b, sems.at[i]) for i, (a, b) in enumerate(pieces)]
    for copy in copies:
        copy.start()
    for copy in copies:
        copy.wait()


def listed_places(plan, lists_ref, head, query_tile, place_of):
    first = query_tile * plan.entries
    listed = jnp.int32(0)
    places, biases = [], []
    for entry in range(plan.entries):
        place = place_of(lists_ref[first + entry, head])
        places.append(place)
        biases.append(bias_where((listed >> place) & 1 == 0))
        listed |= jnp.int32(1) << place
    return places, biases


def temporal_kernel(plan, table_ref, lists_ref, *rest):
    frames, slots = plan.frames, plan.slots
    by_step = [plan.steps(0).index(step) for step in range(frames)]
    tiles = [rest[i] for i in by_step]
    outs = [rest[frames + i] for i in by_step]
    frame, slot = table_ref[plan.frame_at], table_ref[plan.slot_at]

    def one_head(index, _):
        head = plan.head_at(0, table_ref, frame, index)
        biases = []
        for step in range(frames):
            first = ((frame ^ step) * slots + slot) * plan.entries
            listed = jnp.int32(0)
            for entry in range(plan.entries):
                listed |= jnp.int32(1) << (lists_ref[first + entry, head] // slots)
            biases.append(
                [bias_where((listed >> (frame ^ other)) & 1 == 1) for other in range(frames)]
            )
        states = attend_tiles(
            *([tile[index, i] for tile in tiles] for i in range(3)), biases, turned=False
        )
        for out_ref, state in zip(outs, states):
            out_ref[index] = normalized(state)
        return 0

    lax.fori_loop(0, plan.heads_in_group(0, table_ref, frame), one_head, 0)


def mixed_kernel(plan, count, table_ref, lists_ref, *rest):
    frames, slots = plan.frames, plan.slots
    tiles, gathered = rest[:frames], rest[frames : frames + slots]
    outs = rest[-4 - frames : -4]
    q_ref, kv_ref, result_ref, sems = rest[-4:]
    copy_pieces(
        [(tile.at[count - 1, 0], q_ref.at[step]) for step, tile in zip(plan.steps(0), tiles)]
        + [
            (block, kv_ref.at[pl.ds(step * frames, frames)])
            for step, block in zip((0, *reversed(range(1, slots))), gathered)
        ],
        sems,
    )
    frame, slot = table_ref[plan.frame_at], table_ref[plan.slot_at]
    head = plan.head_at(0, table_ref, frame, count - 1)

    def some_tiles(body, _):
        for step in (body * MIXED_TILES + more for more in range(MIXED_TILES)):
            places, biases = listed_places(
                plan,
                lists_ref,
                head,
                (frame ^ step) * slots + slot,
                lambda tile: (lax.rem(tile, slots) ^ slot) * frames + (tile // slots ^ frame),
            )
            (state,) = attend_tiles(
                [q_ref[step]],
                [kv_ref[place, 0, 0] for place in places],
                [kv_ref[place, 0, 1] for place in places],
                [biases],
            )
            result_ref[step] = normalized(state)
        return 0

    lax.fori_loop(0, frames // MIXED_TILES, some_tiles, 0)
    copy_pieces(
        [(result_ref.at[step], out.at[count - 1]) for step, out in zip(plan.steps(0), outs)], sems
    )


def spatial_biases(plan, table_ref, lists_ref, head, step, places):
    slots = plan.slots
    frame, slot = table_ref[plan.frame_at], table_ref[plan.slot_at]
    first = (frame * slots + (slot ^ step)) * plan.entries
    listed = jnp.int32(0)
    for entry in range(plan.entries):
        tile = lists_ref[first + entry, head]
        place = (tile // slots - frame + 1) * slots + (lax.rem(tile, slots) ^ slot)
        listed |= jnp.int32(1) << place
    return [bias_where((listed >> place) & 1 == 1) for place in places]


def own_frame_kernel(plan, table_ref, lists_ref, *rest):
    slots = plan.slots
    here, joined, outs = rest[:slots], rest[slots], rest[slots + 1 :]
    slot = table_ref[plan.slot_at]

    def one_head(index, _):
        head = plan.head_at(1, table_ref, slot, index)
        states = attend_tiles(
            [tile[index, 0] for tile in here],
            [joined[step, index, 0] for step in range(slots)],
            [joined[step, index, 1] for step in range(slots)],
            [
                spatial_biases(plan, table_ref, lists_ref, head, step, range(slots, 2 * slots))
                for step in range(slots)
            ],
        )
        for step, state in enumerate(states):
            for out_ref, value in zip(outs, state):
                out_ref[step, index] = jnp.broadcast_to(value, (TILE, HEAD_DIM))
        return 0

    lax.fori_loop(0, plan.heads_in_group(1, table_ref, slot), one_head, 0)


def halo_kernel(plan, steps, at_once, table_ref, lists_ref, *rest):
    slots, ways = plan.slots, len(steps)
    queries, (below, above) = rest[:ways], rest[ways : ways + 2]
    top_ref, total_ref, sum_ref = rest[ways + 2 : ways + 5]
    outs = rest[-ways:]
    slot = table_ref[plan.slot_at]
    places = [*range(slots), *range(2 * slots, 3 * slots)]

    def one_head(index):
        head = plan.head_at(1, table_ref, slot, index)
        states = attend_tiles(
            [query_ref[index, 0] for query_ref in queries],
            [ref[step, index, 0] for ref in (below, above) for step in range(slots)],
            [ref[step, index, 1] for ref in (below, above) for step in range(slots)],
            [spatial_biases(plan, table_ref, lists_ref, head, step, places) for step in steps],
            [
                (top_ref[step, index], total_ref[step, index], sum_ref[step, index])
                for step in steps
            ],
        )
        for out_ref, state in zip(outs, states):
            out_ref[index] = normalized(state)

    heads_here = plan.heads_in_group(1, table_ref, slot)

    def some_heads(body, _):
        for more in range(at_once):
            one_head(lax.min(body * at_once + more, heads_here - 1))
        return 0

    lax.fori_loop(0, (heads_here + at_once - 1) // at_once, some_heads, 0)


def unpack_kernel(plan, counts, table_ref, *rest):
    pieces, out_ref, sem = list(rest[:-2]), rest[-2], rest[-1]
    for kind, count in enumerate(counts):
        for step in plan.steps(kind):
            piece = pieces.pop(0)
            group = plan.group(kind, table_ref, step)

            def one(index, _, kind=kind, piece=piece, group=group):
                columns = head_columns(plan.head_at(kind, table_ref, group, index))
                pltpu.make_async_copy(piece.at[index], out_ref.at[:, columns], sem).start()
                return 0

            lax.fori_loop(0, plan.heads_in_group(kind, table_ref, group), one, 0)
            if kind == 0:
                filled = (count - 1) * plan.frames + group < table_ref[plan.mixed_at]
                lax.fori_loop(count - 1, count - 1 + filled.astype(jnp.int32), one, 0)
    wait_all(out_ref, sem)


SPACES = {"s": pltpu.SMEM, "v": pltpu.VMEM, "a": pl.ANY}


def call(kernel, outs, operands, places, out_place, scratch=(), flops=0, in_place=None):
    nbytes = sum(math.prod(o.shape) * 2 for o in outs) * 2
    return pl.pallas_call(
        kernel,
        out_shape=outs,
        in_specs=[pl.BlockSpec(memory_space=SPACES[c]) for c in places],
        out_specs=[pl.BlockSpec(memory_space=SPACES[c]) for c in out_place],
        scratch_shapes=list(scratch),
        input_output_aliases=in_place or {},
        compiler_params=pltpu.CompilerParams(vmem_limit_bytes=VMEM_LIMIT),
        cost_estimate=pl.CostEstimate(flops=flops, bytes_accessed=nbytes, transcendentals=0),
    )(*operands)


def after(arrays, others):
    if not arrays or not others:
        return arrays
    return pl.pallas_call(
        lambda *refs: None,
        out_shape=[jax.ShapeDtypeStruct(a.shape, a.dtype) for a in arrays],
        in_specs=[pl.BlockSpec(memory_space=pltpu.VMEM)] * (len(arrays) + len(others)),
        out_specs=[pl.BlockSpec(memory_space=pltpu.VMEM)] * len(arrays),
        input_output_aliases={i: i for i in range(len(arrays))},
        compiler_params=pltpu.CompilerParams(vmem_limit_bytes=VMEM_LIMIT),
    )(*arrays, *others)


def tiles_of(*lead):
    return jax.ShapeDtypeStruct((*lead, TILE, HEAD_DIM), jnp.bfloat16)


def by_kind(plan, t_count, s_count, queries, keys, values, lists, table):
    frames, slots = plan.frames, plan.slots
    pair_flops = 4 * TILE * TILE * HEAD_DIM

    def to_frame(array, step):
        pairs = [(z, z ^ step) for z in range(frames)]
        return array if step == 0 else lax.ppermute(array, "blk", pairs)

    def to_slot(array, step):
        pairs = [(s, s ^ step) for s in range(slots)]
        return array if step == 0 else lax.ppermute(array, MESH_TAIL, pairs)

    def halo(array, step):
        pairs = [(z, z + step) for z in range(frames) if 0 <= z + step < frames]
        return lax.ppermute(array, "blk", pairs)

    packed = call(
        functools.partial(pack_kernel, plan, (t_count, s_count)),
        [tiles_of(t_count, 3)] * frames + [tiles_of(s_count, 3)] * slots,
        (table, queries, keys, values),
        "saaa",
        "v" * (frames + slots),
        [pltpu.SemaphoreType.DMA((frames + slots,))],
    )
    arrived = [to_frame(block, step) for step, block in zip(plan.steps(0), packed[:frames])]
    here = [to_slot(block, step) for step, block in enumerate(packed[frames:])]
    (joined,) = call(
        functools.partial(join_kernel, plan, s_count),
        [tiles_of(slots, s_count, 2)],
        here,
        "v" * slots,
        "v",
        [pltpu.SemaphoreType.DMA((slots,))],
    )
    below, above = halo(joined, 1), halo(joined, -1)
    own_state = call(
        functools.partial(own_frame_kernel, plan),
        [jax.ShapeDtypeStruct((slots, s_count, TILE, HEAD_DIM), jnp.float32)] * 3,
        (table, lists, *here, joined),
        "ss" + "v" * (slots + 1),
        "vvv",
        flops=s_count * slots * slots * pair_flops,
    )
    (mixed,) = call(
        functools.partial(join_mixed_kernel, plan, t_count),
        [tiles_of(frames, 1, 2)],
        (*arrived, own_state[0]),
        "v" * (frames + 1),
        "v",
        [pltpu.SemaphoreType.DMA((frames,))],
    )
    attended = call(
        functools.partial(temporal_kernel, plan),
        [tiles_of(t_count)] * frames,
        (table, lists, *arrived),
        "ss" + "v" * frames,
        "v" * frames,
        flops=t_count * frames * frames * pair_flops,
    )
    gathered = {0: mixed}
    for bit in sorted((1 << n for n in range(slots.bit_length() - 1)), reverse=True):
        for step in list(gathered):
            block = after([gathered[step]], attended[:1])[0] if step else mixed
            gathered[step | bit] = to_slot(block, bit)
    gathered = [gathered[step] for step in (0, *reversed(range(1, slots)))]
    tiles_ahead = 2 * slots * s_count - 4 * frames - 3 * t_count // 2
    flops_ahead = max(tiles_ahead, 1) * 42 * pair_flops
    attended = call(
        functools.partial(mixed_kernel, plan, t_count),
        [tiles_of(t_count)] * frames,
        (table, lists, *arrived, *gathered, *attended),
        "ss" + "v" * (2 * frames + slots),
        "v" * frames,
        [
            pltpu.VMEM((frames, TILE, HEAD_DIM), jnp.bfloat16),
            pltpu.VMEM((slots * frames, 1, 2, TILE, HEAD_DIM), jnp.bfloat16),
            pltpu.VMEM((frames, TILE, HEAD_DIM), jnp.bfloat16),
            pltpu.SemaphoreType.DMA((frames + slots,)),
        ],
        flops=flops_ahead,
        in_place={2 + frames + slots + i: i for i in range(frames)},
    )
    attended = [attended[0], *after(attended[1:-1], (below, above)), attended[-1]]
    pieces = [to_frame(block, step) for step, block in zip(plan.steps(0), attended)]

    def attend_slots(steps, *earlier):
        return call(
            functools.partial(halo_kernel, plan, steps, 1 if earlier else 2),
            [tiles_of(s_count)] * len(steps),
            (table, lists, *(here[step] for step in steps), below, above, *own_state, *earlier),
            "ss" + "v" * (len(steps) + 5 + len(earlier)),
            "v" * len(steps),
            flops=s_count * len(steps) * 2 * slots * pair_flops,
        )

    half = slots // 2
    away = attend_slots(range(half, slots))
    near = attend_slots(range(half), away[0])
    ahead = pieces[-1:] if t_count > s_count else pieces[1:]
    attended = [near[0], *after(near[1:], ahead), *away]
    pieces += [to_slot(block, step) for step, block in enumerate(attended)]
    (out,) = call(
        functools.partial(unpack_kernel, plan, (t_count, s_count)),
        [pltpu.HBM((TILE, plan.heads * HEAD_DIM), jnp.bfloat16)],
        (table, *pieces),
        "s" + "v" * len(pieces),
        "v",
        [pltpu.SemaphoreType.DMA],
    )
    return out


def capacities(heads, frames, slots):
    low, high = heads // 4, heads - heads // 4

    def chunks_for(fewest, most):
        over_frames = max(-(-most // frames), 1)
        shared = max(fewest, (over_frames - 1) * frames)
        left = heads - fewest - (over_frames * frames - shared)
        return over_frames, max(-(-left // slots), 1)

    pairs, begins = [(chunks_for(high + 1, heads)[0], chunks_for(0, low)[1])], []
    for t in range(low + 1, high + 1):
        if t % frames == 1 or t == low + 1:
            begins.append((t, len(pairs)))
            pairs.append(chunks_for(t, min(-(-t // frames) * frames, high)))
    return pairs, begins + [(high + 1, 0)]


def kind_plan(queries, keys, values, block_lists):
    heads, tiles, entries = block_lists.shape
    frames = lax.axis_size("blk")
    slots = lax.axis_size(MESH_TAIL)
    plan = Plan(heads, frames, slots, entries)
    pairs, begins = capacities(heads, frames, slots)
    by_tile = jnp.transpose(block_lists, (1, 2, 0))
    table, branch, *tensors = call(
        functools.partial(table_kernel, plan, pairs, begins),
        [jax.ShapeDtypeStruct((size,), jnp.int32) for size in (plan.table_size, 1)]
        + [jax.ShapeDtypeStruct(queries.shape, queries.dtype)] * 3,
        (
            by_tile,
            *(pltpu.with_memory_space_constraint(x, pltpu.HBM) for x in (queries, keys, values)),
        ),
        "vaaa",
        "ssvvv",
        [pltpu.SMEM((heads // 16,), jnp.int32), pltpu.SemaphoreType.DMA((3,))],
    )
    lists = by_tile.reshape(tiles * entries, heads)
    branches = [functools.partial(by_kind, plan, t, s) for t, s in pairs]
    return lax.switch(branch[0], branches, *tensors, lists, table)


def per_device(queries, keys, values, block_lists):
    slots = lax.axis_size(MESH_TAIL)
    whole_tiles = queries.shape[0] == TILE and slots == FRAME_TILES
    frames = lax.axis_size("blk")
    if whole_tiles and frames & (frames - 1) == 0 and frames * slots == block_lists.shape[1]:
        return kind_plan(queries, keys, values, block_lists)
    return gathered_plan(queries, keys, values, block_lists)


def solution(mesh):
    in_specs = (
        P(("grp", "blk", "head", "sub"), None),
        P(("grp", "blk", "head", "sub"), None),
        P(("grp", "blk", "head", "sub"), None),
        P(),
    )
    out_specs = P(("grp", "blk", "head", "sub"), None)
    return jax.shard_map(
        per_device, mesh=mesh, in_specs=in_specs, out_specs=out_specs, check_vma=False
    )
```

```python
import functools
import math

import jax
import jax.numpy as jnp
from jax import lax
from jax.experimental import pallas as pl
from jax.experimental.pallas import tpu as pltpu
from jax.sharding import PartitionSpec as P

HEADS = 32
HEAD_DIM = 128
TILE = 128
FRAME_TILES = 4


NEG_FLOOR = -1e30


def query_rows(block_lists, first_head, heads_here, query_tokens):
    tile_ids = jnp.arange(block_lists.shape[1], dtype=jnp.int32)
    lists_local = lax.dynamic_slice_in_dim(block_lists, first_head, heads_here, 0)
    tile_mask = jnp.any(lists_local[:, :, :, None] == tile_ids, axis=2).astype(jnp.bfloat16)
    query_onehot = ((query_tokens // TILE)[:, None] == tile_ids[None, :]).astype(jnp.bfloat16)
    listed = jnp.einsum("qi,hij->hqj", query_onehot, tile_mask, preferred_element_type=jnp.float32)
    return listed.astype(jnp.bfloat16)


def attend_block(state_now, key_block, value_block, allowed, query_local, score_scale):
    top_old, total_old, accum_old = state_now
    scores = (
        jnp.einsum("qhd,khd->hqk", query_local, key_block, preferred_element_type=jnp.float32)
        * score_scale
    )
    top_new = jnp.maximum(top_old, jnp.max(jnp.where(allowed, scores, NEG_FLOOR), axis=2))
    factor = jnp.exp(top_old - top_new)
    weights = jnp.where(allowed, jnp.exp(scores - top_new[:, :, None]), 0.0)
    total_new = total_old * factor + jnp.sum(weights, axis=2)
    product = jnp.einsum(
        "hqk,khd->qhd",
        weights.astype(jnp.bfloat16),
        value_block,
        preferred_element_type=jnp.float32,
    )
    accum_new = accum_old * jnp.transpose(factor)[:, :, None] + product
    return (top_new, total_new, accum_new)


def make_step(query_local, listed_rows, key_token, block_len, tile_total):
    score_scale = 1.0 / math.sqrt(HEAD_DIM)
    tile_ids = jnp.arange(tile_total, dtype=jnp.int32)

    def fold_step(state_now, piece, first_row):
        key_piece, value_piece = piece
        block_count = key_piece.shape[0] // block_len

        def one_block(block_index, state_in):
            key_block = lax.dynamic_slice_in_dim(key_piece, block_index * block_len, block_len, 0)
            value_block = lax.dynamic_slice_in_dim(
                value_piece, block_index * block_len, block_len, 0
            )
            positions = block_index * block_len + jnp.arange(block_len, dtype=jnp.int32)
            key_tiles = key_token(positions) // TILE
            key_onehot = (tile_ids[:, None] == key_tiles[None, :]).astype(jnp.bfloat16)
            allowed = (
                jnp.einsum(
                    "hqj,jk->hqk", listed_rows, key_onehot, preferred_element_type=jnp.float32
                )
                > 0.5
            )
            result = attend_block(
                state_in, key_block, value_block, allowed, query_local, score_scale
            )
            return result

        return lax.fori_loop(0, block_count, one_block, state_now)

    return fold_step


def start_state(heads_here, block_len):
    top_all = jnp.full((heads_here, block_len), NEG_FLOOR, jnp.float32)
    total_all = jnp.zeros((heads_here, block_len), jnp.float32)
    accum_all = jnp.zeros((block_len, heads_here, HEAD_DIM), jnp.float32)
    return (top_all, total_all, accum_all)


def normalize(state_end):
    top_all, total_all, accum_all = state_end
    return (accum_all / jnp.transpose(total_all)[:, :, None]).astype(jnp.bfloat16)


def gathered_plan(queries, keys, values, block_lists):
    row_count, col_count = queries.shape
    n_head = lax.axis_size("head")
    n_sub = lax.axis_size("sub")
    blk_index = lax.axis_index("blk")
    head_index = lax.axis_index("head")
    sub_index = lax.axis_index("sub")
    tile_total = block_lists.shape[1]
    heads_here = HEADS // (n_head * n_sub)
    block_len = row_count * n_head * n_sub

    def inward(tensor):
        return tensor.reshape(1, 1, row_count, n_head, n_sub, heads_here * HEAD_DIM)

    query_six, keys_six, values_six = (
        lax.all_to_all(
            lax.all_to_all(inward(queries), "head", split_axis=3, concat_axis=1, tiled=True),
            "sub",
            split_axis=4,
            concat_axis=0,
            tiled=True,
        ),
        lax.all_to_all(
            lax.all_to_all(inward(keys), "head", split_axis=3, concat_axis=1, tiled=True),
            "sub",
            split_axis=4,
            concat_axis=0,
            tiled=True,
        ),
        lax.all_to_all(
            lax.all_to_all(inward(values), "head", split_axis=3, concat_axis=1, tiled=True),
            "sub",
            split_axis=4,
            concat_axis=0,
            tiled=True,
        ),
    )
    query_local = query_six.reshape(block_len, heads_here, HEAD_DIM)
    keys_local = keys_six.reshape(block_len, heads_here, HEAD_DIM)
    values_local = values_six.reshape(block_len, heads_here, HEAD_DIM)

    def key_token(positions):
        source_dev = positions // block_len
        within = positions % block_len
        sub_source = within // (n_head * row_count)
        head_source = within // row_count % n_head
        offset = within % row_count
        return ((source_dev * n_head + head_source) * n_sub + sub_source) * row_count + offset

    query_tokens = key_token(blk_index * block_len + jnp.arange(block_len, dtype=jnp.int32))
    first_head = (head_index * n_sub + sub_index) * heads_here
    listed_rows = query_rows(block_lists, first_head, heads_here, query_tokens)
    fold_step = make_step(query_local, listed_rows, key_token, block_len, tile_total)
    state_end = fold_step(
        start_state(heads_here, block_len),
        (
            lax.all_gather(keys_local, "blk", axis=0, tiled=True),
            lax.all_gather(values_local, "blk", axis=0, tiled=True),
        ),
        jnp.int32(0),
    )
    result_rows = normalize(state_end)
    attended = result_rows.reshape(n_sub, n_head, row_count, 1, 1, heads_here * HEAD_DIM)
    returned = lax.all_to_all(
        lax.all_to_all(attended, "head", split_axis=1, concat_axis=3, tiled=True),
        "sub",
        split_axis=0,
        concat_axis=4,
        tiled=True,
    )
    return returned.reshape(row_count, col_count)


MESH_TAIL = ("head", "sub")
EXP2_SCALE = math.log2(math.e) / math.sqrt(HEAD_DIM)
VMEM_LIMIT = 16 * 1024 * 1024
MIXED_TILES = 2


class Plan:
    def __init__(self, heads, frames, slots, entries):
        self.heads, self.frames, self.slots, self.entries = heads, frames, slots, entries
        self.over_slots_at = heads
        self.pure_at = 2 * heads
        self.mixed_at = 2 * heads + 1
        self.spatial_at = 2 * heads + 2
        self.frame_at = 2 * heads + 3
        self.slot_at = 2 * heads + 4
        self.table_size = 2 * heads + 5

    def sizes(self, kind):
        return (self.frames, self.slots)[kind]

    def head_at(self, kind, table_ref, group, index):
        return table_ref[(0, self.over_slots_at)[kind] + index * self.sizes(kind) + group]

    def group(self, kind, table_ref, step):
        return table_ref[(self.frame_at, self.slot_at)[kind]] ^ step

    def heads_in_group(self, kind, table_ref, group):
        size = self.sizes(kind)
        return (table_ref[(self.pure_at, self.spatial_at)[kind]] - group + size - 1) // size

    def steps(self, kind):
        others = range(1, self.sizes(kind))
        return [0, *others] if kind else [0, *reversed(others)]


def head_columns(head):
    return pl.ds(pl.multiple_of(head * HEAD_DIM, HEAD_DIM), HEAD_DIM)


def table_kernel(plan, pairs, begins, lists_ref, table_ref, branch_ref, mask_ref):
    lists = lists_ref[...]
    tiles = lax.broadcasted_iota(jnp.int32, lists.shape, 0)
    other_slot = ((lists ^ tiles) & (plan.slots - 1)).astype(jnp.float32)
    spatial = jnp.sum(jnp.sum(other_slot, axis=0), axis=0, keepdims=True) > 0
    lanes = lax.broadcasted_iota(jnp.int32, spatial.shape, 1)
    for place in range(plan.heads // 16):
        bit = jnp.where(lanes // 16 == place, jnp.int32(1) << (lanes % 16), 0)
        bits = jnp.where(spatial, bit, 0).astype(jnp.float32)
        mask_ref[place] = jnp.sum(bits).astype(jnp.int32)
    spatial_total = jnp.sum(spatial.astype(jnp.float32)).astype(jnp.int32)
    temporal_total = plan.heads - spatial_total
    branch, chunks, last = 0, pairs[0][0], 0
    for first, place in begins:
        reached = (temporal_total >= first).astype(jnp.int32)
        branch += reached * (place - last)
        chunks += reached * (pairs[place][0] - pairs[last][0])
        last = place
    mixed = (chunks - 1) * plan.frames
    shared = lax.max(temporal_total, mixed)
    room = chunks * plan.frames - shared

    def clear(p, _):
        for more in range(8):
            table_ref[8 * p + more] = 0
        return 0

    def place_heads(first, counts):
        t_rank, s_rank = counts
        for h in (4 * first + more for more in range(4)):
            kind = (mask_ref[h // 16] >> (h % 16)) & 1
            s_place = jnp.where(s_rank < room, shared + s_rank, plan.over_slots_at + s_rank - room)
            table_ref[jnp.where(kind == 1, s_place, t_rank)] = h
            t_rank, s_rank = t_rank + 1 - kind, s_rank + kind
        return t_rank, s_rank

    lax.fori_loop(0, plan.heads // 4, clear, 0)
    lax.fori_loop(0, plan.heads // 4, place_heads, (jnp.int32(0), jnp.int32(0)))
    table_ref[plan.pure_at] = lax.min(temporal_total, mixed)
    table_ref[plan.mixed_at] = shared + lax.min(spatial_total, room)
    table_ref[plan.spatial_at] = lax.max(spatial_total - room, 0)
    table_ref[plan.frame_at] = lax.axis_index("blk")
    n_sub = lax.axis_size("sub")
    table_ref[plan.slot_at] = lax.axis_index("head") * n_sub + lax.axis_index("sub")
    branch_ref[0] = branch


def wait_all(ref, sem):
    pltpu.make_async_copy(ref, ref, sem).wait()


def pack_kernel(plan, counts, table_ref, q_ref, k_ref, v_ref, *rest):
    outs, sems = rest[:-1], rest[-1]
    steps = [(kind, step) for kind in range(2) for step in plan.steps(kind)]
    for sem, (kind, step) in enumerate(steps):
        group = plan.group(kind, table_ref, step)

        def one(index, _, kind=kind, group=group, sem=sem):
            columns = head_columns(plan.head_at(kind, table_ref, group, index))
            for place, ref in enumerate((q_ref, k_ref, v_ref)):
                pltpu.make_async_copy(
                    ref.at[:, columns], outs[sem].at[index, place], sems.at[sem]
                ).start()
            return 0

        lax.fori_loop(0, counts[kind], one, 0)
    for sem, out_ref in enumerate(outs):
        wait_all(out_ref, sems.at[sem])


def turn_keys(kv_ref, place, count):
    def turn(work, _):
        step, index = work // count, lax.rem(work, count)
        kv_ref[step, index, place] = kv_ref[step, index, place].T
        return 0

    lax.fori_loop(0, kv_ref.shape[0] * count, turn, 0)


def join_kernel(plan, count, *refs):
    pieces, out_ref, sems = refs[: plan.slots], refs[-2], refs[-1]
    copy_pieces(
        [(piece.at[:, pl.ds(1, 2)], out_ref.at[step]) for step, piece in enumerate(pieces)], sems
    )
    turn_keys(out_ref, 0, count)


def join_mixed_kernel(plan, count, *refs):
    pieces, out_ref, sems = refs[: plan.frames], refs[-2], refs[-1]
    copy_pieces(
        [
            (piece.at[count - 1, pl.ds(1, 2)], out_ref.at[step, 0])
            for step, piece in zip(plan.steps(0), pieces)
        ],
        sems,
    )
    turn_keys(out_ref, 0, 1)


def attend_tiles(queries, keys, values, biases, before=None, turned=True):
    scores = lax.dot_general(
        jnp.concatenate(queries, 0),
        jnp.concatenate(keys, 1 if turned else 0),
        (((1,), (0 if turned else 1,)), ((), ())),
        preferred_element_type=jnp.float32,
    )
    rows, tops = [], []
    for a, bias in enumerate(biases):
        tiles = [
            scores[a * TILE : (a + 1) * TILE, b * TILE : (b + 1) * TILE] + bias[b]
            for b in range(len(keys))
        ]
        top = jnp.max(functools.reduce(jnp.maximum, tiles), axis=1, keepdims=True)
        if before is not None:
            top = jnp.maximum(top, before[a][0])
        weights = [jnp.exp2((tile - top) * EXP2_SCALE) for tile in tiles]
        tops.append(top)
        rows.append(jnp.concatenate([w.astype(jnp.bfloat16) for w in weights], 1))
    values = jnp.concatenate(values, 0)
    accum = jnp.dot(
        jnp.concatenate(rows, 0),
        jnp.concatenate([values, jnp.ones_like(values)], 1),
        preferred_element_type=jnp.float32,
    )
    states = []
    for a, top in enumerate(tops):
        part = accum[a * TILE : (a + 1) * TILE, :HEAD_DIM]
        total = accum[a * TILE : (a + 1) * TILE, HEAD_DIM:]
        if before is not None:
            factor = jnp.exp2((before[a][0] - top) * EXP2_SCALE)
            total, part = total + before[a][1] * factor, part + before[a][2] * factor
        states.append((top, total, part))
    return states


def normalized(state):
    return (state[2] / state[1]).astype(jnp.bfloat16)


def bias_where(attended):
    return jnp.where(attended, jnp.float32(0), jnp.float32(NEG_FLOOR))


def copy_pieces(pieces, sems):
    copies = [pltpu.make_async_copy(a, b, sems.at[i]) for i, (a, b) in enumerate(pieces)]
    for copy in copies:
        copy.start()
    for copy in copies:
        copy.wait()


def listed_places(plan, lists_ref, head, query_tile, place_of):
    first = query_tile * plan.entries
    listed = jnp.int32(0)
    places, biases = [], []
    for entry in range(plan.entries):
        place = place_of(lists_ref[first + entry, head])
        places.append(place)
        biases.append(bias_where((listed >> place) & 1 == 0))
        listed |= jnp.int32(1) << place
    return places, biases


def temporal_kernel(plan, table_ref, lists_ref, *rest):
    frames, slots = plan.frames, plan.slots
    by_step = [plan.steps(0).index(step) for step in range(frames)]
    tiles = [rest[i] for i in by_step]
    outs = [rest[frames + i] for i in by_step]
    frame, slot = table_ref[plan.frame_at], table_ref[plan.slot_at]

    def one_head(index, _):
        head = plan.head_at(0, table_ref, frame, index)
        biases = []
        for step in range(frames):
            first = ((frame ^ step) * slots + slot) * plan.entries
            listed = jnp.int32(0)
            for entry in range(plan.entries):
                listed |= jnp.int32(1) << (lists_ref[first + entry, head] // slots)
            biases.append(
                [bias_where((listed >> (frame ^ other)) & 1 == 1) for other in range(frames)]
            )
        states = attend_tiles(
            *([tile[index, i] for tile in tiles] for i in range(3)), biases, turned=False
        )
        for out_ref, state in zip(outs, states):
            out_ref[index] = normalized(state)
        return 0

    lax.fori_loop(0, plan.heads_in_group(0, table_ref, frame), one_head, 0)


def mixed_kernel(plan, count, table_ref, lists_ref, *rest):
    frames, slots = plan.frames, plan.slots
    tiles, gathered = rest[:frames], rest[frames : frames + slots]
    outs = rest[-4 - frames : -4]
    q_ref, kv_ref, result_ref, sems = rest[-4:]
    copy_pieces(
        [(tile.at[count - 1, 0], q_ref.at[step]) for step, tile in zip(plan.steps(0), tiles)]
        + [
            (block, kv_ref.at[pl.ds(step * frames, frames)])
            for step, block in zip((0, *reversed(range(1, slots))), gathered)
        ],
        sems,
    )
    frame, slot = table_ref[plan.frame_at], table_ref[plan.slot_at]
    head = plan.head_at(0, table_ref, frame, count - 1)

    def some_tiles(body, _):
        for step in (body * MIXED_TILES + more for more in range(MIXED_TILES)):
            places, biases = listed_places(
                plan,
                lists_ref,
                head,
                (frame ^ step) * slots + slot,
                lambda tile: (lax.rem(tile, slots) ^ slot) * frames + (tile // slots ^ frame),
            )
            (state,) = attend_tiles(
                [q_ref[step]],
                [kv_ref[place, 0, 0] for place in places],
                [kv_ref[place, 0, 1] for place in places],
                [biases],
            )
            result_ref[step] = normalized(state)
        return 0

    lax.fori_loop(0, frames // MIXED_TILES, some_tiles, 0)
    copy_pieces(
        [(result_ref.at[step], out.at[count - 1]) for step, out in zip(plan.steps(0), outs)], sems
    )


def spatial_biases(plan, table_ref, lists_ref, head, step, places):
    slots = plan.slots
    frame, slot = table_ref[plan.frame_at], table_ref[plan.slot_at]
    first = (frame * slots + (slot ^ step)) * plan.entries
    listed = jnp.int32(0)
    for entry in range(plan.entries):
        tile = lists_ref[first + entry, head]
        place = (tile // slots - frame + 1) * slots + (lax.rem(tile, slots) ^ slot)
        listed |= jnp.int32(1) << place
    return [bias_where((listed >> place) & 1 == 1) for place in places]


def own_frame_kernel(plan, table_ref, lists_ref, *rest):
    slots = plan.slots
    here, joined, outs = rest[:slots], rest[slots], rest[slots + 1 :]
    slot = table_ref[plan.slot_at]

    def one_head(index, _):
        head = plan.head_at(1, table_ref, slot, index)
        states = attend_tiles(
            [tile[index, 0] for tile in here],
            [joined[step, index, 0] for step in range(slots)],
            [joined[step, index, 1] for step in range(slots)],
            [
                spatial_biases(plan, table_ref, lists_ref, head, step, range(slots, 2 * slots))
                for step in range(slots)
            ],
        )
        for step, state in enumerate(states):
            for out_ref, value in zip(outs, state):
                out_ref[step, index] = jnp.broadcast_to(value, (TILE, HEAD_DIM))
        return 0

    lax.fori_loop(0, plan.heads_in_group(1, table_ref, slot), one_head, 0)


def halo_kernel(plan, steps, at_once, table_ref, lists_ref, *rest):
    slots, ways = plan.slots, len(steps)
    queries, (below, above) = rest[:ways], rest[ways : ways + 2]
    top_ref, total_ref, sum_ref = rest[ways + 2 : ways + 5]
    outs = rest[-ways:]
    slot = table_ref[plan.slot_at]
    places = [*range(slots), *range(2 * slots, 3 * slots)]

    def one_head(index):
        head = plan.head_at(1, table_ref, slot, index)
        states = attend_tiles(
            [query_ref[index, 0] for query_ref in queries],
            [ref[step, index, 0] for ref in (below, above) for step in range(slots)],
            [ref[step, index, 1] for ref in (below, above) for step in range(slots)],
            [spatial_biases(plan, table_ref, lists_ref, head, step, places) for step in steps],
            [
                (top_ref[step, index], total_ref[step, index], sum_ref[step, index])
                for step in steps
            ],
        )
        for out_ref, state in zip(outs, states):
            out_ref[index] = normalized(state)

    heads_here = plan.heads_in_group(1, table_ref, slot)

    def some_heads(body, _):
        for more in range(at_once):
            one_head(lax.min(body * at_once + more, heads_here - 1))
        return 0

    lax.fori_loop(0, (heads_here + at_once - 1) // at_once, some_heads, 0)


def unpack_kernel(plan, counts, table_ref, *rest):
    pieces, out_ref, sem = list(rest[:-2]), rest[-2], rest[-1]
    for kind, count in enumerate(counts):
        for step in plan.steps(kind):
            piece = pieces.pop(0)
            group = plan.group(kind, table_ref, step)

            def one(index, _, kind=kind, piece=piece, group=group):
                columns = head_columns(plan.head_at(kind, table_ref, group, index))
                pltpu.make_async_copy(piece.at[index], out_ref.at[:, columns], sem).start()
                return 0

            lax.fori_loop(0, plan.heads_in_group(kind, table_ref, group), one, 0)
            if kind == 0:
                filled = (count - 1) * plan.frames + group < table_ref[plan.mixed_at]
                lax.fori_loop(count - 1, count - 1 + filled.astype(jnp.int32), one, 0)
    wait_all(out_ref, sem)


SPACES = {"s": pltpu.SMEM, "v": pltpu.VMEM, "a": pl.ANY}


def call(kernel, outs, operands, places, out_place, scratch=(), flops=0, in_place=None):
    nbytes = sum(math.prod(o.shape) * 2 for o in outs) * 2
    return pl.pallas_call(
        kernel,
        out_shape=outs,
        in_specs=[pl.BlockSpec(memory_space=SPACES[c]) for c in places],
        out_specs=[pl.BlockSpec(memory_space=SPACES[c]) for c in out_place],
        scratch_shapes=list(scratch),
        input_output_aliases=in_place or {},
        compiler_params=pltpu.CompilerParams(vmem_limit_bytes=VMEM_LIMIT),
        cost_estimate=pl.CostEstimate(flops=flops, bytes_accessed=nbytes, transcendentals=0),
    )(*operands)


def after(arrays, others):
    if not arrays or not others:
        return arrays
    return pl.pallas_call(
        lambda *refs: None,
        out_shape=[jax.ShapeDtypeStruct(a.shape, a.dtype) for a in arrays],
        in_specs=[pl.BlockSpec(memory_space=pltpu.VMEM)] * (len(arrays) + len(others)),
        out_specs=[pl.BlockSpec(memory_space=pltpu.VMEM)] * len(arrays),
        input_output_aliases={i: i for i in range(len(arrays))},
        compiler_params=pltpu.CompilerParams(vmem_limit_bytes=VMEM_LIMIT),
    )(*arrays, *others)


def tiles_of(*lead):
    return jax.ShapeDtypeStruct((*lead, TILE, HEAD_DIM), jnp.bfloat16)


def by_kind(plan, t_count, s_count, queries, keys, values, lists, table):
    frames, slots = plan.frames, plan.slots
    pair_flops = 4 * TILE * TILE * HEAD_DIM

    def to_frame(array, step):
        pairs = [(z, z ^ step) for z in range(frames)]
        return array if step == 0 else lax.ppermute(array, "blk", pairs)

    def to_slot(array, step):
        pairs = [(s, s ^ step) for s in range(slots)]
        return array if step == 0 else lax.ppermute(array, MESH_TAIL, pairs)

    def halo(array, step):
        pairs = [(z, z + step) for z in range(frames) if 0 <= z + step < frames]
        return lax.ppermute(array, "blk", pairs)

    packed = call(
        functools.partial(pack_kernel, plan, (t_count, s_count)),
        [tiles_of(t_count, 3)] * frames + [tiles_of(s_count, 3)] * slots,
        (table, queries, keys, values),
        "saaa",
        "v" * (frames + slots),
        [pltpu.SemaphoreType.DMA((frames + slots,))],
    )
    arrived = [to_frame(block, step) for step, block in zip(plan.steps(0), packed[:frames])]
    here = [to_slot(block, step) for step, block in enumerate(packed[frames:])]
    (joined,) = call(
        functools.partial(join_kernel, plan, s_count),
        [tiles_of(slots, s_count, 2)],
        here,
        "v" * slots,
        "v",
        [pltpu.SemaphoreType.DMA((slots,))],
    )
    below, above = halo(joined, 1), halo(joined, -1)
    own_state = call(
        functools.partial(own_frame_kernel, plan),
        [jax.ShapeDtypeStruct((slots, s_count, TILE, HEAD_DIM), jnp.float32)] * 3,
        (table, lists, *here, joined),
        "ss" + "v" * (slots + 1),
        "vvv",
        flops=s_count * slots * slots * pair_flops,
    )
    (mixed,) = call(
        functools.partial(join_mixed_kernel, plan, t_count),
        [tiles_of(frames, 1, 2)],
        (*arrived, own_state[0]),
        "v" * (frames + 1),
        "v",
        [pltpu.SemaphoreType.DMA((frames,))],
    )
    attended = call(
        functools.partial(temporal_kernel, plan),
        [tiles_of(t_count)] * frames,
        (table, lists, *arrived),
        "ss" + "v" * frames,
        "v" * frames,
        flops=t_count * frames * frames * pair_flops,
    )
    gathered = {0: mixed}
    for bit in sorted((1 << n for n in range(slots.bit_length() - 1)), reverse=True):
        for step in list(gathered):
            block = after([gathered[step]], attended[:1])[0] if step else mixed
            gathered[step | bit] = to_slot(block, bit)
    gathered = [gathered[step] for step in (0, *reversed(range(1, slots)))]
    tiles_ahead = 2 * slots * s_count - 4 * frames - 3 * t_count // 2
    flops_ahead = max(tiles_ahead, 1) * 42 * pair_flops
    attended = call(
        functools.partial(mixed_kernel, plan, t_count),
        [tiles_of(t_count)] * frames,
        (table, lists, *arrived, *gathered, *attended),
        "ss" + "v" * (2 * frames + slots),
        "v" * frames,
        [
            pltpu.VMEM((frames, TILE, HEAD_DIM), jnp.bfloat16),
            pltpu.VMEM((slots * frames, 1, 2, TILE, HEAD_DIM), jnp.bfloat16),
            pltpu.VMEM((frames, TILE, HEAD_DIM), jnp.bfloat16),
            pltpu.SemaphoreType.DMA((frames + slots,)),
        ],
        flops=flops_ahead,
        in_place={2 + frames + slots + i: i for i in range(frames)},
    )
    attended = [attended[0], *after(attended[1:-1], (below, above)), attended[-1]]
    pieces = [to_frame(block, step) for step, block in zip(plan.steps(0), attended)]

    def attend_slots(steps, *earlier):
        return call(
            functools.partial(halo_kernel, plan, steps, 1 if earlier or s_count % 2 else 2),
            [tiles_of(s_count)] * len(steps),
            (table, lists, *(here[step] for step in steps), below, above, *own_state, *earlier),
            "ss" + "v" * (len(steps) + 5 + len(earlier)),
            "v" * len(steps),
            flops=s_count * len(steps) * 2 * slots * pair_flops,
        )

    half = slots // 2
    away = attend_slots(range(half, slots))
    near = attend_slots(range(half), away[0])
    ahead = pieces[-1:] if t_count > s_count else pieces[1:]
    attended = [near[0], *after(near[1:], ahead), *away]
    pieces += [to_slot(block, step) for step, block in enumerate(attended)]
    (out,) = call(
        functools.partial(unpack_kernel, plan, (t_count, s_count)),
        [pltpu.HBM((TILE, plan.heads * HEAD_DIM), jnp.bfloat16)],
        (table, *pieces),
        "s" + "v" * len(pieces),
        "v",
        [pltpu.SemaphoreType.DMA],
    )
    return out


def capacities(heads, frames, slots):
    low, high = heads // 4, heads - heads // 4

    def chunks_for(fewest, most):
        over_frames = max(-(-most // frames), 1)
        shared = max(fewest, (over_frames - 1) * frames)
        left = heads - fewest - (over_frames * frames - shared)
        return over_frames, max(-(-left // slots), 1)

    pairs, begins = [(chunks_for(high + 1, heads)[0], chunks_for(0, low)[1])], []
    for t in range(low + 1, high + 1):
        if t % frames == 1 or t == low + 1:
            begins.append((t, len(pairs)))
            pairs.append(chunks_for(t, min(-(-t // frames) * frames, high)))
    return pairs, begins + [(high + 1, 0)]


def kind_plan(queries, keys, values, block_lists):
    heads, tiles, entries = block_lists.shape
    frames = lax.axis_size("blk")
    slots = lax.axis_size(MESH_TAIL)
    plan = Plan(heads, frames, slots, entries)
    pairs, begins = capacities(heads, frames, slots)
    by_tile = jnp.transpose(block_lists, (1, 2, 0))
    table, branch = call(
        functools.partial(table_kernel, plan, pairs, begins),
        [jax.ShapeDtypeStruct((size,), jnp.int32) for size in (plan.table_size, 1)],
        (by_tile,),
        "v",
        "ss",
        [pltpu.SMEM((heads // 16,), jnp.int32)],
    )
    lists = by_tile.reshape(tiles * entries, heads)
    branches = [functools.partial(by_kind, plan, t, s) for t, s in pairs]
    return lax.switch(branch[0], branches, queries, keys, values, lists, table)


def per_device(queries, keys, values, block_lists):
    slots = lax.axis_size(MESH_TAIL)
    whole_tiles = queries.shape[0] == TILE and slots == FRAME_TILES
    frames = lax.axis_size("blk")
    if whole_tiles and frames & (frames - 1) == 0 and frames * slots == block_lists.shape[1]:
        return kind_plan(queries, keys, values, block_lists)
    return gathered_plan(queries, keys, values, block_lists)


def solution(mesh):
    in_specs = (
        P(("grp", "blk", "head", "sub"), None),
        P(("grp", "blk", "head", "sub"), None),
        P(("grp", "blk", "head", "sub"), None),
        P(),
    )
    out_specs = P(("grp", "blk", "head", "sub"), None)
    return jax.shard_map(
        per_device, mesh=mesh, in_specs=in_specs, out_specs=out_specs, check_vma=False
    )
```

```python
import functools
import math

import jax
import jax.numpy as jnp
from jax import lax
from jax.experimental import pallas as pl
from jax.experimental.pallas import tpu as pltpu
from jax.sharding import PartitionSpec as P

HEADS = 32
HEAD_DIM = 128
TILE = 128
FRAME_TILES = 4


NEG_FLOOR = -1e30


def query_rows(block_lists, first_head, heads_here, query_tokens):
    tile_ids = jnp.arange(block_lists.shape[1], dtype=jnp.int32)
    lists_local = lax.dynamic_slice_in_dim(block_lists, first_head, heads_here, 0)
    tile_mask = jnp.any(lists_local[:, :, :, None] == tile_ids, axis=2).astype(jnp.bfloat16)
    query_onehot = ((query_tokens // TILE)[:, None] == tile_ids[None, :]).astype(jnp.bfloat16)
    listed = jnp.einsum("qi,hij->hqj", query_onehot, tile_mask, preferred_element_type=jnp.float32)
    return listed.astype(jnp.bfloat16)


def attend_block(state_now, key_block, value_block, allowed, query_local, score_scale):
    top_old, total_old, accum_old = state_now
    scores = (
        jnp.einsum("qhd,khd->hqk", query_local, key_block, preferred_element_type=jnp.float32)
        * score_scale
    )
    top_new = jnp.maximum(top_old, jnp.max(jnp.where(allowed, scores, NEG_FLOOR), axis=2))
    factor = jnp.exp(top_old - top_new)
    weights = jnp.where(allowed, jnp.exp(scores - top_new[:, :, None]), 0.0)
    total_new = total_old * factor + jnp.sum(weights, axis=2)
    product = jnp.einsum(
        "hqk,khd->qhd",
        weights.astype(jnp.bfloat16),
        value_block,
        preferred_element_type=jnp.float32,
    )
    accum_new = accum_old * jnp.transpose(factor)[:, :, None] + product
    return (top_new, total_new, accum_new)


def make_step(query_local, listed_rows, key_token, block_len, tile_total):
    score_scale = 1.0 / math.sqrt(HEAD_DIM)
    tile_ids = jnp.arange(tile_total, dtype=jnp.int32)

    def fold_step(state_now, piece, first_row):
        key_piece, value_piece = piece
        block_count = key_piece.shape[0] // block_len

        def one_block(block_index, state_in):
            key_block = lax.dynamic_slice_in_dim(key_piece, block_index * block_len, block_len, 0)
            value_block = lax.dynamic_slice_in_dim(
                value_piece, block_index * block_len, block_len, 0
            )
            positions = block_index * block_len + jnp.arange(block_len, dtype=jnp.int32)
            key_tiles = key_token(positions) // TILE
            key_onehot = (tile_ids[:, None] == key_tiles[None, :]).astype(jnp.bfloat16)
            allowed = (
                jnp.einsum(
                    "hqj,jk->hqk", listed_rows, key_onehot, preferred_element_type=jnp.float32
                )
                > 0.5
            )
            result = attend_block(
                state_in, key_block, value_block, allowed, query_local, score_scale
            )
            return result

        return lax.fori_loop(0, block_count, one_block, state_now)

    return fold_step


def start_state(heads_here, block_len):
    top_all = jnp.full((heads_here, block_len), NEG_FLOOR, jnp.float32)
    total_all = jnp.zeros((heads_here, block_len), jnp.float32)
    accum_all = jnp.zeros((block_len, heads_here, HEAD_DIM), jnp.float32)
    return (top_all, total_all, accum_all)


def normalize(state_end):
    top_all, total_all, accum_all = state_end
    return (accum_all / jnp.transpose(total_all)[:, :, None]).astype(jnp.bfloat16)


def gathered_plan(queries, keys, values, block_lists):
    row_count, col_count = queries.shape
    n_head = lax.axis_size("head")
    n_sub = lax.axis_size("sub")
    blk_index = lax.axis_index("blk")
    head_index = lax.axis_index("head")
    sub_index = lax.axis_index("sub")
    tile_total = block_lists.shape[1]
    heads_here = HEADS // (n_head * n_sub)
    block_len = row_count * n_head * n_sub

    def inward(tensor):
        return tensor.reshape(1, 1, row_count, n_head, n_sub, heads_here * HEAD_DIM)

    query_six, keys_six, values_six = (
        lax.all_to_all(
            lax.all_to_all(inward(queries), "head", split_axis=3, concat_axis=1, tiled=True),
            "sub",
            split_axis=4,
            concat_axis=0,
            tiled=True,
        ),
        lax.all_to_all(
            lax.all_to_all(inward(keys), "head", split_axis=3, concat_axis=1, tiled=True),
            "sub",
            split_axis=4,
            concat_axis=0,
            tiled=True,
        ),
        lax.all_to_all(
            lax.all_to_all(inward(values), "head", split_axis=3, concat_axis=1, tiled=True),
            "sub",
            split_axis=4,
            concat_axis=0,
            tiled=True,
        ),
    )
    query_local = query_six.reshape(block_len, heads_here, HEAD_DIM)
    keys_local = keys_six.reshape(block_len, heads_here, HEAD_DIM)
    values_local = values_six.reshape(block_len, heads_here, HEAD_DIM)

    def key_token(positions):
        source_dev = positions // block_len
        within = positions % block_len
        sub_source = within // (n_head * row_count)
        head_source = within // row_count % n_head
        offset = within % row_count
        return ((source_dev * n_head + head_source) * n_sub + sub_source) * row_count + offset

    query_tokens = key_token(blk_index * block_len + jnp.arange(block_len, dtype=jnp.int32))
    first_head = (head_index * n_sub + sub_index) * heads_here
    listed_rows = query_rows(block_lists, first_head, heads_here, query_tokens)
    fold_step = make_step(query_local, listed_rows, key_token, block_len, tile_total)
    state_end = fold_step(
        start_state(heads_here, block_len),
        (
            lax.all_gather(keys_local, "blk", axis=0, tiled=True),
            lax.all_gather(values_local, "blk", axis=0, tiled=True),
        ),
        jnp.int32(0),
    )
    result_rows = normalize(state_end)
    attended = result_rows.reshape(n_sub, n_head, row_count, 1, 1, heads_here * HEAD_DIM)
    returned = lax.all_to_all(
        lax.all_to_all(attended, "head", split_axis=1, concat_axis=3, tiled=True),
        "sub",
        split_axis=0,
        concat_axis=4,
        tiled=True,
    )
    return returned.reshape(row_count, col_count)


MESH_TAIL = ("head", "sub")
EXP2_SCALE = math.log2(math.e) / math.sqrt(HEAD_DIM)
VMEM_LIMIT = 16 * 1024 * 1024
MIXED_TILES = 4


class Plan:
    def __init__(self, heads, frames, slots, entries):
        self.heads, self.frames, self.slots, self.entries = heads, frames, slots, entries
        self.over_slots_at = heads
        self.pure_at = 2 * heads
        self.mixed_at = 2 * heads + 1
        self.spatial_at = 2 * heads + 2
        self.frame_at = 2 * heads + 3
        self.slot_at = 2 * heads + 4
        self.table_size = 2 * heads + 5

    def sizes(self, kind):
        return (self.frames, self.slots)[kind]

    def head_at(self, kind, table_ref, group, index):
        return table_ref[(0, self.over_slots_at)[kind] + index * self.sizes(kind) + group]

    def group(self, kind, table_ref, step):
        return table_ref[(self.frame_at, self.slot_at)[kind]] ^ step

    def heads_in_group(self, kind, table_ref, group):
        size = self.sizes(kind)
        return (table_ref[(self.pure_at, self.spatial_at)[kind]] - group + size - 1) // size

    def steps(self, kind):
        others = range(1, self.sizes(kind))
        return [0, *others] if kind else [0, *reversed(others)]


def head_columns(head):
    return pl.ds(pl.multiple_of(head * HEAD_DIM, HEAD_DIM), HEAD_DIM)


def table_kernel(plan, pairs, begins, lists_ref, table_ref, branch_ref, mask_ref):
    lists = lists_ref[...]
    tiles = lax.broadcasted_iota(jnp.int32, lists.shape, 0)
    other_slot = ((lists ^ tiles) & (plan.slots - 1)).astype(jnp.float32)
    spatial = jnp.sum(jnp.sum(other_slot, axis=0), axis=0, keepdims=True) > 0
    lanes = lax.broadcasted_iota(jnp.int32, spatial.shape, 1)
    for place in range(plan.heads // 16):
        bit = jnp.where(lanes // 16 == place, jnp.int32(1) << (lanes % 16), 0)
        bits = jnp.where(spatial, bit, 0).astype(jnp.float32)
        mask_ref[place] = jnp.sum(bits).astype(jnp.int32)
    spatial_total = jnp.sum(spatial.astype(jnp.float32)).astype(jnp.int32)
    temporal_total = plan.heads - spatial_total
    branch, chunks, last = 0, pairs[0][0], 0
    for first, place in begins:
        reached = (temporal_total >= first).astype(jnp.int32)
        branch += reached * (place - last)
        chunks += reached * (pairs[place][0] - pairs[last][0])
        last = place
    mixed = (chunks - 1) * plan.frames
    shared = lax.max(temporal_total, mixed)
    room = chunks * plan.frames - shared

    def clear(p, _):
        for more in range(8):
            table_ref[8 * p + more] = 0
        return 0

    def place_heads(first, counts):
        t_rank, s_rank = counts
        for h in (4 * first + more for more in range(4)):
            kind = (mask_ref[h // 16] >> (h % 16)) & 1
            s_place = jnp.where(s_rank < room, shared + s_rank, plan.over_slots_at + s_rank - room)
            table_ref[jnp.where(kind == 1, s_place, t_rank)] = h
            t_rank, s_rank = t_rank + 1 - kind, s_rank + kind
        return t_rank, s_rank

    lax.fori_loop(0, plan.heads // 4, clear, 0)
    lax.fori_loop(0, plan.heads // 4, place_heads, (jnp.int32(0), jnp.int32(0)))
    table_ref[plan.pure_at] = lax.min(temporal_total, mixed)
    table_ref[plan.mixed_at] = shared + lax.min(spatial_total, room)
    table_ref[plan.spatial_at] = lax.max(spatial_total - room, 0)
    table_ref[plan.frame_at] = lax.axis_index("blk")
    n_sub = lax.axis_size("sub")
    table_ref[plan.slot_at] = lax.axis_index("head") * n_sub + lax.axis_index("sub")
    branch_ref[0] = branch


def wait_all(ref, sem):
    pltpu.make_async_copy(ref, ref, sem).wait()


def pack_kernel(plan, counts, table_ref, q_ref, k_ref, v_ref, *rest):
    outs, sems = rest[:-1], rest[-1]
    steps = [(kind, step) for kind in range(2) for step in plan.steps(kind)]
    for sem, (kind, step) in enumerate(steps):
        group = plan.group(kind, table_ref, step)

        def one(index, _, kind=kind, group=group, sem=sem):
            columns = head_columns(plan.head_at(kind, table_ref, group, index))
            for place, ref in enumerate((q_ref, k_ref, v_ref)):
                pltpu.make_async_copy(
                    ref.at[:, columns], outs[sem].at[index, place], sems.at[sem]
                ).start()
            return 0

        lax.fori_loop(0, counts[kind], one, 0)
    for sem, out_ref in enumerate(outs):
        wait_all(out_ref, sems.at[sem])


def turn_keys(kv_ref, place, count):
    def turn(work, _):
        step, index = work // count, lax.rem(work, count)
        kv_ref[step, index, place] = kv_ref[step, index, place].T
        return 0

    lax.fori_loop(0, kv_ref.shape[0] * count, turn, 0)


def join_kernel(plan, count, *refs):
    pieces, out_ref, sems = refs[: plan.slots], refs[-2], refs[-1]
    copy_pieces(
        [(piece.at[:, pl.ds(1, 2)], out_ref.at[step]) for step, piece in enumerate(pieces)], sems
    )
    turn_keys(out_ref, 0, count)


def join_mixed_kernel(plan, count, *refs):
    pieces, out_ref, sems = refs[: plan.frames], refs[-2], refs[-1]
    copy_pieces(
        [
            (piece.at[count - 1, pl.ds(1, 2)], out_ref.at[step, 0])
            for step, piece in zip(plan.steps(0), pieces)
        ],
        sems,
    )
    turn_keys(out_ref, 0, 1)


def attend_tiles(queries, keys, values, biases, before=None, turned=True):
    scores = lax.dot_general(
        jnp.concatenate(queries, 0),
        jnp.concatenate(keys, 1 if turned else 0),
        (((1,), (0 if turned else 1,)), ((), ())),
        preferred_element_type=jnp.float32,
    )
    rows, tops = [], []
    for a, bias in enumerate(biases):
        tiles = [
            scores[a * TILE : (a + 1) * TILE, b * TILE : (b + 1) * TILE] + bias[b]
            for b in range(len(keys))
        ]
        top = jnp.max(functools.reduce(jnp.maximum, tiles), axis=1, keepdims=True)
        if before is not None:
            top = jnp.maximum(top, before[a][0])
        weights = [jnp.exp2((tile - top) * EXP2_SCALE) for tile in tiles]
        tops.append(top)
        rows.append(jnp.concatenate([w.astype(jnp.bfloat16) for w in weights], 1))
    values = jnp.concatenate(values, 0)
    accum = jnp.dot(
        jnp.concatenate(rows, 0),
        jnp.concatenate([values, jnp.ones_like(values)], 1),
        preferred_element_type=jnp.float32,
    )
    states = []
    for a, top in enumerate(tops):
        part = accum[a * TILE : (a + 1) * TILE, :HEAD_DIM]
        total = accum[a * TILE : (a + 1) * TILE, HEAD_DIM:]
        if before is not None:
            factor = jnp.exp2((before[a][0] - top) * EXP2_SCALE)
            total, part = total + before[a][1] * factor, part + before[a][2] * factor
        states.append((top, total, part))
    return states


def normalized(state):
    return (state[2] / state[1]).astype(jnp.bfloat16)


def bias_where(attended):
    return jnp.where(attended, jnp.float32(0), jnp.float32(NEG_FLOOR))


def copy_pieces(pieces, sems):
    copies = [pltpu.make_async_copy(a, b, sems.at[i]) for i, (a, b) in enumerate(pieces)]
    for copy in copies:
        copy.start()
    for copy in copies:
        copy.wait()


def listed_places(plan, lists_ref, head, query_tile, place_of):
    first = query_tile * plan.entries
    listed = jnp.int32(0)
    places, biases = [], []
    for entry in range(plan.entries):
        place = place_of(lists_ref[first + entry, head])
        places.append(place)
        biases.append(bias_where((listed >> place) & 1 == 0))
        listed |= jnp.int32(1) << place
    return places, biases


def temporal_kernel(plan, table_ref, lists_ref, *rest):
    frames, slots = plan.frames, plan.slots
    by_step = [plan.steps(0).index(step) for step in range(frames)]
    tiles = [rest[i] for i in by_step]
    outs = [rest[frames + i] for i in by_step]
    frame, slot = table_ref[plan.frame_at], table_ref[plan.slot_at]

    def one_head(index, _):
        head = plan.head_at(0, table_ref, frame, index)
        biases = []
        for step in range(frames):
            first = ((frame ^ step) * slots + slot) * plan.entries
            listed = jnp.int32(0)
            for entry in range(plan.entries):
                listed |= jnp.int32(1) << (lists_ref[first + entry, head] // slots)
            biases.append(
                [bias_where((listed >> (frame ^ other)) & 1 == 1) for other in range(frames)]
            )
        states = attend_tiles(
            *([tile[index, i] for tile in tiles] for i in range(3)), biases, turned=False
        )
        for out_ref, state in zip(outs, states):
            out_ref[index] = normalized(state)
        return 0

    lax.fori_loop(0, plan.heads_in_group(0, table_ref, frame), one_head, 0)


def mixed_kernel(plan, count, table_ref, lists_ref, *rest):
    frames, slots = plan.frames, plan.slots
    tiles, gathered = rest[:frames], rest[frames : frames + slots]
    outs = rest[-4 - frames : -4]
    q_ref, kv_ref, result_ref, sems = rest[-4:]
    copy_pieces(
        [(tile.at[count - 1, 0], q_ref.at[step]) for step, tile in zip(plan.steps(0), tiles)]
        + [
            (block, kv_ref.at[pl.ds(step * frames, frames)])
            for step, block in zip((0, *reversed(range(1, slots))), gathered)
        ],
        sems,
    )
    frame, slot = table_ref[plan.frame_at], table_ref[plan.slot_at]
    head = plan.head_at(0, table_ref, frame, count - 1)

    def some_tiles(body, _):
        for step in (body * MIXED_TILES + more for more in range(MIXED_TILES)):
            places, biases = listed_places(
                plan,
                lists_ref,
                head,
                (frame ^ step) * slots + slot,
                lambda tile: (lax.rem(tile, slots) ^ slot) * frames + (tile // slots ^ frame),
            )
            (state,) = attend_tiles(
                [q_ref[step]],
                [kv_ref[place, 0, 0] for place in places],
                [kv_ref[place, 0, 1] for place in places],
                [biases],
            )
            result_ref[step] = normalized(state)
        return 0

    lax.fori_loop(0, frames // MIXED_TILES, some_tiles, 0)
    copy_pieces(
        [(result_ref.at[step], out.at[count - 1]) for step, out in zip(plan.steps(0), outs)], sems
    )


def spatial_biases(plan, table_ref, lists_ref, head, step, places):
    slots = plan.slots
    frame, slot = table_ref[plan.frame_at], table_ref[plan.slot_at]
    first = (frame * slots + (slot ^ step)) * plan.entries
    listed = jnp.int32(0)
    for entry in range(plan.entries):
        tile = lists_ref[first + entry, head]
        place = (tile // slots - frame + 1) * slots + (lax.rem(tile, slots) ^ slot)
        listed |= jnp.int32(1) << place
    return [bias_where((listed >> place) & 1 == 1) for place in places]


def own_frame_kernel(plan, table_ref, lists_ref, *rest):
    slots = plan.slots
    here, joined, outs = rest[:slots], rest[slots], rest[slots + 1 :]
    slot = table_ref[plan.slot_at]

    def one_head(index, _):
        head = plan.head_at(1, table_ref, slot, index)
        states = attend_tiles(
            [tile[index, 0] for tile in here],
            [joined[step, index, 0] for step in range(slots)],
            [joined[step, index, 1] for step in range(slots)],
            [
                spatial_biases(plan, table_ref, lists_ref, head, step, range(slots, 2 * slots))
                for step in range(slots)
            ],
        )
        for step, state in enumerate(states):
            for out_ref, value in zip(outs, state):
                out_ref[step, index] = jnp.broadcast_to(value, (TILE, HEAD_DIM))
        return 0

    lax.fori_loop(0, plan.heads_in_group(1, table_ref, slot), one_head, 0)


def halo_kernel(plan, steps, at_once, table_ref, lists_ref, *rest):
    slots, ways = plan.slots, len(steps)
    queries, (below, above) = rest[:ways], rest[ways : ways + 2]
    top_ref, total_ref, sum_ref = rest[ways + 2 : ways + 5]
    outs = rest[-ways:]
    slot = table_ref[plan.slot_at]
    places = [*range(slots), *range(2 * slots, 3 * slots)]

    def one_head(index):
        head = plan.head_at(1, table_ref, slot, index)
        states = attend_tiles(
            [query_ref[index, 0] for query_ref in queries],
            [ref[step, index, 0] for ref in (below, above) for step in range(slots)],
            [ref[step, index, 1] for ref in (below, above) for step in range(slots)],
            [spatial_biases(plan, table_ref, lists_ref, head, step, places) for step in steps],
            [
                (top_ref[step, index], total_ref[step, index], sum_ref[step, index])
                for step in steps
            ],
        )
        for out_ref, state in zip(outs, states):
            out_ref[index] = normalized(state)

    heads_here = plan.heads_in_group(1, table_ref, slot)

    def some_heads(body, _):
        for more in range(at_once):
            one_head(lax.min(body * at_once + more, heads_here - 1))
        return 0

    lax.fori_loop(0, (heads_here + at_once - 1) // at_once, some_heads, 0)


def unpack_kernel(plan, counts, table_ref, *rest):
    pieces, out_ref, sem = list(rest[:-2]), rest[-2], rest[-1]
    for kind, count in enumerate(counts):
        for step in plan.steps(kind):
            piece = pieces.pop(0)
            group = plan.group(kind, table_ref, step)

            def one(index, _, kind=kind, piece=piece, group=group):
                columns = head_columns(plan.head_at(kind, table_ref, group, index))
                pltpu.make_async_copy(piece.at[index], out_ref.at[:, columns], sem).start()
                return 0

            lax.fori_loop(0, plan.heads_in_group(kind, table_ref, group), one, 0)
            if kind == 0:
                filled = (count - 1) * plan.frames + group < table_ref[plan.mixed_at]
                lax.fori_loop(count - 1, count - 1 + filled.astype(jnp.int32), one, 0)
    wait_all(out_ref, sem)


SPACES = {"s": pltpu.SMEM, "v": pltpu.VMEM, "a": pl.ANY}


def call(kernel, outs, operands, places, out_place, scratch=(), flops=0, in_place=None):
    nbytes = sum(math.prod(o.shape) * 2 for o in outs) * 2
    return pl.pallas_call(
        kernel,
        out_shape=outs,
        in_specs=[pl.BlockSpec(memory_space=SPACES[c]) for c in places],
        out_specs=[pl.BlockSpec(memory_space=SPACES[c]) for c in out_place],
        scratch_shapes=list(scratch),
        input_output_aliases=in_place or {},
        compiler_params=pltpu.CompilerParams(vmem_limit_bytes=VMEM_LIMIT),
        cost_estimate=pl.CostEstimate(flops=flops, bytes_accessed=nbytes, transcendentals=0),
    )(*operands)


def after(arrays, others):
    if not arrays or not others:
        return arrays
    return pl.pallas_call(
        lambda *refs: None,
        out_shape=[jax.ShapeDtypeStruct(a.shape, a.dtype) for a in arrays],
        in_specs=[pl.BlockSpec(memory_space=pltpu.VMEM)] * (len(arrays) + len(others)),
        out_specs=[pl.BlockSpec(memory_space=pltpu.VMEM)] * len(arrays),
        input_output_aliases={i: i for i in range(len(arrays))},
        compiler_params=pltpu.CompilerParams(vmem_limit_bytes=VMEM_LIMIT),
    )(*arrays, *others)


def tiles_of(*lead):
    return jax.ShapeDtypeStruct((*lead, TILE, HEAD_DIM), jnp.bfloat16)


def by_kind(plan, t_count, s_count, queries, keys, values, lists, table):
    frames, slots = plan.frames, plan.slots
    pair_flops = 4 * TILE * TILE * HEAD_DIM

    def to_frame(array, step):
        pairs = [(z, z ^ step) for z in range(frames)]
        return array if step == 0 else lax.ppermute(array, "blk", pairs)

    def to_slot(array, step):
        pairs = [(s, s ^ step) for s in range(slots)]
        return array if step == 0 else lax.ppermute(array, MESH_TAIL, pairs)

    def halo(array, step):
        pairs = [(z, z + step) for z in range(frames) if 0 <= z + step < frames]
        return lax.ppermute(array, "blk", pairs)

    packed = call(
        functools.partial(pack_kernel, plan, (t_count, s_count)),
        [tiles_of(t_count, 3)] * frames + [tiles_of(s_count, 3)] * slots,
        (table, queries, keys, values),
        "saaa",
        "v" * (frames + slots),
        [pltpu.SemaphoreType.DMA((frames + slots,))],
    )
    arrived = [to_frame(block, step) for step, block in zip(plan.steps(0), packed[:frames])]
    here = [to_slot(block, step) for step, block in enumerate(packed[frames:])]
    (joined,) = call(
        functools.partial(join_kernel, plan, s_count),
        [tiles_of(slots, s_count, 2)],
        here,
        "v" * slots,
        "v",
        [pltpu.SemaphoreType.DMA((slots,))],
    )
    below, above = halo(joined, 1), halo(joined, -1)
    own_state = call(
        functools.partial(own_frame_kernel, plan),
        [jax.ShapeDtypeStruct((slots, s_count, TILE, HEAD_DIM), jnp.float32)] * 3,
        (table, lists, *here, joined),
        "ss" + "v" * (slots + 1),
        "vvv",
        flops=s_count * slots * slots * pair_flops,
    )
    (mixed,) = call(
        functools.partial(join_mixed_kernel, plan, t_count),
        [tiles_of(frames, 1, 2)],
        (*arrived, own_state[0]),
        "v" * (frames + 1),
        "v",
        [pltpu.SemaphoreType.DMA((frames,))],
    )
    attended = call(
        functools.partial(temporal_kernel, plan),
        [tiles_of(t_count)] * frames,
        (table, lists, *arrived),
        "ss" + "v" * frames,
        "v" * frames,
        flops=t_count * frames * frames * pair_flops,
    )
    gathered = {0: mixed}
    for bit in sorted((1 << n for n in range(slots.bit_length() - 1)), reverse=True):
        for step in list(gathered):
            block = after([gathered[step]], attended[:1])[0] if step else mixed
            gathered[step | bit] = to_slot(block, bit)
    gathered = [gathered[step] for step in (0, *reversed(range(1, slots)))]
    tiles_ahead = 2 * slots * s_count - 4 * frames - 3 * t_count // 2
    flops_ahead = max(tiles_ahead, 1) * 42 * pair_flops
    attended = call(
        functools.partial(mixed_kernel, plan, t_count),
        [tiles_of(t_count)] * frames,
        (table, lists, *arrived, *gathered, *attended),
        "ss" + "v" * (2 * frames + slots),
        "v" * frames,
        [
            pltpu.VMEM((frames, TILE, HEAD_DIM), jnp.bfloat16),
            pltpu.VMEM((slots * frames, 1, 2, TILE, HEAD_DIM), jnp.bfloat16),
            pltpu.VMEM((frames, TILE, HEAD_DIM), jnp.bfloat16),
            pltpu.SemaphoreType.DMA((frames + slots,)),
        ],
        flops=flops_ahead,
        in_place={2 + frames + slots + i: i for i in range(frames)},
    )
    attended = [attended[0], *after(attended[1:-1], (below, above)), attended[-1]]
    pieces = [to_frame(block, step) for step, block in zip(plan.steps(0), attended)]

    def attend_slots(steps, *earlier):
        return call(
            functools.partial(halo_kernel, plan, steps, 1 if earlier or s_count % 2 else 2),
            [tiles_of(s_count)] * len(steps),
            (table, lists, *(here[step] for step in steps), below, above, *own_state, *earlier),
            "ss" + "v" * (len(steps) + 5 + len(earlier)),
            "v" * len(steps),
            flops=s_count * len(steps) * 2 * slots * pair_flops,
        )

    half = slots // 2
    away = attend_slots(range(half, slots))
    near = attend_slots(range(half), away[0])
    ahead = pieces[-1:] if t_count > s_count else pieces[1:]
    attended = [near[0], *after(near[1:], ahead), *away]
    pieces += [to_slot(block, step) for step, block in enumerate(attended)]
    (out,) = call(
        functools.partial(unpack_kernel, plan, (t_count, s_count)),
        [pltpu.HBM((TILE, plan.heads * HEAD_DIM), jnp.bfloat16)],
        (table, *pieces),
        "s" + "v" * len(pieces),
        "v",
        [pltpu.SemaphoreType.DMA],
    )
    return out


def capacities(heads, frames, slots):
    low, high = heads // 4, heads - heads // 4

    def chunks_for(fewest, most):
        over_frames = max(-(-most // frames), 1)
        shared = max(fewest, (over_frames - 1) * frames)
        left = heads - fewest - (over_frames * frames - shared)
        return over_frames, max(-(-left // slots), 1)

    pairs, begins = [(chunks_for(high + 1, heads)[0], chunks_for(0, low)[1])], []
    for t in range(low + 1, high + 1):
        if t % frames == 1 or t == low + 1:
            begins.append((t, len(pairs)))
            pairs.append(chunks_for(t, min(-(-t // frames) * frames, high)))
    return pairs, begins + [(high + 1, 0)]


def kind_plan(queries, keys, values, block_lists):
    heads, tiles, entries = block_lists.shape
    frames = lax.axis_size("blk")
    slots = lax.axis_size(MESH_TAIL)
    plan = Plan(heads, frames, slots, entries)
    pairs, begins = capacities(heads, frames, slots)
    by_tile = jnp.transpose(block_lists, (1, 2, 0))
    table, branch = call(
        functools.partial(table_kernel, plan, pairs, begins),
        [jax.ShapeDtypeStruct((size,), jnp.int32) for size in (plan.table_size, 1)],
        (by_tile,),
        "v",
        "ss",
        [pltpu.SMEM((heads // 16,), jnp.int32)],
    )
    lists = by_tile.reshape(tiles * entries, heads)
    branches = [functools.partial(by_kind, plan, t, s) for t, s in pairs]
    return lax.switch(branch[0], branches, queries, keys, values, lists, table)


def per_device(queries, keys, values, block_lists):
    slots = lax.axis_size(MESH_TAIL)
    whole_tiles = queries.shape[0] == TILE and slots == FRAME_TILES
    frames = lax.axis_size("blk")
    if whole_tiles and frames & (frames - 1) == 0 and frames * slots == block_lists.shape[1]:
        return kind_plan(queries, keys, values, block_lists)
    return gathered_plan(queries, keys, values, block_lists)


def solution(mesh):
    in_specs = (
        P(("grp", "blk", "head", "sub"), None),
        P(("grp", "blk", "head", "sub"), None),
        P(("grp", "blk", "head", "sub"), None),
        P(),
    )
    out_specs = P(("grp", "blk", "head", "sub"), None)
    return jax.shard_map(
        per_device, mesh=mesh, in_specs=in_specs, out_specs=out_specs, check_vma=False
    )
```
